32 devices in a mesh: batch: 4 (over x, core), patch: 8 (over z, y).
Axes of the slice: x: 2, y: 2, z: 4, core: 2. Of those that a mesh axis runs over, the one named last changes fastest.
Arguments:
- latent: bfloat16 [64, 64, 1280], P(('batch', 'patch')), parts along dimension 0, may hold values from -100 to 100
- conv_weight: bfloat16 [3, 3, 1280, 1280], P(None, None, 'patch'), may hold values from -0.25 to 0.25
- channel_bias: float32 [1280], P('patch'), may hold values from -6 to 6
- w_query: bfloat16 [1280, 1280], P('patch'), may hold values from -0.5 to 0.5
- w_key: bfloat16 [1280, 1280], P('patch'), may hold values from -0.5 to 0.5
- w_value: bfloat16 [1280, 1280], P('patch'), may hold values from -0.15625 to 0.15625
- w_out: bfloat16 [1280, 1280], P('patch'), may hold values from -0.15625 to 0.15625
Outputs:
- output: bfloat16 [64, 64, 1280], P(('batch', 'patch')), parts along dimension 0
The draws below stay inside these ranges and needn't reach their ends.
There are 4 independent parts, one for each index of `batch`. The reference program is written for one: setup_inputs(seed, part) draws one part's arguments, and reference() takes and returns one part's arrays. A program takes and returns all parts, laid end to end along the dimension named above; an argument that names none is the same for every part. Nothing has to cross between parts.
All inputs are finite; a program needn't handle non-finite values.
Results may differ from the reference program's by a relative error of at most 0.015.
Values may be sent and summed in bfloat16 or wider, within the bound.
No kernel may reach another device: no remote copies, remote signals or barrier semaphores. Data moves between devices by JAX's collectives and lax.ppermute only.
A program may use at most 128 MiB of HBM per device.

```python
import math
import jax
import jax.numpy as jnp
from jax import lax

C = 1280
HEADS = 20
HEAD_DIM = 64
GROUPS = 32
COLS = 64
ROWS = 16


def shared_query(key):
    return jax.random.normal(jax.random.fold_in(key, 7), (C, C), jnp.float32) * (1.5 / math.sqrt(C))


def draw_w_query(key, part):
    return jnp.clip(shared_query(key), -0.5, 0.5).astype(jnp.bfloat16)


def draw_w_key(key, part):
    fresh = jax.random.normal(jax.random.fold_in(key, 13), (C, C), jnp.float32) * (1.5 / math.sqrt(C))
    return jnp.clip(fresh, -0.5, 0.5).astype(jnp.bfloat16)


def draw_conv_weight(key, part):
    stream = jax.random.fold_in(key, 41)
    raw = jax.random.normal(stream, (3, 3, C, C), jnp.float32) * (4.0 / math.sqrt(9 * C))
    return jnp.clip(raw, -0.25, 0.25).astype(jnp.bfloat16)


def draw_latent(key, part):
    streams = jax.random.split(jax.random.fold_in(key, 29), 9)
    position = jnp.arange(ROWS, dtype=jnp.float32) / max(ROWS - 1, 1)
    channel_scale = jnp.exp(jax.random.uniform(streams[1], (C,), jnp.float32, math.log(0.3), math.log(3.0)))
    group_offset = jax.random.normal(streams[8], (GROUPS,), jnp.float32) * 1.5
    channel_mean = jax.random.normal(streams[2], (C,), jnp.float32) * 0.3 + jnp.repeat(group_offset, C // GROUPS)
    roughness = jnp.exp(jax.random.uniform(streams[3], (ROWS, COLS, 1), jnp.float32, -0.7, 0.7))
    base = jax.random.normal(streams[0], (ROWS, COLS, C), jnp.float32)
    rising = jnp.exp(math.log(3.0) * position)
    mean_rise = jnp.exp(math.log(3.0) * position)
    field = base * rising[:, None, None] * roughness * channel_scale + channel_mean * mean_rise[:, None, None]
    return jnp.clip(field, -100.0, 100.0).astype(jnp.bfloat16)


def level_of(stream_key, dims, shards, smallest, high):
    def one(axis_at, parts):
        heights = jax.random.uniform(jax.random.fold_in(jax.random.fold_in(stream_key, 6), axis_at), (parts,), jnp.float32, smallest / len(shards), high / len(shards))
        return jnp.repeat(jnp.exp(heights), dims[axis_at] // parts).reshape((-1,) + (1,) * (len(dims) - axis_at - 1))

    level = one(*shards[0])
    for cut in shards[1:]:
        level = level * one(*cut)
    return level


def centred(rng, dims, scale, limit, cuts=(), kind=jnp.bfloat16):
    drawn = scale * jax.random.normal(rng, dims, jnp.float32)
    if cuts:
        drawn = drawn * level_of(rng, dims, cuts, -0.22, 0.18)
    return jnp.clip(drawn, -limit, limit).astype(kind)


def setup_inputs(seed: int = 0, part: int = 0) -> dict:
    key_list = jax.random.split(jax.random.key(seed), 8)
    own_keys = jax.random.split(jax.random.fold_in(key_list[7], part), 8)
    latent = draw_latent(jax.random.fold_in(jax.random.fold_in(key_list[7], part), 71), part)
    conv_weight = draw_conv_weight(jax.random.fold_in(key_list[7], 71), part)
    channel_bias = centred(key_list[2], (C,), 1.0, 6.0, ((0, 8),), jnp.float32)
    w_query = draw_w_query(jax.random.fold_in(key_list[7], 71), part)
    w_key = draw_w_key(jax.random.fold_in(key_list[7], 71), part)
    w_value = centred(key_list[5], (C, C), C ** -0.5, 0.15625, ((0, 8),))
    w_out = centred(key_list[6], (C, C), C ** -0.5, 0.15625, ((0, 8),))
    return {"latent": latent, "conv_weight": conv_weight, "channel_bias": channel_bias, "w_query": w_query, "w_key": w_key, "w_value": w_value, "w_out": w_out}


epsilon = 1e-05

def contract(left, right):
    return lax.dot_general(left, right, (((1,), (1,)), ((), ())), preferred_element_type=jnp.float32)

def group_norm(values):
    grouped = values.reshape(-1, GROUPS, C // GROUPS)
    centre = lax.optimization_barrier(jnp.mean(grouped, axis=(0, 2), keepdims=True))
    spread = lax.optimization_barrier(jnp.mean(jnp.square(grouped - centre), axis=(0, 2), keepdims=True))
    return ((grouped - centre) * lax.rsqrt(spread + epsilon)).reshape(values.shape)

def convolve(padded, kernel, row_count):
    running = jnp.zeros((row_count * COLS, kernel.shape[2]), jnp.float32)
    for row_shift in range(3):
        for col_shift in range(3):
            window = padded[row_shift:row_shift + row_count, col_shift:col_shift + COLS, :].reshape(-1, C)
            running = running + contract(window, kernel[row_shift, col_shift])
    return running

def attend(queries, key_all, value_all):
    query_heads = queries.reshape(-1, HEADS, HEAD_DIM).transpose(1, 0, 2)
    key_heads = key_all.reshape(-1, HEADS, HEAD_DIM).transpose(1, 0, 2)
    value_heads = value_all.reshape(-1, HEADS, HEAD_DIM).transpose(1, 0, 2)

    def one_head(triple):
        query_one, key_one, value_one = triple
        scores = jnp.dot(query_one, key_one.T, preferred_element_type=jnp.float32) * HEAD_DIM ** (-0.5)
        row_peak = lax.optimization_barrier(jnp.max(scores, axis=1, keepdims=True))
        unnormalized = jnp.exp(scores - row_peak)
        row_total = lax.optimization_barrier(jnp.sum(unnormalized, axis=1, keepdims=True))
        mixture = jnp.dot(unnormalized.astype(jnp.bfloat16), value_one, preferred_element_type=jnp.float32)
        return mixture / row_total
    heads_out = lax.map(one_head, (query_heads, key_heads, value_heads))
    return heads_out.transpose(1, 0, 2).reshape(-1, C).astype(jnp.bfloat16)

def reference(latent, conv_weight, channel_bias, w_query, w_key, w_value, w_out):
    inputs = latent.astype(jnp.float32)
    activated = jax.nn.silu(group_norm(inputs)).astype(jnp.bfloat16)
    padded = jnp.pad(activated, ((1, 1), (1, 1), (0, 0)))
    convolved = convolve(padded, conv_weight, ROWS).reshape(ROWS, COLS, C)
    hidden = (inputs + convolved + channel_bias).astype(jnp.bfloat16)
    hidden = lax.optimization_barrier(hidden)
    residual = hidden.astype(jnp.float32).reshape(-1, C)
    normed = group_norm(residual).astype(jnp.bfloat16)
    queries = contract(normed, w_query).astype(jnp.bfloat16)
    key_all = contract(normed, w_key).astype(jnp.bfloat16)
    value_all = contract(normed, w_value).astype(jnp.bfloat16)
    attended = attend(queries, key_all, value_all)
    output = (residual + contract(attended, w_out)).astype(jnp.bfloat16)
    return output.reshape(ROWS, COLS, C)
```

```python
import functools

import jax
import jax.numpy as jnp
from jax import lax
from jax.experimental import pallas as pl
from jax.experimental.pallas import tpu as pltpu
from jax.sharding import PartitionSpec as P

C = 1280
HEADS = 20
HEAD_DIM = 64
GROUPS = 32
SPAN = C // GROUPS
OUTER = 4
SET_HEADS = HEADS // OUTER
SET_CHANNELS = SET_HEADS * HEAD_DIM
SHARED = SET_HEADS // 2
EPSILON = 1e-05
VMEM_LIMIT = 48 * 1024 * 1024

f32 = jnp.float32
bf16 = jnp.bfloat16

NT = (((1,), (1,)), ((), ()))
NN = (((1,), (0,)), ((), ()))


def dot(left, right, dims=NN, precision=None):
    return lax.dot_general(left, right, dims, preferred_element_type=f32, precision=precision)


def exact(left, right, dims=NN):
    return dot(left, right, dims, lax.Precision.HIGHEST)


def conv_kernel(n, columns, me_ref, *refs):
    pieces = refs[:n]
    kernel_ref, bias_ref, normed_ref = refs[n : n + 3]
    hidden_refs = refs[n + 3 : 2 * n + 3]
    act_ref, kept_ref, hidden_ref = refs[2 * n + 3 :]
    block = pieces[0].shape[0]
    positions = block * n
    own = normed_ref.shape[0]
    inner = n // OUTER
    me = me_ref[0]
    entries = float(positions * SPAN)

    def source(index):
        return gather_source(me, index, inner)

    chunk = 16
    steps = block // chunk

    def add(step, total):
        for piece in pieces:
            total = total + piece[pl.ds(step * chunk, chunk), :].astype(f32)
        return total

    member = (
        lax.broadcasted_iota(jnp.int32, (C, 128), 0) // SPAN
        == lax.broadcasted_iota(jnp.int32, (C, 128), 1)
    ).astype(f32)

    def group_mean(total):
        summed = jnp.sum(total, axis=0, keepdims=True)
        per_group = exact(jnp.broadcast_to(summed, (8, C)), member) / entries
        return exact(per_group, member, NT)[0:1, :]

    zero = jnp.zeros((chunk, C), f32)
    centre = group_mean(lax.fori_loop(0, steps, add, zero))

    def add_square(step, total):
        for piece in pieces:
            away = piece[pl.ds(step * chunk, chunk), :].astype(f32) - centre
            total = total + away * away
        return total

    spread = group_mean(lax.fori_loop(0, steps, add_square, zero))
    half_scale = 0.5 * lax.rsqrt(spread + EPSILON)

    act_ref[0:columns, :] = jnp.zeros((columns, C), bf16)
    act_ref[positions + columns :, :] = jnp.zeros((columns, C), bf16)
    starts = [pl.multiple_of(source(index) * block, block) for index in range(n)]

    def activate(step, carry):
        for start, piece in zip(starts, pieces):
            half = (piece[pl.ds(step * chunk, chunk), :].astype(f32) - centre) * half_scale
            value = half + half * jnp.tanh(half)
            row = pl.multiple_of(columns + start + step * chunk, chunk)
            act_ref[pl.ds(row, chunk), :] = value.astype(bf16)
        return carry

    lax.fori_loop(0, steps, activate, 0)

    choose = (
        lax.broadcasted_iota(jnp.int32, (own, C), 0) + me * own
        == lax.broadcasted_iota(jnp.int32, (own, C), 1)
    ).astype(bf16)
    for start, piece in zip(starts, pieces):
        kept_ref[:, pl.ds(start, block)] = dot(choose, piece[...], NT)

    wide = 256
    column = lax.broadcasted_iota(jnp.int32, (own, wide), 1) % columns
    bias = bias_ref[...]
    for at in range(0, positions, wide):
        taps = dot(kernel_ref[0], act_ref[at : at + wide, :], NT)
        for shift in (1, 2):
            low = at + shift * columns
            taps = taps + dot(kernel_ref[shift], act_ref[low : low + wide, :], NT)
        before = jnp.where(column > 0, pltpu.roll(taps[0:own], 1, 1), 0.0)
        after = jnp.where(column < columns - 1, pltpu.roll(taps[2 * own :], wide - 1, 1), 0.0)
        convolved = taps[own : 2 * own] + before + after
        hidden = kept_ref[:, at : at + wide] + convolved + bias
        hidden_ref[:, at : at + wide] = hidden.astype(bf16).astype(f32)

    for shift, target in enumerate(hidden_refs):
        start = pl.multiple_of(lax.rem(me + shift, n) * block, block)
        target[...] = hidden_ref[:, pl.ds(start, block)].astype(bf16)

    for low in range(0, own, SPAN):
        group = hidden_ref[low : low + SPAN, :]
        mean = jnp.sum(jnp.sum(group, axis=0, keepdims=True), axis=1, keepdims=True) / entries
        away = group - mean
        square = away * away
        var = jnp.sum(jnp.sum(square, axis=0, keepdims=True), axis=1, keepdims=True) / entries
        hidden_ref[low : low + SPAN, :] = away * lax.rsqrt(var + EPSILON)
    normed_ref[...] = hidden_ref[...].astype(bf16)


def attention_kernel(n, me_ref, *refs):
    pieces = refs[:n]
    weight_ref = refs[n]
    outs = refs[n + 1 : 2 * n + 1]
    normed_ref, query_ref, key_ref, value_ref, sems = refs[2 * n + 1 :]
    own, positions = pieces[0].shape
    inner = n // OUTER
    block = positions // n
    full = (SET_HEADS - 1) // inner * HEAD_DIM
    rows = full + HEAD_DIM
    me = me_ref[0]

    copies = []
    for index, piece in enumerate(pieces):
        row = pl.multiple_of(gather_source(me, index, inner) * own, own)
        copy = pltpu.make_async_copy(piece, normed_ref.at[pl.ds(row, own), :], sems.at[index])
        copy.start()
        copies.append(copy)
    for copy in copies:
        copy.wait()

    wide = 256
    for at in range(0, positions, wide):
        made = dot(weight_ref[...], normed_ref[:, at : at + wide])
        query = made[0:rows].astype(bf16).astype(f32) * HEAD_DIM ** (-0.5)
        query_ref[:, at : at + wide] = query.astype(bf16)
        key_ref[at : at + wide, :] = made[rows : 2 * rows].T.astype(bf16)
        value_ref[:, at : at + wide] = made[2 * rows :].astype(bf16)

    def attend(head, shifts):
        low = head * HEAD_DIM
        starts = [pl.multiple_of(lax.rem(me + shift, n) * block, block) for shift in shifts]
        query = jnp.concatenate(
            [query_ref[low : low + HEAD_DIM, pl.ds(start, block)] for start in starts], axis=1
        )
        scores = dot(key_ref[:, low : low + HEAD_DIM], query)
        peak = jnp.max(scores, axis=0, keepdims=True)
        unnormalized = jnp.exp(scores - peak)
        total = jnp.sum(unnormalized, axis=0, keepdims=True)
        mixture = dot(value_ref[low : low + HEAD_DIM, :], unnormalized.astype(bf16))
        attended = (mixture / total).astype(bf16)
        for place, shift in enumerate(shifts):
            outs[shift][low : low + HEAD_DIM, :] = attended[:, place * block : (place + 1) * block]

    for head in range(full // HEAD_DIM):
        for shift in range(0, n, 2):
            attend(head, (shift, shift + 1))
    shared = list(range(0, n, inner))
    for at in range(0, len(shared), 2):
        attend(full // HEAD_DIM, tuple(shared[at : at + 2]))


def output_kernel(n, me_ref, *refs):
    attended_refs = refs[:n]
    hidden_refs = refs[n : 2 * n]
    mine_ref, other_ref, out_ref = refs[2 * n : 2 * n + 3]
    attended_ref, total_ref = refs[2 * n + 3 :]
    me, half = me_ref[0], me_ref[1]
    inner = n // OUTER
    own = C // n
    heads = (SET_HEADS - 1) // inner
    full = heads * HEAD_DIM
    for shift in range(n):
        origin = lax.rem(me + n - shift, n)
        member = lax.rem(origin, inner)
        base = lax.div(origin, inner) * SET_CHANNELS
        first = member * heads + (member >= inner // 2).astype(jnp.int32)
        row = pl.multiple_of(base + first * HEAD_DIM, HEAD_DIM)
        attended_ref[pl.ds(row, full), :] = attended_refs[shift][0:full, :]
        if shift % inner == 0:
            row = pl.multiple_of(base + SHARED * HEAD_DIM, HEAD_DIM)
            attended_ref[pl.ds(row, HEAD_DIM), :] = attended_refs[shift][full:, :]
        row = pl.multiple_of(origin * own, own)
        total_ref[pl.ds(row, own), :] = hidden_refs[shift][...].astype(f32)
    attended = attended_ref[...]
    part = own // 2
    for weight_ref, which in ((mine_ref, half), (other_ref, 1 - half)):
        made = dot(weight_ref[...], attended)
        for origin in range(n):
            row = pl.multiple_of(origin * own + which * part, 8)
            total_ref[pl.ds(row, part), :] += made[origin * part : (origin + 1) * part]
    out_ref[...] = total_ref[...].T.astype(bf16)


def gather_source(me, index, inner):
    outer_step, inner_step = divmod(index, inner)
    outer_at = lax.rem(lax.div(me, inner) + OUTER - outer_step, OUTER)
    inner_at = lax.rem(lax.rem(me, inner) + inner - inner_step, inner)
    return outer_at * inner + inner_at


def moves(n, inner, outer_step, inner_step):
    pairs = []
    for start in range(n):
        outer_at = (start // inner + outer_step) % OUTER
        inner_at = (start % inner + inner_step) % inner
        pairs.append((start, outer_at * inner + inner_at))
    return pairs


def gather(shard, n):
    inner = n // OUTER
    pieces = []
    along = shard
    for outer_step in range(OUTER):
        if outer_step:
            along = lax.ppermute(along, "patch", moves(n, inner, 1, 0))
        across = along
        pieces.append(across)
        for _ in range(1, inner):
            across = lax.ppermute(across, "patch", moves(n, inner, 0, 1))
            pieces.append(across)
    return pieces


def exchange(blocks, n):
    received = [blocks[0]]
    for shift in range(1, n):
        pairs = [(start, (start + shift) % n) for start in range(n)]
        received.append(lax.ppermute(blocks[shift], "patch", pairs))
    return received


def head_weights(weights, me, n):
    inner = n // OUTER
    own = C // n
    heads = (SET_HEADS - 1) // inner
    member = lax.rem(me, inner)
    if inner == 2:
        rest = own - heads * HEAD_DIM
        whole = lax.dynamic_slice_in_dim(weights, member * rest, own - rest, 1)
        part = lax.dynamic_slice_in_dim(weights, (1 - member) * (own - rest), rest, 1)
        other = lax.ppermute(part, "patch", moves(n, inner, 0, 1))
        first = jnp.where(member == 0, part, other)
        second = jnp.where(member == 0, other, part)
        return jnp.concatenate([whole, first, second], axis=1)
    sets = [list(range(at, at + inner)) for at in range(0, n, inner)]
    every = lax.all_gather(weights, "patch", axis=1, tiled=True, axis_index_groups=sets)
    first = member * heads + (member >= inner // 2).astype(jnp.int32)
    whole = lax.dynamic_slice_in_dim(every, first * HEAD_DIM, heads * HEAD_DIM, 1)
    shared = every[:, SHARED * HEAD_DIM : (SHARED + 1) * HEAD_DIM]
    return jnp.concatenate([whole, shared], axis=1)


def after(values, *others):
    return lax.optimization_barrier((values, *others))[0]


def on_device(latent, conv_weight, channel_bias, w_query, w_key, w_value, w_out):
    rows_local, columns, channels = latent.shape
    n = lax.axis_size("patch")
    inner = n // OUTER
    own = channels // n
    block = rows_local * columns
    positions = block * n
    me = lax.axis_index("patch")
    half = lax.rem(lax.axis_index("batch"), 2)
    place = jnp.stack([me, half]).astype(jnp.int32)
    vmem = pl.BlockSpec(memory_space=pltpu.VMEM)
    smem = pl.BlockSpec(memory_space=pltpu.SMEM)
    anywhere = pl.BlockSpec(memory_space=pl.ANY)
    params = pltpu.CompilerParams(vmem_limit_bytes=VMEM_LIMIT)

    pieces = gather(latent.reshape(block, channels), n)

    ready = pieces[-1]
    weights = jnp.stack([w_query, w_key, w_value])
    weights, w_out = after((weights, w_out), ready)
    weights = head_weights(weights, me, n)
    rows = weights.shape[1]
    weights = weights.reshape(3 * rows, channels)
    w_mine = lax.dynamic_slice_in_dim(w_out, half * (own // 2), own // 2, 0)
    w_mine = lax.all_gather(w_mine, "patch", axis=0, tiled=True)
    swap = [(at, at ^ 1) for at in range(lax.axis_size("batch"))]
    w_other = lax.ppermute(w_mine, "batch", swap)

    made = pl.pallas_call(
        functools.partial(conv_kernel, n, columns),
        out_shape=[jax.ShapeDtypeStruct((own, positions), bf16)]
        + [jax.ShapeDtypeStruct((own, block), bf16)] * n,
        in_specs=[smem] + [vmem] * (n + 2),
        out_specs=[vmem] * (n + 1),
        scratch_shapes=[
            pltpu.VMEM((positions + 2 * columns, channels), bf16),
            pltpu.VMEM((own, positions), f32),
            pltpu.VMEM((own, positions), f32),
        ],
        compiler_params=params,
        cost_estimate=pl.CostEstimate(
            flops=2 * 9 * positions * channels * own,
            bytes_accessed=2 * (positions * channels + 9 * channels * own),
            transcendentals=positions * channels,
        ),
        name="norm_conv_norm",
    )(
        place,
        *pieces,
        conv_weight.reshape(3, 3 * own, channels),
        channel_bias.reshape(own, 1),
    )
    normed, hidden_blocks = made[0], list(made[1:])

    normed_pieces = gather(normed, n)
    hidden_blocks = after(hidden_blocks, normed_pieces[-1])
    hidden_blocks = exchange(hidden_blocks, n)

    full = rows - HEAD_DIM
    attended = pl.pallas_call(
        functools.partial(attention_kernel, n),
        out_shape=[
            jax.ShapeDtypeStruct((rows if shift % inner == 0 else full, block), bf16)
            for shift in range(n)
        ],
        in_specs=[smem] + [anywhere] * n + [vmem],
        out_specs=[vmem] * n,
        scratch_shapes=[
            pltpu.VMEM((channels, positions), bf16),
            pltpu.VMEM((rows, positions), bf16),
            pltpu.VMEM((positions, rows), bf16),
            pltpu.VMEM((rows, positions), bf16),
            pltpu.SemaphoreType.DMA((n,)),
        ],
        compiler_params=params,
        cost_estimate=pl.CostEstimate(
            flops=2 * positions * channels * 3 * rows + 4 * positions * positions * rows,
            bytes_accessed=2 * (positions * channels + 3 * rows * channels),
            transcendentals=positions * positions * rows // HEAD_DIM,
        ),
        name="attention",
    )(place, *normed_pieces, weights)
    attended = exchange(list(attended), n)

    output = pl.pallas_call(
        functools.partial(output_kernel, n),
        out_shape=jax.ShapeDtypeStruct((block, channels), bf16),
        in_specs=[smem] + [vmem] * (2 * n + 2),
        out_specs=vmem,
        scratch_shapes=[
            pltpu.VMEM((channels, block), bf16),
            pltpu.VMEM((channels, block), f32),
        ],
        compiler_params=params,
        cost_estimate=pl.CostEstimate(
            flops=2 * block * channels * channels,
            bytes_accessed=2 * channels * (channels + 3 * block),
            transcendentals=0,
        ),
        name="project",
    )(place, *attended, *hidden_blocks, w_mine, w_other)
    return output.reshape(rows_local, columns, channels)


def solution(mesh):
    return jax.shard_map(
        on_device,
        mesh=mesh,
        in_specs=(
            P(("batch", "patch"), None, None),
            P(None, None, "patch", None),
            P("patch"),
            P("patch", None),
            P("patch", None),
            P("patch", None),
            P("patch", None),
        ),
        out_specs=P(("batch", "patch"), None, None),
        check_vma=False,
    )
```

```python
import functools

import jax
import jax.numpy as jnp
from jax import lax
from jax.experimental import pallas as pl
from jax.experimental.pallas import tpu as pltpu
from jax.sharding import PartitionSpec as P

C = 1280
HEADS = 20
HEAD_DIM = 64
GROUPS = 32
SPAN = C // GROUPS
OUTER = 4
SET_HEADS = HEADS // OUTER
SET_CHANNELS = SET_HEADS * HEAD_DIM
FIXED = 4
EPSILON = 1e-05
VMEM_LIMIT = 48 * 1024 * 1024

f32 = jnp.float32
bf16 = jnp.bfloat16

NT = (((1,), (1,)), ((), ()))
NN = (((1,), (0,)), ((), ()))


def dot(left, right, dims=NN, precision=None):
    return lax.dot_general(left, right, dims, preferred_element_type=f32, precision=precision)


def exact(left, right, dims=NN):
    return dot(left, right, dims, lax.Precision.HIGHEST)


def conv_kernel(columns, place_ref, *refs):
    count = len(refs) - 6
    pieces = refs[:count]
    kernel_ref, bias_ref = refs[count : count + 2]
    out_refs = refs[count + 2 : count + 4]
    act_ref, kept_ref = refs[count + 4 :]
    block = pieces[0].shape[0]
    positions = block * count
    own = out_refs[0].shape[0]
    me = place_ref[0]
    entries = float(positions * SPAN)
    chunk = 16
    steps = block // chunk
    starts = [
        pl.multiple_of(place_ref[FIXED + index] * (2 * block) + (index % 2) * block, block)
        for index in range(count)
    ]

    def add(step, total):
        for piece in pieces:
            total = total + piece[pl.ds(step * chunk, chunk), :].astype(f32)
        return total

    member = (
        lax.broadcasted_iota(jnp.int32, (C, 128), 0) // SPAN
        == lax.broadcasted_iota(jnp.int32, (C, 128), 1)
    ).astype(f32)

    def group_mean(total):
        summed = jnp.sum(total, axis=0, keepdims=True)
        per_group = exact(jnp.broadcast_to(summed, (8, C)), member) / entries
        return exact(per_group, member, NT)[0:1, :]

    zero = jnp.zeros((chunk, C), f32)
    centre = group_mean(lax.fori_loop(0, steps, add, zero))

    def add_square(step, total):
        for piece in pieces:
            away = piece[pl.ds(step * chunk, chunk), :].astype(f32) - centre
            total = total + away * away
        return total

    spread = group_mean(lax.fori_loop(0, steps, add_square, zero))
    half_scale = 0.5 * lax.rsqrt(spread + EPSILON)

    act_ref[0:columns, :] = jnp.zeros((columns, C), bf16)
    act_ref[positions + columns :, :] = jnp.zeros((columns, C), bf16)

    def activate(step, carry):
        for start, piece in zip(starts, pieces):
            half = (piece[pl.ds(step * chunk, chunk), :].astype(f32) - centre) * half_scale
            value = half + half * jnp.tanh(half)
            row = pl.multiple_of(columns + start + step * chunk, chunk)
            act_ref[pl.ds(row, chunk), :] = value.astype(bf16)
        return carry

    lax.fori_loop(0, steps, activate, 0)

    choose = (
        lax.broadcasted_iota(jnp.int32, (own, C), 0) + me * own
        == lax.broadcasted_iota(jnp.int32, (own, C), 1)
    ).astype(bf16)
    for index in range(0, count, 2):
        pair = jnp.concatenate([pieces[index][...], pieces[index + 1][...]], axis=0)
        start = pl.multiple_of(starts[index], 2 * block)
        kept_ref[:, pl.ds(start, 2 * block)] = dot(choose, pair, NT)

    wide = 256
    column = lax.broadcasted_iota(jnp.int32, (own, wide), 1) % columns
    bias = bias_ref[...]
    for at in range(0, positions, wide):
        taps = dot(kernel_ref[0], act_ref[at : at + wide, :], NT)
        for shift in (1, 2):
            low = at + shift * columns
            taps = taps + dot(kernel_ref[shift], act_ref[low : low + wide, :], NT)
        before = jnp.where(column > 0, pltpu.roll(taps[0:own], 1, 1), 0.0)
        after_ = jnp.where(column < columns - 1, pltpu.roll(taps[2 * own :], wide - 1, 1), 0.0)
        convolved = taps[own : 2 * own] + before + after_
        hidden = kept_ref[:, at : at + wide] + convolved + bias
        which, low = divmod(at, positions // 2)
        out_refs[which][:, low : low + wide] = hidden.astype(bf16)


def attention_kernel(inner, place_ref, *refs):
    count = len(refs) - 8 - OUTER
    pieces = refs[:count]
    weight_ref = refs[count]
    outs = refs[count + 1 : count + 1 + OUTER]
    kept_ref = refs[count + 1 + OUTER]
    hidden_ref, normed_ref, query_ref, key_ref, value_ref, sems = refs[count + 2 + OUTER :]
    own, part = pieces[0].shape
    n = count // 2
    positions = 2 * part
    block = positions // n
    me, outer_at, inner_at = place_ref[0], place_ref[1], place_ref[2]
    entries = float(positions * SPAN)

    copies = []
    for index, piece in enumerate(pieces):
        row = pl.multiple_of(place_ref[FIXED + index] * own, own)
        low = (index % 2) * part
        target = hidden_ref.at[pl.ds(row, own), low : low + part]
        copy = pltpu.make_async_copy(piece, target, sems.at[index])
        copy.start()
        copies.append(copy)
    for copy in copies:
        copy.wait()

    kept_ref[...] = hidden_ref[:, pl.ds(pl.multiple_of(me * block, block), block)]
    for at in range(0, C, 2 * SPAN):
        pair = hidden_ref[at : at + 2 * SPAN, :].astype(f32)
        scaled = []
        for low in (0, SPAN):
            group = pair[low : low + SPAN]
            mean = jnp.sum(jnp.sum(group, axis=0, keepdims=True), axis=1, keepdims=True) / entries
            away = group - mean
            square = jnp.sum(away * away, axis=0, keepdims=True)
            var = jnp.sum(square, axis=1, keepdims=True) / entries
            scaled.append(away * lax.rsqrt(var + EPSILON))
        normed_ref[at : at + 2 * SPAN, :] = jnp.concatenate(scaled, axis=0).astype(bf16)

    wide = 256
    for at in range(0, positions, wide):
        made = dot(weight_ref[SET_CHANNELS:, :], normed_ref[:, at : at + wide])
        for head in range(SET_HEADS):
            low = head * HEAD_DIM
            key_ref[head, at : at + wide, :] = made[low : low + HEAD_DIM].T.astype(bf16)
        value_ref[:, at : at + wide] = made[SET_CHANNELS:].astype(bf16)

    for at in range(0, OUTER, 2):
        normed = []
        for step in (at, at + 1):
            target = lax.rem(outer_at + step, OUTER) * inner + inner_at
            normed.append(normed_ref[:, pl.ds(pl.multiple_of(target * block, block), block)])
        made = dot(weight_ref[:SET_CHANNELS, :], jnp.concatenate(normed, axis=1))
        scaled = made.astype(bf16).astype(f32) * HEAD_DIM ** (-0.5)
        query_ref[:, at * block : (at + 2) * block] = scaled.astype(bf16)

    for at in range(0, OUTER, 2):
        for head in range(SET_HEADS):
            low = head * HEAD_DIM
            query = query_ref[low : low + HEAD_DIM, at * block : (at + 2) * block]
            scores = dot(key_ref[head], query)
            peak = jnp.max(scores, axis=0, keepdims=True)
            unnormalized = jnp.exp(scores - peak)
            total = jnp.sum(unnormalized, axis=0, keepdims=True)
            mixture = dot(value_ref[low : low + HEAD_DIM, :], unnormalized.astype(bf16))
            attended = (mixture / total).astype(bf16)
            outs[at][low : low + HEAD_DIM, :] = attended[:, :block]
            outs[at + 1][low : low + HEAD_DIM, :] = attended[:, block:]


def output_kernel(n, splits, place_ref, *refs):
    attended_refs = refs[:OUTER]
    hidden_ref = refs[OUTER]
    weight_refs = refs[OUTER + 1 : OUTER + 1 + splits]
    out_ref, attended_ref, total_ref = refs[OUTER + 1 + splits :]
    outer_at, mine = place_ref[1], place_ref[3]
    for step in range(OUTER):
        origin = lax.rem(outer_at + OUTER - step, OUTER)
        row = pl.multiple_of(origin * SET_CHANNELS, SET_CHANNELS)
        attended_ref[pl.ds(row, SET_CHANNELS), :] = attended_refs[step][...]
    total_ref[...] = hidden_ref[...].astype(f32)
    attended = attended_ref[...]
    own = C // n
    part = own // splits
    for step, weight_ref in enumerate(weight_refs):
        which = jnp.bitwise_xor(mine, step)
        made = dot(weight_ref[...], attended)
        for origin in range(n):
            row = pl.multiple_of(origin * own + which * part, 8)
            total_ref[pl.ds(row, part), :] += made[origin * part : (origin + 1) * part]
    out_ref[...] = total_ref[...].T.astype(bf16)


def ring_of(n):
    inner = n // OUTER
    path = [(0, 0)]
    for outer_at in range(OUTER):
        across = range(1, inner) if outer_at % 2 == 0 else range(inner - 1, 0, -1)
        path += [(outer_at, inner_at) for inner_at in across]
    path += [(outer_at, 0) for outer_at in range(OUTER - 1, 0, -1)]
    return [outer_at * inner + inner_at for outer_at, inner_at in path]


def pieces_of(n):
    far = n // 2
    return [0] + [away for step in range(1, far) for away in (-step, step)] + [far]


def sources_of(n):
    ring = ring_of(n)
    table = []
    for device in range(n):
        at = ring.index(device)
        table.append([ring[(at + away) % n] for away in pieces_of(n) for _ in (0, 1)])
    return table


def gather(halves, n):
    ring = ring_of(n)
    forward = [(ring[at], ring[(at + 1) % n]) for at in range(n)]
    backward = [(target, start) for start, target in forward]
    far = n // 2
    found = {(0, 0): halves[0], (1, 0): halves[1]}
    for step in range(1, far + 1):
        for half in (0, 1):
            for sign, pairs in ((-1, forward), (1, backward)):
                if step == far and (half == 0) != (sign == -1):
                    continue
                found[half, sign * step] = lax.ppermute(
                    found[half, sign * (step - 1)], "patch", pairs
                )
    found[0, far] = found[0, -far]
    return [found[half, away] for away in pieces_of(n) for half in (0, 1)]


def swap_weights(weights, core, n, ready):
    if n // OUTER != 2:
        return None
    rows = weights.reshape(-1, C)
    part = rows.shape[0] // 2
    own_half = after(lax.dynamic_slice_in_dim(rows, core * part, part, 0), *ready)
    return lax.ppermute(own_half, "patch", [(at, at ^ 1) for at in range(n)])


def set_weights(weights, first, inner_at, core, n, ready):
    inner = n // OUTER
    if inner == 2:
        first = after(first, ready)
        cores = [(at, at ^ 1) for at in range(lax.axis_size("batch"))]
        second = lax.ppermute(first, "batch", cores)
        low = jnp.where(core == 0, first, second)
        high = jnp.where(core == 0, second, first)
        other = jnp.concatenate([low, high], axis=0).reshape(weights.shape)
        return jnp.concatenate(
            [jnp.where(inner_at == 0, weights, other), jnp.where(inner_at == 0, other, weights)],
            axis=1,
        )
    sets = [list(range(at, at + inner)) for at in range(0, n, inner)]
    return lax.all_gather(weights, "patch", axis=1, tiled=True, axis_index_groups=sets)


def output_weights(w_out, mine, splits, ready):
    part = w_out.shape[0] // splits
    shard = after(lax.dynamic_slice_in_dim(w_out, mine * part, part, 0), *ready)
    parts = [lax.all_gather(shard, "patch", axis=0, tiled=True)]
    batch = lax.axis_size("batch")
    step = splits // 2
    while step:
        swap = [(at, at ^ step) for at in range(batch)]
        parts = parts + [lax.ppermute(one, "batch", swap) for one in parts]
        step //= 2
    order = [0]
    step = splits // 2
    while step:
        order = order + [one ^ step for one in order]
        step //= 2
    return [parts[order.index(at)] for at in range(splits)]


def after(value, *ready):
    anywhere = pl.BlockSpec(memory_space=pl.ANY)
    return pl.pallas_call(
        lambda *refs: None,
        out_shape=jax.ShapeDtypeStruct(value.shape, value.dtype),
        in_specs=[anywhere] * (1 + len(ready)),
        out_specs=anywhere,
        input_output_aliases={0: 0},
        name="after",
    )(value, *ready)


def on_device(latent, conv_weight, channel_bias, w_query, w_key, w_value, w_out):
    rows_local, columns, channels = latent.shape
    n = lax.axis_size("patch")
    inner = n // OUTER
    own = channels // n
    block = rows_local * columns
    positions = block * n
    splits = 4 if own % 32 == 0 else 2
    me = lax.axis_index("patch")
    batch_at = lax.axis_index("batch")
    inner_at = lax.rem(me, inner)
    mine = lax.rem(batch_at, splits)
    fixed = jnp.stack([me, lax.div(me, inner), inner_at, mine]).astype(jnp.int32)
    sources = jnp.asarray(sources_of(n), jnp.int32)
    place = jnp.concatenate([fixed, lax.dynamic_index_in_dim(sources, me, 0, keepdims=False)])
    vmem = pl.BlockSpec(memory_space=pltpu.VMEM)
    smem = pl.BlockSpec(memory_space=pltpu.SMEM)
    anywhere = pl.BlockSpec(memory_space=pl.ANY)
    params = pltpu.CompilerParams(vmem_limit_bytes=VMEM_LIMIT)

    whole = latent.reshape(block, channels)
    pieces = gather((whole[: block // 2], whole[block // 2 :]), n)

    weights = jnp.stack([w_query, w_key, w_value])
    core = lax.rem(batch_at, 2)
    first = swap_weights(weights, core, n, pieces[-5:])
    out_parts = output_weights(w_out, mine, splits, pieces[-5:])

    hidden = pl.pallas_call(
        functools.partial(conv_kernel, columns),
        out_shape=[jax.ShapeDtypeStruct((own, positions // 2), bf16)] * 2,
        in_specs=[smem] + [vmem] * (2 * n + 2),
        out_specs=[vmem] * 2,
        scratch_shapes=[
            pltpu.VMEM((positions + 2 * columns, channels), bf16),
            pltpu.VMEM((own, positions), f32),
        ],
        compiler_params=params,
        cost_estimate=pl.CostEstimate(
            flops=2 * 9 * positions * channels * own,
            bytes_accessed=2 * (positions * channels + 9 * channels * own),
            transcendentals=positions * channels,
        ),
        name="norm_conv",
    )(
        place,
        *pieces,
        conv_weight.reshape(3, 3 * own, channels),
        channel_bias.reshape(own, 1),
    )

    hidden_pieces = gather(tuple(hidden), n)
    weights = set_weights(weights, first, inner_at, core, n, hidden_pieces[4])
    weights = weights.reshape(3 * SET_CHANNELS, channels)

    *attended, kept = pl.pallas_call(
        functools.partial(attention_kernel, inner),
        out_shape=[jax.ShapeDtypeStruct((SET_CHANNELS, block), bf16)] * OUTER
        + [jax.ShapeDtypeStruct((channels, block), bf16)],
        in_specs=[smem] + [anywhere] * (2 * n) + [vmem],
        out_specs=[vmem] * (OUTER + 1),
        scratch_shapes=[
            pltpu.VMEM((channels, positions), bf16),
            pltpu.VMEM((channels, positions), bf16),
            pltpu.VMEM((SET_CHANNELS, OUTER * block), bf16),
            pltpu.VMEM((SET_HEADS, positions, HEAD_DIM), bf16),
            pltpu.VMEM((SET_CHANNELS, positions), bf16),
            pltpu.SemaphoreType.DMA((2 * n,)),
        ],
        compiler_params=params,
        cost_estimate=pl.CostEstimate(
            flops=2 * positions * channels * 3 * SET_CHANNELS
            + 4 * positions * OUTER * block * SET_CHANNELS,
            bytes_accessed=2 * (positions * channels + 3 * SET_CHANNELS * channels),
            transcendentals=positions * OUTER * block * SET_HEADS,
        ),
        name="attention",
    )(place, *hidden_pieces, weights)

    received = [attended[0]]
    for step in range(1, OUTER):
        pairs = [(at, (at + step * inner) % n) for at in range(n)]
        received.append(lax.ppermute(attended[step], "patch", pairs))

    output = pl.pallas_call(
        functools.partial(output_kernel, n, splits),
        out_shape=jax.ShapeDtypeStruct((block, channels), bf16),
        in_specs=[smem] + [vmem] * (OUTER + 1 + splits),
        out_specs=vmem,
        scratch_shapes=[
            pltpu.VMEM((channels, block), bf16),
            pltpu.VMEM((channels, block), f32),
        ],
        compiler_params=params,
        cost_estimate=pl.CostEstimate(
            flops=2 * block * channels * channels,
            bytes_accessed=2 * channels * (channels + 3 * block),
            transcendentals=0,
        ),
        name="project",
    )(place, *received, kept, *out_parts)
    return output.reshape(rows_local, columns, channels)


def solution(mesh):
    return jax.shard_map(
        on_device,
        mesh=mesh,
        in_specs=(
            P(("batch", "patch"), None, None),
            P(None, None, "patch", None),
            P("patch"),
            P("patch", None),
            P("patch", None),
            P("patch", None),
            P("patch", None),
        ),
        out_specs=P(("batch", "patch"), None, None),
        check_vma=False,
    )
```

```python
import functools

import jax
import jax.numpy as jnp
from jax import lax
from jax.experimental import pallas as pl
from jax.experimental.pallas import tpu as pltpu
from jax.sharding import PartitionSpec as P

C = 1280
HEADS = 20
HEAD_DIM = 64
GROUPS = 32
SPAN = C // GROUPS
OUTER = 4
SET_HEADS = HEADS // OUTER
SET_CHANNELS = SET_HEADS * HEAD_DIM
FIXED = 5
GRANULE = 32
EPSILON = 1e-05
VMEM_LIMIT = 48 * 1024 * 1024

f32 = jnp.float32
bf16 = jnp.bfloat16

NT = (((1,), (1,)), ((), ()))
NN = (((1,), (0,)), ((), ()))


def dot(left, right, dims=NN, precision=None):
    return lax.dot_general(left, right, dims, preferred_element_type=f32, precision=precision)


def exact(left, right, dims=NN):
    return dot(left, right, dims, lax.Precision.HIGHEST)


def conv_kernel(columns, place_ref, *refs):
    count = len(refs) - 8
    pieces = refs[:count]
    source_ref, bias_ref = refs[count : count + 2]
    out_refs = refs[count + 2 : count + 4]
    act_ref, kept_ref, kernel_ref, sem = refs[count + 4 :]
    load = pltpu.make_async_copy(source_ref, kernel_ref, sem)
    load.start()
    block = pieces[0].shape[0]
    positions = block * count
    own = out_refs[0].shape[0]
    me = place_ref[0]
    entries = float(positions * SPAN)
    chunk = 16
    steps = block // chunk
    starts = [
        pl.multiple_of(place_ref[FIXED + index] * (2 * block) + (index % 2) * block, block)
        for index in range(count)
    ]

    def add(step, total):
        for piece in pieces:
            total = total + piece[pl.ds(step * chunk, chunk), :].astype(f32)
        return total

    member = (
        lax.broadcasted_iota(jnp.int32, (C, 128), 0) // SPAN
        == lax.broadcasted_iota(jnp.int32, (C, 128), 1)
    ).astype(f32)

    def group_mean(total):
        summed = jnp.sum(total, axis=0, keepdims=True)
        per_group = exact(jnp.broadcast_to(summed, (8, C)), member) / entries
        return exact(per_group, member, NT)[0:1, :]

    zero = jnp.zeros((chunk, C), f32)
    centre = group_mean(lax.fori_loop(0, steps, add, zero))

    def add_square(step, total):
        for piece in pieces:
            away = piece[pl.ds(step * chunk, chunk), :].astype(f32) - centre
            total = total + away * away
        return total

    spread = group_mean(lax.fori_loop(0, steps, add_square, zero))
    half_scale = 0.5 * lax.rsqrt(spread + EPSILON)

    act_ref[0:columns, :] = jnp.zeros((columns, C), bf16)
    act_ref[positions + columns :, :] = jnp.zeros((columns, C), bf16)

    def activate(step, carry):
        for start, piece in zip(starts, pieces):
            half = (piece[pl.ds(step * chunk, chunk), :].astype(f32) - centre) * half_scale
            value = half + half * jnp.tanh(half)
            row = pl.multiple_of(columns + start + step * chunk, chunk)
            act_ref[pl.ds(row, chunk), :] = value.astype(bf16)
        return carry

    lax.fori_loop(0, steps, activate, 0)

    choose = (
        lax.broadcasted_iota(jnp.int32, (own, C), 0) + me * own
        == lax.broadcasted_iota(jnp.int32, (own, C), 1)
    ).astype(bf16)
    for index in range(0, count, 2):
        pair = jnp.concatenate([pieces[index][...], pieces[index + 1][...]], axis=0)
        start = pl.multiple_of(starts[index], 2 * block)
        kept_ref[:, pl.ds(start, 2 * block)] = dot(choose, pair, NT)

    load.wait()
    wide = 256
    column = lax.broadcasted_iota(jnp.int32, (own, wide), 1) % columns
    bias = bias_ref[...]
    for at in range(0, positions, wide):
        taps = dot(kernel_ref[0], act_ref[at : at + wide, :], NT)
        for shift in (1, 2):
            low = at + shift * columns
            taps = taps + dot(kernel_ref[shift], act_ref[low : low + wide, :], NT)
        before = jnp.where(column > 0, pltpu.roll(taps[0:own], 1, 1), 0.0)
        after_ = jnp.where(column < columns - 1, pltpu.roll(taps[2 * own :], wide - 1, 1), 0.0)
        convolved = taps[own : 2 * own] + before + after_
        hidden = kept_ref[:, at : at + wide] + convolved + bias
        which, low = divmod(at, positions // 2)
        out_refs[which][:, low : low + wide] = hidden.astype(bf16)


def attention_kernel(count, inner, place_ref, *refs):
    pieces = refs[:count]
    parts = refs[count : -8 - OUTER]
    outs = refs[-8 - OUTER : -8]
    kept_ref, hidden_ref, normed_ref, weight_ref, query_ref, key_ref, value_ref, sems = refs[-8:]
    own, part = pieces[0].shape
    n = count // 2
    positions = 2 * part
    block = positions // n
    me, outer_at, inner_at = place_ref[0], place_ref[1], place_ref[2]
    entries = float(positions * SPAN)

    copies = []
    for index, piece in enumerate(pieces):
        row = pl.multiple_of(place_ref[FIXED + index] * own, own)
        low = (index % 2) * part
        target = hidden_ref.at[pl.ds(row, own), low : low + part]
        copy = pltpu.make_async_copy(piece, target, sems.at[index])
        copy.start()
        copies.append(copy)
    loads = []

    def load(source, row):
        loads.append(pltpu.make_async_copy(source, weight_ref.at[pl.ds(row, source.shape[0]), :], sems.at[count]))
        loads[-1].start()

    if inner == 2:
        for kind in range(3):
            row = kind * SET_CHANNELS + inner_at * own
            load(parts[kind], pl.multiple_of(row, GRANULE))
        quarters = quarter_starts(3 * own)
        for step, part_ref in enumerate(parts[3:]):
            which = jnp.bitwise_xor(place_ref[4], step)
            first = jnp.int32(quarters[0])
            for at in range(1, 4):
                first = jnp.where(which == at, quarters[at], first)
            for at in range(part_ref.shape[0] // GRANULE):
                granule = first + at
                kind = lax.div(granule, own // GRANULE)
                row = kind * SET_CHANNELS + (1 - inner_at) * own
                row = row + lax.rem(granule, own // GRANULE) * GRANULE
                load(part_ref.at[at * GRANULE : (at + 1) * GRANULE, :], pl.multiple_of(row, GRANULE))
    else:
        load(parts[0], 0)
    for copy in copies:
        copy.wait()

    kept_ref[...] = hidden_ref[:, pl.ds(pl.multiple_of(me * block, block), block)]
    for at in range(0, C, 2 * SPAN):
        pair = hidden_ref[at : at + 2 * SPAN, :].astype(f32)
        scaled = []
        for low in (0, SPAN):
            group = pair[low : low + SPAN]
            mean = jnp.sum(jnp.sum(group, axis=0, keepdims=True), axis=1, keepdims=True) / entries
            away = group - mean
            square = jnp.sum(away * away, axis=0, keepdims=True)
            var = jnp.sum(square, axis=1, keepdims=True) / entries
            scaled.append(away * lax.rsqrt(var + EPSILON))
        normed_ref[at : at + 2 * SPAN, :] = jnp.concatenate(scaled, axis=0).astype(bf16)

    for copy in loads:
        copy.wait()
    wide = 256
    for at in range(0, positions, wide):
        made = dot(weight_ref[SET_CHANNELS:, :], normed_ref[:, at : at + wide])
        for head in range(SET_HEADS):
            low = head * HEAD_DIM
            key_ref[head, at : at + wide, :] = made[low : low + HEAD_DIM].T.astype(bf16)
        value_ref[:, at : at + wide] = made[SET_CHANNELS:].astype(bf16)

    for at in range(0, OUTER, 2):
        normed = []
        for step in (at, at + 1):
            target = lax.rem(outer_at + step, OUTER) * inner + inner_at
            normed.append(normed_ref[:, pl.ds(pl.multiple_of(target * block, block), block)])
        made = dot(weight_ref[:SET_CHANNELS, :], jnp.concatenate(normed, axis=1))
        scaled = made.astype(bf16).astype(f32) * HEAD_DIM ** (-0.5)
        query_ref[:, at * block : (at + 2) * block] = scaled.astype(bf16)

    for at in range(0, OUTER, 2):
        for head in range(SET_HEADS):
            low = head * HEAD_DIM
            query = query_ref[low : low + HEAD_DIM, at * block : (at + 2) * block]
            scores = dot(key_ref[head], query)
            peak = jnp.max(scores, axis=0, keepdims=True)
            unnormalized = jnp.exp(scores - peak)
            total = jnp.sum(unnormalized, axis=0, keepdims=True)
            mixture = dot(value_ref[low : low + HEAD_DIM, :], unnormalized.astype(bf16))
            attended = (mixture / total).astype(bf16)
            outs[at][low : low + HEAD_DIM, :] = attended[:, :block]
            outs[at + 1][low : low + HEAD_DIM, :] = attended[:, block:]


def output_kernel(n, place_ref, *refs):
    attended_refs = refs[:OUTER]
    hidden_ref = refs[OUTER]
    weight_refs = refs[OUTER + 1 : OUTER + 3]
    out_ref, attended_ref, total_ref = refs[OUTER + 3 :]
    outer_at, core = place_ref[1], place_ref[3]
    for step in range(OUTER):
        origin = lax.rem(outer_at + OUTER - step, OUTER)
        row = pl.multiple_of(origin * SET_CHANNELS, SET_CHANNELS)
        attended_ref[pl.ds(row, SET_CHANNELS), :] = attended_refs[step][...]
    total_ref[...] = hidden_ref[...].astype(f32)
    attended = attended_ref[...]
    own = C // n
    part = own // 2
    for which, weight_ref in zip((core, 1 - core), weight_refs):
        made = dot(weight_ref[...], attended)
        for origin in range(n):
            row = pl.multiple_of(origin * own + which * part, 8)
            total_ref[pl.ds(row, part), :] += made[origin * part : (origin + 1) * part]
    out_ref[...] = total_ref[...].T.astype(bf16)


def ring_of(n):
    inner = n // OUTER
    path = [(0, 0)]
    for outer_at in range(OUTER):
        across = range(1, inner) if outer_at % 2 == 0 else range(inner - 1, 0, -1)
        path += [(outer_at, inner_at) for inner_at in across]
    path += [(outer_at, 0) for outer_at in range(OUTER - 1, 0, -1)]
    return [outer_at * inner + inner_at for outer_at, inner_at in path]


def pieces_of(n):
    far = n // 2
    return [0] + [away for step in range(1, far) for away in (-step, step)] + [far]


def sources_of(n):
    ring = ring_of(n)
    table = []
    for device in range(n):
        at = ring.index(device)
        table.append([ring[(at + away) % n] for away in pieces_of(n) for _ in (0, 1)])
    return table


def gather(halves, n):
    ring = ring_of(n)
    forward = [(ring[at], ring[(at + 1) % n]) for at in range(n)]
    backward = [(target, start) for start, target in forward]
    far = n // 2
    found = {(0, 0): halves[0], (1, 0): halves[1]}
    for step in range(1, far + 1):
        for half in (0, 1):
            for sign, pairs in ((-1, forward), (1, backward)):
                if step == far and (half == 0) != (sign == -1):
                    continue
                found[half, sign * step] = lax.ppermute(
                    found[half, sign * (step - 1)], "patch", pairs
                )
    found[0, far] = found[0, -far]
    return [found[half, away] for away in pieces_of(n) for half in (0, 1)]


def swap_weights(weights, core, side, n, ready):
    rows = jnp.concatenate(weights, axis=0)
    quarters = jnp.asarray(quarter_starts(rows.shape[0]), jnp.int32)
    start = lax.dynamic_index_in_dim(quarters, 2 * core + side, 0, keepdims=False) * GRANULE
    own_part = after(lax.dynamic_slice_in_dim(rows, start, quarter_rows(rows.shape[0]), 0), *ready)
    return lax.ppermute(own_part, "patch", [(at, at ^ 1) for at in range(n)])


def spread_weights(first, ready):
    batch = lax.axis_size("batch")
    across, cores = ([(at, at ^ bit) for at in range(batch)] for bit in (2, 1))
    first = after(first, *ready)
    second = lax.ppermute(first, "batch", across)
    return [first, second] + [lax.ppermute(one, "batch", cores) for one in (first, second)]


def quarter_rows(rows):
    return -(-rows // (4 * GRANULE)) * GRANULE


def quarter_starts(rows):
    part = quarter_rows(rows)
    return [min(at * part, rows - part) // GRANULE for at in range(4)]


def output_weights(w_out, core, ready):
    part = w_out.shape[0] // 2
    shard = after(lax.dynamic_slice_in_dim(w_out, core * part, part, 0), *ready)
    return lax.all_gather(shard, "patch", axis=0, tiled=True)


def after(value, *ready):
    anywhere = pl.BlockSpec(memory_space=pl.ANY)
    vmem = pl.BlockSpec(memory_space=pltpu.VMEM)
    return pl.pallas_call(
        lambda *refs: None,
        out_shape=jax.ShapeDtypeStruct(value.shape, value.dtype),
        in_specs=[anywhere] + [vmem] * len(ready),
        out_specs=anywhere,
        input_output_aliases={0: 0},
        cost_estimate=pl.CostEstimate(flops=0, bytes_accessed=0, transcendentals=0),
        name="after",
    )(value, *ready)


def on_device(latent, conv_weight, channel_bias, w_query, w_key, w_value, w_out):
    rows_local, columns, channels = latent.shape
    n = lax.axis_size("patch")
    inner = n // OUTER
    own = channels // n
    block = rows_local * columns
    positions = block * n
    me = lax.axis_index("patch")
    batch_at = lax.axis_index("batch")
    inner_at = lax.rem(me, inner)
    core = lax.rem(batch_at, 2)
    side = lax.rem(lax.div(batch_at, 2), 2)
    fixed = jnp.stack([me, lax.div(me, inner), inner_at, core, 2 * core + side])
    fixed = fixed.astype(jnp.int32)
    sources = jnp.asarray(sources_of(n), jnp.int32)
    place = jnp.concatenate([fixed, lax.dynamic_index_in_dim(sources, me, 0, keepdims=False)])
    vmem = pl.BlockSpec(memory_space=pltpu.VMEM)
    smem = pl.BlockSpec(memory_space=pltpu.SMEM)
    anywhere = pl.BlockSpec(memory_space=pl.ANY)
    params = pltpu.CompilerParams(vmem_limit_bytes=VMEM_LIMIT)

    whole = latent.reshape(block, channels)
    pieces = gather((whole[: block // 2], whole[block // 2 :]), n)

    if inner == 2:
        first = swap_weights((w_query, w_key, w_value), core, side, n, pieces[-5:])
    else:
        sets = [list(range(at, at + inner)) for at in range(0, n, inner)]
        weights = jnp.stack([w_query, w_key, w_value])
        weights = lax.all_gather(weights, "patch", axis=1, tiled=True, axis_index_groups=sets)
        weights = [weights.reshape(3 * SET_CHANNELS, channels)]
    out_half = output_weights(w_out, core, pieces[-5:])

    hidden = pl.pallas_call(
        functools.partial(conv_kernel, columns),
        out_shape=[jax.ShapeDtypeStruct((own, positions // 2), bf16)] * 2,
        in_specs=[smem] + [vmem] * (2 * n) + [anywhere, vmem],
        out_specs=[vmem] * 2,
        scratch_shapes=[
            pltpu.VMEM((positions + 2 * columns, channels), bf16),
            pltpu.VMEM((own, positions), f32),
            pltpu.VMEM((3, 3 * own, channels), bf16),
            pltpu.SemaphoreType.DMA,
        ],
        compiler_params=params,
        cost_estimate=pl.CostEstimate(
            flops=2 * 9 * positions * channels * own,
            bytes_accessed=2 * (positions * channels + 9 * channels * own),
            transcendentals=positions * channels,
        ),
        name="norm_conv",
    )(
        place,
        *pieces,
        conv_weight.reshape(3, 3 * own, channels),
        channel_bias.reshape(own, 1),
    )

    hidden_pieces = gather(tuple(hidden), n)
    if inner == 2:
        weights = [w_query, w_key, w_value] + spread_weights(first, hidden[:1])
    out_half = after(out_half, *hidden_pieces[-5:], *weights[3:])
    cores = [(at, at ^ 1) for at in range(lax.axis_size("batch"))]
    out_other = lax.ppermute(out_half, "batch", cores)

    *attended, kept = pl.pallas_call(
        functools.partial(attention_kernel, 2 * n, inner),
        out_shape=[jax.ShapeDtypeStruct((SET_CHANNELS, block), bf16)] * OUTER
        + [jax.ShapeDtypeStruct((channels, block), bf16)],
        in_specs=[smem] + [anywhere] * (2 * n + len(weights)),
        out_specs=[vmem] * (OUTER + 1),
        scratch_shapes=[
            pltpu.VMEM((channels, positions), bf16),
            pltpu.VMEM((channels, positions), bf16),
            pltpu.VMEM((3 * SET_CHANNELS, channels), bf16),
            pltpu.VMEM((SET_CHANNELS, OUTER * block), bf16),
            pltpu.VMEM((SET_HEADS, positions, HEAD_DIM), bf16),
            pltpu.VMEM((SET_CHANNELS, positions), bf16),
            pltpu.SemaphoreType.DMA((2 * n + 1,)),
        ],
        compiler_params=params,
        cost_estimate=pl.CostEstimate(
            flops=2 * positions * channels * 3 * SET_CHANNELS
            + 4 * positions * OUTER * block * SET_CHANNELS,
            bytes_accessed=2 * (positions * channels + 3 * SET_CHANNELS * channels),
            transcendentals=positions * OUTER * block * SET_HEADS,
        ),
        name="attention",
    )(place, *hidden_pieces, *weights)

    received = [attended[0]]
    for step in range(1, OUTER):
        pairs = [(at, (at + step * inner) % n) for at in range(n)]
        received.append(lax.ppermute(attended[step], "patch", pairs))

    output = pl.pallas_call(
        functools.partial(output_kernel, n),
        out_shape=jax.ShapeDtypeStruct((block, channels), bf16),
        in_specs=[smem] + [vmem] * (OUTER + 3),
        out_specs=vmem,
        scratch_shapes=[
            pltpu.VMEM((channels, block), bf16),
            pltpu.VMEM((channels, block), f32),
        ],
        compiler_params=params,
        cost_estimate=pl.CostEstimate(
            flops=2 * block * channels * channels,
            bytes_accessed=2 * channels * (channels + 3 * block),
            transcendentals=0,
        ),
        name="project",
    )(place, *received, kept, out_half, out_other)
    return output.reshape(rows_local, columns, channels)


def solution(mesh):
    return jax.shard_map(
        on_device,
        mesh=mesh,
        in_specs=(
            P(("batch", "patch"), None, None),
            P(None, None, "patch", None),
            P("patch"),
            P("patch", None),
            P("patch", None),
            P("patch", None),
            P("patch", None),
        ),
        out_specs=P(("batch", "patch"), None, None),
        check_vma=False,
    )
```

```python
import functools

import jax
import jax.numpy as jnp
from jax import lax
from jax.experimental import pallas as pl
from jax.experimental.pallas import tpu as pltpu
from jax.sharding import PartitionSpec as P

C = 1280
HEADS = 20
HEAD_DIM = 64
GROUPS = 32
SPAN = C // GROUPS
OUTER = 4
SET_HEADS = HEADS // OUTER
SET_CHANNELS = SET_HEADS * HEAD_DIM
QUAD = 4
HANDED = (0, 1, 2, 3)
GRANULE = 32
EPSILON = 1e-05
MEBI = 1024 * 1024

f32 = jnp.float32
bf16 = jnp.bfloat16

NT = (((1,), (1,)), ((), ()))
NN = (((1,), (0,)), ((), ()))


def dot(left, right, dims=NN, precision=None):
    return lax.dot_general(left, right, dims, preferred_element_type=f32, precision=precision)


def exact(left, right, dims=NN):
    return dot(left, right, dims, lax.Precision.HIGHEST)


def conv_kernel(columns, sources_ref, *refs):
    count = len(refs) - 8
    pieces = refs[:count]
    source_ref, bias_ref = refs[count : count + 2]
    out_refs = refs[count + 2 : count + 4]
    act_ref, kept_ref, kernel_ref, sem = refs[count + 4 :]
    load = pltpu.make_async_copy(source_ref, kernel_ref, sem)
    load.start()
    block = pieces[0].shape[0]
    positions = block * count
    own = out_refs[0].shape[0]
    me = lax.axis_index("patch")
    entries = float(positions * SPAN)
    chunk = 16
    steps = block // chunk
    starts = [
        pl.multiple_of(sources_ref[me * count + index] * (2 * block) + (index % 2) * block, block)
        for index in range(count)
    ]

    def add(step, total):
        for piece in pieces:
            total = total + piece[pl.ds(step * chunk, chunk), :].astype(f32)
        return total

    member = (
        lax.broadcasted_iota(jnp.int32, (C, 128), 0) // SPAN
        == lax.broadcasted_iota(jnp.int32, (C, 128), 1)
    ).astype(f32)

    def group_mean(total):
        summed = jnp.sum(total, axis=0, keepdims=True)
        per_group = exact(jnp.broadcast_to(summed, (8, C)), member) / entries
        return exact(per_group, member, NT)[0:1, :]

    zero = jnp.zeros((chunk, C), f32)
    centre = group_mean(lax.fori_loop(0, steps, add, zero))

    def add_square(step, total):
        for piece in pieces:
            away = piece[pl.ds(step * chunk, chunk), :].astype(f32) - centre
            total = total + away * away
        return total

    spread = group_mean(lax.fori_loop(0, steps, add_square, zero))
    half_scale = 0.5 * lax.rsqrt(spread + EPSILON)

    act_ref[0:columns, :] = jnp.zeros((columns, C), bf16)
    act_ref[positions + columns :, :] = jnp.zeros((columns, C), bf16)

    def activate(step, carry):
        for start, piece in zip(starts, pieces):
            half = (piece[pl.ds(step * chunk, chunk), :].astype(f32) - centre) * half_scale
            value = half + half * jnp.tanh(half)
            row = pl.multiple_of(columns + start + step * chunk, chunk)
            act_ref[pl.ds(row, chunk), :] = value.astype(bf16)
        return carry

    lax.fori_loop(0, steps, activate, 0)

    choose = (
        lax.broadcasted_iota(jnp.int32, (own, C), 0) + me * own
        == lax.broadcasted_iota(jnp.int32, (own, C), 1)
    ).astype(bf16)
    for index in range(0, count, 2):
        pair = jnp.concatenate([pieces[index][...], pieces[index + 1][...]], axis=0)
        start = pl.multiple_of(starts[index], 2 * block)
        kept_ref[:, pl.ds(start, 2 * block)] = dot(choose, pair, NT)

    load.wait()
    wide = 256
    column = lax.broadcasted_iota(jnp.int32, (own, wide), 1) % columns
    square = (own, own)
    bias = jnp.where(
        lax.broadcasted_iota(jnp.int32, square, 0) == lax.broadcasted_iota(jnp.int32, square, 1),
        bias_ref[...],
        0.0,
    )
    bias = jnp.sum(bias, axis=1, keepdims=True)
    for at in range(0, positions, wide):
        taps = dot(kernel_ref[0], act_ref[at : at + wide, :], NT)
        for shift in (1, 2):
            low = at + shift * columns
            taps = taps + dot(kernel_ref[shift], act_ref[low : low + wide, :], NT)
        before = jnp.where(column > 0, pltpu.roll(taps[0:own], 1, 1), 0.0)
        after_ = jnp.where(column < columns - 1, pltpu.roll(taps[2 * own :], wide - 1, 1), 0.0)
        convolved = taps[own : 2 * own] + before + after_
        hidden = kept_ref[:, at : at + wide] + convolved + bias
        which, low = divmod(at, positions // 2)
        out_refs[which][:, low : low + wide] = hidden.astype(bf16)


def attention_kernel(count, inner, sources_ref, *refs):
    pieces = refs[:count]
    parts = refs[count : -8 - OUTER]
    outs = refs[-8 - OUTER : -8]
    kept_ref, hidden_ref, normed_ref, weight_ref, query_ref, key_ref, value_ref, sems = refs[-8:]
    own, part = pieces[0].shape
    n = count // 2
    positions = 2 * part
    block = positions // n
    me = lax.axis_index("patch")
    outer_at, inner_at = lax.div(me, inner), lax.rem(me, inner)
    entries = float(positions * SPAN)

    copies = []
    for index, piece in enumerate(pieces):
        row = pl.multiple_of(sources_ref[me * count + index] * own, own)
        low = (index % 2) * part
        target = hidden_ref.at[pl.ds(row, own), low : low + part]
        copies.append(pltpu.make_async_copy(piece, target, sems.at[index]))
    loads = []

    def load(source, row):
        target = weight_ref.at[pl.ds(row, source.shape[0]), :]
        loads.append(pltpu.make_async_copy(source, target, sems.at[count + len(loads)]))

    if inner == 2:
        for kind in range(3):
            row = kind * SET_CHANNELS + inner_at * own
            load(parts[kind], pl.multiple_of(row, own))
        mine = quad_place()
        for step, part_ref in zip(HANDED, parts[3 : 3 + QUAD]):
            first = quarter_start(jnp.bitwise_xor(mine, step), own)
            for at in range(part_ref.shape[0] // GRANULE):
                kind, low = granule_at(first + at, own)
                row = kind * SET_CHANNELS + (1 - inner_at) * own + low
                source = part_ref.at[at * GRANULE : (at + 1) * GRANULE, :]
                load(source, pl.multiple_of(row, GRANULE))
    else:
        load(parts[0], 0)
    for copy in copies + loads:
        copy.start()
    for copy in copies:
        copy.wait()

    kept_ref[...] = hidden_ref[:, pl.ds(pl.multiple_of(me * block, block), block)]
    for at in range(0, C, 2 * SPAN):
        pair = hidden_ref[at : at + 2 * SPAN, :].astype(f32)
        scaled = []
        for low in (0, SPAN):
            group = pair[low : low + SPAN]
            mean = jnp.sum(jnp.sum(group, axis=0, keepdims=True), axis=1, keepdims=True) / entries
            away = group - mean
            square = jnp.sum(away * away, axis=0, keepdims=True)
            var = jnp.sum(square, axis=1, keepdims=True) / entries
            scaled.append(away * lax.rsqrt(var + EPSILON))
        normed_ref[at : at + 2 * SPAN, :] = jnp.concatenate(scaled, axis=0).astype(bf16)

    for copy in loads:
        copy.wait()
    wide = 256
    for at in range(0, positions, wide):
        made = dot(weight_ref[SET_CHANNELS:, :], normed_ref[:, at : at + wide])
        for head in range(SET_HEADS):
            low = head * HEAD_DIM
            key_ref[head, at : at + wide, :] = made[low : low + HEAD_DIM].T.astype(bf16)
        value_ref[:, at : at + wide] = made[SET_CHANNELS:].astype(bf16)

    for at in range(0, OUTER, 2):
        normed = []
        for step in (at, at + 1):
            target = lax.rem(outer_at + step, OUTER) * inner + inner_at
            normed.append(normed_ref[:, pl.ds(pl.multiple_of(target * block, block), block)])
        made = dot(weight_ref[:SET_CHANNELS, :], jnp.concatenate(normed, axis=1))
        scaled = made.astype(bf16).astype(f32) * HEAD_DIM ** (-0.5)
        query_ref[:, at * block : (at + 2) * block] = scaled.astype(bf16)

    for at in range(0, OUTER, 2):
        for head in range(SET_HEADS):
            low = head * HEAD_DIM
            query = query_ref[low : low + HEAD_DIM, at * block : (at + 2) * block]
            scores = dot(key_ref[head], query)
            peak = jnp.max(scores, axis=0, keepdims=True)
            unnormalized = jnp.exp(scores - peak)
            total = jnp.sum(unnormalized, axis=0, keepdims=True)
            mixture = dot(value_ref[low : low + HEAD_DIM, :], unnormalized.astype(bf16))
            attended = (mixture / total).astype(bf16)
            outs[at][low : low + HEAD_DIM, :] = attended[:, :block]
            outs[at + 1][low : low + HEAD_DIM, :] = attended[:, block:]


def output_kernel(n, *refs):
    attended_refs = refs[:OUTER]
    hidden_ref = refs[OUTER]
    weight_refs = refs[OUTER + 1 : -3]
    out_ref, attended_ref, total_ref = refs[-3:]
    own = C // n
    outer_at = lax.div(lax.axis_index("patch"), n // OUTER)
    for step in range(OUTER):
        origin = lax.rem(outer_at + OUTER - step, OUTER)
        row = pl.multiple_of(origin * SET_CHANNELS, SET_CHANNELS)
        attended_ref[pl.ds(row, SET_CHANNELS), :] = attended_refs[step][...]
    attended = attended_ref[...]
    total_ref[...] = hidden_ref[...].astype(f32)
    core = lax.rem(lax.axis_index("batch"), 2)
    part = own // 2
    for which, weight_ref in zip((core, 1 - core), weight_refs):
        made = dot(weight_ref[...], attended)
        for origin in range(n):
            row = pl.multiple_of(origin * own + which * part, 8)
            total_ref[pl.ds(row, part), :] += made[origin * part : (origin + 1) * part]
    out_ref[...] = total_ref[...].T.astype(bf16)


def pick_kernel(*refs):
    weight_refs = refs[:3]
    source_ref, quarter_ref, half_ref, sems = refs[3:]
    own = source_ref.shape[0]
    half = half_ref.shape[0]
    row = pl.multiple_of(lax.rem(lax.axis_index("batch"), 2) * half, half)
    copy = pltpu.make_async_copy(source_ref.at[pl.ds(row, half), :], half_ref, sems.at[0])
    copy.start()
    count = quarter_ref.shape[0] // GRANULE
    first = quarter_start(quad_place(), own)

    def each(act):
        for at in range(count):
            kind, low = granule_at(first + at, own)
            rows = pl.ds(pl.multiple_of(low, GRANULE), GRANULE)
            target = quarter_ref.at[at * GRANULE : (at + 1) * GRANULE, :]
            for which, weight_ref in enumerate(weight_refs):

                @pl.when(kind == which)
                def _(weight_ref=weight_ref):
                    act(pltpu.make_async_copy(weight_ref.at[rows, :], target, sems.at[1 + at]))

    each(lambda one: one.start())
    each(lambda one: one.wait())
    copy.wait()


def quad_place():
    at = lax.rem(lax.axis_index("batch"), QUAD)
    return 2 * lax.rem(at, 2) + lax.div(at, 2)


def quarter_rows(own):
    return -(-3 * own // (QUAD * GRANULE)) * GRANULE


def quarter_start(place, own):
    part = quarter_rows(own) // GRANULE
    return jnp.minimum(place * part, 3 * own // GRANULE - part)


def granule_at(granule, own):
    count = own // GRANULE
    return lax.div(granule, count), lax.rem(granule, count) * GRANULE


def ring_of(n):
    inner = n // OUTER
    path = [(0, 0)]
    for outer_at in range(OUTER):
        across = range(1, inner) if outer_at % 2 == 0 else range(inner - 1, 0, -1)
        path += [(outer_at, inner_at) for inner_at in across]
    path += [(outer_at, 0) for outer_at in range(OUTER - 1, 0, -1)]
    return [outer_at * inner + inner_at for outer_at, inner_at in path]


def pieces_of(n):
    far = n // 2
    return [0] + [away for step in range(1, far) for away in (-step, step)] + [far]


def sources_of(n):
    ring = ring_of(n)
    table = []
    for device in range(n):
        at = ring.index(device)
        table.append([ring[(at + away) % n] for away in pieces_of(n) for _ in (0, 1)])
    return table


def gather(halves, n, beside=()):
    ring = ring_of(n)
    forward = [(ring[at], ring[(at + 1) % n]) for at in range(n)]
    backward = [(target, start) for start, target in forward]
    far = n // 2
    found = {(0, 0): halves[0], (1, 0): halves[1]}
    for step in range(1, far + 1):
        for half in (0, 1):
            for sign, pairs in ((-1, forward), (1, backward)):
                if step == far and (half == 0) != (sign == -1):
                    continue
                found[half, sign * step] = lax.ppermute(
                    found[half, sign * (step - 1)], "patch", pairs
                )
        if step == 1 and beside:
            (found[0, -1],) = after([found[0, -1]], beside)
    found[0, far] = found[0, -far]
    return [found[half, away] for away in pieces_of(n) for half in (0, 1)]


def pick(weights):
    hbm = pl.BlockSpec(memory_space=pltpu.HBM)
    anywhere = pl.BlockSpec(memory_space=pl.ANY)
    own = weights[0].shape[0]
    shapes = [(quarter_rows(own), C), (own // 2, C)]
    return pl.pallas_call(
        pick_kernel,
        out_shape=[jax.ShapeDtypeStruct(shape, bf16) for shape in shapes],
        in_specs=[hbm] * len(weights),
        out_specs=[anywhere] * len(shapes),
        scratch_shapes=[pltpu.SemaphoreType.DMA((1 + quarter_rows(own) // GRANULE,))],
        compiler_params=pltpu.CompilerParams(vmem_limit_bytes=MEBI),
        cost_estimate=pl.CostEstimate(flops=0, bytes_accessed=0, transcendentals=0),
        name="pick",
    )(*weights)


def hand_on(block):
    batch = lax.axis_size("batch")
    across, cores = ([(at, at ^ bit) for at in range(batch)] for bit in (2, 1))
    blocks = [block, lax.ppermute(block, "batch", across)]
    return blocks + [lax.ppermute(one, "batch", cores) for one in blocks]


def moves(n, outer_step, inner_step):
    inner = n // OUTER
    pairs = []
    for start in range(n):
        outer_at = (start // inner + outer_step) % OUTER
        inner_at = (start % inner + inner_step) % inner
        pairs.append((start, outer_at * inner + inner_at))
    return pairs


def after(values, ready):
    anywhere = pl.BlockSpec(memory_space=pl.ANY)
    return pl.pallas_call(
        lambda *refs: None,
        out_shape=[jax.ShapeDtypeStruct(value.shape, value.dtype) for value in values],
        in_specs=[anywhere] * (len(values) + len(ready)),
        out_specs=[anywhere] * len(values),
        input_output_aliases={at: at for at in range(len(values))},
        compiler_params=pltpu.CompilerParams(vmem_limit_bytes=MEBI),
        cost_estimate=pl.CostEstimate(flops=0, bytes_accessed=0, transcendentals=0),
        name="after",
    )(*values, *ready)


def on_device(latent, conv_weight, channel_bias, w_query, w_key, w_value, w_out):
    rows_local, columns, channels = latent.shape
    n = lax.axis_size("patch")
    inner = n // OUTER
    own = channels // n
    block = rows_local * columns
    positions = block * n
    sources = jnp.asarray(sources_of(n), jnp.int32).reshape(-1)
    vmem = pl.BlockSpec(memory_space=pltpu.VMEM)
    smem = pl.BlockSpec(memory_space=pltpu.SMEM)
    anywhere = pl.BlockSpec(memory_space=pl.ANY)

    whole = latent.reshape(block, channels)
    halves = whole[: block // 2], whole[block // 2 :]
    if inner == 2:
        quarter, out_half = pick((w_query, w_key, w_value, w_out))
        pieces = gather(halves, n, [quarter, out_half])
        quarter, out_half = after([quarter, out_half], pieces[-5:])
        quarter = lax.ppermute(quarter, "patch", moves(n, 0, 1))
    else:
        pieces = gather(halves, n)
        sets = [list(range(at, at + inner)) for at in range(0, n, inner)]
        weights = jnp.stack([w_query, w_key, w_value])
        weights = lax.all_gather(weights, "patch", axis=1, tiled=True, axis_index_groups=sets)
        weights = [weights.reshape(3 * SET_CHANNELS, channels)]
        core = lax.rem(lax.axis_index("batch"), 2)
        out_half = lax.dynamic_slice_in_dim(w_out, core * (own // 2), own // 2, 0)
    out_half = lax.all_gather(out_half, "patch", axis=0, tiled=True)

    hidden = pl.pallas_call(
        functools.partial(conv_kernel, columns),
        out_shape=[jax.ShapeDtypeStruct((own, positions // 2), bf16)] * 2,
        in_specs=[smem] + [vmem] * (2 * n) + [anywhere, vmem],
        out_specs=[vmem] * 2,
        scratch_shapes=[
            pltpu.VMEM((positions + 2 * columns, channels), bf16),
            pltpu.VMEM((own, positions), f32),
            pltpu.VMEM((3, 3 * own, channels), bf16),
            pltpu.SemaphoreType.DMA,
        ],
        compiler_params=pltpu.CompilerParams(vmem_limit_bytes=20 * MEBI),
        cost_estimate=pl.CostEstimate(
            flops=2 * 9 * positions * channels * own,
            bytes_accessed=2 * (positions * channels + 9 * channels * own),
            transcendentals=positions * channels,
        ),
        name="norm_conv",
    )(
        sources,
        *pieces,
        conv_weight.reshape(3, 3 * own, channels),
        channel_bias.reshape(1, own),
    )

    hidden_pieces = gather(tuple(hidden), n)
    if inner == 2:
        weights = [w_query, w_key, w_value] + hand_on(after([quarter], hidden[:1])[0])
    (out_half,) = after([out_half], hidden_pieces[-5:] + weights[3:])
    cores = [(at, at ^ 1) for at in range(lax.axis_size("batch"))]
    out_weights = [out_half, lax.ppermute(out_half, "batch", cores)]

    *attended, kept = pl.pallas_call(
        functools.partial(attention_kernel, 2 * n, inner),
        out_shape=[jax.ShapeDtypeStruct((SET_CHANNELS, block), bf16)] * OUTER
        + [jax.ShapeDtypeStruct((channels, block), bf16)],
        in_specs=[smem] + [anywhere] * (2 * n + len(weights)),
        out_specs=[vmem] * (OUTER + 1),
        scratch_shapes=[
            pltpu.VMEM((channels, positions), bf16),
            pltpu.VMEM((channels, positions), bf16),
            pltpu.VMEM((3 * SET_CHANNELS, channels), bf16),
            pltpu.VMEM((SET_CHANNELS, OUTER * block), bf16),
            pltpu.VMEM((SET_HEADS, positions, HEAD_DIM), bf16),
            pltpu.VMEM((SET_CHANNELS, positions), bf16),
            pltpu.SemaphoreType.DMA((2 * n + 3 + QUAD * quarter_rows(own) // GRANULE,)),
        ],
        compiler_params=pltpu.CompilerParams(vmem_limit_bytes=28 * MEBI),
        cost_estimate=pl.CostEstimate(
            flops=2 * positions * channels * 3 * SET_CHANNELS
            + 4 * positions * OUTER * block * SET_CHANNELS,
            bytes_accessed=2 * (positions * channels + 3 * SET_CHANNELS * channels),
            transcendentals=positions * OUTER * block * SET_HEADS,
        ),
        name="attention",
    )(sources, *hidden_pieces, *weights)

    received = [attended[0]]
    for step in range(1, OUTER):
        pairs = [(at, (at + step * inner) % n) for at in range(n)]
        received.append(lax.ppermute(attended[step], "patch", pairs))

    output = pl.pallas_call(
        functools.partial(output_kernel, n),
        out_shape=jax.ShapeDtypeStruct((block, channels), bf16),
        in_specs=[vmem] * (OUTER + 1 + len(out_weights)),
        out_specs=vmem,
        scratch_shapes=[
            pltpu.VMEM((channels, block), bf16),
            pltpu.VMEM((channels, block), f32),
        ],
        compiler_params=pltpu.CompilerParams(vmem_limit_bytes=12 * MEBI),
        cost_estimate=pl.CostEstimate(
            flops=2 * block * channels * channels,
            bytes_accessed=2 * channels * (channels + 3 * block),
            transcendentals=0,
        ),
        name="project",
    )(*received, kept, *out_weights)
    return output.reshape(rows_local, columns, channels)


def solution(mesh):
    return jax.shard_map(
        on_device,
        mesh=mesh,
        in_specs=(
            P(("batch", "patch"), None, None),
            P(None, None, "patch", None),
            P("patch"),
            P("patch", None),
            P("patch", None),
            P("patch", None),
            P("patch", None),
        ),
        out_specs=P(("batch", "patch"), None, None),
        check_vma=False,
    )
```

```python
import functools

import jax
import jax.numpy as jnp
from jax import lax
from jax.experimental import pallas as pl
from jax.experimental.pallas import tpu as pltpu
from jax.sharding import PartitionSpec as P

C = 1280
HEADS = 20
HEAD_DIM = 64
GROUPS = 32
SPAN = C // GROUPS
OUTER = 4
SET_HEADS = HEADS // OUTER
SET_CHANNELS = SET_HEADS * HEAD_DIM
QUAD = 4
HANDED = (0, 2, 1, 3)
FAR = ((1, 0), (2, 0), (3, 0), (2, 1))
LAST = ((1, 1), (3, 1))
EPSILON = 1e-05
MEBI = 1024 * 1024

f32 = jnp.float32
bf16 = jnp.bfloat16

NT = (((1,), (1,)), ((), ()))
NN = (((1,), (0,)), ((), ()))


def dot(left, right, dims=NN, precision=None):
    return lax.dot_general(left, right, dims, preferred_element_type=f32, precision=precision)


def exact(left, right, dims=NN):
    return dot(left, right, dims, lax.Precision.HIGHEST)


def conv_kernel(columns, sources_ref, *refs):
    count = len(refs) - 8
    pieces = refs[:count]
    source_ref, bias_ref = refs[count : count + 2]
    out_refs = refs[count + 2 : count + 4]
    act_ref, kept_ref, kernel_ref, sem = refs[count + 4 :]
    load = pltpu.make_async_copy(source_ref, kernel_ref, sem)
    load.start()
    block = pieces[0].shape[0]
    positions = block * count
    own = out_refs[0].shape[0]
    me = lax.axis_index("patch")
    entries = float(positions * SPAN)
    chunk = 16
    steps = block // chunk
    starts = [
        pl.multiple_of(sources_ref[me * count + index] * (2 * block) + (index % 2) * block, block)
        for index in range(count)
    ]

    def add(step, total):
        for piece in pieces:
            total = total + piece[pl.ds(step * chunk, chunk), :].astype(f32)
        return total

    member = (
        lax.broadcasted_iota(jnp.int32, (C, 128), 0) // SPAN
        == lax.broadcasted_iota(jnp.int32, (C, 128), 1)
    ).astype(f32)

    def group_mean(total):
        summed = jnp.sum(total, axis=0, keepdims=True)
        per_group = exact(jnp.broadcast_to(summed, (8, C)), member) / entries
        return exact(per_group, member, NT)[0:1, :]

    zero = jnp.zeros((chunk, C), f32)
    centre = group_mean(lax.fori_loop(0, steps, add, zero))

    def add_square(step, total):
        for piece in pieces:
            away = piece[pl.ds(step * chunk, chunk), :].astype(f32) - centre
            total = total + away * away
        return total

    spread = group_mean(lax.fori_loop(0, steps, add_square, zero))
    half_scale = 0.5 * lax.rsqrt(spread + EPSILON)

    act_ref[0:columns, :] = jnp.zeros((columns, C), bf16)
    act_ref[positions + columns :, :] = jnp.zeros((columns, C), bf16)

    def activate(step, carry):
        for start, piece in zip(starts, pieces):
            half = (piece[pl.ds(step * chunk, chunk), :].astype(f32) - centre) * half_scale
            value = half + half * jnp.tanh(half)
            row = pl.multiple_of(columns + start + step * chunk, chunk)
            act_ref[pl.ds(row, chunk), :] = value.astype(bf16)
        return carry

    lax.fori_loop(0, steps, activate, 0)

    choose = (
        lax.broadcasted_iota(jnp.int32, (own, C), 0) + me * own
        == lax.broadcasted_iota(jnp.int32, (own, C), 1)
    ).astype(bf16)
    for index in range(0, count, 2):
        pair = jnp.concatenate([pieces[index][...], pieces[index + 1][...]], axis=0)
        start = pl.multiple_of(starts[index], 2 * block)
        kept_ref[:, pl.ds(start, 2 * block)] = dot(choose, pair, NT)

    load.wait()
    wide = 256
    column = lax.broadcasted_iota(jnp.int32, (own, wide), 1) % columns
    square = (own, own)
    bias = jnp.where(
        lax.broadcasted_iota(jnp.int32, square, 0) == lax.broadcasted_iota(jnp.int32, square, 1),
        bias_ref[...],
        0.0,
    )
    bias = jnp.sum(bias, axis=1, keepdims=True)
    for at in range(0, positions, wide):
        taps = dot(kernel_ref[0], act_ref[at : at + wide, :], NT)
        for shift in (1, 2):
            low = at + shift * columns
            taps = taps + dot(kernel_ref[shift], act_ref[low : low + wide, :], NT)
        before = jnp.where(column > 0, pltpu.roll(taps[0:own], 1, 1), 0.0)
        after_ = jnp.where(column < columns - 1, pltpu.roll(taps[2 * own :], wide - 1, 1), 0.0)
        convolved = taps[own : 2 * own] + before + after_
        hidden = kept_ref[:, at : at + wide] + convolved + bias
        which, low = divmod(at, positions // 2)
        out_refs[which][:, low : low + wide] = hidden.astype(bf16)


def attention_kernel(count, inner, sources_ref, *refs):
    pieces = refs[:count]
    parts = refs[count : -8 - OUTER]
    outs = refs[-8 - OUTER : -8]
    kept_ref, hidden_ref, normed_ref, weight_ref, query_ref, key_ref, value_ref, sems = refs[-8:]
    own, part = pieces[0].shape
    n = count // 2
    positions = 2 * part
    block = positions // n
    me = lax.axis_index("patch")
    outer_at, inner_at = lax.div(me, inner), lax.rem(me, inner)
    entries = float(positions * SPAN)

    copies = []
    for index, piece in enumerate(pieces):
        row = pl.multiple_of(sources_ref[me * count + index] * own, own)
        low = (index % 2) * part
        target = hidden_ref.at[pl.ds(row, own), low : low + part]
        copies.append(pltpu.make_async_copy(piece, target, sems.at[index]))
    loads = []

    def load(source, row):
        target = weight_ref.at[pl.ds(row, source.shape[0]), :]
        loads.append(pltpu.make_async_copy(source, target, sems.at[count + len(loads)]))

    if inner == 2:
        for kind in range(3):
            row = kind * SET_CHANNELS + inner_at * own
            load(parts[kind], pl.multiple_of(row, own))
        mine = lax.rem(lax.axis_index("batch"), QUAD)
        for step, part_ref in zip(HANDED, parts[3:]):
            row = jnp.bitwise_xor(mine, step) * SET_CHANNELS + (1 - inner_at) * own
            load(part_ref, pl.multiple_of(row, own))
    else:
        load(parts[0], 0)
    for copy in copies + loads:
        copy.start()
    for copy in copies:
        copy.wait()

    kept_ref[...] = hidden_ref[:, pl.ds(pl.multiple_of(me * block, block), block)]
    for at in range(0, C, 2 * SPAN):
        pair = hidden_ref[at : at + 2 * SPAN, :].astype(f32)
        scaled = []
        for low in (0, SPAN):
            group = pair[low : low + SPAN]
            mean = jnp.sum(jnp.sum(group, axis=0, keepdims=True), axis=1, keepdims=True) / entries
            away = group - mean
            square = jnp.sum(away * away, axis=0, keepdims=True)
            var = jnp.sum(square, axis=1, keepdims=True) / entries
            scaled.append(away * lax.rsqrt(var + EPSILON))
        normed_ref[at : at + 2 * SPAN, :] = jnp.concatenate(scaled, axis=0).astype(bf16)

    for copy in loads:
        copy.wait()
    wide = 256
    for at in range(0, positions, wide):
        made = dot(weight_ref[SET_CHANNELS : 3 * SET_CHANNELS, :], normed_ref[:, at : at + wide])
        for head in range(SET_HEADS):
            low = head * HEAD_DIM
            key_ref[head, at : at + wide, :] = made[low : low + HEAD_DIM].T.astype(bf16)
        value_ref[:, at : at + wide] = made[SET_CHANNELS:].astype(bf16)

    for at in range(0, OUTER, 2):
        normed = []
        for step in (at, at + 1):
            target = lax.rem(outer_at + step, OUTER) * inner + inner_at
            normed.append(normed_ref[:, pl.ds(pl.multiple_of(target * block, block), block)])
        made = dot(weight_ref[:SET_CHANNELS, :], jnp.concatenate(normed, axis=1))
        scaled = made.astype(bf16).astype(f32) * HEAD_DIM ** (-0.5)
        query_ref[:, at * block : (at + 2) * block] = scaled.astype(bf16)

    for at in range(0, OUTER, 2):
        for head in range(SET_HEADS):
            low = head * HEAD_DIM
            query = query_ref[low : low + HEAD_DIM, at * block : (at + 2) * block]
            scores = dot(key_ref[head], query)
            peak = jnp.max(scores, axis=0, keepdims=True)
            unnormalized = jnp.exp(scores - peak)
            total = jnp.sum(unnormalized, axis=0, keepdims=True)
            mixture = dot(value_ref[low : low + HEAD_DIM, :], unnormalized.astype(bf16))
            attended = (mixture / total).astype(bf16)
            outs[at][low : low + HEAD_DIM, :] = attended[:, :block]
            outs[at + 1][low : low + HEAD_DIM, :] = attended[:, block:]


def output_kernel(n, *refs):
    attended_refs = refs[:OUTER]
    hidden_ref = refs[OUTER]
    weight_refs = refs[OUTER + 1 : -3]
    out_ref, attended_ref, total_ref = refs[-3:]
    inner = n // OUTER
    own = C // n
    me = lax.axis_index("patch")
    outer_at, inner_at = lax.div(me, inner), lax.rem(me, inner)
    for step in range(OUTER):
        origin = lax.rem(outer_at + OUTER - step, OUTER)
        row = pl.multiple_of(origin * SET_CHANNELS, SET_CHANNELS)
        attended_ref[pl.ds(row, SET_CHANNELS), :] = attended_refs[step][...]
    attended = attended_ref[...]
    if inner != 2:
        total = dot(weight_refs[0][...], attended) + hidden_ref[...].astype(f32)
        out_ref[...] = total.T.astype(bf16)
        return

    total_ref[...] = hidden_ref[...].astype(f32)
    mine = lax.rem(lax.axis_index("batch"), QUAD)
    near, far = weight_refs[1 : 1 + QUAD], blocks_of(weight_refs[-4:-2], own)

    def add(weight_ref, outer_step, inner_step):
        origin = lax.rem(outer_at + OUTER - outer_step, OUTER) * inner
        origin = origin + lax.rem(inner_at + inner_step, inner)
        rows = pl.ds(pl.multiple_of(origin * own, own), own)
        total_ref[rows, :] += dot(weight_ref[...], attended)

    add(weight_refs[0], 0, 0)
    for step, weight_ref in zip(HANDED, near):

        @pl.when(jnp.bitwise_xor(mine, step) == QUAD - 1)
        def _(weight_ref=weight_ref):
            add(weight_ref, 0, 1)

    for step, weight_ref in zip(HANDED, far):
        holder = jnp.bitwise_xor(mine, step)
        outer_step = jnp.where(holder == 0, 1, jnp.where(holder == 2, 3, 2))
        add(weight_ref, outer_step, lax.div(holder, QUAD - 1))
    core = lax.rem(mine, 2)
    for which, weight_ref in zip((core, 1 - core), weight_refs[-2:]):
        add(weight_ref, 1 + 2 * which, 1)
    out_ref[...] = total_ref[...].T.astype(bf16)


def blocks_of(refs, rows):
    return [ref.at[at : at + rows, :] for ref in refs for at in range(0, ref.shape[0], rows)]


def ring_of(n):
    inner = n // OUTER
    path = [(0, 0)]
    for outer_at in range(OUTER):
        across = range(1, inner) if outer_at % 2 == 0 else range(inner - 1, 0, -1)
        path += [(outer_at, inner_at) for inner_at in across]
    path += [(outer_at, 0) for outer_at in range(OUTER - 1, 0, -1)]
    return [outer_at * inner + inner_at for outer_at, inner_at in path]


def pieces_of(n):
    far = n // 2
    return [0] + [away for step in range(1, far) for away in (-step, step)] + [far]


def sources_of(n):
    ring = ring_of(n)
    table = []
    for device in range(n):
        at = ring.index(device)
        table.append([ring[(at + away) % n] for away in pieces_of(n) for _ in (0, 1)])
    return table


def gather(halves, n, beside=()):
    ring = ring_of(n)
    forward = [(ring[at], ring[(at + 1) % n]) for at in range(n)]
    backward = [(target, start) for start, target in forward]
    far = n // 2
    found = {(0, 0): halves[0], (1, 0): halves[1]}
    for step in range(1, far + 1):
        for half in (0, 1):
            for sign, pairs in ((-1, forward), (1, backward)):
                if step == far and (half == 0) != (sign == -1):
                    continue
                found[half, sign * step] = lax.ppermute(
                    found[half, sign * (step - 1)], "patch", pairs
                )
        if step == 1 and beside:
            (found[0, -1],) = after([found[0, -1]], beside)
    found[0, far] = found[0, -far]
    return [found[half, away] for away in pieces_of(n) for half in (0, 1)]


def send(block, shifts):
    batch, n = lax.axis_size("batch"), lax.axis_size("patch")
    pairs = []
    for at in range(batch):
        for start, target in moves(n, *shifts[at % len(shifts)]):
            pairs.append((at * n + start, at * n + target))
    return lax.ppermute(block, ("batch", "patch"), pairs)


def swap(block, bit):
    pairs = [(at, at ^ bit) for at in range(lax.axis_size("batch"))]
    return lax.ppermute(block, "batch", pairs)


def moves(n, outer_step, inner_step):
    inner = n // OUTER
    pairs = []
    for start in range(n):
        outer_at = (start // inner + outer_step) % OUTER
        inner_at = (start % inner + inner_step) % inner
        pairs.append((start, outer_at * inner + inner_at))
    return pairs


def after(values, ready):
    anywhere = pl.BlockSpec(memory_space=pl.ANY)
    made = pl.pallas_call(
        lambda *refs: None,
        out_shape=[jax.ShapeDtypeStruct(value.shape, value.dtype) for value in values],
        in_specs=[anywhere] * (len(values) + len(ready)),
        out_specs=[anywhere] * len(values),
        input_output_aliases={at: at for at in range(len(values))},
        compiler_params=pltpu.CompilerParams(vmem_limit_bytes=MEBI),
        cost_estimate=pl.CostEstimate(flops=0, bytes_accessed=0, transcendentals=0),
        name="after",
    )(*values, *ready)
    return list(made)


def on_device(latent, conv_weight, channel_bias, w_query, w_key, w_value, w_out):
    rows_local, columns, channels = latent.shape
    n = lax.axis_size("patch")
    inner = n // OUTER
    own = channels // n
    block = rows_local * columns
    positions = block * n
    sources = jnp.asarray(sources_of(n), jnp.int32).reshape(-1)
    vmem = pl.BlockSpec(memory_space=pltpu.VMEM)
    smem = pl.BlockSpec(memory_space=pltpu.SMEM)
    anywhere = pl.BlockSpec(memory_space=pl.ANY)

    whole = latent.reshape(block, channels)
    halves = whole[: block // 2], whole[block // 2 :]
    if inner == 2:
        place = lax.rem(lax.axis_index("batch"), QUAD)
        chosen = jnp.where(place == 0, w_query, jnp.where(place == 1, w_key, w_value))
        chosen = jnp.where(place == 3, w_out, chosen)
        pieces = gather(halves, n, [chosen])
        chosen, out_own = after([chosen, w_out], pieces[-5:])
        near = [send(chosen, [(0, 1)])]
        far = [send(out_own, FAR)]
    else:
        pieces = gather(halves, n)
        sets = [list(range(at, at + inner)) for at in range(0, n, inner)]
        weights = jnp.stack([w_query, w_key, w_value])
        weights = lax.all_gather(weights, "patch", axis=1, tiled=True, axis_index_groups=sets)
        weights = [weights.reshape(3 * SET_CHANNELS, channels)]
        out_weights = [lax.all_gather(w_out, "patch", axis=0, tiled=True)]

    hidden = pl.pallas_call(
        functools.partial(conv_kernel, columns),
        out_shape=[jax.ShapeDtypeStruct((own, positions // 2), bf16)] * 2,
        in_specs=[smem] + [vmem] * (2 * n) + [anywhere, vmem],
        out_specs=[vmem] * 2,
        scratch_shapes=[
            pltpu.VMEM((positions + 2 * columns, channels), bf16),
            pltpu.VMEM((own, positions), f32),
            pltpu.VMEM((3, 3 * own, channels), bf16),
            pltpu.SemaphoreType.DMA,
        ],
        compiler_params=pltpu.CompilerParams(vmem_limit_bytes=20 * MEBI),
        cost_estimate=pl.CostEstimate(
            flops=2 * 9 * positions * channels * own,
            bytes_accessed=2 * (positions * channels + 9 * channels * own),
            transcendentals=positions * channels,
        ),
        name="norm_conv",
    )(
        sources,
        *pieces,
        conv_weight.reshape(3, 3 * own, channels),
        channel_bias.reshape(1, own),
    )

    hidden_pieces = gather(tuple(hidden), n)
    if inner == 2:
        *near, far = after(near + far, hidden[:1])
        near.append(swap(near[0], 2))
        near += [swap(one, 1) for one in near]
        weights = [w_query, w_key, w_value] + near
        far, out_own = after([far, out_own], hidden_pieces[-5:] + near)
        across = swap(far, 2)
        last = send(out_own, LAST)

    *attended, kept = pl.pallas_call(
        functools.partial(attention_kernel, 2 * n, inner),
        out_shape=[jax.ShapeDtypeStruct((SET_CHANNELS, block), bf16)] * OUTER
        + [jax.ShapeDtypeStruct((channels, block), bf16)],
        in_specs=[smem] + [anywhere] * (2 * n + len(weights)),
        out_specs=[vmem] * (OUTER + 1),
        scratch_shapes=[
            pltpu.VMEM((channels, positions), bf16),
            pltpu.VMEM((channels, positions), bf16),
            pltpu.VMEM((QUAD * SET_CHANNELS, channels), bf16),
            pltpu.VMEM((SET_CHANNELS, OUTER * block), bf16),
            pltpu.VMEM((SET_HEADS, positions, HEAD_DIM), bf16),
            pltpu.VMEM((SET_CHANNELS, positions), bf16),
            pltpu.SemaphoreType.DMA((2 * n + 3 + QUAD,)),
        ],
        compiler_params=pltpu.CompilerParams(vmem_limit_bytes=28 * MEBI),
        cost_estimate=pl.CostEstimate(
            flops=2 * positions * channels * 3 * SET_CHANNELS
            + 4 * positions * OUTER * block * SET_CHANNELS,
            bytes_accessed=2 * (positions * channels + 3 * SET_CHANNELS * channels),
            transcendentals=positions * OUTER * block * SET_HEADS,
        ),
        name="attention",
    )(sources, *hidden_pieces, *weights)

    if inner == 2:
        far, last = after([jnp.concatenate([far, across], axis=0), last], [kept])
        out_weights = [w_out] + near + [far, swap(far, 1), last, swap(last, 1)]
    received = [attended[0]]
    for step in range(1, OUTER):
        pairs = [(at, (at + step * inner) % n) for at in range(n)]
        received.append(lax.ppermute(attended[step], "patch", pairs))

    output = pl.pallas_call(
        functools.partial(output_kernel, n),
        out_shape=jax.ShapeDtypeStruct((block, channels), bf16),
        in_specs=[vmem] * (OUTER + 1 + len(out_weights)),
        out_specs=vmem,
        scratch_shapes=[
            pltpu.VMEM((channels, block), bf16),
            pltpu.VMEM((channels, block), f32),
        ],
        compiler_params=pltpu.CompilerParams(vmem_limit_bytes=12 * MEBI),
        cost_estimate=pl.CostEstimate(
            flops=2 * block * channels * channels,
            bytes_accessed=2 * channels * (channels + 3 * block),
            transcendentals=0,
        ),
        name="project",
    )(*received, kept, *out_weights)
    return output.reshape(rows_local, columns, channels)


def solution(mesh):
    return jax.shard_map(
        on_device,
        mesh=mesh,
        in_specs=(
            P(("batch", "patch"), None, None),
            P(None, None, "patch", None),
            P("patch"),
            P("patch", None),
            P("patch", None),
            P("patch", None),
            P("patch", None),
        ),
        out_specs=P(("batch", "patch"), None, None),
        check_vma=False,
    )
```

```python
import functools

import jax
import jax.numpy as jnp
from jax import lax
from jax.experimental import pallas as pl
from jax.experimental.pallas import tpu as pltpu
from jax.sharding import PartitionSpec as P

C = 1280
HEADS = 20
HEAD_DIM = 64
GROUPS = 32
SPAN = C // GROUPS
OUTER = 4
SET_HEADS = HEADS // OUTER
SET_CHANNELS = SET_HEADS * HEAD_DIM
QUAD = 4
GRANULE = 32
HANDED = (0, 2, 1, 3)
FAR = ((1, 0), (2, 0), (3, 0), (2, 1))
LAST = ((1, 1), (3, 1))
SOONER, LATER = (1, 2), (3, 0)
EPSILON = 1e-05
MEBI = 1024 * 1024

f32 = jnp.float32
bf16 = jnp.bfloat16

NT = (((1,), (1,)), ((), ()))
NN = (((1,), (0,)), ((), ()))


def dot(left, right, dims=NN):
    return lax.dot_general(left, right, dims, preferred_element_type=f32)


def exact(row, member, dims=NN):
    high = row.astype(bf16).astype(f32)
    middle = (row - high).astype(bf16).astype(f32)
    parts = [high, middle, row - high - middle, jnp.zeros((13, row.shape[1]), f32)]
    return jnp.sum(dot(jnp.concatenate(parts, axis=0).astype(bf16), member, dims), axis=0, keepdims=True)


def conv_kernel(columns, sources_ref, *refs):
    count = len(refs) - 6
    pieces = refs[:count]
    kernel_ref, bias_ref = refs[count : count + 2]
    out_refs = refs[count + 2 : count + 4]
    act_ref, kept_ref = refs[count + 4 :]
    block = pieces[0].shape[0]
    positions = block * count
    own = out_refs[0].shape[0]
    me = lax.axis_index("patch")
    entries = float(positions * SPAN)
    chunk = 16
    steps = block // chunk
    starts = [
        pl.multiple_of(sources_ref[me * count + index] * (2 * block) + (index % 2) * block, block)
        for index in range(count)
    ]

    def add(step, total):
        for piece in pieces:
            total = total + piece[pl.ds(step * chunk, chunk), :].astype(f32)
        return total

    member = (
        lax.broadcasted_iota(jnp.int32, (C, 128), 0) // SPAN
        == lax.broadcasted_iota(jnp.int32, (C, 128), 1)
    ).astype(bf16)

    def group_mean(total):
        summed = jnp.sum(total, axis=0, keepdims=True)
        return exact(exact(summed, member) / entries, member, NT)

    zero = jnp.zeros((chunk, C), f32)
    centre = group_mean(lax.fori_loop(0, steps, add, zero))

    def add_square(step, total):
        for piece in pieces:
            away = piece[pl.ds(step * chunk, chunk), :].astype(f32) - centre
            total = total + away * away
        return total

    spread = group_mean(lax.fori_loop(0, steps, add_square, zero))
    half_scale = 0.5 * lax.rsqrt(spread + EPSILON)

    act_ref[0:columns, :] = jnp.zeros((columns, C), bf16)
    act_ref[positions + columns :, :] = jnp.zeros((columns, C), bf16)

    def activate(step, carry):
        for start, piece in zip(starts, pieces):
            half = (piece[pl.ds(step * chunk, chunk), :].astype(f32) - centre) * half_scale
            value = half + half * jnp.tanh(half)
            row = pl.multiple_of(columns + start + step * chunk, chunk)
            act_ref[pl.ds(row, chunk), :] = value.astype(bf16)
        return carry

    lax.fori_loop(0, steps, activate, 0)

    window = min(C, (own + 127) // 128 * 128 + 128)
    base = jnp.minimum(lax.div(me * own, 128) * 128, C - window)
    lanes = pl.ds(pl.multiple_of(base, 128), window)
    choose = (
        lax.broadcasted_iota(jnp.int32, (own, window), 0) + (me * own - base)
        == lax.broadcasted_iota(jnp.int32, (own, window), 1)
    ).astype(bf16)
    for index in range(0, count, 2):
        pair = jnp.concatenate([pieces[index][:, lanes], pieces[index + 1][:, lanes]], axis=0)
        start = pl.multiple_of(starts[index], 2 * block)
        kept_ref[:, pl.ds(start, 2 * block)] = dot(choose, pair, NT)

    wide = 256
    column = lax.broadcasted_iota(jnp.int32, (own, wide), 1) % columns
    square = (own, own)
    bias = jnp.where(
        lax.broadcasted_iota(jnp.int32, square, 0) == lax.broadcasted_iota(jnp.int32, square, 1),
        bias_ref[...],
        0.0,
    )
    bias = jnp.sum(bias, axis=1, keepdims=True)
    for at in range(0, positions, wide):
        taps = dot(kernel_ref[0], act_ref[at : at + wide, :], NT)
        for shift in (1, 2):
            low = at + shift * columns
            taps = taps + dot(kernel_ref[shift], act_ref[low : low + wide, :], NT)
        before = jnp.where(column > 0, pltpu.roll(taps[0:own], 1, 1), 0.0)
        after_ = jnp.where(column < columns - 1, pltpu.roll(taps[2 * own :], wide - 1, 1), 0.0)
        convolved = taps[own : 2 * own] + before + after_
        hidden = kept_ref[:, at : at + wide] + convolved + bias
        which, low = divmod(at, positions // 2)
        out_refs[which][:, low : low + wide] = hidden.astype(bf16)


def attention_kernel(count, inner, sources_ref, *refs):
    pieces = refs[:count]
    parts = refs[count:-9]
    outs = refs[-9:-7]
    kept_ref, later_ref, key_ref, value_ref, normed_ref, weight_ref, sems = refs[-7:]
    own, part = pieces[0].shape
    n = count // 2
    positions = 2 * part
    block = positions // n
    me = lax.axis_index("patch")
    outer_at, inner_at = lax.div(me, inner), lax.rem(me, inner)
    entries = float(positions * SPAN)
    loads = []

    def load(source, row):
        target = weight_ref.at[pl.ds(row, source.shape[0]), :]
        loads.append(pltpu.make_async_copy(source, target, sems.at[len(loads)]))

    if inner == 2:
        for kind in range(3):
            row = kind * SET_CHANNELS + inner_at * own
            load(parts[kind], pl.multiple_of(row, own))
        mine = lax.rem(lax.axis_index("batch"), QUAD)
        for step, part_ref in zip(HANDED, parts[3:]):
            place = jnp.bitwise_xor(mine, step)
            first = quarter_start(place, own)
            twice = QUAD * (part_ref.shape[0] // GRANULE) - 3 * own // GRANULE
            for at in range(part_ref.shape[0] // GRANULE):
                granule = first + at
                kind = lax.div(granule, own // GRANULE)
                row = kind * SET_CHANNELS + (1 - inner_at) * own
                row = row + lax.rem(granule, own // GRANULE) * GRANULE
                if at < twice:
                    spare = 3 * SET_CHANNELS + at * GRANULE
                    row = jnp.where(place == QUAD - 1, spare, row)
                source = part_ref.at[at * GRANULE : (at + 1) * GRANULE, :]
                load(source, pl.multiple_of(row, GRANULE))
    else:
        load(parts[0], 0)
    for copy in loads:
        copy.start()

    groups = [(at, low) for at in range(0, count, 2) for low in range(0, own, SPAN)]

    def whole(values):
        return jnp.sum(jnp.sum(values, axis=0, keepdims=True), axis=1, keepdims=True)

    def group_of(at, low):
        halves = []
        for piece in pieces[at : at + 2]:
            first = low // 16 * 16
            rows = piece[first : -(-(low + SPAN) // 16) * 16, :].astype(f32)
            halves.append(rows[low - first : low - first + SPAN])
        return halves

    means = [sum(whole(half) for half in group_of(*group)) / entries for group in groups]
    scales = []
    for mean, group in zip(means, groups):
        square = sum(whole(jnp.square(half - mean)) for half in group_of(*group))
        scales.append(lax.rsqrt(square / entries + EPSILON))
    for at in range(0, count, 2):
        row = pl.multiple_of(sources_ref[me * count + at] * own, own)
        which = [index for index, group in enumerate(groups) if group[0] == at]
        mean = jnp.concatenate([jnp.broadcast_to(means[index], (SPAN, 1)) for index in which], axis=0)
        scale = jnp.concatenate([jnp.broadcast_to(scales[index], (SPAN, 1)) for index in which], axis=0)
        for half, piece in enumerate(pieces[at : at + 2]):
            normed = (piece[...].astype(f32) - mean) * scale
            normed_ref[pl.ds(row, own), half * part : (half + 1) * part] = normed.astype(bf16)
        start = pl.multiple_of(lax.rem(me, n // 2) * block, block)
        low, high = (piece[:, pl.ds(start, block)] for piece in pieces[at : at + 2])
        kept_ref[pl.ds(row, own), :] = jnp.where(me < n // 2, low, high)

    for copy in loads:
        copy.wait()
    wide = 256
    for at in range(0, positions, wide):
        made = dot(weight_ref[SET_CHANNELS : 3 * SET_CHANNELS, :], normed_ref[:, at : at + wide])
        for head in range(SET_HEADS):
            low = head * HEAD_DIM
            key_ref[head, at : at + wide, :] = made[low : low + HEAD_DIM].T.astype(bf16)
        value_ref[:, at : at + wide] = made[SET_CHANNELS:].astype(bf16)

    def queries(steps):
        normed = []
        for step in steps:
            target = lax.rem(outer_at + step, OUTER) * inner + inner_at
            normed.append(normed_ref[:, pl.ds(pl.multiple_of(target * block, block), block)])
        made = dot(weight_ref[:SET_CHANNELS, :], jnp.concatenate(normed, axis=1))
        return (made.astype(bf16).astype(f32) * HEAD_DIM ** (-0.5)).astype(bf16)

    later_ref[...] = queries(LATER)
    attend(queries(SOONER), key_ref, value_ref, outs)


def later_kernel(query_ref, key_ref, value_ref, *outs):
    attend(query_ref[...], key_ref, value_ref, outs)


def attend(query, key_ref, value_ref, outs):
    block = outs[0].shape[1]
    for head in range(SET_HEADS):
        low = head * HEAD_DIM
        scores = dot(key_ref[head], query[low : low + HEAD_DIM])
        peak = jnp.max(scores, axis=0, keepdims=True)
        unnormalized = jnp.exp(scores - peak)
        total = jnp.sum(unnormalized, axis=0, keepdims=True)
        mixture = dot(value_ref[low : low + HEAD_DIM, :], unnormalized.astype(bf16))
        attended = (mixture / total).astype(bf16)
        for place, out in enumerate(outs):
            out[low : low + HEAD_DIM, :] = attended[:, place * block : (place + 1) * block]


def output_kernel(n, *refs):
    attended_refs = refs[:OUTER]
    hidden_ref = refs[OUTER]
    weight_refs = refs[OUTER + 1 : -3]
    out_ref, attended_ref, total_ref = refs[-3:]
    inner = n // OUTER
    own = C // n
    me = lax.axis_index("patch")
    outer_at, inner_at = lax.div(me, inner), lax.rem(me, inner)
    for step in range(OUTER):
        origin = lax.rem(outer_at + OUTER - step, OUTER)
        row = pl.multiple_of(origin * SET_CHANNELS, SET_CHANNELS)
        attended_ref[pl.ds(row, SET_CHANNELS), :] = attended_refs[step][...]
    attended = attended_ref[...]
    if inner != 2:
        total = dot(weight_refs[0][...], attended) + hidden_ref[...].astype(f32)
        out_ref[...] = total.T.astype(bf16)
        return

    total_ref[...] = hidden_ref[...].astype(f32)
    mine = lax.rem(lax.axis_index("batch"), QUAD)
    core = lax.rem(mine, 2)

    def add(weights, outer_step, inner_step, low=0):
        origin = lax.rem(outer_at + OUTER - outer_step, OUTER) * inner
        origin = origin + lax.rem(inner_at + inner_step, inner)
        rows = pl.ds(pl.multiple_of(origin * own + low, 16), weights.shape[0])
        total_ref[rows, :] += dot(weights, attended)

    own_ref, far_ref, far_other_ref, last_ref, last_other_ref = weight_refs
    add(own_ref[...], 0, 0)
    for holder, ref in ((mine, far_ref), (jnp.bitwise_xor(mine, 1), far_other_ref)):
        for step in (0, 1):
            which = jnp.bitwise_xor(holder, 2 * step)
            outer_step = jnp.where(which == 0, 1, jnp.where(which == 2, 3, 2))
            add(ref[step * own : (step + 1) * own, :], outer_step, lax.div(which, QUAD - 1))
        add(ref[2 * own :, :], 0, 1, lax.rem(holder, 2) * (own // 2))
    add(last_ref[...], 1 + 2 * core, 1)
    add(last_other_ref[...], 3 - 2 * core, 1)
    out_ref[...] = total_ref[...].T.astype(bf16)


def quarter_rows(own):
    return -(-3 * own // (QUAD * GRANULE)) * GRANULE


def quarter_start(place, own):
    part = quarter_rows(own) // GRANULE
    return jnp.minimum(place * part, 3 * own // GRANULE - part)


def ring_of(n):
    inner = n // OUTER
    path = [(0, 0)]
    for outer_at in range(OUTER):
        across = range(1, inner) if outer_at % 2 == 0 else range(inner - 1, 0, -1)
        path += [(outer_at, inner_at) for inner_at in across]
    path += [(outer_at, 0) for outer_at in range(OUTER - 1, 0, -1)]
    return [outer_at * inner + inner_at for outer_at, inner_at in path]


def pieces_of(n):
    far = n // 2
    return [0] + [away for step in range(1, far) for away in (-step, step)] + [far]


def sources_of(n):
    ring = ring_of(n)
    table = []
    for device in range(n):
        at = ring.index(device)
        table.append([ring[(at + away) % n] for away in pieces_of(n) for _ in (0, 1)])
    return table


def gather(halves, n, beside=()):
    ring = ring_of(n)
    forward = [(ring[at], ring[(at + 1) % n]) for at in range(n)]
    backward = [(target, start) for start, target in forward]
    far = n // 2
    found = {(0, 0): halves[0], (1, 0): halves[1]}
    for step in range(1, far + 1):
        for half in (0, 1):
            for sign, pairs in ((-1, forward), (1, backward)):
                if step == far and (half == 0) != (sign == -1):
                    continue
                found[half, sign * step] = lax.ppermute(
                    found[half, sign * (step - 1)], "patch", pairs
                )
        if step == 1 and beside:
            (found[0, -1],) = after([found[0, -1]], beside)
    found[0, far] = found[0, -far]
    return [found[half, away] for away in pieces_of(n) for half in (0, 1)]


def send(block, shifts):
    batch, n = lax.axis_size("batch"), lax.axis_size("patch")
    pairs = []
    for at in range(batch):
        for start, target in moves(n, *shifts[at % len(shifts)]):
            pairs.append((at * n + start, at * n + target))
    return lax.ppermute(block, ("batch", "patch"), pairs)


def swap(block, bit):
    pairs = [(at, at ^ bit) for at in range(lax.axis_size("batch"))]
    return lax.ppermute(block, "batch", pairs)


def moves(n, outer_step, inner_step):
    inner = n // OUTER
    pairs = []
    for start in range(n):
        outer_at = (start // inner + outer_step) % OUTER
        inner_at = (start % inner + inner_step) % inner
        pairs.append((start, outer_at * inner + inner_at))
    return pairs


def after(values, ready):
    anywhere = pl.BlockSpec(memory_space=pl.ANY)
    made = pl.pallas_call(
        lambda *refs: None,
        out_shape=[jax.ShapeDtypeStruct(value.shape, value.dtype) for value in values],
        in_specs=[anywhere] * (len(values) + len(ready)),
        out_specs=[anywhere] * len(values),
        input_output_aliases={at: at for at in range(len(values))},
        compiler_params=pltpu.CompilerParams(vmem_limit_bytes=MEBI),
        cost_estimate=pl.CostEstimate(flops=0, bytes_accessed=0, transcendentals=0),
        name="after",
    )(*values, *ready)
    return list(made)


def on_device(latent, conv_weight, channel_bias, w_query, w_key, w_value, w_out):
    rows_local, columns, channels = latent.shape
    n = lax.axis_size("patch")
    inner = n // OUTER
    own = channels // n
    block = rows_local * columns
    positions = block * n
    sources = jnp.asarray(sources_of(n), jnp.int32).reshape(-1)
    vmem = pl.BlockSpec(memory_space=pltpu.VMEM)
    smem = pl.BlockSpec(memory_space=pltpu.SMEM)
    anywhere = pl.BlockSpec(memory_space=pl.ANY)

    whole = latent.reshape(block, channels)
    halves = whole[: block // 2], whole[block // 2 :]
    if inner == 2:
        quarter = quarter_rows(own)
        core = lax.rem(lax.axis_index("batch"), 2)
        start = quarter_start(lax.rem(lax.axis_index("batch"), QUAD), own) * GRANULE
        stacked = jnp.concatenate([w_query, w_key, w_value], axis=0)
        chosen = jnp.concatenate(
            [
                lax.dynamic_slice_in_dim(stacked, start, quarter, 0),
                lax.dynamic_slice_in_dim(w_out, core * (own // 2), own // 2, 0),
            ],
            axis=0,
        )
        pieces = gather(halves, n, [chosen])
        chosen, out_own = after([chosen, w_out], pieces[-5:])
        chosen = send(chosen, [(0, 1)])
        far = send(out_own, FAR)
    else:
        pieces = gather(halves, n)
        sets = [list(range(at, at + inner)) for at in range(0, n, inner)]
        weights = jnp.stack([w_query, w_key, w_value])
        weights = lax.all_gather(weights, "patch", axis=1, tiled=True, axis_index_groups=sets)
        weights = [weights.reshape(3 * SET_CHANNELS, channels)]
        out_weights = [lax.all_gather(w_out, "patch", axis=0, tiled=True)]

    hidden = pl.pallas_call(
        functools.partial(conv_kernel, columns),
        out_shape=[jax.ShapeDtypeStruct((own, positions // 2), bf16)] * 2,
        in_specs=[smem] + [vmem] * (2 * n + 2),
        out_specs=[vmem] * 2,
        scratch_shapes=[
            pltpu.VMEM((positions + 2 * columns, channels), bf16),
            pltpu.VMEM((own, positions), f32),
        ],
        compiler_params=pltpu.CompilerParams(vmem_limit_bytes=20 * MEBI),
        cost_estimate=pl.CostEstimate(
            flops=2 * 9 * positions * channels * own,
            bytes_accessed=2 * (positions * channels + 9 * channels * own),
            transcendentals=positions * channels,
        ),
        name="norm_conv",
    )(
        sources,
        *pieces,
        conv_weight.reshape(3, 3 * own, channels),
        channel_bias.reshape(1, own),
    )

    hidden_pieces = gather(tuple(hidden), n)
    if inner == 2:
        chosen, far = after([chosen, far], hidden[:1])
        near = [chosen[:quarter]]
        near.append(swap(near[0], 2))
        near += [swap(one, 1) for one in near]
        weights = [w_query, w_key, w_value] + near
        far, out_own = after([far, out_own], hidden_pieces[-5:] + near)
        across = swap(far, 2)
        last = send(out_own, LAST)

    pair = [jax.ShapeDtypeStruct((SET_CHANNELS, block), bf16)] * 2
    attended = {}
    attended[SOONER[0]], attended[SOONER[1]], kept, query, key, value = pl.pallas_call(
        functools.partial(attention_kernel, 2 * n, inner),
        out_shape=pair
        + [
            jax.ShapeDtypeStruct((channels, block), bf16),
            jax.ShapeDtypeStruct((SET_CHANNELS, 2 * block), bf16),
            jax.ShapeDtypeStruct((SET_HEADS, positions, HEAD_DIM), bf16),
            jax.ShapeDtypeStruct((SET_CHANNELS, positions), bf16),
        ],
        in_specs=[smem] + [vmem] * (2 * n) + [anywhere] * len(weights),
        out_specs=[vmem] * 6,
        scratch_shapes=[
            pltpu.VMEM((channels, positions), bf16),
            pltpu.VMEM((QUAD * SET_CHANNELS, channels), bf16),
            pltpu.SemaphoreType.DMA((3 + QUAD * quarter_rows(own) // GRANULE,)),
        ],
        compiler_params=pltpu.CompilerParams(vmem_limit_bytes=28 * MEBI),
        cost_estimate=pl.CostEstimate(
            flops=2 * positions * channels * 3 * SET_CHANNELS
            + 8 * positions * block * SET_CHANNELS,
            bytes_accessed=2 * (positions * channels + 3 * SET_CHANNELS * channels),
            transcendentals=positions * 2 * block * SET_HEADS,
        ),
        name="attention",
    )(sources, *hidden_pieces, *weights)
    attended[LATER[0]], attended[LATER[1]] = pl.pallas_call(
        later_kernel,
        out_shape=pair,
        in_specs=[vmem] * 3,
        out_specs=[vmem] * 2,
        compiler_params=pltpu.CompilerParams(vmem_limit_bytes=16 * MEBI),
        cost_estimate=pl.CostEstimate(
            flops=8 * positions * block * SET_CHANNELS,
            bytes_accessed=8 * positions * SET_CHANNELS,
            transcendentals=positions * 2 * block * SET_HEADS,
        ),
        name="later_attention",
    )(query, key, value)

    def hand_over(step):
        pairs = [(at, (at + step * inner) % n) for at in range(n)]
        return lax.ppermute(attended[step], "patch", pairs)

    received = {step: hand_over(step) for step in SOONER}
    first, last_step = list(received.values()), LATER[0]
    (attended[last_step],) = after([attended[last_step]], first)
    received[last_step] = hand_over(last_step)
    received[0] = attended[0]
    if inner == 2:
        far = jnp.concatenate([far, across, chosen[quarter:]], axis=0)
        far, last = after([far, last], [attended[SOONER[0]]])
        out_weights = [w_out, far, swap(far, 1), last, swap(last, 1)]

    output = pl.pallas_call(
        functools.partial(output_kernel, n),
        out_shape=jax.ShapeDtypeStruct((block, channels), bf16),
        in_specs=[vmem] * (OUTER + 1 + len(out_weights)),
        out_specs=vmem,
        scratch_shapes=[
            pltpu.VMEM((channels, block), bf16),
            pltpu.VMEM((channels, block), f32),
        ],
        compiler_params=pltpu.CompilerParams(vmem_limit_bytes=12 * MEBI),
        cost_estimate=pl.CostEstimate(
            flops=2 * block * channels * channels,
            bytes_accessed=2 * channels * (channels + 3 * block),
            transcendentals=0,
        ),
        name="project",
    )(*[received[step] for step in range(OUTER)], kept, *out_weights)
    return output.reshape(rows_local, columns, channels)


def solution(mesh):
    return jax.shard_map(
        on_device,
        mesh=mesh,
        in_specs=(
            P(("batch", "patch"), None, None),
            P(None, None, "patch", None),
            P("patch"),
            P("patch", None),
            P("patch", None),
            P("patch", None),
            P("patch", None),
        ),
        out_specs=P(("batch", "patch"), None, None),
        check_vma=False,
    )
```

```python
import functools

import jax
import jax.numpy as jnp
from jax import lax
from jax.experimental import pallas as pl
from jax.experimental.pallas import tpu as pltpu
from jax.sharding import PartitionSpec as P

C = 1280
HEADS = 20
HEAD_DIM = 64
GROUPS = 32
SPAN = C // GROUPS
OUTER = 4
SET_HEADS = HEADS // OUTER
SET_CHANNELS = SET_HEADS * HEAD_DIM
QUAD = 4
GRANULE = 32
HANDED = (0, 2, 1, 3)
FAR = ((1, 0), (2, 0), (3, 0), (2, 1))
LAST = ((1, 1), (3, 1))
SOONER = tuple(range(1, OUTER))
WIDE = 256
EPSILON = 1e-05
CHUNK = 16
MEBI = 1024 * 1024

f32 = jnp.float32
bf16 = jnp.bfloat16

NT = (((1,), (1,)), ((), ()))
NN = (((1,), (0,)), ((), ()))


def dot(left, right, dims=NN):
    return lax.dot_general(left, right, dims, preferred_element_type=f32)


def exact(row, member, dims=NN):
    high = row.astype(bf16).astype(f32)
    middle = (row - high).astype(bf16).astype(f32)
    parts = [high, middle, row - high - middle, jnp.zeros((13, row.shape[1]), f32)]
    return jnp.sum(dot(jnp.concatenate(parts, axis=0).astype(bf16), member, dims), axis=0, keepdims=True)


def stats_kernel(*refs):
    pieces, out_ref = refs[:-1], refs[-1]
    block = pieces[0].shape[0]
    steps = block // CHUNK

    def add(step, total):
        for piece in pieces[:2]:
            total = total + folded(piece[pl.ds(step * CHUNK, CHUNK), :].astype(f32))
        return total

    zero = jnp.zeros((8, C), f32)
    pivot = jnp.sum(lax.fori_loop(0, steps, add, zero), axis=0, keepdims=True) / (2 * block)
    first, second = add_moments(pieces, pivot, zero, zero)
    out_ref[0:8, :] = jnp.broadcast_to(pivot, (8, C))
    out_ref[8:16, :] = first
    out_ref[16:24, :] = second


def folded(rows):
    return rows[:8] + rows[8:]


def add_moments(pieces, pivot, first, second):
    def add(step, sums):
        first, second = sums
        for piece in pieces:
            away = piece[pl.ds(step * CHUNK, CHUNK), :].astype(f32) - pivot
            first = first + folded(away)
            second = second + folded(away * away)
        return first, second

    return lax.fori_loop(0, pieces[0].shape[0] // CHUNK, add, (first, second))


def conv_kernel(columns, sources_ref, *refs):
    count = len(refs) - 7
    pieces = refs[:count]
    stats_ref, kernel_ref, bias_ref = refs[count : count + 3]
    out_refs = refs[count + 3 : count + 5]
    act_ref, kept_ref = refs[count + 5 :]
    block = pieces[0].shape[0]
    positions = block * count
    own = out_refs[0].shape[0]
    me = lax.axis_index("patch")
    steps = block // CHUNK
    starts = [
        pl.multiple_of(sources_ref[me * count + index] * (2 * block) + (index % 2) * block, block)
        for index in range(count)
    ]

    member = (
        lax.broadcasted_iota(jnp.int32, (C, 128), 0) // SPAN
        == lax.broadcasted_iota(jnp.int32, (C, 128), 1)
    ).astype(bf16)

    def group_mean(per_channel):
        return exact(exact(per_channel, member) / SPAN, member, NT)

    pivot = stats_ref[0:1, :]
    first, second = add_moments(pieces[-2:], pivot, stats_ref[8:16, :], stats_ref[16:24, :])
    above = jnp.sum(first, axis=0, keepdims=True) / positions
    within = jnp.sum(second, axis=0, keepdims=True) / positions - above * above
    mean = pivot + above
    centre = group_mean(mean)
    spread = group_mean(within + (mean - centre) * (mean - centre))
    half_scale = 0.5 * lax.rsqrt(spread + EPSILON)

    act_ref[0:columns, :] = jnp.zeros((columns, C), bf16)
    act_ref[positions + columns :, :] = jnp.zeros((columns, C), bf16)

    def activate(step, carry):
        for start, piece in zip(starts, pieces):
            half = (piece[pl.ds(step * CHUNK, CHUNK), :].astype(f32) - centre) * half_scale
            value = half + half * jnp.tanh(half)
            row = pl.multiple_of(columns + start + step * CHUNK, CHUNK)
            act_ref[pl.ds(row, CHUNK), :] = value.astype(bf16)
        return carry

    lax.fori_loop(0, steps, activate, 0)

    window = window_of(own)
    base = jnp.minimum(lax.div(me * own, 128) * 128, C - window)
    lanes = pl.ds(pl.multiple_of(base, 128), window)
    choose = (
        lax.broadcasted_iota(jnp.int32, (own, window), 0) + (me * own - base)
        == lax.broadcasted_iota(jnp.int32, (own, window), 1)
    ).astype(bf16)
    for index in range(0, count, 2):
        pair = jnp.concatenate([pieces[index][:, lanes], pieces[index + 1][:, lanes]], axis=0)
        start = pl.multiple_of(starts[index], 2 * block)
        kept_ref[:, pl.ds(start, 2 * block)] = dot(choose, pair, NT)

    wide = WIDE
    column = lax.broadcasted_iota(jnp.int32, (own, wide), 1) % columns
    square = (own, own)
    bias = jnp.where(
        lax.broadcasted_iota(jnp.int32, square, 0) == lax.broadcasted_iota(jnp.int32, square, 1),
        bias_ref[...],
        0.0,
    )
    bias = jnp.sum(bias, axis=1, keepdims=True)
    for at in range(0, positions, wide):
        taps = dot(kernel_ref[0], act_ref[at : at + wide, :], NT)
        for shift in (1, 2):
            low = at + shift * columns
            taps = taps + dot(kernel_ref[shift], act_ref[low : low + wide, :], NT)
        before = jnp.where(column > 0, pltpu.roll(taps[0:own], 1, 1), 0.0)
        after_ = jnp.where(column < columns - 1, pltpu.roll(taps[2 * own :], wide - 1, 1), 0.0)
        convolved = taps[own : 2 * own] + before + after_
        hidden = kept_ref[:, at : at + wide] + convolved + bias
        which, low = divmod(at, positions // 2)
        out_refs[which][:, low : low + wide] = hidden.astype(bf16)


def window_of(own):
    return min(C, (own + 127) // 128 * 128 + 128)


def norm_pair(pair):
    own = pair[0].shape[0]
    entries = float(2 * pair[0].shape[1] * SPAN)

    def whole(values):
        return jnp.sum(jnp.sum(values, axis=0, keepdims=True), axis=1, keepdims=True)

    def group_at(low):
        first, last = low // 16 * 16, -(-(low + SPAN) // 16) * 16
        return [ref[first:last, :].astype(f32)[low - first : low - first + SPAN] for ref in pair]

    lows = range(0, own, SPAN)
    means = [sum(whole(half) for half in group_at(low)) / entries for low in lows]
    squares = [
        sum(whole(jnp.square(half - mean)) for half in group_at(low))
        for low, mean in zip(lows, means)
    ]
    scales = [lax.rsqrt(square / entries + EPSILON) for square in squares]
    mean = jnp.concatenate([jnp.broadcast_to(one, (SPAN, 1)) for one in means], axis=0)
    scale = jnp.concatenate([jnp.broadcast_to(one, (SPAN, 1)) for one in scales], axis=0)
    return [((ref[...].astype(f32) - mean) * scale).astype(bf16) for ref in pair]


def own_lanes(pair, me, n):
    block = 2 * pair[0].shape[1] // n
    start = pl.multiple_of(lax.rem(me, n // 2) * block, block)
    low, high = (ref[:, pl.ds(start, block)] for ref in pair)
    return jnp.where(me < n // 2, low, high)


def project_kernel(count, sources_ref, *refs):
    pieces = refs[: count - 2]
    weight_refs = refs[count - 2 : -3]
    sums_ref, kept_ref, normed_ref = refs[-3:]
    own, part = pieces[0].shape
    me = lax.axis_index("patch")
    for at in range(0, count - 2, 2):
        pair = pieces[at : at + 2]
        rows = pl.ds(pl.multiple_of(sources_ref[me * count + at] * own, own), own)
        for half, normed in enumerate(norm_pair(pair)):
            normed_ref[rows, half * part : (half + 1) * part] = normed
        kept_ref[rows, :] = own_lanes(pair, me, count // 2)
    missing = pl.multiple_of(sources_ref[me * count + count - 2] * own, own)
    normed_ref[pl.ds(missing, own), :] = jnp.zeros((own, 2 * part), bf16)
    weights = jnp.concatenate([ref[...] for ref in weight_refs], axis=0)
    for at in range(0, 2 * part, WIDE):
        sums_ref[:, at : at + WIDE] = dot(weights, normed_ref[:, at : at + WIDE])


def attention_kernel(count, inner, sources_ref, *refs):
    pair = refs[:2]
    weight_refs = refs[2:-9]
    sums_ref, some_ref = refs[-9:-7]
    outs = refs[-7:-4]
    kept_ref, made_ref, key_ref, last_ref = refs[-4:]
    own, part = pair[0].shape
    n = count // 2
    me = lax.axis_index("patch")
    outer_at, inner_at = lax.div(me, inner), lax.rem(me, inner)
    source = sources_ref[me * count + count - 2]
    row = pl.multiple_of(source * own, own)
    kept_ref[...] = some_ref[...]
    kept_ref[pl.ds(row, own), :] = own_lanes(pair, me, n)

    window = last_ref.shape[0]
    base = jnp.minimum(lax.div(source * own, 128) * 128, C - window)
    lanes = pl.ds(pl.multiple_of(base, 128), window)
    last_ref[...] = jnp.zeros_like(last_ref)
    within = pl.ds(pl.multiple_of(source * own - base, 16), own)
    for half, normed in enumerate(norm_pair(pair)):
        last_ref[within, half * part : (half + 1) * part] = normed
    weights = jnp.concatenate([ref[:, lanes] for ref in weight_refs], axis=0)
    places = rows_of(weight_refs, own, inner, inner_at)
    for at in range(0, 2 * part, WIDE):
        made = dot(weights, last_ref[:, at : at + WIDE]) + sums_ref[:, at : at + WIDE]
        made = made.astype(bf16)
        for low, size, target in places:
            made_ref[pl.ds(target, size), at : at + WIDE] = made[low : low + size]

    for at in range(0, 2 * part, WIDE):
        for head in range(SET_HEADS):
            low = SET_CHANNELS + head * HEAD_DIM
            key = made_ref[low : low + HEAD_DIM, at : at + WIDE].astype(f32)
            key_ref[head, at : at + WIDE, :] = key.T.astype(bf16)

    targets = [lax.rem(outer_at + step, OUTER) * inner + inner_at for step in SOONER]
    attend(targets, made_ref, key_ref, outs)


def rows_of(weight_refs, own, inner, inner_at):
    if inner != 2:
        return [(0, weight_refs[0].shape[0], 0)]
    places = []
    for kind in range(3):
        place = kind * SET_CHANNELS + inner_at * own
        places.append((kind * own, own, pl.multiple_of(place, own)))
    mine = lax.rem(lax.axis_index("batch"), QUAD)
    size = weight_refs[3].shape[0]
    twice = QUAD * (size // GRANULE) - 3 * own // GRANULE
    for order, step in enumerate(HANDED):
        which = jnp.bitwise_xor(mine, step)
        first = quarter_start(which, own)
        for at in range(size // GRANULE):
            granule = first + at
            place = lax.div(granule, own // GRANULE) * SET_CHANNELS + (1 - inner_at) * own
            place = place + lax.rem(granule, own // GRANULE) * GRANULE
            if at < twice:
                place = jnp.where(which == QUAD - 1, 3 * SET_CHANNELS + at * GRANULE, place)
            low = 3 * own + order * size + at * GRANULE
            places.append((low, GRANULE, pl.multiple_of(place, GRANULE)))
    return places


def later_kernel(made_ref, key_ref, out_ref):
    attend([lax.axis_index("patch")], made_ref, key_ref, [out_ref])


def attend(targets, made_ref, key_ref, outs):
    block = outs[0].shape[1]
    starts = [pl.multiple_of(target * block, block) for target in targets]
    for head in range(SET_HEADS):
        low = head * HEAD_DIM
        query = [made_ref[low : low + HEAD_DIM, pl.ds(start, block)] for start in starts]
        query = jnp.concatenate(query, axis=1).astype(f32) * HEAD_DIM ** (-0.5)
        scores = dot(key_ref[head], query.astype(bf16))
        peak = jnp.max(scores, axis=0, keepdims=True)
        unnormalized = jnp.exp(scores - peak)
        total = jnp.sum(unnormalized, axis=0, keepdims=True)
        value = made_ref[2 * SET_CHANNELS + low : 2 * SET_CHANNELS + low + HEAD_DIM, :]
        mixture = dot(value, unnormalized.astype(bf16))
        attended = (mixture / total).astype(bf16)
        for place, out in enumerate(outs):
            out[low : low + HEAD_DIM, :] = attended[:, place * block : (place + 1) * block]


def output_kernel(n, *refs):
    attended_refs = refs[:OUTER]
    hidden_ref = refs[OUTER]
    weight_refs = refs[OUTER + 1 : -3]
    out_ref, attended_ref, total_ref = refs[-3:]
    inner = n // OUTER
    own = C // n
    me = lax.axis_index("patch")
    outer_at, inner_at = lax.div(me, inner), lax.rem(me, inner)
    for step in range(OUTER):
        origin = lax.rem(outer_at + OUTER - step, OUTER)
        row = pl.multiple_of(origin * SET_CHANNELS, SET_CHANNELS)
        attended_ref[pl.ds(row, SET_CHANNELS), :] = attended_refs[step][...]
    attended = attended_ref[...]
    if inner != 2:
        total = dot(weight_refs[0][...], attended) + hidden_ref[...].astype(f32)
        out_ref[...] = total.T.astype(bf16)
        return

    total_ref[...] = hidden_ref[...].astype(f32)
    mine = lax.rem(lax.axis_index("batch"), QUAD)
    core = lax.rem(mine, 2)

    def add(weights, outer_step, inner_step, low=0):
        origin = lax.rem(outer_at + OUTER - outer_step, OUTER) * inner
        origin = origin + lax.rem(inner_at + inner_step, inner)
        rows = pl.ds(pl.multiple_of(origin * own + low, 16), weights.shape[0])
        total_ref[rows, :] += dot(weights, attended)

    own_ref, far_ref, far_other_ref, last_ref, last_other_ref = weight_refs
    add(own_ref[...], 0, 0)
    for holder, ref in ((mine, far_ref), (jnp.bitwise_xor(mine, 1), far_other_ref)):
        for step in (0, 1):
            which = jnp.bitwise_xor(holder, 2 * step)
            outer_step = jnp.where(which == 0, 1, jnp.where(which == 2, 3, 2))
            add(ref[step * own : (step + 1) * own, :], outer_step, lax.div(which, QUAD - 1))
        add(ref[2 * own :, :], 0, 1, lax.rem(holder, 2) * (own // 2))
    add(last_ref[...], 1 + 2 * core, 1)
    add(last_other_ref[...], 3 - 2 * core, 1)
    out_ref[...] = total_ref[...].T.astype(bf16)


def quarter_rows(own):
    return -(-3 * own // (QUAD * GRANULE)) * GRANULE


def quarter_start(place, own):
    part = quarter_rows(own) // GRANULE
    return jnp.minimum(place * part, 3 * own // GRANULE - part)


def ring_of(n):
    inner = n // OUTER
    path = [(0, 0)]
    for outer_at in range(OUTER):
        across = range(1, inner) if outer_at % 2 == 0 else range(inner - 1, 0, -1)
        path += [(outer_at, inner_at) for inner_at in across]
    path += [(outer_at, 0) for outer_at in range(OUTER - 1, 0, -1)]
    return [outer_at * inner + inner_at for outer_at, inner_at in path]


def pieces_of(n):
    far = n // 2
    return [0] + [away for step in range(1, far) for away in (-step, step)] + [far]


def sources_of(n):
    ring = ring_of(n)
    table = []
    for device in range(n):
        at = ring.index(device)
        table.append([ring[(at + away) % n] for away in pieces_of(n) for _ in (0, 1)])
    return table


def gather(halves, n, beside=()):
    ring = ring_of(n)
    forward = [(ring[at], ring[(at + 1) % n]) for at in range(n)]
    backward = [(target, start) for start, target in forward]
    far = n // 2
    found = {(0, 0): halves[0], (1, 0): halves[1]}
    for step in range(1, far + 1):
        for half in (0, 1):
            for sign, pairs in ((-1, forward), (1, backward)):
                if step == far and (half == 0) != (sign == -1):
                    continue
                found[half, sign * step] = lax.ppermute(
                    found[half, sign * (step - 1)], "patch", pairs
                )
        if step == 1 and beside:
            (found[0, -1],) = after([found[0, -1]], beside)
    found[0, far] = found[0, -far]
    return [found[half, away] for away in pieces_of(n) for half in (0, 1)]


def send(block, shifts):
    batch, n = lax.axis_size("batch"), lax.axis_size("patch")
    pairs = []
    for at in range(batch):
        for start, target in moves(n, *shifts[at % len(shifts)]):
            pairs.append((at * n + start, at * n + target))
    return lax.ppermute(block, ("batch", "patch"), pairs)


def swap(block, bit):
    pairs = [(at, at ^ bit) for at in range(lax.axis_size("batch"))]
    return lax.ppermute(block, "batch", pairs)


def moves(n, outer_step, inner_step):
    inner = n // OUTER
    pairs = []
    for start in range(n):
        outer_at = (start // inner + outer_step) % OUTER
        inner_at = (start % inner + inner_step) % inner
        pairs.append((start, outer_at * inner + inner_at))
    return pairs


def after(values, ready):
    anywhere = pl.BlockSpec(memory_space=pl.ANY)
    made = pl.pallas_call(
        lambda *refs: None,
        out_shape=[jax.ShapeDtypeStruct(value.shape, value.dtype) for value in values],
        in_specs=[anywhere] * (len(values) + len(ready)),
        out_specs=[anywhere] * len(values),
        input_output_aliases={at: at for at in range(len(values))},
        compiler_params=pltpu.CompilerParams(vmem_limit_bytes=MEBI),
        cost_estimate=pl.CostEstimate(flops=0, bytes_accessed=0, transcendentals=0),
        name="after",
    )(*values, *ready)
    return list(made)


def on_device(latent, conv_weight, channel_bias, w_query, w_key, w_value, w_out):
    rows_local, columns, channels = latent.shape
    n = lax.axis_size("patch")
    inner = n // OUTER
    own = channels // n
    block = rows_local * columns
    positions = block * n
    sources = jnp.asarray(sources_of(n), jnp.int32).reshape(-1)
    vmem = pl.BlockSpec(memory_space=pltpu.VMEM)
    smem = pl.BlockSpec(memory_space=pltpu.SMEM)
    anywhere = pl.BlockSpec(memory_space=pl.ANY)

    whole = latent.reshape(block, channels)
    halves = whole[: block // 2], whole[block // 2 :]
    chosen = []
    if inner == 2:
        quarter = quarter_rows(own)
        core = lax.rem(lax.axis_index("batch"), 2)
        start = quarter_start(lax.rem(lax.axis_index("batch"), QUAD), own) * GRANULE
        stacked = jnp.concatenate([w_query, w_key, w_value], axis=0)
        chosen = [
            lax.dynamic_slice_in_dim(stacked, start, quarter, 0),
            lax.dynamic_slice_in_dim(w_out, core * (own // 2), own // 2, 0),
        ]
        chosen = [jnp.concatenate(chosen, axis=0)]
    pieces = gather(halves, n, chosen)
    stats = pl.pallas_call(
        stats_kernel,
        out_shape=jax.ShapeDtypeStruct((24, channels), f32),
        in_specs=[vmem] * (2 * n - 2),
        out_specs=vmem,
        compiler_params=pltpu.CompilerParams(vmem_limit_bytes=2 * MEBI),
        cost_estimate=pl.CostEstimate(
            flops=6 * positions * channels,
            bytes_accessed=2 * positions * channels,
            transcendentals=0,
        ),
        name="stats",
    )(*pieces[:-2])
    if inner == 2:
        chosen, out_own = after(chosen + [w_out], pieces[-5:] + [stats])
        chosen = send(chosen, [(0, 1)])
        far = send(out_own, FAR)
    else:
        sets = [list(range(at, at + inner)) for at in range(0, n, inner)]
        weights = jnp.stack([w_query, w_key, w_value])
        weights = lax.all_gather(weights, "patch", axis=1, tiled=True, axis_index_groups=sets)
        weights = [weights.reshape(3 * SET_CHANNELS, channels)]
        out_weights = [lax.all_gather(w_out, "patch", axis=0, tiled=True)]

    hidden = pl.pallas_call(
        functools.partial(conv_kernel, columns),
        out_shape=[jax.ShapeDtypeStruct((own, positions // 2), bf16)] * 2,
        in_specs=[smem] + [vmem] * (2 * n + 3),
        out_specs=[vmem] * 2,
        scratch_shapes=[
            pltpu.VMEM((positions + 2 * columns, channels), bf16),
            pltpu.VMEM((own, positions), f32),
        ],
        compiler_params=pltpu.CompilerParams(vmem_limit_bytes=20 * MEBI),
        cost_estimate=pl.CostEstimate(
            flops=2 * 9 * positions * channels * own,
            bytes_accessed=2 * (positions * channels + 9 * channels * own),
            transcendentals=positions * channels,
        ),
        name="norm_conv",
    )(
        sources,
        *pieces,
        stats,
        conv_weight.reshape(3, 3 * own, channels),
        channel_bias.reshape(1, own),
    )

    hidden_pieces = gather(tuple(hidden), n)
    if inner == 2:
        (chosen,) = after([chosen], hidden[:1])
        near = [chosen[:quarter]]
        near.append(swap(near[0], 2))
        near[0], far = after([near[0], far], near[1:])
        near += [swap(one, 1) for one in near]
        weights = [w_query, w_key, w_value] + near
    made_rows = sum(weight.shape[0] for weight in weights)
    sums, some = pl.pallas_call(
        functools.partial(project_kernel, 2 * n),
        out_shape=[
            jax.ShapeDtypeStruct((made_rows, positions), f32),
            jax.ShapeDtypeStruct((channels, block), bf16),
        ],
        in_specs=[smem] + [vmem] * (2 * n - 2 + len(weights)),
        out_specs=[vmem] * 2,
        scratch_shapes=[pltpu.VMEM((channels, positions), bf16)],
        compiler_params=pltpu.CompilerParams(vmem_limit_bytes=20 * MEBI),
        cost_estimate=pl.CostEstimate(
            flops=2 * positions * channels * made_rows,
            bytes_accessed=2 * (positions * channels + made_rows * channels),
            transcendentals=0,
        ),
        name="norm_project",
    )(sources, *hidden_pieces[:-2], *weights)
    if inner == 2:
        far, out_own = after([far, out_own], hidden_pieces[-5:] + [sums])
        across = swap(far, 2)
        last = send(out_own, LAST)
    one_block = jax.ShapeDtypeStruct((SET_CHANNELS, block), bf16)
    *sent, kept, made, key = pl.pallas_call(
        functools.partial(attention_kernel, 2 * n, inner),
        out_shape=[one_block] * len(SOONER)
        + [
            jax.ShapeDtypeStruct((channels, block), bf16),
            jax.ShapeDtypeStruct((made_rows, positions), bf16),
            jax.ShapeDtypeStruct((SET_HEADS, positions, HEAD_DIM), bf16),
        ],
        in_specs=[smem] + [vmem] * (4 + len(weights)),
        out_specs=[vmem] * (3 + len(SOONER)),
        scratch_shapes=[pltpu.VMEM((window_of(own), positions), bf16)],
        compiler_params=pltpu.CompilerParams(vmem_limit_bytes=28 * MEBI),
        cost_estimate=pl.CostEstimate(
            flops=2 * positions * window_of(own) * made_rows
            + 12 * positions * block * SET_CHANNELS,
            bytes_accessed=6 * made_rows * positions,
            transcendentals=positions * 3 * block * SET_HEADS,
        ),
        name="attention",
    )(sources, *hidden_pieces[-2:], *weights, sums, some)
    received = [None]
    for step, sent_block in zip(SOONER, sent):
        pairs = [(at, (at + step * inner) % n) for at in range(n)]
        received.append(lax.ppermute(sent_block, "patch", pairs))
    received[0] = pl.pallas_call(
        later_kernel,
        out_shape=one_block,
        in_specs=[vmem] * 2,
        out_specs=vmem,
        compiler_params=pltpu.CompilerParams(vmem_limit_bytes=16 * MEBI),
        cost_estimate=pl.CostEstimate(
            flops=4 * positions * block * SET_CHANNELS,
            bytes_accessed=8 * positions * SET_CHANNELS,
            transcendentals=positions * block * SET_HEADS,
        ),
        name="own_attention",
    )(made, key)
    if inner == 2:
        far = jnp.concatenate([far, across, chosen[quarter:]], axis=0)
        far, last = after([far, last], sent[:1])
        out_weights = [w_out, far, swap(far, 1), last, swap(last, 1)]

    output = pl.pallas_call(
        functools.partial(output_kernel, n),
        out_shape=jax.ShapeDtypeStruct((block, channels), bf16),
        in_specs=[vmem] * (OUTER + 1 + len(out_weights)),
        out_specs=vmem,
        scratch_shapes=[
            pltpu.VMEM((channels, block), bf16),
            pltpu.VMEM((channels, block), f32),
        ],
        compiler_params=pltpu.CompilerParams(vmem_limit_bytes=12 * MEBI),
        cost_estimate=pl.CostEstimate(
            flops=2 * block * channels * channels,
            bytes_accessed=2 * channels * (channels + 3 * block),
            transcendentals=0,
        ),
        name="project",
    )(*received, kept, *out_weights)
    return output.reshape(rows_local, columns, channels)


def solution(mesh):
    return jax.shard_map(
        on_device,
        mesh=mesh,
        in_specs=(
            P(("batch", "patch"), None, None),
            P(None, None, "patch", None),
            P("patch"),
            P("patch", None),
            P("patch", None),
            P("patch", None),
            P("patch", None),
        ),
        out_specs=P(("batch", "patch"), None, None),
        check_vma=False,
    )
```

```python
import functools

import jax
import jax.numpy as jnp
from jax import lax
from jax.experimental import pallas as pl
from jax.experimental.pallas import tpu as pltpu
from jax.sharding import PartitionSpec as P

C = 1280
HEADS = 20
HEAD_DIM = 64
GROUPS = 32
SPAN = C // GROUPS
OUTER = 4
SET_HEADS = HEADS // OUTER
SET_CHANNELS = SET_HEADS * HEAD_DIM
QUAD = 4
GRANULE = 32
HANDED = (0, 2, 1, 3)
FAR = ((1, 0), (2, 0), (3, 0), (2, 1))
LAST = ((1, 1), (3, 1))
SOONER = tuple(range(1, OUTER))
WIDE = 256
EPSILON = 1e-05
CHUNK = 16
MEBI = 1024 * 1024

f32 = jnp.float32
bf16 = jnp.bfloat16

NT = (((1,), (1,)), ((), ()))
NN = (((1,), (0,)), ((), ()))


def dot(left, right, dims=NN):
    return lax.dot_general(left, right, dims, preferred_element_type=f32)


def exact(row, member, dims=NN):
    high = row.astype(bf16).astype(f32)
    middle = (row - high).astype(bf16).astype(f32)
    parts = [high, middle, row - high - middle, jnp.zeros((13, row.shape[1]), f32)]
    return jnp.sum(dot(jnp.concatenate(parts, axis=0).astype(bf16), member, dims), axis=0, keepdims=True)


def stats_kernel(*refs):
    pieces, out_ref = refs[:-1], refs[-1]
    block = pieces[0].shape[0]
    steps = block // CHUNK

    def add(step, total):
        for piece in pieces[:2]:
            total = total + folded(piece[pl.ds(step * CHUNK, CHUNK), :].astype(f32))
        return total

    zero = jnp.zeros((8, C), f32)
    pivot = jnp.sum(lax.fori_loop(0, steps, add, zero), axis=0, keepdims=True) / (2 * block)
    first, second = add_moments(pieces, pivot, zero, zero)
    out_ref[0:8, :] = jnp.broadcast_to(pivot, (8, C))
    out_ref[8:16, :] = first
    out_ref[16:24, :] = second


def folded(rows):
    return rows[:8] + rows[8:]


def add_moments(pieces, pivot, first, second):
    def add(step, sums):
        first, second = sums
        for piece in pieces:
            away = piece[pl.ds(step * CHUNK, CHUNK), :].astype(f32) - pivot
            first = first + folded(away)
            second = second + folded(away * away)
        return first, second

    return lax.fori_loop(0, pieces[0].shape[0] // CHUNK, add, (first, second))


def conv_kernel(columns, sources_ref, *refs):
    count = len(refs) - 7
    pieces = refs[:count]
    stats_ref, kernel_ref, bias_ref = refs[count : count + 3]
    out_refs = refs[count + 3 : count + 5]
    act_ref, kept_ref = refs[count + 5 :]
    block = pieces[0].shape[0]
    positions = block * count
    own = out_refs[0].shape[0]
    me = lax.axis_index("patch")
    steps = block // CHUNK
    starts = [
        pl.multiple_of(sources_ref[me * count + index] * (2 * block) + (index % 2) * block, block)
        for index in range(count)
    ]

    member = (
        lax.broadcasted_iota(jnp.int32, (C, 128), 0) // SPAN
        == lax.broadcasted_iota(jnp.int32, (C, 128), 1)
    ).astype(bf16)

    def group_mean(per_channel):
        return exact(exact(per_channel, member) / SPAN, member, NT)

    pivot = stats_ref[0:1, :]
    first, second = add_moments(pieces[-2:], pivot, stats_ref[8:16, :], stats_ref[16:24, :])
    above = jnp.sum(first, axis=0, keepdims=True) / positions
    within = jnp.sum(second, axis=0, keepdims=True) / positions - above * above
    mean = pivot + above
    centre = group_mean(mean)
    spread = group_mean(within + (mean - centre) * (mean - centre))
    half_scale = 0.5 * lax.rsqrt(spread + EPSILON)

    act_ref[0:columns, :] = jnp.zeros((columns, C), bf16)
    act_ref[positions + columns :, :] = jnp.zeros((columns, C), bf16)

    def activate(step, carry):
        for start, piece in zip(starts, pieces):
            half = (piece[pl.ds(step * CHUNK, CHUNK), :].astype(f32) - centre) * half_scale
            value = half + half * jnp.tanh(half)
            row = pl.multiple_of(columns + start + step * CHUNK, CHUNK)
            act_ref[pl.ds(row, CHUNK), :] = value.astype(bf16)
        return carry

    lax.fori_loop(0, steps, activate, 0)

    window = window_of(own)
    base = jnp.minimum(lax.div(me * own, 128) * 128, C - window)
    lanes = pl.ds(pl.multiple_of(base, 128), window)
    choose = (
        lax.broadcasted_iota(jnp.int32, (own, window), 0) + (me * own - base)
        == lax.broadcasted_iota(jnp.int32, (own, window), 1)
    ).astype(bf16)
    for index in range(0, count, 2):
        pair = jnp.concatenate([pieces[index][:, lanes], pieces[index + 1][:, lanes]], axis=0)
        start = pl.multiple_of(starts[index], 2 * block)
        kept_ref[:, pl.ds(start, 2 * block)] = dot(choose, pair, NT)

    wide = WIDE
    column = lax.broadcasted_iota(jnp.int32, (own, wide), 1) % columns
    square = (own, own)
    bias = jnp.where(
        lax.broadcasted_iota(jnp.int32, square, 0) == lax.broadcasted_iota(jnp.int32, square, 1),
        bias_ref[...],
        0.0,
    )
    bias = jnp.sum(bias, axis=1, keepdims=True)
    for at in range(0, positions, wide):
        taps = dot(kernel_ref[0], act_ref[at : at + wide, :], NT)
        for shift in (1, 2):
            low = at + shift * columns
            taps = taps + dot(kernel_ref[shift], act_ref[low : low + wide, :], NT)
        before = jnp.where(column > 0, pltpu.roll(taps[0:own], 1, 1), 0.0)
        after_ = jnp.where(column < columns - 1, pltpu.roll(taps[2 * own :], wide - 1, 1), 0.0)
        convolved = taps[own : 2 * own] + before + after_
        hidden = kept_ref[:, at : at + wide] + convolved + bias
        which, low = divmod(at, positions // 2)
        out_refs[which][:, low : low + wide] = hidden.astype(bf16)


def window_of(own):
    return min(C, (own + 127) // 128 * 128 + 128)


def norm_pair(pair):
    own = pair[0].shape[0]
    entries = float(2 * pair[0].shape[1] * SPAN)

    def whole(values):
        return jnp.sum(jnp.sum(values, axis=0, keepdims=True), axis=1, keepdims=True)

    def group_at(low):
        first, last = low // 16 * 16, -(-(low + SPAN) // 16) * 16
        return [ref[first:last, :].astype(f32)[low - first : low - first + SPAN] for ref in pair]

    lows = range(0, own, SPAN)
    means = [sum(whole(half) for half in group_at(low)) / entries for low in lows]
    squares = [
        sum(whole(jnp.square(half - mean)) for half in group_at(low))
        for low, mean in zip(lows, means)
    ]
    scales = [lax.rsqrt(square / entries + EPSILON) for square in squares]
    mean = jnp.concatenate([jnp.broadcast_to(one, (SPAN, 1)) for one in means], axis=0)
    scale = jnp.concatenate([jnp.broadcast_to(one, (SPAN, 1)) for one in scales], axis=0)
    return [((ref[...].astype(f32) - mean) * scale).astype(bf16) for ref in pair]


def own_lanes(pair, me, n):
    block = 2 * pair[0].shape[1] // n
    start = pl.multiple_of(lax.rem(me, n // 2) * block, block)
    low, high = (ref[:, pl.ds(start, block)] for ref in pair)
    return jnp.where(me < n // 2, low, high)


def project_kernel(count, sources_ref, *refs):
    pieces = refs[: count - 2]
    weight_refs = refs[count - 2 : -3]
    sums_ref, kept_ref, normed_ref = refs[-3:]
    own, part = pieces[0].shape
    me = lax.axis_index("patch")
    for at in range(0, count - 2, 2):
        pair = pieces[at : at + 2]
        rows = pl.ds(pl.multiple_of(sources_ref[me * count + at] * own, own), own)
        for half, normed in enumerate(norm_pair(pair)):
            normed_ref[rows, half * part : (half + 1) * part] = normed
        kept_ref[rows, :] = own_lanes(pair, me, count // 2)
    missing = pl.multiple_of(sources_ref[me * count + count - 2] * own, own)
    normed_ref[pl.ds(missing, own), :] = jnp.zeros((own, 2 * part), bf16)
    weights = jnp.concatenate([ref[...] for ref in weight_refs], axis=0)
    for at in range(0, 2 * part, WIDE):
        sums_ref[:, at : at + WIDE] = dot(weights, normed_ref[:, at : at + WIDE])


def attention_kernel(count, inner, sources_ref, *refs):
    pair = refs[:2]
    weight_refs = refs[2:-9]
    sums_ref, some_ref = refs[-9:-7]
    outs = refs[-7:-4]
    kept_ref, made_ref, key_ref, last_ref = refs[-4:]
    own, part = pair[0].shape
    n = count // 2
    me = lax.axis_index("patch")
    outer_at, inner_at = lax.div(me, inner), lax.rem(me, inner)
    source = sources_ref[me * count + count - 2]
    row = pl.multiple_of(source * own, own)
    kept_ref[...] = some_ref[...]
    kept_ref[pl.ds(row, own), :] = own_lanes(pair, me, n)

    window = last_ref.shape[0]
    base = jnp.minimum(lax.div(source * own, 128) * 128, C - window)
    lanes = pl.ds(pl.multiple_of(base, 128), window)
    last_ref[...] = jnp.zeros_like(last_ref)
    within = pl.ds(pl.multiple_of(source * own - base, 16), own)
    for half, normed in enumerate(norm_pair(pair)):
        last_ref[within, half * part : (half + 1) * part] = normed
    weights = jnp.concatenate([ref[:, lanes] for ref in weight_refs], axis=0)
    places = rows_of(weight_refs, own, inner, inner_at)
    for at in range(0, 2 * part, WIDE):
        made = dot(weights, last_ref[:, at : at + WIDE]) + sums_ref[:, at : at + WIDE]
        made = made.astype(bf16)
        for low, size, target in places:
            made_ref[pl.ds(target, size), at : at + WIDE] = made[low : low + size]

    for at in range(0, 2 * part, WIDE):
        for head in range(SET_HEADS):
            low = SET_CHANNELS + head * HEAD_DIM
            key = made_ref[low : low + HEAD_DIM, at : at + WIDE].astype(f32)
            key_ref[head, at : at + WIDE, :] = key.T.astype(bf16)

    targets = [lax.rem(outer_at + step, OUTER) * inner + inner_at for step in SOONER]
    attend(targets, made_ref, key_ref, outs)


def rows_of(weight_refs, own, inner, inner_at):
    if inner != 2:
        return [(0, weight_refs[0].shape[0], 0)]
    places = []
    for kind in range(3):
        place = kind * SET_CHANNELS + inner_at * own
        places.append((kind * own, own, pl.multiple_of(place, own)))
    mine = lax.rem(lax.axis_index("batch"), QUAD)
    size = weight_refs[3].shape[0]
    twice = QUAD * (size // GRANULE) - 3 * own // GRANULE
    for order, step in enumerate(HANDED):
        which = jnp.bitwise_xor(mine, step)
        first = quarter_start(which, own)
        for at in range(size // GRANULE):
            granule = first + at
            place = lax.div(granule, own // GRANULE) * SET_CHANNELS + (1 - inner_at) * own
            place = place + lax.rem(granule, own // GRANULE) * GRANULE
            if at < twice:
                place = jnp.where(which == QUAD - 1, 3 * SET_CHANNELS + at * GRANULE, place)
            low = 3 * own + order * size + at * GRANULE
            places.append((low, GRANULE, pl.multiple_of(place, GRANULE)))
    return places


def later_kernel(made_ref, key_ref, out_ref):
    attend([lax.axis_index("patch")], made_ref, key_ref, [out_ref])


def attend(targets, made_ref, key_ref, outs):
    block = outs[0].shape[1]
    starts = [pl.multiple_of(target * block, block) for target in targets]
    for head in range(SET_HEADS):
        low = head * HEAD_DIM
        query = [made_ref[low : low + HEAD_DIM, pl.ds(start, block)] for start in starts]
        query = jnp.concatenate(query, axis=1).astype(f32) * HEAD_DIM ** (-0.5)
        scores = dot(key_ref[head], query.astype(bf16))
        peak = jnp.max(scores, axis=0, keepdims=True)
        unnormalized = jnp.exp(scores - peak)
        total = jnp.sum(unnormalized, axis=0, keepdims=True)
        value = made_ref[2 * SET_CHANNELS + low : 2 * SET_CHANNELS + low + HEAD_DIM, :]
        mixture = dot(value, unnormalized.astype(bf16))
        attended = (mixture / total).astype(bf16)
        for place, out in enumerate(outs):
            out[low : low + HEAD_DIM, :] = attended[:, place * block : (place + 1) * block]


def output_kernel(n, *refs):
    attended_refs = refs[:OUTER]
    hidden_ref = refs[OUTER]
    weight_refs = refs[OUTER + 1 : -3]
    out_ref, attended_ref, total_ref = refs[-3:]
    inner = n // OUTER
    own = C // n
    me = lax.axis_index("patch")
    outer_at, inner_at = lax.div(me, inner), lax.rem(me, inner)
    for step in range(OUTER):
        origin = lax.rem(outer_at + OUTER - step, OUTER)
        row = pl.multiple_of(origin * SET_CHANNELS, SET_CHANNELS)
        attended_ref[pl.ds(row, SET_CHANNELS), :] = attended_refs[step][...]
    attended = attended_ref[...]
    if inner != 2:
        total = dot(weight_refs[0][...], attended) + hidden_ref[...].astype(f32)
        out_ref[...] = total.T.astype(bf16)
        return

    total_ref[...] = hidden_ref[...].astype(f32)
    mine = lax.rem(lax.axis_index("batch"), QUAD)
    core = lax.rem(mine, 2)

    def add(weights, outer_step, inner_step, low=0):
        origin = lax.rem(outer_at + OUTER - outer_step, OUTER) * inner
        origin = origin + lax.rem(inner_at + inner_step, inner)
        rows = pl.ds(pl.multiple_of(origin * own + low, 16), weights.shape[0])
        total_ref[rows, :] += dot(weights, attended)

    own_ref, far_ref, far_other_ref, last_ref, last_other_ref = weight_refs
    add(own_ref[...], 0, 0)
    for holder, ref in ((mine, far_ref), (jnp.bitwise_xor(mine, 1), far_other_ref)):
        for step in (0, 1):
            which = jnp.bitwise_xor(holder, 2 * step)
            outer_step = jnp.where(which == 0, 1, jnp.where(which == 2, 3, 2))
            add(ref[step * own : (step + 1) * own, :], outer_step, lax.div(which, QUAD - 1))
        add(ref[2 * own :, :], 0, 1, lax.rem(holder, 2) * (own // 2))
    add(last_ref[...], 1 + 2 * core, 1)
    add(last_other_ref[...], 3 - 2 * core, 1)
    out_ref[...] = total_ref[...].T.astype(bf16)


def quarter_rows(own):
    return -(-3 * own // (QUAD * GRANULE)) * GRANULE


def quarter_start(place, own):
    part = quarter_rows(own) // GRANULE
    return jnp.minimum(place * part, 3 * own // GRANULE - part)


def ring_of(n):
    inner = n // OUTER
    path = [(0, 0)]
    for outer_at in range(OUTER):
        across = range(1, inner) if outer_at % 2 == 0 else range(inner - 1, 0, -1)
        path += [(outer_at, inner_at) for inner_at in across]
    path += [(outer_at, 0) for outer_at in range(OUTER - 1, 0, -1)]
    return [outer_at * inner + inner_at for outer_at, inner_at in path]


def pieces_of(n):
    far = n // 2
    return [0] + [away for step in range(1, far) for away in (-step, step)] + [far]


def sources_of(n):
    ring = ring_of(n)
    table = []
    for device in range(n):
        at = ring.index(device)
        table.append([ring[(at + away) % n] for away in pieces_of(n) for _ in (0, 1)])
    return table


def gather(halves, n, beside=()):
    ring = ring_of(n)
    forward = [(ring[at], ring[(at + 1) % n]) for at in range(n)]
    backward = [(target, start) for start, target in forward]
    far = n // 2
    found = {(0, 0): halves[0], (1, 0): halves[1]}
    for step in range(1, far + 1):
        for half in (0, 1):
            for sign, pairs in ((-1, forward), (1, backward)):
                if step == far and (half == 0) != (sign == -1):
                    continue
                found[half, sign * step] = lax.ppermute(
                    found[half, sign * (step - 1)], "patch", pairs
                )
        if step == 1 and beside:
            (found[0, -1],) = after([found[0, -1]], beside)
    found[0, far] = found[0, -far]
    return [found[half, away] for away in pieces_of(n) for half in (0, 1)]


def send(block, shifts):
    batch, n = lax.axis_size("batch"), lax.axis_size("patch")
    pairs = []
    for at in range(batch):
        for start, target in moves(n, *shifts[at % len(shifts)]):
            pairs.append((at * n + start, at * n + target))
    return lax.ppermute(block, ("batch", "patch"), pairs)


def swap(block, bit):
    pairs = [(at, at ^ bit) for at in range(lax.axis_size("batch"))]
    return lax.ppermute(block, "batch", pairs)


def moves(n, outer_step, inner_step):
    inner = n // OUTER
    pairs = []
    for start in range(n):
        outer_at = (start // inner + outer_step) % OUTER
        inner_at = (start % inner + inner_step) % inner
        pairs.append((start, outer_at * inner + inner_at))
    return pairs


def after(values, ready):
    anywhere = pl.BlockSpec(memory_space=pl.ANY)
    made = pl.pallas_call(
        lambda *refs: None,
        out_shape=[jax.ShapeDtypeStruct(value.shape, value.dtype) for value in values],
        in_specs=[anywhere] * (len(values) + len(ready)),
        out_specs=[anywhere] * len(values),
        input_output_aliases={at: at for at in range(len(values))},
        compiler_params=pltpu.CompilerParams(vmem_limit_bytes=MEBI),
        cost_estimate=pl.CostEstimate(flops=0, bytes_accessed=0, transcendentals=0),
        name="after",
    )(*values, *ready)
    return list(made)


def on_device(latent, conv_weight, channel_bias, w_query, w_key, w_value, w_out):
    rows_local, columns, channels = latent.shape
    n = lax.axis_size("patch")
    inner = n // OUTER
    own = channels // n
    block = rows_local * columns
    positions = block * n
    sources = jnp.asarray(sources_of(n), jnp.int32).reshape(-1)
    vmem = pl.BlockSpec(memory_space=pltpu.VMEM)
    smem = pl.BlockSpec(memory_space=pltpu.SMEM)
    anywhere = pl.BlockSpec(memory_space=pl.ANY)

    whole = latent.reshape(block, channels)
    halves = whole[: block // 2], whole[block // 2 :]
    chosen = []
    if inner == 2:
        quarter = quarter_rows(own)
        core = lax.rem(lax.axis_index("batch"), 2)
        start = quarter_start(lax.rem(lax.axis_index("batch"), QUAD), own) * GRANULE
        stacked = jnp.concatenate([w_query, w_key, w_value], axis=0)
        chosen = [
            lax.dynamic_slice_in_dim(stacked, start, quarter, 0),
            lax.dynamic_slice_in_dim(w_out, core * (own // 2), own // 2, 0),
        ]
        chosen = [jnp.concatenate(chosen, axis=0)]
    pieces = gather(halves, n, chosen)
    stats = pl.pallas_call(
        stats_kernel,
        out_shape=jax.ShapeDtypeStruct((24, channels), f32),
        in_specs=[vmem] * (2 * n - 2),
        out_specs=vmem,
        compiler_params=pltpu.CompilerParams(vmem_limit_bytes=2 * MEBI),
        cost_estimate=pl.CostEstimate(
            flops=6 * positions * channels,
            bytes_accessed=2 * positions * channels,
            transcendentals=0,
        ),
        name="stats",
    )(*pieces[:-2])
    if inner == 2:
        chosen, out_own = after(chosen + [w_out], pieces[-6:-2])
        chosen = send(chosen, [(0, 1)])
        far = send(out_own, FAR)
    else:
        sets = [list(range(at, at + inner)) for at in range(0, n, inner)]
        weights = jnp.stack([w_query, w_key, w_value])
        weights = lax.all_gather(weights, "patch", axis=1, tiled=True, axis_index_groups=sets)
        weights = [weights.reshape(3 * SET_CHANNELS, channels)]
        out_weights = [lax.all_gather(w_out, "patch", axis=0, tiled=True)]

    hidden = pl.pallas_call(
        functools.partial(conv_kernel, columns),
        out_shape=[jax.ShapeDtypeStruct((own, positions // 2), bf16)] * 2,
        in_specs=[smem] + [vmem] * (2 * n + 3),
        out_specs=[vmem] * 2,
        scratch_shapes=[
            pltpu.VMEM((positions + 2 * columns, channels), bf16),
            pltpu.VMEM((own, positions), f32),
        ],
        compiler_params=pltpu.CompilerParams(vmem_limit_bytes=20 * MEBI),
        cost_estimate=pl.CostEstimate(
            flops=2 * 9 * positions * channels * own,
            bytes_accessed=2 * (positions * channels + 9 * channels * own),
            transcendentals=positions * channels,
        ),
        name="norm_conv",
    )(
        sources,
        *pieces,
        stats,
        conv_weight.reshape(3, 3 * own, channels),
        channel_bias.reshape(1, own),
    )

    hidden_pieces = gather(tuple(hidden), n)
    if inner == 2:
        (chosen,) = after([chosen], hidden[:1])
        near = [chosen[:quarter]]
        near.append(swap(near[0], 2))
        near[0], far = after([near[0], far], near[1:])
        near += [swap(one, 1) for one in near]
        weights = [w_query, w_key, w_value] + near
    made_rows = sum(weight.shape[0] for weight in weights)
    sums, some = pl.pallas_call(
        functools.partial(project_kernel, 2 * n),
        out_shape=[
            jax.ShapeDtypeStruct((made_rows, positions), f32),
            jax.ShapeDtypeStruct((channels, block), bf16),
        ],
        in_specs=[smem] + [vmem] * (2 * n - 2 + len(weights)),
        out_specs=[vmem] * 2,
        scratch_shapes=[pltpu.VMEM((channels, positions), bf16)],
        compiler_params=pltpu.CompilerParams(vmem_limit_bytes=20 * MEBI),
        cost_estimate=pl.CostEstimate(
            flops=2 * positions * channels * made_rows,
            bytes_accessed=2 * (positions * channels + made_rows * channels),
            transcendentals=0,
        ),
        name="norm_project",
    )(sources, *hidden_pieces[:-2], *weights)
    if inner == 2:
        far, out_own = after([far, out_own], hidden_pieces[-6:-2])
        across = swap(far, 2)
        last = send(out_own, LAST)
    one_block = jax.ShapeDtypeStruct((SET_CHANNELS, block), bf16)
    *sent, kept, made, key = pl.pallas_call(
        functools.partial(attention_kernel, 2 * n, inner),
        out_shape=[one_block] * len(SOONER)
        + [
            jax.ShapeDtypeStruct((channels, block), bf16),
            jax.ShapeDtypeStruct((made_rows, positions), bf16),
            jax.ShapeDtypeStruct((SET_HEADS, positions, HEAD_DIM), bf16),
        ],
        in_specs=[smem] + [vmem] * (4 + len(weights)),
        out_specs=[vmem] * (3 + len(SOONER)),
        scratch_shapes=[pltpu.VMEM((window_of(own), positions), bf16)],
        compiler_params=pltpu.CompilerParams(vmem_limit_bytes=28 * MEBI),
        cost_estimate=pl.CostEstimate(
            flops=2 * positions * window_of(own) * made_rows
            + 12 * positions * block * SET_CHANNELS,
            bytes_accessed=6 * made_rows * positions,
            transcendentals=positions * 3 * block * SET_HEADS,
        ),
        name="attention",
    )(sources, *hidden_pieces[-2:], *weights, sums, some)
    received = [None]
    for step, sent_block in zip(SOONER, sent):
        pairs = [(at, (at + step * inner) % n) for at in range(n)]
        received.append(lax.ppermute(sent_block, "patch", pairs))
    received[0] = pl.pallas_call(
        later_kernel,
        out_shape=one_block,
        in_specs=[vmem] * 2,
        out_specs=vmem,
        compiler_params=pltpu.CompilerParams(vmem_limit_bytes=16 * MEBI),
        cost_estimate=pl.CostEstimate(
            flops=4 * positions * block * SET_CHANNELS,
            bytes_accessed=8 * positions * SET_CHANNELS,
            transcendentals=positions * block * SET_HEADS,
        ),
        name="own_attention",
    )(made, key)
    if inner == 2:
        far = jnp.concatenate([far, across, chosen[quarter:]], axis=0)
        far, last = after([far, last], sent[:1])
        out_weights = [w_out, far, swap(far, 1), last, swap(last, 1)]

    output = pl.pallas_call(
        functools.partial(output_kernel, n),
        out_shape=jax.ShapeDtypeStruct((block, channels), bf16),
        in_specs=[vmem] * (OUTER + 1 + len(out_weights)),
        out_specs=vmem,
        scratch_shapes=[
            pltpu.VMEM((channels, block), bf16),
            pltpu.VMEM((channels, block), f32),
        ],
        compiler_params=pltpu.CompilerParams(vmem_limit_bytes=12 * MEBI),
        cost_estimate=pl.CostEstimate(
            flops=2 * block * channels * channels,
            bytes_accessed=2 * channels * (channels + 3 * block),
            transcendentals=0,
        ),
        name="project",
    )(*received, kept, *out_weights)
    return output.reshape(rows_local, columns, channels)


def solution(mesh):
    return jax.shard_map(
        on_device,
        mesh=mesh,
        in_specs=(
            P(("batch", "patch"), None, None),
            P(None, None, "patch", None),
            P("patch"),
            P("patch", None),
            P("patch", None),
            P("patch", None),
            P("patch", None),
        ),
        out_specs=P(("batch", "patch"), None, None),
        check_vma=False,
    )
```

```python
import functools

import jax
import jax.numpy as jnp
from jax import lax
from jax.experimental import pallas as pl
from jax.experimental.pallas import tpu as pltpu
from jax.sharding import PartitionSpec as P

C = 1280
HEADS = 20
HEAD_DIM = 64
GROUPS = 32
SPAN = C // GROUPS
OUTER = 4
SET_HEADS = HEADS // OUTER
SET_CHANNELS = SET_HEADS * HEAD_DIM
QUAD = 4
GRANULE = 32
HANDED = (0, 2, 1, 3)
FAR = ((1, 0), (2, 0), (3, 0), (2, 1))
LAST = ((1, 1), (3, 1))
SOONER = tuple(range(1, OUTER))
WIDE = 256
EPSILON = 1e-05
CHUNK = 16
MEBI = 1024 * 1024

f32 = jnp.float32
bf16 = jnp.bfloat16

NT = (((1,), (1,)), ((), ()))
NN = (((1,), (0,)), ((), ()))


def dot(left, right, dims=NN):
    return lax.dot_general(left, right, dims, preferred_element_type=f32)


def exact(row, member, dims=NN):
    high = row.astype(bf16).astype(f32)
    middle = (row - high).astype(bf16).astype(f32)
    parts = [high, middle, row - high - middle, jnp.zeros((13, row.shape[1]), f32)]
    return jnp.sum(dot(jnp.concatenate(parts, axis=0).astype(bf16), member, dims), axis=0, keepdims=True)


def stats_kernel(*refs):
    pieces, out_ref = refs[:-1], refs[-1]
    block = pieces[0].shape[0]
    steps = block // CHUNK

    def add(step, total):
        for piece in pieces[:2]:
            total = total + folded(piece[pl.ds(step * CHUNK, CHUNK), :].astype(f32))
        return total

    zero = jnp.zeros((8, C), f32)
    pivot = jnp.sum(lax.fori_loop(0, steps, add, zero), axis=0, keepdims=True) / (2 * block)
    first, second = add_moments(pieces, pivot, zero, zero)
    out_ref[0:8, :] = jnp.broadcast_to(pivot, (8, C))
    out_ref[8:16, :] = first
    out_ref[16:24, :] = second


def folded(rows):
    return rows[:8] + rows[8:]


def add_moments(pieces, pivot, first, second):
    def add(step, sums):
        first, second = sums
        for piece in pieces:
            away = piece[pl.ds(step * CHUNK, CHUNK), :].astype(f32) - pivot
            first = first + folded(away)
            second = second + folded(away * away)
        return first, second

    return lax.fori_loop(0, pieces[0].shape[0] // CHUNK, add, (first, second))


def conv_kernel(columns, sources_ref, *refs):
    count = len(refs) - 7
    pieces = refs[:count]
    stats_ref, kernel_ref, bias_ref = refs[count : count + 3]
    out_refs = refs[count + 3 : count + 5]
    act_ref, kept_ref = refs[count + 5 :]
    block = pieces[0].shape[0]
    positions = block * count
    own = out_refs[0].shape[0]
    me = lax.axis_index("patch")
    steps = block // CHUNK
    starts = [
        pl.multiple_of(sources_ref[me * count + index] * (2 * block) + (index % 2) * block, block)
        for index in range(count)
    ]

    member = (
        lax.broadcasted_iota(jnp.int32, (C, 128), 0) // SPAN
        == lax.broadcasted_iota(jnp.int32, (C, 128), 1)
    ).astype(bf16)

    def group_mean(per_channel):
        return exact(exact(per_channel, member) / SPAN, member, NT)

    pivot = stats_ref[0:1, :]
    first, second = add_moments(pieces[-2:], pivot, stats_ref[8:16, :], stats_ref[16:24, :])
    above = jnp.sum(first, axis=0, keepdims=True) / positions
    within = jnp.sum(second, axis=0, keepdims=True) / positions - above * above
    mean = pivot + above
    centre = group_mean(mean)
    spread = group_mean(within + (mean - centre) * (mean - centre))
    half_scale = 0.5 * lax.rsqrt(spread + EPSILON)

    act_ref[0:columns, :] = jnp.zeros((columns, C), bf16)
    act_ref[positions + columns :, :] = jnp.zeros((columns, C), bf16)

    def activate(step, carry):
        for start, piece in zip(starts, pieces):
            half = (piece[pl.ds(step * CHUNK, CHUNK), :].astype(f32) - centre) * half_scale
            value = half + half * jnp.tanh(half)
            row = pl.multiple_of(columns + start + step * CHUNK, CHUNK)
            act_ref[pl.ds(row, CHUNK), :] = value.astype(bf16)
        return carry

    lax.fori_loop(0, steps, activate, 0)

    window = window_of(own)
    base = jnp.minimum(lax.div(me * own, 128) * 128, C - window)
    lanes = pl.ds(pl.multiple_of(base, 128), window)
    choose = (
        lax.broadcasted_iota(jnp.int32, (own, window), 0) + (me * own - base)
        == lax.broadcasted_iota(jnp.int32, (own, window), 1)
    ).astype(bf16)
    for index in range(0, count, 2):
        pair = jnp.concatenate([pieces[index][:, lanes], pieces[index + 1][:, lanes]], axis=0)
        start = pl.multiple_of(starts[index], 2 * block)
        kept_ref[:, pl.ds(start, 2 * block)] = dot(choose, pair, NT)

    wide = WIDE
    column = lax.broadcasted_iota(jnp.int32, (own, wide), 1) % columns
    square = (own, own)
    bias = jnp.where(
        lax.broadcasted_iota(jnp.int32, square, 0) == lax.broadcasted_iota(jnp.int32, square, 1),
        bias_ref[...],
        0.0,
    )
    bias = jnp.sum(bias, axis=1, keepdims=True)
    for at in range(0, positions, wide):
        taps = dot(kernel_ref[0], act_ref[at : at + wide, :], NT)
        for shift in (1, 2):
            low = at + shift * columns
            taps = taps + dot(kernel_ref[shift], act_ref[low : low + wide, :], NT)
        before = jnp.where(column > 0, pltpu.roll(taps[0:own], 1, 1), 0.0)
        after_ = jnp.where(column < columns - 1, pltpu.roll(taps[2 * own :], wide - 1, 1), 0.0)
        convolved = taps[own : 2 * own] + before + after_
        hidden = kept_ref[:, at : at + wide] + convolved + bias
        which, low = divmod(at, positions // 2)
        out_refs[which][:, low : low + wide] = hidden.astype(bf16)


def window_of(own):
    return min(C, (own + 127) // 128 * 128 + 128)


def norm_pair(pair):
    own = pair[0].shape[0]
    entries = float(2 * pair[0].shape[1] * SPAN)

    def whole(values):
        return jnp.sum(jnp.sum(values, axis=0, keepdims=True), axis=1, keepdims=True)

    def group_at(low):
        first, last = low // 16 * 16, -(-(low + SPAN) // 16) * 16
        return [ref[first:last, :].astype(f32)[low - first : low - first + SPAN] for ref in pair]

    lows = range(0, own, SPAN)
    means = [sum(whole(half) for half in group_at(low)) / entries for low in lows]
    squares = [
        sum(whole(jnp.square(half - mean)) for half in group_at(low))
        for low, mean in zip(lows, means)
    ]
    scales = [lax.rsqrt(square / entries + EPSILON) for square in squares]
    mean = jnp.concatenate([jnp.broadcast_to(one, (SPAN, 1)) for one in means], axis=0)
    scale = jnp.concatenate([jnp.broadcast_to(one, (SPAN, 1)) for one in scales], axis=0)
    return [((ref[...].astype(f32) - mean) * scale).astype(bf16) for ref in pair]


def own_lanes(pair, me, n):
    block = 2 * pair[0].shape[1] // n
    start = pl.multiple_of(lax.rem(me, n // 2) * block, block)
    low, high = (ref[:, pl.ds(start, block)] for ref in pair)
    return jnp.where(me < n // 2, low, high)


def project_kernel(count, sources_ref, *refs):
    pieces = refs[: count - 2]
    weight_refs = refs[count - 2 : -3]
    sums_ref, kept_ref, normed_ref = refs[-3:]
    own, part = pieces[0].shape
    me = lax.axis_index("patch")
    for at in range(0, count - 2, 2):
        pair = pieces[at : at + 2]
        rows = pl.ds(pl.multiple_of(sources_ref[me * count + at] * own, own), own)
        for half, normed in enumerate(norm_pair(pair)):
            normed_ref[rows, half * part : (half + 1) * part] = normed
        kept_ref[rows, :] = own_lanes(pair, me, count // 2)
    missing = pl.multiple_of(sources_ref[me * count + count - 2] * own, own)
    normed_ref[pl.ds(missing, own), :] = jnp.zeros((own, 2 * part), bf16)
    weights = jnp.concatenate([ref[...] for ref in weight_refs], axis=0)
    for at in range(0, 2 * part, WIDE):
        sums_ref[:, at : at + WIDE] = dot(weights, normed_ref[:, at : at + WIDE])


def attention_kernel(count, inner, sources_ref, *refs):
    pair = refs[:2]
    weight_refs = refs[2:-9]
    sums_ref, some_ref = refs[-9:-7]
    outs = refs[-7:-4]
    kept_ref, made_ref, key_ref, last_ref = refs[-4:]
    own, part = pair[0].shape
    n = count // 2
    me = lax.axis_index("patch")
    outer_at, inner_at = lax.div(me, inner), lax.rem(me, inner)
    source = sources_ref[me * count + count - 2]
    row = pl.multiple_of(source * own, own)
    kept_ref[...] = some_ref[...]
    kept_ref[pl.ds(row, own), :] = own_lanes(pair, me, n)

    window = last_ref.shape[0]
    base = jnp.minimum(lax.div(source * own, 128) * 128, C - window)
    lanes = pl.ds(pl.multiple_of(base, 128), window)
    last_ref[...] = jnp.zeros_like(last_ref)
    within = pl.ds(pl.multiple_of(source * own - base, 16), own)
    for half, normed in enumerate(norm_pair(pair)):
        last_ref[within, half * part : (half + 1) * part] = normed
    weights = jnp.concatenate([ref[:, lanes] for ref in weight_refs], axis=0)
    places = rows_of(weight_refs, own, inner, inner_at)
    for at in range(0, 2 * part, WIDE):
        made = dot(weights, last_ref[:, at : at + WIDE]) + sums_ref[:, at : at + WIDE]
        made = made.astype(bf16)
        for low, size, target in places:
            made_ref[pl.ds(target, size), at : at + WIDE] = made[low : low + size]

    for at in range(0, 2 * part, WIDE):
        for head in range(SET_HEADS):
            low = SET_CHANNELS + head * HEAD_DIM
            key = made_ref[low : low + HEAD_DIM, at : at + WIDE].astype(f32)
            key_ref[head, at : at + WIDE, :] = key.T.astype(bf16)

    targets = [lax.rem(outer_at + step, OUTER) * inner + inner_at for step in SOONER]
    attend(targets, made_ref, key_ref, outs)


def rows_of(weight_refs, own, inner, inner_at):
    if inner != 2:
        return [(0, weight_refs[0].shape[0], 0)]
    places = []
    for kind in range(3):
        place = kind * SET_CHANNELS + inner_at * own
        places.append((kind * own, own, pl.multiple_of(place, own)))
    mine = lax.rem(lax.axis_index("batch"), QUAD)
    size = weight_refs[3].shape[0]
    twice = QUAD * (size // GRANULE) - 3 * own // GRANULE
    for order, step in enumerate(HANDED):
        which = jnp.bitwise_xor(mine, step)
        first = quarter_start(which, own)
        for at in range(size // GRANULE):
            granule = first + at
            place = lax.div(granule, own // GRANULE) * SET_CHANNELS + (1 - inner_at) * own
            place = place + lax.rem(granule, own // GRANULE) * GRANULE
            if at < twice:
                place = jnp.where(which == QUAD - 1, 3 * SET_CHANNELS + at * GRANULE, place)
            low = 3 * own + order * size + at * GRANULE
            places.append((low, GRANULE, pl.multiple_of(place, GRANULE)))
    return places


def later_kernel(made_ref, key_ref, out_ref):
    attend([lax.axis_index("patch")], made_ref, key_ref, [out_ref])


def attend(targets, made_ref, key_ref, outs):
    block = outs[0].shape[1]
    starts = [pl.multiple_of(target * block, block) for target in targets]
    for head in range(SET_HEADS):
        low = head * HEAD_DIM
        query = [made_ref[low : low + HEAD_DIM, pl.ds(start, block)] for start in starts]
        query = jnp.concatenate(query, axis=1).astype(f32) * HEAD_DIM ** (-0.5)
        scores = dot(key_ref[head], query.astype(bf16))
        peak = jnp.max(scores, axis=0, keepdims=True)
        unnormalized = jnp.exp(scores - peak)
        total = jnp.sum(unnormalized, axis=0, keepdims=True)
        value = made_ref[2 * SET_CHANNELS + low : 2 * SET_CHANNELS + low + HEAD_DIM, :]
        mixture = dot(value, unnormalized.astype(bf16))
        attended = (mixture / total).astype(bf16)
        for place, out in enumerate(outs):
            out[low : low + HEAD_DIM, :] = attended[:, place * block : (place + 1) * block]


def output_kernel(n, *refs):
    attended_refs = refs[:OUTER]
    hidden_ref = refs[OUTER]
    weight_refs = refs[OUTER + 1 : -3]
    out_ref, attended_ref, total_ref = refs[-3:]
    inner = n // OUTER
    own = C // n
    me = lax.axis_index("patch")
    outer_at, inner_at = lax.div(me, inner), lax.rem(me, inner)
    for step in range(OUTER):
        origin = lax.rem(outer_at + OUTER - step, OUTER)
        row = pl.multiple_of(origin * SET_CHANNELS, SET_CHANNELS)
        attended_ref[pl.ds(row, SET_CHANNELS), :] = attended_refs[step][...]
    attended = attended_ref[...]
    if inner != 2:
        total = dot(weight_refs[0][...], attended) + hidden_ref[...].astype(f32)
        out_ref[...] = total.T.astype(bf16)
        return

    total_ref[...] = hidden_ref[...].astype(f32)
    mine = lax.rem(lax.axis_index("batch"), QUAD)
    core = lax.rem(mine, 2)

    def add(weights, outer_step, inner_step, low=0):
        origin = lax.rem(outer_at + OUTER - outer_step, OUTER) * inner
        origin = origin + lax.rem(inner_at + inner_step, inner)
        rows = pl.ds(pl.multiple_of(origin * own + low, 16), weights.shape[0])
        total_ref[rows, :] += dot(weights, attended)

    own_ref, far_ref, far_other_ref, last_ref, last_other_ref = weight_refs
    add(own_ref[...], 0, 0)
    for holder, ref in ((mine, far_ref), (jnp.bitwise_xor(mine, 1), far_other_ref)):
        for step in (0, 1):
            which = jnp.bitwise_xor(holder, 2 * step)
            outer_step = jnp.where(which == 0, 1, jnp.where(which == 2, 3, 2))
            add(ref[step * own : (step + 1) * own, :], outer_step, lax.div(which, QUAD - 1))
        add(ref[2 * own :, :], 0, 1, lax.rem(holder, 2) * (own // 2))
    add(last_ref[...], 1 + 2 * core, 1)
    add(last_other_ref[...], 3 - 2 * core, 1)
    out_ref[...] = total_ref[...].T.astype(bf16)


def quarter_rows(own):
    return -(-3 * own // (QUAD * GRANULE)) * GRANULE


def quarter_start(place, own):
    part = quarter_rows(own) // GRANULE
    return jnp.minimum(place * part, 3 * own // GRANULE - part)


def ring_of(n):
    inner = n // OUTER
    path = [(0, 0)]
    for outer_at in range(OUTER):
        across = range(1, inner) if outer_at % 2 == 0 else range(inner - 1, 0, -1)
        path += [(outer_at, inner_at) for inner_at in across]
    path += [(outer_at, 0) for outer_at in range(OUTER - 1, 0, -1)]
    return [outer_at * inner + inner_at for outer_at, inner_at in path]


def pieces_of(n):
    far = n // 2
    return [0] + [away for step in range(1, far) for away in (-step, step)] + [far]


def sources_of(n):
    ring = ring_of(n)
    table = []
    for device in range(n):
        at = ring.index(device)
        table.append([ring[(at + away) % n] for away in pieces_of(n) for _ in (0, 1)])
    return table


def gather(halves, n, beside=()):
    ring = ring_of(n)
    forward = [(ring[at], ring[(at + 1) % n]) for at in range(n)]
    backward = [(target, start) for start, target in forward]
    far = n // 2
    found = {(0, 0): halves[0], (1, 0): halves[1]}
    for step in range(1, far + 1):
        for half in (0, 1):
            for sign, pairs in ((-1, forward), (1, backward)):
                if step == far and (half == 0) != (sign == -1):
                    continue
                found[half, sign * step] = lax.ppermute(
                    found[half, sign * (step - 1)], "patch", pairs
                )
        if step == 1 and beside:
            (found[0, -1],) = after([found[0, -1]], beside)
    found[0, far] = found[0, -far]
    return [found[half, away] for away in pieces_of(n) for half in (0, 1)]


def send(block, shifts):
    batch, n = lax.axis_size("batch"), lax.axis_size("patch")
    pairs = []
    for at in range(batch):
        for start, target in moves(n, *shifts[at % len(shifts)]):
            pairs.append((at * n + start, at * n + target))
    return lax.ppermute(block, ("batch", "patch"), pairs)


def swap(block, bit):
    pairs = [(at, at ^ bit) for at in range(lax.axis_size("batch"))]
    return lax.ppermute(block, "batch", pairs)


def moves(n, outer_step, inner_step):
    inner = n // OUTER
    pairs = []
    for start in range(n):
        outer_at = (start // inner + outer_step) % OUTER
        inner_at = (start % inner + inner_step) % inner
        pairs.append((start, outer_at * inner + inner_at))
    return pairs


def after(values, ready):
    anywhere = pl.BlockSpec(memory_space=pl.ANY)
    made = pl.pallas_call(
        lambda *refs: None,
        out_shape=[jax.ShapeDtypeStruct(value.shape, value.dtype) for value in values],
        in_specs=[anywhere] * (len(values) + len(ready)),
        out_specs=[anywhere] * len(values),
        input_output_aliases={at: at for at in range(len(values))},
        compiler_params=pltpu.CompilerParams(vmem_limit_bytes=MEBI),
        cost_estimate=pl.CostEstimate(flops=0, bytes_accessed=0, transcendentals=0),
        name="after",
    )(*values, *ready)
    return list(made)


def on_device(latent, conv_weight, channel_bias, w_query, w_key, w_value, w_out):
    rows_local, columns, channels = latent.shape
    n = lax.axis_size("patch")
    inner = n // OUTER
    own = channels // n
    block = rows_local * columns
    positions = block * n
    sources = jnp.asarray(sources_of(n), jnp.int32).reshape(-1)
    vmem = pl.BlockSpec(memory_space=pltpu.VMEM)
    smem = pl.BlockSpec(memory_space=pltpu.SMEM)
    anywhere = pl.BlockSpec(memory_space=pl.ANY)

    whole = latent.reshape(block, channels)
    halves = whole[: block // 2], whole[block // 2 :]
    chosen = []
    if inner == 2:
        quarter = quarter_rows(own)
        core = lax.rem(lax.axis_index("batch"), 2)
        start = quarter_start(lax.rem(lax.axis_index("batch"), QUAD), own) * GRANULE
        stacked = jnp.concatenate([w_query, w_key, w_value], axis=0)
        chosen = [
            lax.dynamic_slice_in_dim(stacked, start, quarter, 0),
            lax.dynamic_slice_in_dim(w_out, core * (own // 2), own // 2, 0),
        ]
        chosen = [jnp.concatenate(chosen, axis=0)]
    pieces = gather(halves, n, chosen)
    if inner == 2:
        far = send(w_out, FAR)
    stats = pl.pallas_call(
        stats_kernel,
        out_shape=jax.ShapeDtypeStruct((24, channels), f32),
        in_specs=[vmem] * (2 * n - 2),
        out_specs=vmem,
        compiler_params=pltpu.CompilerParams(vmem_limit_bytes=2 * MEBI),
        cost_estimate=pl.CostEstimate(
            flops=6 * positions * channels,
            bytes_accessed=2 * positions * channels,
            transcendentals=0,
        ),
        name="stats",
    )(*pieces[:-2])
    if inner == 2:
        chosen, far = after(chosen + [far], pieces[-6:-2])
        chosen = send(chosen, [(0, 1)])
        across = swap(far, 2)
    else:
        sets = [list(range(at, at + inner)) for at in range(0, n, inner)]
        weights = jnp.stack([w_query, w_key, w_value])
        weights = lax.all_gather(weights, "patch", axis=1, tiled=True, axis_index_groups=sets)
        weights = [weights.reshape(3 * SET_CHANNELS, channels)]
        out_weights = [lax.all_gather(w_out, "patch", axis=0, tiled=True)]

    hidden = pl.pallas_call(
        functools.partial(conv_kernel, columns),
        out_shape=[jax.ShapeDtypeStruct((own, positions // 2), bf16)] * 2,
        in_specs=[smem] + [vmem] * (2 * n + 3),
        out_specs=[vmem] * 2,
        scratch_shapes=[
            pltpu.VMEM((positions + 2 * columns, channels), bf16),
            pltpu.VMEM((own, positions), f32),
        ],
        compiler_params=pltpu.CompilerParams(vmem_limit_bytes=20 * MEBI),
        cost_estimate=pl.CostEstimate(
            flops=2 * 9 * positions * channels * own,
            bytes_accessed=2 * (positions * channels + 9 * channels * own),
            transcendentals=positions * channels,
        ),
        name="norm_conv",
    )(
        sources,
        *pieces,
        stats,
        conv_weight.reshape(3, 3 * own, channels),
        channel_bias.reshape(1, own),
    )

    hidden_pieces = gather(tuple(hidden), n)
    if inner == 2:
        chosen, across = after([chosen, across], hidden[:1])
        near = [chosen[:quarter]]
        near.append(swap(near[0], 2))
        near += [swap(one, 1) for one in near]
        weights = [w_query, w_key, w_value] + near
    made_rows = sum(weight.shape[0] for weight in weights)
    sums, some = pl.pallas_call(
        functools.partial(project_kernel, 2 * n),
        out_shape=[
            jax.ShapeDtypeStruct((made_rows, positions), f32),
            jax.ShapeDtypeStruct((channels, block), bf16),
        ],
        in_specs=[smem] + [vmem] * (2 * n - 2 + len(weights)),
        out_specs=[vmem] * 2,
        scratch_shapes=[pltpu.VMEM((channels, positions), bf16)],
        compiler_params=pltpu.CompilerParams(vmem_limit_bytes=20 * MEBI),
        cost_estimate=pl.CostEstimate(
            flops=2 * positions * channels * made_rows,
            bytes_accessed=2 * (positions * channels + made_rows * channels),
            transcendentals=0,
        ),
        name="norm_project",
    )(sources, *hidden_pieces[:-2], *weights)
    if inner == 2:
        far = jnp.concatenate([far, across, chosen[quarter:]], axis=0)
        far, out_own = after([far, w_out], hidden_pieces[-6:-2])
        far = [far, swap(far, 1)]
        last = send(out_own, LAST)
    one_block = jax.ShapeDtypeStruct((SET_CHANNELS, block), bf16)
    *sent, kept, made, key = pl.pallas_call(
        functools.partial(attention_kernel, 2 * n, inner),
        out_shape=[one_block] * len(SOONER)
        + [
            jax.ShapeDtypeStruct((channels, block), bf16),
            jax.ShapeDtypeStruct((made_rows, positions), bf16),
            jax.ShapeDtypeStruct((SET_HEADS, positions, HEAD_DIM), bf16),
        ],
        in_specs=[smem] + [vmem] * (4 + len(weights)),
        out_specs=[vmem] * (3 + len(SOONER)),
        scratch_shapes=[pltpu.VMEM((window_of(own), positions), bf16)],
        compiler_params=pltpu.CompilerParams(vmem_limit_bytes=28 * MEBI),
        cost_estimate=pl.CostEstimate(
            flops=2 * positions * window_of(own) * made_rows
            + 12 * positions * block * SET_CHANNELS,
            bytes_accessed=6 * made_rows * positions,
            transcendentals=positions * 3 * block * SET_HEADS,
        ),
        name="attention",
    )(sources, *hidden_pieces[-2:], *weights, sums, some)
    received = [None]
    for step, sent_block in zip(SOONER, sent):
        pairs = [(at, (at + step * inner) % n) for at in range(n)]
        received.append(lax.ppermute(sent_block, "patch", pairs))
    received[0] = pl.pallas_call(
        later_kernel,
        out_shape=one_block,
        in_specs=[vmem] * 2,
        out_specs=vmem,
        compiler_params=pltpu.CompilerParams(vmem_limit_bytes=16 * MEBI),
        cost_estimate=pl.CostEstimate(
            flops=4 * positions * block * SET_CHANNELS,
            bytes_accessed=8 * positions * SET_CHANNELS,
            transcendentals=positions * block * SET_HEADS,
        ),
        name="own_attention",
    )(made, key)
    if inner == 2:
        (last,) = after([last], sent[:1])
        out_weights = [w_out] + far + [last, swap(last, 1)]

    output = pl.pallas_call(
        functools.partial(output_kernel, n),
        out_shape=jax.ShapeDtypeStruct((block, channels), bf16),
        in_specs=[vmem] * (OUTER + 1 + len(out_weights)),
        out_specs=vmem,
        scratch_shapes=[
            pltpu.VMEM((channels, block), bf16),
            pltpu.VMEM((channels, block), f32),
        ],
        compiler_params=pltpu.CompilerParams(vmem_limit_bytes=12 * MEBI),
        cost_estimate=pl.CostEstimate(
            flops=2 * block * channels * channels,
            bytes_accessed=2 * channels * (channels + 3 * block),
            transcendentals=0,
        ),
        name="project",
    )(*received, kept, *out_weights)
    return output.reshape(rows_local, columns, channels)


def solution(mesh):
    return jax.shard_map(
        on_device,
        mesh=mesh,
        in_specs=(
            P(("batch", "patch"), None, None),
            P(None, None, "patch", None),
            P("patch"),
            P("patch", None),
            P("patch", None),
            P("patch", None),
            P("patch", None),
        ),
        out_specs=P(("batch", "patch"), None, None),
        check_vma=False,
    )
```

```python
import functools

import jax
import jax.numpy as jnp
from jax import lax
from jax.experimental import pallas as pl
from jax.experimental.pallas import tpu as pltpu
from jax.sharding import PartitionSpec as P

C = 1280
HEADS = 20
HEAD_DIM = 64
GROUPS = 32
SPAN = C // GROUPS
OUTER = 4
SET_HEADS = HEADS // OUTER
SET_CHANNELS = SET_HEADS * HEAD_DIM
QUAD = 4
GRANULE = 32
HANDED = (0, 2, 1, 3)
FAR = ((1, 0), (3, 0), (2, 0), (0, 1))
SOONER = tuple(range(1, OUTER))
WIDE = 256
EPSILON = 1e-05
CHUNK = 16
MEBI = 1024 * 1024

f32 = jnp.float32
bf16 = jnp.bfloat16

NT = (((1,), (1,)), ((), ()))
NN = (((1,), (0,)), ((), ()))


def dot(left, right, dims=NN):
    return lax.dot_general(left, right, dims, preferred_element_type=f32)


def exact(row, member, dims=NN):
    high = row.astype(bf16).astype(f32)
    middle = (row - high).astype(bf16).astype(f32)
    parts = [high, middle, row - high - middle, jnp.zeros((13, row.shape[1]), f32)]
    return jnp.sum(dot(jnp.concatenate(parts, axis=0).astype(bf16), member, dims), axis=0, keepdims=True)


def stats_kernel(*refs):
    pieces, out_ref = refs[:-1], refs[-1]
    block = pieces[0].shape[0]
    steps = block // CHUNK

    def add(step, total):
        for piece in pieces[:2]:
            total = total + folded(piece[pl.ds(step * CHUNK, CHUNK), :].astype(f32))
        return total

    zero = jnp.zeros((8, C), f32)
    pivot = jnp.sum(lax.fori_loop(0, steps, add, zero), axis=0, keepdims=True) / (2 * block)
    first, second = add_moments(pieces, pivot, zero, zero)
    out_ref[0:8, :] = jnp.broadcast_to(pivot, (8, C))
    out_ref[8:16, :] = first
    out_ref[16:24, :] = second


def folded(rows):
    return rows[:8] + rows[8:]


def add_moments(pieces, pivot, first, second):
    def add(step, sums):
        first, second = sums
        for piece in pieces:
            away = piece[pl.ds(step * CHUNK, CHUNK), :].astype(f32) - pivot
            first = first + folded(away)
            second = second + folded(away * away)
        return first, second

    return lax.fori_loop(0, pieces[0].shape[0] // CHUNK, add, (first, second))


def conv_kernel(columns, sources_ref, *refs):
    count = len(refs) - 7
    pieces = refs[:count]
    stats_ref, kernel_ref, bias_ref = refs[count : count + 3]
    out_refs = refs[count + 3 : count + 5]
    act_ref, kept_ref = refs[count + 5 :]
    block = pieces[0].shape[0]
    positions = block * count
    own = out_refs[0].shape[0]
    me = lax.axis_index("patch")
    steps = block // CHUNK
    starts = [
        pl.multiple_of(sources_ref[me * count + index] * (2 * block) + (index % 2) * block, block)
        for index in range(count)
    ]

    member = (
        lax.broadcasted_iota(jnp.int32, (C, 128), 0) // SPAN
        == lax.broadcasted_iota(jnp.int32, (C, 128), 1)
    ).astype(bf16)

    def group_mean(per_channel):
        return exact(exact(per_channel, member) / SPAN, member, NT)

    pivot = stats_ref[0:1, :]
    first, second = add_moments(pieces[-2:], pivot, stats_ref[8:16, :], stats_ref[16:24, :])
    above = jnp.sum(first, axis=0, keepdims=True) / positions
    within = jnp.sum(second, axis=0, keepdims=True) / positions - above * above
    mean = pivot + above
    centre = group_mean(mean)
    spread = group_mean(within + (mean - centre) * (mean - centre))
    half_scale = 0.5 * lax.rsqrt(spread + EPSILON)

    act_ref[0:columns, :] = jnp.zeros((columns, C), bf16)
    act_ref[positions + columns :, :] = jnp.zeros((columns, C), bf16)

    def activate(step, carry):
        for start, piece in zip(starts, pieces):
            half = (piece[pl.ds(step * CHUNK, CHUNK), :].astype(f32) - centre) * half_scale
            value = half + half * jnp.tanh(half)
            row = pl.multiple_of(columns + start + step * CHUNK, CHUNK)
            act_ref[pl.ds(row, CHUNK), :] = value.astype(bf16)
        return carry

    lax.fori_loop(0, steps, activate, 0)

    window = window_of(own)
    base = jnp.minimum(lax.div(me * own, 128) * 128, C - window)
    lanes = pl.ds(pl.multiple_of(base, 128), window)
    choose = (
        lax.broadcasted_iota(jnp.int32, (own, window), 0) + (me * own - base)
        == lax.broadcasted_iota(jnp.int32, (own, window), 1)
    ).astype(bf16)
    for index in range(0, count, 2):
        pair = jnp.concatenate([pieces[index][:, lanes], pieces[index + 1][:, lanes]], axis=0)
        start = pl.multiple_of(starts[index], 2 * block)
        kept_ref[:, pl.ds(start, 2 * block)] = dot(choose, pair, NT)

    wide = WIDE
    column = lax.broadcasted_iota(jnp.int32, (own, wide), 1) % columns
    square = (own, own)
    bias = jnp.where(
        lax.broadcasted_iota(jnp.int32, square, 0) == lax.broadcasted_iota(jnp.int32, square, 1),
        bias_ref[...],
        0.0,
    )
    bias = jnp.sum(bias, axis=1, keepdims=True)
    for at in range(0, positions, wide):
        taps = dot(kernel_ref[0], act_ref[at : at + wide, :], NT)
        for shift in (1, 2):
            low = at + shift * columns
            taps = taps + dot(kernel_ref[shift], act_ref[low : low + wide, :], NT)
        before = jnp.where(column > 0, pltpu.roll(taps[0:own], 1, 1), 0.0)
        after_ = jnp.where(column < columns - 1, pltpu.roll(taps[2 * own :], wide - 1, 1), 0.0)
        convolved = taps[own : 2 * own] + before + after_
        hidden = kept_ref[:, at : at + wide] + convolved + bias
        which, low = divmod(at, positions // 2)
        out_refs[which][:, low : low + wide] = hidden.astype(bf16)


def window_of(own):
    return min(C, (own + 127) // 128 * 128 + 128)


def norm_pair(pair):
    own = pair[0].shape[0]
    entries = float(2 * pair[0].shape[1] * SPAN)

    def whole(values):
        return jnp.sum(jnp.sum(values, axis=0, keepdims=True), axis=1, keepdims=True)

    def group_at(low):
        first, last = low // 16 * 16, -(-(low + SPAN) // 16) * 16
        return [ref[first:last, :].astype(f32)[low - first : low - first + SPAN] for ref in pair]

    lows = range(0, own, SPAN)
    means = [sum(whole(half) for half in group_at(low)) / entries for low in lows]
    squares = [
        sum(whole(jnp.square(half - mean)) for half in group_at(low))
        for low, mean in zip(lows, means)
    ]
    scales = [lax.rsqrt(square / entries + EPSILON) for square in squares]
    mean = jnp.concatenate([jnp.broadcast_to(one, (SPAN, 1)) for one in means], axis=0)
    scale = jnp.concatenate([jnp.broadcast_to(one, (SPAN, 1)) for one in scales], axis=0)
    return [((ref[...].astype(f32) - mean) * scale).astype(bf16) for ref in pair]


def own_lanes(pair, me, n):
    block = 2 * pair[0].shape[1] // n
    start = pl.multiple_of(lax.rem(me, n // 2) * block, block)
    low, high = (ref[:, pl.ds(start, block)] for ref in pair)
    return jnp.where(me < n // 2, low, high)


def project_kernel(count, sources_ref, *refs):
    pieces = refs[: count - 2]
    weight_refs = refs[count - 2 : -3]
    sums_ref, kept_ref, normed_ref = refs[-3:]
    own, part = pieces[0].shape
    me = lax.axis_index("patch")
    for at in range(0, count - 2, 2):
        pair = pieces[at : at + 2]
        rows = pl.ds(pl.multiple_of(sources_ref[me * count + at] * own, own), own)
        for half, normed in enumerate(norm_pair(pair)):
            normed_ref[rows, half * part : (half + 1) * part] = normed
        kept_ref[rows, :] = own_lanes(pair, me, count // 2)
    missing = pl.multiple_of(sources_ref[me * count + count - 2] * own, own)
    normed_ref[pl.ds(missing, own), :] = jnp.zeros((own, 2 * part), bf16)
    weights = jnp.concatenate([ref[...] for ref in weight_refs], axis=0)
    for at in range(0, 2 * part, WIDE):
        sums_ref[:, at : at + WIDE] = dot(weights, normed_ref[:, at : at + WIDE])


def attention_kernel(count, inner, sources_ref, *refs):
    pair = refs[:2]
    weight_refs = refs[2:-9]
    sums_ref, some_ref = refs[-9:-7]
    outs = refs[-7:-4]
    kept_ref, made_ref, key_ref, last_ref = refs[-4:]
    own, part = pair[0].shape
    n = count // 2
    me = lax.axis_index("patch")
    outer_at, inner_at = lax.div(me, inner), lax.rem(me, inner)
    source = sources_ref[me * count + count - 2]
    row = pl.multiple_of(source * own, own)
    kept_ref[...] = some_ref[...]
    kept_ref[pl.ds(row, own), :] = own_lanes(pair, me, n)

    window = last_ref.shape[0]
    base = jnp.minimum(lax.div(source * own, 128) * 128, C - window)
    lanes = pl.ds(pl.multiple_of(base, 128), window)
    last_ref[...] = jnp.zeros_like(last_ref)
    within = pl.ds(pl.multiple_of(source * own - base, 16), own)
    for half, normed in enumerate(norm_pair(pair)):
        last_ref[within, half * part : (half + 1) * part] = normed
    weights = jnp.concatenate([ref[:, lanes] for ref in weight_refs], axis=0)
    places = rows_of(weight_refs, own, inner, inner_at)
    for at in range(0, 2 * part, WIDE):
        made = dot(weights, last_ref[:, at : at + WIDE]) + sums_ref[:, at : at + WIDE]
        made = made.astype(bf16)
        for low, size, target in places:
            made_ref[pl.ds(target, size), at : at + WIDE] = made[low : low + size]

    for at in range(0, 2 * part, WIDE):
        for head in range(SET_HEADS):
            low = SET_CHANNELS + head * HEAD_DIM
            key = made_ref[low : low + HEAD_DIM, at : at + WIDE].astype(f32)
            key_ref[head, at : at + WIDE, :] = key.T.astype(bf16)

    targets = [lax.rem(outer_at + step, OUTER) * inner + inner_at for step in SOONER]
    attend(targets, made_ref, key_ref, outs)


def rows_of(weight_refs, own, inner, inner_at):
    if inner != 2:
        return [(0, weight_refs[0].shape[0], 0)]
    places = []
    for kind in range(3):
        place = kind * SET_CHANNELS + inner_at * own
        places.append((kind * own, own, pl.multiple_of(place, own)))
    mine = lax.rem(lax.axis_index("batch"), QUAD)
    size = weight_refs[3].shape[0]
    twice = QUAD * (size // GRANULE) - 3 * own // GRANULE
    for order, step in enumerate(HANDED):
        which = jnp.bitwise_xor(mine, step)
        first = quarter_start(which, own)
        for at in range(size // GRANULE):
            granule = first + at
            place = lax.div(granule, own // GRANULE) * SET_CHANNELS + (1 - inner_at) * own
            place = place + lax.rem(granule, own // GRANULE) * GRANULE
            if at < twice:
                place = jnp.where(which == QUAD - 1, 3 * SET_CHANNELS + at * GRANULE, place)
            low = 3 * own + order * size + at * GRANULE
            places.append((low, GRANULE, pl.multiple_of(place, GRANULE)))
    return places


def later_kernel(made_ref, key_ref, out_ref):
    attend([lax.axis_index("patch")], made_ref, key_ref, [out_ref])


def attend(targets, made_ref, key_ref, outs):
    block = outs[0].shape[1]
    starts = [pl.multiple_of(target * block, block) for target in targets]
    for head in range(SET_HEADS):
        low = head * HEAD_DIM
        query = [made_ref[low : low + HEAD_DIM, pl.ds(start, block)] for start in starts]
        query = jnp.concatenate(query, axis=1).astype(f32) * HEAD_DIM ** (-0.5)
        scores = dot(key_ref[head], query.astype(bf16))
        peak = jnp.max(scores, axis=0, keepdims=True)
        unnormalized = jnp.exp(scores - peak)
        total = jnp.sum(unnormalized, axis=0, keepdims=True)
        value = made_ref[2 * SET_CHANNELS + low : 2 * SET_CHANNELS + low + HEAD_DIM, :]
        mixture = dot(value, unnormalized.astype(bf16))
        attended = (mixture / total).astype(bf16)
        for place, out in enumerate(outs):
            out[low : low + HEAD_DIM, :] = attended[:, place * block : (place + 1) * block]


def output_kernel(n, *refs):
    attended_refs = refs[:OUTER]
    hidden_ref = refs[OUTER]
    weight_refs = refs[OUTER + 1 : -3]
    out_ref, attended_ref, total_ref = refs[-3:]
    inner = n // OUTER
    own = C // n
    me = lax.axis_index("patch")
    outer_at, inner_at = lax.div(me, inner), lax.rem(me, inner)
    for step in range(OUTER):
        origin = lax.rem(outer_at + OUTER - step, OUTER)
        row = pl.multiple_of(origin * SET_CHANNELS, SET_CHANNELS)
        attended_ref[pl.ds(row, SET_CHANNELS), :] = attended_refs[step][...]
    attended = attended_ref[...]
    if inner != 2:
        total = dot(weight_refs[0][...], attended) + hidden_ref[...].astype(f32)
        out_ref[...] = total.T.astype(bf16)
        return

    total_ref[...] = hidden_ref[...].astype(f32)
    mine = lax.rem(lax.axis_index("batch"), QUAD)
    core = lax.rem(mine, 2)

    def add(weights, outer_step, inner_step, low=0):
        origin = lax.rem(outer_at + OUTER - outer_step, OUTER) * inner
        origin = origin + lax.rem(inner_at + inner_step, inner)
        rows = pl.ds(pl.multiple_of(origin * own + low, 16), weights.shape[0])
        total_ref[rows, :] += dot(weights, attended)

    own_ref, far_ref, across_ref, other_ref, mine_ref, others_ref = weight_refs
    side = lax.div(mine, 2)
    add(own_ref[...], 0, 0)
    far = [far_ref[...], across_ref[...], other_ref[:own, :], other_ref[own:, :]]
    for step, weights in zip(HANDED, far):
        which = jnp.bitwise_xor(mine, step)
        outer_step = jnp.where(which == 0, 1, jnp.where(which == 1, 3, jnp.where(which == 2, 2, 0)))
        add(weights, outer_step, lax.div(which, QUAD - 1))

    def add_relayed(two_ref, one_ref):
        add(two_ref[:own, :], 1 + side, 1)
        add(two_ref[own:, :], 2 - side, 1)
        add(one_ref[:own, :], 3, 1)

    @pl.when(core == 0)
    def _():
        add_relayed(mine_ref, others_ref)

    @pl.when(core == 1)
    def _():
        add_relayed(others_ref, mine_ref)

    out_ref[...] = total_ref[...].T.astype(bf16)


def quarter_rows(own):
    return -(-3 * own // (QUAD * GRANULE)) * GRANULE


def quarter_start(place, own):
    part = quarter_rows(own) // GRANULE
    return jnp.minimum(place * part, 3 * own // GRANULE - part)


def ring_of(n):
    inner = n // OUTER
    path = [(0, 0)]
    for outer_at in range(OUTER):
        across = range(1, inner) if outer_at % 2 == 0 else range(inner - 1, 0, -1)
        path += [(outer_at, inner_at) for inner_at in across]
    path += [(outer_at, 0) for outer_at in range(OUTER - 1, 0, -1)]
    return [outer_at * inner + inner_at for outer_at, inner_at in path]


def pieces_of(n):
    far = n // 2
    return [0] + [away for step in range(1, far) for away in (-step, step)] + [far]


def sources_of(n):
    ring = ring_of(n)
    table = []
    for device in range(n):
        at = ring.index(device)
        table.append([ring[(at + away) % n] for away in pieces_of(n) for _ in (0, 1)])
    return table


def gather(halves, n, beside=()):
    ring = ring_of(n)
    forward = [(ring[at], ring[(at + 1) % n]) for at in range(n)]
    backward = [(target, start) for start, target in forward]
    far = n // 2
    found = {(0, 0): halves[0], (1, 0): halves[1]}
    for step in range(1, far + 1):
        for half in (0, 1):
            for sign, pairs in ((-1, forward), (1, backward)):
                if step == far and (half == 0) != (sign == -1):
                    continue
                found[half, sign * step] = lax.ppermute(
                    found[half, sign * (step - 1)], "patch", pairs
                )
        if step == 1 and beside:
            (found[0, -1],) = after([found[0, -1]], beside)
    found[0, far] = found[0, -far]
    return [found[half, away] for away in pieces_of(n) for half in (0, 1)]


def send(block, shifts):
    batch, n = lax.axis_size("batch"), lax.axis_size("patch")
    pairs = []
    for at in range(batch):
        shift = shifts[at % len(shifts)]
        for start, target in moves(n, *shift) if shift else ():
            pairs.append((at * n + start, at * n + target))
    return lax.ppermute(block, ("batch", "patch"), pairs)


def swap(block, bit):
    pairs = [(at, at ^ bit) for at in range(lax.axis_size("batch"))]
    return lax.ppermute(block, "batch", pairs)


def moves(n, outer_step, inner_step):
    inner = n // OUTER
    pairs = []
    for start in range(n):
        outer_at = (start // inner + outer_step) % OUTER
        inner_at = (start % inner + inner_step) % inner
        pairs.append((start, outer_at * inner + inner_at))
    return pairs


def after(values, ready):
    anywhere = pl.BlockSpec(memory_space=pl.ANY)
    made = pl.pallas_call(
        lambda *refs: None,
        out_shape=[jax.ShapeDtypeStruct(value.shape, value.dtype) for value in values],
        in_specs=[anywhere] * (len(values) + len(ready)),
        out_specs=[anywhere] * len(values),
        input_output_aliases={at: at for at in range(len(values))},
        compiler_params=pltpu.CompilerParams(vmem_limit_bytes=MEBI),
        cost_estimate=pl.CostEstimate(flops=0, bytes_accessed=0, transcendentals=0),
        name="after",
    )(*values, *ready)
    return list(made)


def on_device(latent, conv_weight, channel_bias, w_query, w_key, w_value, w_out):
    rows_local, columns, channels = latent.shape
    n = lax.axis_size("patch")
    inner = n // OUTER
    own = channels // n
    block = rows_local * columns
    positions = block * n
    sources = jnp.asarray(sources_of(n), jnp.int32).reshape(-1)
    vmem = pl.BlockSpec(memory_space=pltpu.VMEM)
    smem = pl.BlockSpec(memory_space=pltpu.SMEM)
    anywhere = pl.BlockSpec(memory_space=pl.ANY)

    whole = latent.reshape(block, channels)
    halves = whole[: block // 2], whole[block // 2 :]
    chosen = []
    if inner == 2:
        quarter = quarter_rows(own)
        start = quarter_start(lax.rem(lax.axis_index("batch"), QUAD), own) * GRANULE
        stacked = jnp.concatenate([w_query, w_key, w_value], axis=0)
        chosen = [lax.dynamic_slice_in_dim(stacked, start, quarter, 0)]
    pieces = gather(halves, n, chosen)
    stats = pl.pallas_call(
        stats_kernel,
        out_shape=jax.ShapeDtypeStruct((24, channels), f32),
        in_specs=[vmem] * (2 * n - 2),
        out_specs=vmem,
        compiler_params=pltpu.CompilerParams(vmem_limit_bytes=2 * MEBI),
        cost_estimate=pl.CostEstimate(
            flops=6 * positions * channels,
            bytes_accessed=2 * positions * channels,
            transcendentals=0,
        ),
        name="stats",
    )(*pieces[:-2])
    if inner == 2:
        chosen, out_own = after(chosen + [w_out], pieces[-6:-2])
        chosen = send(chosen, [(0, 1)])
        far = send(out_own, FAR)
    else:
        sets = [list(range(at, at + inner)) for at in range(0, n, inner)]
        weights = jnp.stack([w_query, w_key, w_value])
        weights = lax.all_gather(weights, "patch", axis=1, tiled=True, axis_index_groups=sets)
        weights = [weights.reshape(3 * SET_CHANNELS, channels)]
        out_weights = [lax.all_gather(w_out, "patch", axis=0, tiled=True)]

    hidden = pl.pallas_call(
        functools.partial(conv_kernel, columns),
        out_shape=[jax.ShapeDtypeStruct((own, positions // 2), bf16)] * 2,
        in_specs=[smem] + [vmem] * (2 * n + 3),
        out_specs=[vmem] * 2,
        scratch_shapes=[
            pltpu.VMEM((positions + 2 * columns, channels), bf16),
            pltpu.VMEM((own, positions), f32),
        ],
        compiler_params=pltpu.CompilerParams(vmem_limit_bytes=20 * MEBI),
        cost_estimate=pl.CostEstimate(
            flops=2 * 9 * positions * channels * own,
            bytes_accessed=2 * (positions * channels + 9 * channels * own),
            transcendentals=positions * channels,
        ),
        name="norm_conv",
    )(
        sources,
        *pieces,
        stats,
        conv_weight.reshape(3, 3 * own, channels),
        channel_bias.reshape(1, own),
    )

    hidden_pieces = gather(tuple(hidden), n)
    if inner == 2:
        near = after([chosen], hidden[:1])
        near.append(swap(near[0], 2))
        near += [swap(one, 1) for one in near]
        weights = [w_query, w_key, w_value] + near
        far = [far, swap(far, 2)]

    made_rows = sum(weight.shape[0] for weight in weights)
    sums, some = pl.pallas_call(
        functools.partial(project_kernel, 2 * n),
        out_shape=[
            jax.ShapeDtypeStruct((made_rows, positions), f32),
            jax.ShapeDtypeStruct((channels, block), bf16),
        ],
        in_specs=[smem] + [vmem] * (2 * n - 2 + len(weights)),
        out_specs=[vmem] * 2,
        scratch_shapes=[pltpu.VMEM((channels, positions), bf16)],
        compiler_params=pltpu.CompilerParams(vmem_limit_bytes=20 * MEBI),
        cost_estimate=pl.CostEstimate(
            flops=2 * positions * channels * made_rows,
            bytes_accessed=2 * (positions * channels + made_rows * channels),
            transcendentals=0,
        ),
        name="norm_project",
    )(sources, *hidden_pieces[:-2], *weights)
    if inner == 2:
        far = after(far, hidden_pieces[-6:-2])
        place = lax.rem(lax.axis_index("batch"), QUAD)
        relayed = [send(jnp.where(place == QUAD - 1, far[1], far[0]), [(0, 1)])]
        relayed.append(send(far[1], [(0, 1), None]))
        far.append(swap(jnp.concatenate(far, axis=0), 1))
    one_block = jax.ShapeDtypeStruct((SET_CHANNELS, block), bf16)
    *sent, kept, made, key = pl.pallas_call(
        functools.partial(attention_kernel, 2 * n, inner),
        out_shape=[one_block] * len(SOONER)
        + [
            jax.ShapeDtypeStruct((channels, block), bf16),
            jax.ShapeDtypeStruct((made_rows, positions), bf16),
            jax.ShapeDtypeStruct((SET_HEADS, positions, HEAD_DIM), bf16),
        ],
        in_specs=[smem] + [vmem] * (4 + len(weights)),
        out_specs=[vmem] * (3 + len(SOONER)),
        scratch_shapes=[pltpu.VMEM((window_of(own), positions), bf16)],
        compiler_params=pltpu.CompilerParams(vmem_limit_bytes=28 * MEBI),
        cost_estimate=pl.CostEstimate(
            flops=2 * positions * window_of(own) * made_rows
            + 12 * positions * block * SET_CHANNELS,
            bytes_accessed=6 * made_rows * positions,
            transcendentals=positions * 3 * block * SET_HEADS,
        ),
        name="attention",
    )(sources, *hidden_pieces[-2:], *weights, sums, some)
    received = [None]
    for step, sent_block in zip(SOONER, sent):
        pairs = [(at, (at + step * inner) % n) for at in range(n)]
        received.append(lax.ppermute(sent_block, "patch", pairs))
    received[0] = pl.pallas_call(
        later_kernel,
        out_shape=one_block,
        in_specs=[vmem] * 2,
        out_specs=vmem,
        compiler_params=pltpu.CompilerParams(vmem_limit_bytes=16 * MEBI),
        cost_estimate=pl.CostEstimate(
            flops=4 * positions * block * SET_CHANNELS,
            bytes_accessed=8 * positions * SET_CHANNELS,
            transcendentals=positions * block * SET_HEADS,
        ),
        name="own_attention",
    )(made, key)
    if inner == 2:
        (relayed,) = after([jnp.concatenate(relayed, axis=0)], sent[:1])
        out_weights = [w_out] + far + [relayed, swap(relayed, 1)]

    output = pl.pallas_call(
        functools.partial(output_kernel, n),
        out_shape=jax.ShapeDtypeStruct((block, channels), bf16),
        in_specs=[vmem] * (OUTER + 1 + len(out_weights)),
        out_specs=vmem,
        scratch_shapes=[
            pltpu.VMEM((channels, block), bf16),
            pltpu.VMEM((channels, block), f32),
        ],
        compiler_params=pltpu.CompilerParams(vmem_limit_bytes=12 * MEBI),
        cost_estimate=pl.CostEstimate(
            flops=2 * block * channels * channels,
            bytes_accessed=2 * channels * (channels + 3 * block),
            transcendentals=0,
        ),
        name="project",
    )(*received, kept, *out_weights)
    return output.reshape(rows_local, columns, channels)


def solution(mesh):
    return jax.shard_map(
        on_device,
        mesh=mesh,
        in_specs=(
            P(("batch", "patch"), None, None),
            P(None, None, "patch", None),
            P("patch"),
            P("patch", None),
            P("patch", None),
            P("patch", None),
            P("patch", None),
        ),
        out_specs=P(("batch", "patch"), None, None),
        check_vma=False,
    )
```

```python
import functools

import jax
import jax.numpy as jnp
from jax import lax
from jax.experimental import pallas as pl
from jax.experimental.pallas import tpu as pltpu
from jax.sharding import PartitionSpec as P

C = 1280
HEADS = 20
HEAD_DIM = 64
GROUPS = 32
SPAN = C // GROUPS
OUTER = 4
SET_HEADS = HEADS // OUTER
SET_CHANNELS = SET_HEADS * HEAD_DIM
QUAD = 4
HANDED = (0, 2, 1, 3)
FAR = ((1, 0), (3, 0), (2, 0), (0, 1))
SOONER = tuple(range(1, OUTER))
WIDE = 256
EPSILON = 1e-05
CHUNK = 16
MEBI = 1024 * 1024

f32 = jnp.float32
bf16 = jnp.bfloat16

NT = (((1,), (1,)), ((), ()))
NN = (((1,), (0,)), ((), ()))


def dot(left, right, dims=NN):
    return lax.dot_general(left, right, dims, preferred_element_type=f32)


def exact(row, member, dims=NN):
    high = row.astype(bf16).astype(f32)
    middle = (row - high).astype(bf16).astype(f32)
    parts = [high, middle, row - high - middle, jnp.zeros((13, row.shape[1]), f32)]
    return jnp.sum(dot(jnp.concatenate(parts, axis=0).astype(bf16), member, dims), axis=0, keepdims=True)


def stats_kernel(*refs):
    pieces, out_ref = refs[:-1], refs[-1]
    block = pieces[0].shape[0]
    steps = block // CHUNK

    def add(step, total):
        for piece in pieces[:2]:
            total = total + folded(piece[pl.ds(step * CHUNK, CHUNK), :].astype(f32))
        return total

    zero = jnp.zeros((8, C), f32)
    pivot = jnp.sum(lax.fori_loop(0, steps, add, zero), axis=0, keepdims=True) / (2 * block)
    first, second = add_moments(pieces, pivot, zero, zero)
    out_ref[0:8, :] = jnp.broadcast_to(pivot, (8, C))
    out_ref[8:16, :] = first
    out_ref[16:24, :] = second


def folded(rows):
    return rows[:8] + rows[8:]


def add_moments(pieces, pivot, first, second):
    def add(step, sums):
        first, second = sums
        for piece in pieces:
            away = piece[pl.ds(step * CHUNK, CHUNK), :].astype(f32) - pivot
            first = first + folded(away)
            second = second + folded(away * away)
        return first, second

    return lax.fori_loop(0, pieces[0].shape[0] // CHUNK, add, (first, second))


def conv_kernel(columns, sources_ref, *refs):
    count = len(refs) - 7
    pieces = refs[:count]
    stats_ref, kernel_ref, bias_ref = refs[count : count + 3]
    out_refs = refs[count + 3 : count + 5]
    act_ref, kept_ref = refs[count + 5 :]
    block = pieces[0].shape[0]
    positions = block * count
    own = out_refs[0].shape[0]
    me = lax.axis_index("patch")
    steps = block // CHUNK
    starts = [
        pl.multiple_of(sources_ref[me * count + index] * (2 * block) + (index % 2) * block, block)
        for index in range(count)
    ]

    member = (
        lax.broadcasted_iota(jnp.int32, (C, 128), 0) // SPAN
        == lax.broadcasted_iota(jnp.int32, (C, 128), 1)
    ).astype(bf16)

    def group_mean(per_channel):
        return exact(exact(per_channel, member) / SPAN, member, NT)

    pivot = stats_ref[0:1, :]
    first, second = add_moments(pieces[-2:], pivot, stats_ref[8:16, :], stats_ref[16:24, :])
    above = jnp.sum(first, axis=0, keepdims=True) / positions
    within = jnp.sum(second, axis=0, keepdims=True) / positions - above * above
    mean = pivot + above
    centre = group_mean(mean)
    spread = group_mean(within + (mean - centre) * (mean - centre))
    half_scale = 0.5 * lax.rsqrt(spread + EPSILON)

    act_ref[0:columns, :] = jnp.zeros((columns, C), bf16)
    act_ref[positions + columns :, :] = jnp.zeros((columns, C), bf16)

    def activate(step, carry):
        for start, piece in zip(starts, pieces):
            half = (piece[pl.ds(step * CHUNK, CHUNK), :].astype(f32) - centre) * half_scale
            value = half + half * jnp.tanh(half)
            row = pl.multiple_of(columns + start + step * CHUNK, CHUNK)
            act_ref[pl.ds(row, CHUNK), :] = value.astype(bf16)
        return carry

    lax.fori_loop(0, steps, activate, 0)

    window = window_of(own)
    base = jnp.minimum(lax.div(me * own, 128) * 128, C - window)
    lanes = pl.ds(pl.multiple_of(base, 128), window)
    choose = (
        lax.broadcasted_iota(jnp.int32, (own, window), 0) + (me * own - base)
        == lax.broadcasted_iota(jnp.int32, (own, window), 1)
    ).astype(bf16)
    for index in range(0, count, 2):
        pair = jnp.concatenate([pieces[index][:, lanes], pieces[index + 1][:, lanes]], axis=0)
        start = pl.multiple_of(starts[index], 2 * block)
        kept_ref[:, pl.ds(start, 2 * block)] = dot(choose, pair, NT)

    wide = WIDE
    column = lax.broadcasted_iota(jnp.int32, (own, wide), 1) % columns
    square = (own, own)
    bias = jnp.where(
        lax.broadcasted_iota(jnp.int32, square, 0) == lax.broadcasted_iota(jnp.int32, square, 1),
        bias_ref[...],
        0.0,
    )
    bias = jnp.sum(bias, axis=1, keepdims=True)
    for at in range(0, positions, wide):
        taps = dot(kernel_ref[0], act_ref[at : at + wide, :], NT)
        for shift in (1, 2):
            low = at + shift * columns
            taps = taps + dot(kernel_ref[shift], act_ref[low : low + wide, :], NT)
        before = jnp.where(column > 0, pltpu.roll(taps[0:own], 1, 1), 0.0)
        after_ = jnp.where(column < columns - 1, pltpu.roll(taps[2 * own :], wide - 1, 1), 0.0)
        convolved = taps[own : 2 * own] + before + after_
        hidden = kept_ref[:, at : at + wide] + convolved + bias
        which, low = divmod(at, positions // 2)
        out_refs[which][:, low : low + wide] = hidden.astype(bf16)


def window_of(own):
    return min(C, (own + 127) // 128 * 128 + 128)


def norm_pair(pair):
    own = pair[0].shape[0]
    entries = float(2 * pair[0].shape[1] * SPAN)

    def whole(values):
        return jnp.sum(jnp.sum(values, axis=0, keepdims=True), axis=1, keepdims=True)

    def group_at(low):
        first, last = low // 16 * 16, -(-(low + SPAN) // 16) * 16
        return [ref[first:last, :].astype(f32)[low - first : low - first + SPAN] for ref in pair]

    lows = range(0, own, SPAN)
    means = [sum(whole(half) for half in group_at(low)) / entries for low in lows]
    squares = [
        sum(whole(jnp.square(half - mean)) for half in group_at(low))
        for low, mean in zip(lows, means)
    ]
    scales = [lax.rsqrt(square / entries + EPSILON) for square in squares]
    mean = jnp.concatenate([jnp.broadcast_to(one, (SPAN, 1)) for one in means], axis=0)
    scale = jnp.concatenate([jnp.broadcast_to(one, (SPAN, 1)) for one in scales], axis=0)
    return [((ref[...].astype(f32) - mean) * scale).astype(bf16) for ref in pair]


def own_lanes(pair, me, n):
    block = 2 * pair[0].shape[1] // n
    start = pl.multiple_of(lax.rem(me, n // 2) * block, block)
    low, high = (ref[:, pl.ds(start, block)] for ref in pair)
    return jnp.where(me < n // 2, low, high)


def project_kernel(count, sources_ref, *refs):
    pieces = refs[: count - 2]
    weight_refs = refs[count - 2 : -3]
    sums_ref, kept_ref, normed_ref = refs[-3:]
    own, part = pieces[0].shape
    me = lax.axis_index("patch")
    for at in range(0, count - 2, 2):
        pair = pieces[at : at + 2]
        rows = pl.ds(pl.multiple_of(sources_ref[me * count + at] * own, own), own)
        for half, normed in enumerate(norm_pair(pair)):
            normed_ref[rows, half * part : (half + 1) * part] = normed
        kept_ref[rows, :] = own_lanes(pair, me, count // 2)
    missing = pl.multiple_of(sources_ref[me * count + count - 2] * own, own)
    normed_ref[pl.ds(missing, own), :] = jnp.zeros((own, 2 * part), bf16)
    weights = jnp.concatenate([ref[...] for ref in weight_refs], axis=0)
    for at in range(0, 2 * part, WIDE):
        sums_ref[:, at : at + WIDE] = dot(weights, normed_ref[:, at : at + WIDE])


def attention_kernel(count, inner, sources_ref, *refs):
    pair = refs[:2]
    weight_refs = refs[2:-9]
    sums_ref, some_ref = refs[-9:-7]
    outs = refs[-7:-4]
    kept_ref, made_ref, key_ref, last_ref = refs[-4:]
    own, part = pair[0].shape
    n = count // 2
    me = lax.axis_index("patch")
    outer_at, inner_at = lax.div(me, inner), lax.rem(me, inner)
    source = sources_ref[me * count + count - 2]
    row = pl.multiple_of(source * own, own)
    kept_ref[...] = some_ref[...]
    kept_ref[pl.ds(row, own), :] = own_lanes(pair, me, n)

    window = last_ref.shape[0]
    base = jnp.minimum(lax.div(source * own, 128) * 128, C - window)
    lanes = pl.ds(pl.multiple_of(base, 128), window)
    last_ref[...] = jnp.zeros_like(last_ref)
    within = pl.ds(pl.multiple_of(source * own - base, 16), own)
    for half, normed in enumerate(norm_pair(pair)):
        last_ref[within, half * part : (half + 1) * part] = normed
    weights = jnp.concatenate([ref[:, lanes] for ref in weight_refs], axis=0)
    places = rows_of(weight_refs, own, inner, inner_at)
    for at in range(0, 2 * part, WIDE):
        made = dot(weights, last_ref[:, at : at + WIDE]) + sums_ref[:, at : at + WIDE]
        made = made.astype(bf16)
        for low, size, target in places:
            made_ref[pl.ds(target, size), at : at + WIDE] = made[low : low + size]

    for at in range(0, 2 * part, WIDE):
        for head in range(SET_HEADS):
            low = SET_CHANNELS + head * HEAD_DIM
            key = made_ref[low : low + HEAD_DIM, at : at + WIDE].astype(f32)
            key_ref[head, at : at + WIDE, :] = key.T.astype(bf16)

    targets = [lax.rem(outer_at + step, OUTER) * inner + inner_at for step in SOONER]
    attend(targets, made_ref, key_ref, outs)


def rows_of(weight_refs, own, inner, inner_at):
    if inner != 2:
        return [(0, weight_refs[0].shape[0], 0)]
    places = []
    for kind in range(3):
        place = kind * SET_CHANNELS + inner_at * own
        places.append((kind * own, own, pl.multiple_of(place, own)))
    core = lax.rem(lax.axis_index("batch"), 2)
    size = own // 2
    for order in range(2):
        half = core if order == 0 else 1 - core
        for at in range(3):
            part = 3 * half + at
            place = lax.div(part, 2) * SET_CHANNELS + (1 - inner_at) * own + lax.rem(part, 2) * size
            places.append((3 * own + (3 * order + at) * size, size, pl.multiple_of(place, 16)))
    return places


def later_kernel(made_ref, key_ref, out_ref):
    attend([lax.axis_index("patch")], made_ref, key_ref, [out_ref])


def attend(targets, made_ref, key_ref, outs):
    block = outs[0].shape[1]
    starts = [pl.multiple_of(target * block, block) for target in targets]
    for head in range(SET_HEADS):
        low = head * HEAD_DIM
        query = [made_ref[low : low + HEAD_DIM, pl.ds(start, block)] for start in starts]
        query = jnp.concatenate(query, axis=1).astype(f32) * HEAD_DIM ** (-0.5)
        scores = dot(key_ref[head], query.astype(bf16))
        peak = jnp.max(scores, axis=0, keepdims=True)
        unnormalized = jnp.exp(scores - peak)
        total = jnp.sum(unnormalized, axis=0, keepdims=True)
        value = made_ref[2 * SET_CHANNELS + low : 2 * SET_CHANNELS + low + HEAD_DIM, :]
        mixture = dot(value, unnormalized.astype(bf16))
        attended = (mixture / total).astype(bf16)
        for place, out in enumerate(outs):
            out[low : low + HEAD_DIM, :] = attended[:, place * block : (place + 1) * block]


def output_kernel(n, *refs):
    attended_refs = refs[:OUTER]
    hidden_ref = refs[OUTER]
    weight_refs = refs[OUTER + 1 : -3]
    out_ref, attended_ref, total_ref = refs[-3:]
    inner = n // OUTER
    own = C // n
    me = lax.axis_index("patch")
    outer_at, inner_at = lax.div(me, inner), lax.rem(me, inner)
    for step in range(OUTER):
        origin = lax.rem(outer_at + OUTER - step, OUTER)
        row = pl.multiple_of(origin * SET_CHANNELS, SET_CHANNELS)
        attended_ref[pl.ds(row, SET_CHANNELS), :] = attended_refs[step][...]
    attended = attended_ref[...]
    if inner != 2:
        total = dot(weight_refs[0][...], attended) + hidden_ref[...].astype(f32)
        out_ref[...] = total.T.astype(bf16)
        return

    total_ref[...] = hidden_ref[...].astype(f32)
    mine = lax.rem(lax.axis_index("batch"), QUAD)
    core = lax.rem(mine, 2)

    def add(weights, outer_step, inner_step, low=0):
        origin = lax.rem(outer_at + OUTER - outer_step, OUTER) * inner
        origin = origin + lax.rem(inner_at + inner_step, inner)
        rows = pl.ds(pl.multiple_of(origin * own + low, 16), weights.shape[0])
        total_ref[rows, :] += dot(weights, attended)

    own_ref, far_ref, across_ref, other_ref, mine_ref, others_ref = weight_refs
    side = lax.div(mine, 2)
    add(own_ref[...], 0, 0)
    far = [far_ref[...], across_ref[...], other_ref[:own, :], other_ref[own:, :]]
    for step, weights in zip(HANDED, far):
        which = jnp.bitwise_xor(mine, step)
        outer_step = jnp.where(which == 0, 1, jnp.where(which == 1, 3, jnp.where(which == 2, 2, 0)))
        add(weights, outer_step, lax.div(which, QUAD - 1))

    def add_relayed(two_ref, one_ref):
        add(two_ref[:own, :], 1 + side, 1)
        add(two_ref[own:, :], 2 - side, 1)
        add(one_ref[:own, :], 3, 1)

    @pl.when(core == 0)
    def _():
        add_relayed(mine_ref, others_ref)

    @pl.when(core == 1)
    def _():
        add_relayed(others_ref, mine_ref)

    out_ref[...] = total_ref[...].T.astype(bf16)


def ring_of(n):
    inner = n // OUTER
    path = [(0, 0)]
    for outer_at in range(OUTER):
        across = range(1, inner) if outer_at % 2 == 0 else range(inner - 1, 0, -1)
        path += [(outer_at, inner_at) for inner_at in across]
    path += [(outer_at, 0) for outer_at in range(OUTER - 1, 0, -1)]
    return [outer_at * inner + inner_at for outer_at, inner_at in path]


def pieces_of(n):
    far = n // 2
    return [0] + [away for step in range(1, far) for away in (-step, step)] + [far]


def sources_of(n):
    ring = ring_of(n)
    table = []
    for device in range(n):
        at = ring.index(device)
        table.append([ring[(at + away) % n] for away in pieces_of(n) for _ in (0, 1)])
    return table


def gather(halves, n, beside=()):
    ring = ring_of(n)
    forward = [(ring[at], ring[(at + 1) % n]) for at in range(n)]
    backward = [(target, start) for start, target in forward]
    far = n // 2
    found = {(0, 0): halves[0], (1, 0): halves[1]}
    for step in range(1, far + 1):
        for half in (0, 1):
            for sign, pairs in ((-1, forward), (1, backward)):
                if step == far and (half == 0) != (sign == -1):
                    continue
                found[half, sign * step] = lax.ppermute(
                    found[half, sign * (step - 1)], "patch", pairs
                )
        if step == 1 and beside:
            (found[0, -1],) = after([found[0, -1]], beside)
    found[0, far] = found[0, -far]
    return [found[half, away] for away in pieces_of(n) for half in (0, 1)]


def send(block, shifts):
    batch, n = lax.axis_size("batch"), lax.axis_size("patch")
    pairs = []
    for at in range(batch):
        shift = shifts[at % len(shifts)]
        for start, target in moves(n, *shift) if shift else ():
            pairs.append((at * n + start, at * n + target))
    return lax.ppermute(block, ("batch", "patch"), pairs)


def swap(block, bit):
    pairs = [(at, at ^ bit) for at in range(lax.axis_size("batch"))]
    return lax.ppermute(block, "batch", pairs)


def moves(n, outer_step, inner_step):
    inner = n // OUTER
    pairs = []
    for start in range(n):
        outer_at = (start // inner + outer_step) % OUTER
        inner_at = (start % inner + inner_step) % inner
        pairs.append((start, outer_at * inner + inner_at))
    return pairs


def after(values, ready):
    anywhere = pl.BlockSpec(memory_space=pl.ANY)
    made = pl.pallas_call(
        lambda *refs: None,
        out_shape=[jax.ShapeDtypeStruct(value.shape, value.dtype) for value in values],
        in_specs=[anywhere] * (len(values) + len(ready)),
        out_specs=[anywhere] * len(values),
        input_output_aliases={at: at for at in range(len(values))},
        compiler_params=pltpu.CompilerParams(vmem_limit_bytes=MEBI),
        cost_estimate=pl.CostEstimate(flops=0, bytes_accessed=0, transcendentals=0),
        name="after",
    )(*values, *ready)
    return list(made)


def on_device(latent, conv_weight, channel_bias, w_query, w_key, w_value, w_out):
    rows_local, columns, channels = latent.shape
    n = lax.axis_size("patch")
    inner = n // OUTER
    own = channels // n
    block = rows_local * columns
    positions = block * n
    sources = jnp.asarray(sources_of(n), jnp.int32).reshape(-1)
    vmem = pl.BlockSpec(memory_space=pltpu.VMEM)
    smem = pl.BlockSpec(memory_space=pltpu.SMEM)
    anywhere = pl.BlockSpec(memory_space=pl.ANY)

    whole = latent.reshape(block, channels)
    halves = whole[: block // 2], whole[block // 2 :]
    chosen = []
    if inner == 2:
        core = lax.rem(lax.axis_index("batch"), 2)
        stacked = jnp.concatenate([w_query, w_key, w_value], axis=0)
        chosen = [lax.dynamic_slice_in_dim(stacked, core * (3 * own // 2), 3 * own // 2, 0)]
    pieces = gather(halves, n, chosen)
    stats = pl.pallas_call(
        stats_kernel,
        out_shape=jax.ShapeDtypeStruct((24, channels), f32),
        in_specs=[vmem] * (2 * n - 2),
        out_specs=vmem,
        compiler_params=pltpu.CompilerParams(vmem_limit_bytes=2 * MEBI),
        cost_estimate=pl.CostEstimate(
            flops=6 * positions * channels,
            bytes_accessed=2 * positions * channels,
            transcendentals=0,
        ),
        name="stats",
    )(*pieces[:-2])
    if inner == 2:
        chosen, out_own = after(chosen + [w_out], pieces[-6:-2])
        chosen = send(chosen, [(0, 1)])
        far = send(out_own, FAR)
    else:
        sets = [list(range(at, at + inner)) for at in range(0, n, inner)]
        weights = jnp.stack([w_query, w_key, w_value])
        weights = lax.all_gather(weights, "patch", axis=1, tiled=True, axis_index_groups=sets)
        weights = [weights.reshape(3 * SET_CHANNELS, channels)]
        out_weights = [lax.all_gather(w_out, "patch", axis=0, tiled=True)]

    hidden = pl.pallas_call(
        functools.partial(conv_kernel, columns),
        out_shape=[jax.ShapeDtypeStruct((own, positions // 2), bf16)] * 2,
        in_specs=[smem] + [vmem] * (2 * n + 3),
        out_specs=[vmem] * 2,
        scratch_shapes=[
            pltpu.VMEM((positions + 2 * columns, channels), bf16),
            pltpu.VMEM((own, positions), f32),
        ],
        compiler_params=pltpu.CompilerParams(vmem_limit_bytes=20 * MEBI),
        cost_estimate=pl.CostEstimate(
            flops=2 * 9 * positions * channels * own,
            bytes_accessed=2 * (positions * channels + 9 * channels * own),
            transcendentals=positions * channels,
        ),
        name="norm_conv",
    )(
        sources,
        *pieces,
        stats,
        conv_weight.reshape(3, 3 * own, channels),
        channel_bias.reshape(1, own),
    )

    hidden_pieces = gather(tuple(hidden), n)
    if inner == 2:
        chosen, far = after([chosen, far], hidden_pieces[2:4])
        near = [chosen]
        near.append(swap(near[0], 1))
        weights = [w_query, w_key, w_value] + near
        far = [far, swap(far, 2)]

    made_rows = sum(weight.shape[0] for weight in weights)
    sums, some = pl.pallas_call(
        functools.partial(project_kernel, 2 * n),
        out_shape=[
            jax.ShapeDtypeStruct((made_rows, positions), f32),
            jax.ShapeDtypeStruct((channels, block), bf16),
        ],
        in_specs=[smem] + [vmem] * (2 * n - 2 + len(weights)),
        out_specs=[vmem] * 2,
        scratch_shapes=[pltpu.VMEM((channels, positions), bf16)],
        compiler_params=pltpu.CompilerParams(vmem_limit_bytes=20 * MEBI),
        cost_estimate=pl.CostEstimate(
            flops=2 * positions * channels * made_rows,
            bytes_accessed=2 * (positions * channels + made_rows * channels),
            transcendentals=0,
        ),
        name="norm_project",
    )(sources, *hidden_pieces[:-2], *weights)
    if inner == 2:
        far = after(far, hidden_pieces[-6:-2])
        place = lax.rem(lax.axis_index("batch"), QUAD)
        relayed = [send(jnp.where(place == QUAD - 1, far[1], far[0]), [(0, 1)])]
        relayed.append(send(far[1], [(0, 1), None]))
        far.append(swap(jnp.concatenate(far, axis=0), 1))
    one_block = jax.ShapeDtypeStruct((SET_CHANNELS, block), bf16)
    *sent, kept, made, key = pl.pallas_call(
        functools.partial(attention_kernel, 2 * n, inner),
        out_shape=[one_block] * len(SOONER)
        + [
            jax.ShapeDtypeStruct((channels, block), bf16),
            jax.ShapeDtypeStruct((made_rows, positions), bf16),
            jax.ShapeDtypeStruct((SET_HEADS, positions, HEAD_DIM), bf16),
        ],
        in_specs=[smem] + [vmem] * (4 + len(weights)),
        out_specs=[vmem] * (3 + len(SOONER)),
        scratch_shapes=[pltpu.VMEM((window_of(own), positions), bf16)],
        compiler_params=pltpu.CompilerParams(vmem_limit_bytes=28 * MEBI),
        cost_estimate=pl.CostEstimate(
            flops=2 * positions * window_of(own) * made_rows
            + 12 * positions * block * SET_CHANNELS,
            bytes_accessed=6 * made_rows * positions,
            transcendentals=positions * 3 * block * SET_HEADS,
        ),
        name="attention",
    )(sources, *hidden_pieces[-2:], *weights, sums, some)
    received = [None]
    for step, sent_block in zip(SOONER, sent):
        pairs = [(at, (at + step * inner) % n) for at in range(n)]
        received.append(lax.ppermute(sent_block, "patch", pairs))
    received[0] = pl.pallas_call(
        later_kernel,
        out_shape=one_block,
        in_specs=[vmem] * 2,
        out_specs=vmem,
        compiler_params=pltpu.CompilerParams(vmem_limit_bytes=16 * MEBI),
        cost_estimate=pl.CostEstimate(
            flops=4 * positions * block * SET_CHANNELS,
            bytes_accessed=8 * positions * SET_CHANNELS,
            transcendentals=positions * block * SET_HEADS,
        ),
        name="own_attention",
    )(made, key)
    if inner == 2:
        (relayed,) = after([jnp.concatenate(relayed, axis=0)], sent[:1])
        out_weights = [w_out] + far + [relayed, swap(relayed, 1)]

    output = pl.pallas_call(
        functools.partial(output_kernel, n),
        out_shape=jax.ShapeDtypeStruct((block, channels), bf16),
        in_specs=[vmem] * (OUTER + 1 + len(out_weights)),
        out_specs=vmem,
        scratch_shapes=[
            pltpu.VMEM((channels, block), bf16),
            pltpu.VMEM((channels, block), f32),
        ],
        compiler_params=pltpu.CompilerParams(vmem_limit_bytes=12 * MEBI),
        cost_estimate=pl.CostEstimate(
            flops=2 * block * channels * channels,
            bytes_accessed=2 * channels * (channels + 3 * block),
            transcendentals=0,
        ),
        name="project",
    )(*received, kept, *out_weights)
    return output.reshape(rows_local, columns, channels)


def solution(mesh):
    return jax.shard_map(
        on_device,
        mesh=mesh,
        in_specs=(
            P(("batch", "patch"), None, None),
            P(None, None, "patch", None),
            P("patch"),
            P("patch", None),
            P("patch", None),
            P("patch", None),
            P("patch", None),
        ),
        out_specs=P(("batch", "patch"), None, None),
        check_vma=False,
    )
```

```python
import functools

import jax
import jax.numpy as jnp
from jax import lax
from jax.experimental import pallas as pl
from jax.experimental.pallas import tpu as pltpu
from jax.sharding import PartitionSpec as P

C = 1280
HEADS = 20
HEAD_DIM = 64
GROUPS = 32
SPAN = C // GROUPS
OUTER = 4
SET_HEADS = HEADS // OUTER
SET_CHANNELS = SET_HEADS * HEAD_DIM
QUAD = 4
HANDED = (0, 2, 1, 3)
FAR = ((1, 0), (3, 0), (2, 0), (0, 1))
SOONER = tuple(range(1, OUTER))
WIDE = 256
EPSILON = 1e-05
LATE = 6
CHUNK = 16
MEBI = 1024 * 1024

f32 = jnp.float32
bf16 = jnp.bfloat16

NT = (((1,), (1,)), ((), ()))
NN = (((1,), (0,)), ((), ()))


def dot(left, right, dims=NN):
    return lax.dot_general(left, right, dims, preferred_element_type=f32)


def exact(row, member, dims=NN):
    high = row.astype(bf16).astype(f32)
    middle = (row - high).astype(bf16).astype(f32)
    parts = [high, middle, row - high - middle, jnp.zeros((13, row.shape[1]), f32)]
    return jnp.sum(dot(jnp.concatenate(parts, axis=0).astype(bf16), member, dims), axis=0, keepdims=True)


def stats_kernel(*refs):
    pieces, out_ref = refs[:-1], refs[-1]
    block = pieces[0].shape[0]
    steps = block // CHUNK

    def add(step, total):
        for piece in pieces[:2]:
            total = total + folded(piece[pl.ds(step * CHUNK, CHUNK), :].astype(f32))
        return total

    zero = jnp.zeros((8, C), f32)
    pivot = jnp.sum(lax.fori_loop(0, steps, add, zero), axis=0, keepdims=True) / (2 * block)
    first, second = add_moments(pieces, pivot, zero, zero)
    out_ref[0:8, :] = jnp.broadcast_to(pivot, (8, C))
    out_ref[8:16, :] = first
    out_ref[16:24, :] = second


def folded(rows):
    return rows[:8] + rows[8:]


def add_moments(pieces, pivot, first, second):
    def add(step, sums):
        first, second = sums
        for piece in pieces:
            away = piece[pl.ds(step * CHUNK, CHUNK), :].astype(f32) - pivot
            first = first + folded(away)
            second = second + folded(away * away)
        return first, second

    return lax.fori_loop(0, pieces[0].shape[0] // CHUNK, add, (first, second))


def conv_kernel(columns, sources_ref, *refs):
    count = len(refs) - 6
    pieces = refs[:count]
    stats_ref, kernel_ref, bias_ref = refs[count : count + 3]
    out_ref, act_ref, kept_ref = refs[count + 3 :]
    block = pieces[0].shape[0]
    positions = block * count
    own = out_ref.shape[0]
    me = lax.axis_index("patch")
    steps = block // CHUNK
    starts = [
        pl.multiple_of(sources_ref[me * count + index] * (2 * block) + (index % 2) * block, block)
        for index in range(count)
    ]

    member = (
        lax.broadcasted_iota(jnp.int32, (C, 128), 0) // SPAN
        == lax.broadcasted_iota(jnp.int32, (C, 128), 1)
    ).astype(bf16)

    def group_mean(per_channel):
        return exact(exact(per_channel, member) / SPAN, member, NT)

    pivot = stats_ref[0:1, :]
    first, second = add_moments(pieces[-LATE:], pivot, stats_ref[8:16, :], stats_ref[16:24, :])
    above = jnp.sum(first, axis=0, keepdims=True) / positions
    within = jnp.sum(second, axis=0, keepdims=True) / positions - above * above
    mean = pivot + above
    centre = group_mean(mean)
    spread = group_mean(within + (mean - centre) * (mean - centre))
    half_scale = 0.5 * lax.rsqrt(spread + EPSILON)

    act_ref[0:columns, :] = jnp.zeros((columns, C), bf16)
    act_ref[positions + columns :, :] = jnp.zeros((columns, C), bf16)

    def activate(step, carry):
        for start, piece in zip(starts, pieces):
            half = (piece[pl.ds(step * CHUNK, CHUNK), :].astype(f32) - centre) * half_scale
            value = half + half * jnp.tanh(half)
            row = pl.multiple_of(columns + start + step * CHUNK, CHUNK)
            act_ref[pl.ds(row, CHUNK), :] = value.astype(bf16)
        return carry

    lax.fori_loop(0, steps, activate, 0)

    window = window_of(own)
    base = jnp.minimum(lax.div(me * own, 128) * 128, C - window)
    lanes = pl.ds(pl.multiple_of(base, 128), window)
    choose = (
        lax.broadcasted_iota(jnp.int32, (own, window), 0) + (me * own - base)
        == lax.broadcasted_iota(jnp.int32, (own, window), 1)
    ).astype(bf16)
    for index in range(0, count, 2):
        pair = jnp.concatenate([pieces[index][:, lanes], pieces[index + 1][:, lanes]], axis=0)
        start = pl.multiple_of(starts[index], 2 * block)
        kept_ref[:, pl.ds(start, 2 * block)] = dot(choose, pair, NT)

    convolve(columns, 0, act_ref, kept_ref, kernel_ref, bias_ref, out_ref)


def second_conv_kernel(columns, act_ref, kept_ref, kernel_ref, bias_ref, out_ref):
    convolve(columns, out_ref.shape[1], act_ref, kept_ref, kernel_ref, bias_ref, out_ref)


def convolve(columns, start, act_ref, kept_ref, kernel_ref, bias_ref, out_ref):
    own = out_ref.shape[0]
    column = lax.broadcasted_iota(jnp.int32, (own, WIDE), 1) % columns
    square = (own, own)
    bias = jnp.where(
        lax.broadcasted_iota(jnp.int32, square, 0) == lax.broadcasted_iota(jnp.int32, square, 1),
        bias_ref[...],
        0.0,
    )
    bias = jnp.sum(bias, axis=1, keepdims=True)
    for low in range(0, out_ref.shape[1], WIDE):
        at = start + low
        taps = dot(kernel_ref[0], act_ref[at : at + WIDE, :], NT)
        for shift in (1, 2):
            first = at + shift * columns
            taps = taps + dot(kernel_ref[shift], act_ref[first : first + WIDE, :], NT)
        before = jnp.where(column > 0, pltpu.roll(taps[0:own], 1, 1), 0.0)
        after_ = jnp.where(column < columns - 1, pltpu.roll(taps[2 * own :], WIDE - 1, 1), 0.0)
        convolved = taps[own : 2 * own] + before + after_
        hidden = kept_ref[:, at : at + WIDE] + convolved + bias
        out_ref[:, low : low + WIDE] = hidden.astype(bf16)


def window_of(own):
    return min(C, (own + 127) // 128 * 128 + 128)


def norm_pair(pair):
    own = pair[0].shape[0]
    entries = float(2 * pair[0].shape[1] * SPAN)

    def whole(values):
        return jnp.sum(jnp.sum(values, axis=0, keepdims=True), axis=1, keepdims=True)

    def group_at(low):
        first, last = low // 16 * 16, -(-(low + SPAN) // 16) * 16
        return [ref[first:last, :].astype(f32)[low - first : low - first + SPAN] for ref in pair]

    lows = range(0, own, SPAN)
    means = [sum(whole(half) for half in group_at(low)) / entries for low in lows]
    squares = [
        sum(whole(jnp.square(half - mean)) for half in group_at(low))
        for low, mean in zip(lows, means)
    ]
    scales = [lax.rsqrt(square / entries + EPSILON) for square in squares]
    mean = jnp.concatenate([jnp.broadcast_to(one, (SPAN, 1)) for one in means], axis=0)
    scale = jnp.concatenate([jnp.broadcast_to(one, (SPAN, 1)) for one in scales], axis=0)
    return [((ref[...].astype(f32) - mean) * scale).astype(bf16) for ref in pair]


def own_lanes(pair, me, n):
    block = 2 * pair[0].shape[1] // n
    start = pl.multiple_of(lax.rem(me, n // 2) * block, block)
    low, high = (ref[:, pl.ds(start, block)] for ref in pair)
    return jnp.where(me < n // 2, low, high)


def early_kernel(n, *refs):
    pieces, outs = refs[:-2], refs[-2:]
    me = lax.axis_index("patch")
    own, part = pieces[0].shape
    for at in range(0, len(pieces), 2):
        pair = pieces[at : at + 2]
        rows = slice(at // 2 * own, (at // 2 + 1) * own)
        for half, normed in enumerate(norm_pair(pair)):
            outs[0][rows, half * part : (half + 1) * part] = normed
        outs[1][rows, :] = own_lanes(pair, me, n)


def project_kernel(count, sources_ref, *refs):
    early_ref, some_ref = refs[:2]
    pieces = refs[2:LATE]
    weight_refs = refs[LATE:-3]
    sums_ref, kept_ref, normed_ref = refs[-3:]
    own, part = pieces[0].shape
    me = lax.axis_index("patch")
    for at in range(0, count - 2, 2):
        rows = pl.ds(pl.multiple_of(sources_ref[me * count + at] * own, own), own)
        if at < count - LATE:
            there = slice(at // 2 * own, (at // 2 + 1) * own)
            normed_ref[rows, :] = early_ref[there, :]
            kept_ref[rows, :] = some_ref[there, :]
            continue
        pair = pieces[at - count + LATE :][:2]
        for half, normed in enumerate(norm_pair(pair)):
            normed_ref[rows, half * part : (half + 1) * part] = normed
        kept_ref[rows, :] = own_lanes(pair, me, count // 2)
    missing = pl.multiple_of(sources_ref[me * count + count - 2] * own, own)
    normed_ref[pl.ds(missing, own), :] = jnp.zeros((own, 2 * part), bf16)
    weights = jnp.concatenate([ref[...] for ref in weight_refs], axis=0)
    for at in range(0, 2 * part, WIDE):
        sums_ref[:, at : at + WIDE] = dot(weights, normed_ref[:, at : at + WIDE])


def attention_kernel(count, inner, sources_ref, *refs):
    pair = refs[:2]
    weight_refs = refs[2:-9]
    sums_ref, some_ref = refs[-9:-7]
    outs = refs[-7:-4]
    kept_ref, made_ref, key_ref, last_ref = refs[-4:]
    own, part = pair[0].shape
    n = count // 2
    me = lax.axis_index("patch")
    outer_at, inner_at = lax.div(me, inner), lax.rem(me, inner)
    source = sources_ref[me * count + count - 2]
    row = pl.multiple_of(source * own, own)
    kept_ref[...] = some_ref[...]
    kept_ref[pl.ds(row, own), :] = own_lanes(pair, me, n)

    window = last_ref.shape[0]
    base = jnp.minimum(lax.div(source * own, 128) * 128, C - window)
    lanes = pl.ds(pl.multiple_of(base, 128), window)
    last_ref[...] = jnp.zeros_like(last_ref)
    within = pl.ds(pl.multiple_of(source * own - base, 16), own)
    for half, normed in enumerate(norm_pair(pair)):
        last_ref[within, half * part : (half + 1) * part] = normed
    weights = jnp.concatenate([ref[:, lanes] for ref in weight_refs], axis=0)
    places = rows_of(weight_refs, own, inner, inner_at)
    for at in range(0, 2 * part, WIDE):
        made = dot(weights, last_ref[:, at : at + WIDE]) + sums_ref[:, at : at + WIDE]
        made = made.astype(bf16)
        for low, size, target in places:
            made_ref[pl.ds(target, size), at : at + WIDE] = made[low : low + size]

    for at in range(0, 2 * part, WIDE):
        for head in range(SET_HEADS):
            low = SET_CHANNELS + head * HEAD_DIM
            key = made_ref[low : low + HEAD_DIM, at : at + WIDE].astype(f32)
            key_ref[head, at : at + WIDE, :] = key.T.astype(bf16)

    targets = [lax.rem(outer_at + step, OUTER) * inner + inner_at for step in SOONER]
    attend(targets, made_ref, key_ref, outs)


def rows_of(weight_refs, own, inner, inner_at):
    if inner != 2:
        return [(0, weight_refs[0].shape[0], 0)]
    places = []
    for kind in range(3):
        place = kind * SET_CHANNELS + inner_at * own
        places.append((kind * own, own, pl.multiple_of(place, own)))
    core = lax.rem(lax.axis_index("batch"), 2)
    size = own // 2
    for order in range(2):
        half = core if order == 0 else 1 - core
        for at in range(3):
            part = 3 * half + at
            place = lax.div(part, 2) * SET_CHANNELS + (1 - inner_at) * own + lax.rem(part, 2) * size
            places.append((3 * own + (3 * order + at) * size, size, pl.multiple_of(place, 16)))
    return places


def later_kernel(made_ref, key_ref, out_ref):
    attend([lax.axis_index("patch")], made_ref, key_ref, [out_ref])


def attend(targets, made_ref, key_ref, outs):
    block = outs[0].shape[1]
    starts = [pl.multiple_of(target * block, block) for target in targets]
    for head in range(SET_HEADS):
        low = head * HEAD_DIM
        query = [made_ref[low : low + HEAD_DIM, pl.ds(start, block)] for start in starts]
        query = jnp.concatenate(query, axis=1).astype(f32) * HEAD_DIM ** (-0.5)
        scores = dot(key_ref[head], query.astype(bf16))
        peak = jnp.max(scores, axis=0, keepdims=True)
        unnormalized = jnp.exp(scores - peak)
        total = jnp.sum(unnormalized, axis=0, keepdims=True)
        value = made_ref[2 * SET_CHANNELS + low : 2 * SET_CHANNELS + low + HEAD_DIM, :]
        mixture = dot(value, unnormalized.astype(bf16))
        attended = (mixture / total).astype(bf16)
        for place, out in enumerate(outs):
            out[low : low + HEAD_DIM, :] = attended[:, place * block : (place + 1) * block]


def output_kernel(n, *refs):
    attended_refs = refs[:OUTER]
    hidden_ref = refs[OUTER]
    weight_refs = refs[OUTER + 1 : -3]
    out_ref, attended_ref, total_ref = refs[-3:]
    inner = n // OUTER
    own = C // n
    me = lax.axis_index("patch")
    outer_at, inner_at = lax.div(me, inner), lax.rem(me, inner)
    for step in range(OUTER):
        origin = lax.rem(outer_at + OUTER - step, OUTER)
        row = pl.multiple_of(origin * SET_CHANNELS, SET_CHANNELS)
        attended_ref[pl.ds(row, SET_CHANNELS), :] = attended_refs[step][...]
    attended = attended_ref[...]
    if inner != 2:
        total = dot(weight_refs[0][...], attended) + hidden_ref[...].astype(f32)
        out_ref[...] = total.T.astype(bf16)
        return

    total_ref[...] = hidden_ref[...].astype(f32)
    mine = lax.rem(lax.axis_index("batch"), QUAD)
    core = lax.rem(mine, 2)

    def add(weights, outer_step, inner_step, low=0):
        origin = lax.rem(outer_at + OUTER - outer_step, OUTER) * inner
        origin = origin + lax.rem(inner_at + inner_step, inner)
        rows = pl.ds(pl.multiple_of(origin * own + low, 16), weights.shape[0])
        total_ref[rows, :] += dot(weights, attended)

    own_ref, far_ref, across_ref, other_ref, mine_ref, others_ref = weight_refs
    side = lax.div(mine, 2)
    add(own_ref[...], 0, 0)
    far = [far_ref[...], across_ref[...], other_ref[:own, :], other_ref[own:, :]]
    for step, weights in zip(HANDED, far):
        which = jnp.bitwise_xor(mine, step)
        outer_step = jnp.where(which == 0, 1, jnp.where(which == 1, 3, jnp.where(which == 2, 2, 0)))
        add(weights, outer_step, lax.div(which, QUAD - 1))

    def add_relayed(two_ref, one_ref):
        add(two_ref[:own, :], 1 + side, 1)
        add(two_ref[own:, :], 2 - side, 1)
        add(one_ref[:own, :], 3, 1)

    @pl.when(core == 0)
    def _():
        add_relayed(mine_ref, others_ref)

    @pl.when(core == 1)
    def _():
        add_relayed(others_ref, mine_ref)

    out_ref[...] = total_ref[...].T.astype(bf16)


def ring_of(n):
    inner = n // OUTER
    path = [(0, 0)]
    for outer_at in range(OUTER):
        across = range(1, inner) if outer_at % 2 == 0 else range(inner - 1, 0, -1)
        path += [(outer_at, inner_at) for inner_at in across]
    path += [(outer_at, 0) for outer_at in range(OUTER - 1, 0, -1)]
    return [outer_at * inner + inner_at for outer_at, inner_at in path]


def pieces_of(n):
    far = n // 2
    return [0] + [away for step in range(1, far) for away in (-step, step)] + [far]


def sources_of(n):
    ring = ring_of(n)
    table = []
    for device in range(n):
        at = ring.index(device)
        table.append([ring[(at + away) % n] for away in pieces_of(n) for _ in (0, 1)])
    return table


def gather(halves, n, beside):
    ring = ring_of(n)
    forward = [(ring[at], ring[(at + 1) % n]) for at in range(n)]
    backward = [(target, start) for start, target in forward]
    far = n // 2
    found = {(0, 0): halves[0], (1, 0): halves[1]}
    for step in range(1, far + 1):
        for half in (0, 1):
            for sign, pairs in ((-1, forward), (1, backward)):
                if step == far and (half == 0) != (sign == -1):
                    continue
                found[half, sign * step] = lax.ppermute(
                    found[half, sign * (step - 1)], "patch", pairs
                )
        others = beside(step, found)
        if others:
            (found[0, -step],) = after([found[0, -step]], others)
    found[0, far] = found[0, -far]
    return in_order(found, n)


def in_order(found, n):
    places = [(half, away) for away in pieces_of(n) for half in (0, 1)]
    return [found[place] for place in places if place in found]


def send(block, shifts):
    batch, n = lax.axis_size("batch"), lax.axis_size("patch")
    pairs = []
    for at in range(batch):
        shift = shifts[at % len(shifts)]
        for start, target in moves(n, *shift) if shift else ():
            pairs.append((at * n + start, at * n + target))
    return lax.ppermute(block, ("batch", "patch"), pairs)


def swap(block, bit):
    pairs = [(at, at ^ bit) for at in range(lax.axis_size("batch"))]
    return lax.ppermute(block, "batch", pairs)


def moves(n, outer_step, inner_step):
    inner = n // OUTER
    pairs = []
    for start in range(n):
        outer_at = (start // inner + outer_step) % OUTER
        inner_at = (start % inner + inner_step) % inner
        pairs.append((start, outer_at * inner + inner_at))
    return pairs


def after(values, ready):
    anywhere = pl.BlockSpec(memory_space=pl.ANY)
    made = pl.pallas_call(
        lambda *refs: None,
        out_shape=[jax.ShapeDtypeStruct(value.shape, value.dtype) for value in values],
        in_specs=[anywhere] * (len(values) + len(ready)),
        out_specs=[anywhere] * len(values),
        input_output_aliases={at: at for at in range(len(values))},
        compiler_params=pltpu.CompilerParams(vmem_limit_bytes=MEBI),
        cost_estimate=pl.CostEstimate(flops=0, bytes_accessed=0, transcendentals=0),
        name="after",
    )(*values, *ready)
    return list(made)


def on_device(latent, conv_weight, channel_bias, w_query, w_key, w_value, w_out):
    rows_local, columns, channels = latent.shape
    n = lax.axis_size("patch")
    inner = n // OUTER
    own = channels // n
    block = rows_local * columns
    positions = block * n
    sources = jnp.asarray(sources_of(n), jnp.int32).reshape(-1)
    vmem = pl.BlockSpec(memory_space=pltpu.VMEM)
    smem = pl.BlockSpec(memory_space=pltpu.SMEM)
    anywhere = pl.BlockSpec(memory_space=pl.ANY)

    whole = latent.reshape(block, channels)
    halves = whole[: block // 2], whole[block // 2 :]
    chosen = []
    if inner == 2:
        core = lax.rem(lax.axis_index("batch"), 2)
        stacked = jnp.concatenate([w_query, w_key, w_value], axis=0)
        chosen = [lax.dynamic_slice_in_dim(stacked, core * (3 * own // 2), 3 * own // 2, 0)]
    far_step = n // 2
    made_beside = []

    def beside_first(step, found):
        if step == 1:
            return chosen
        if step != far_step - 1:
            return []
        made_beside.append(
            pl.pallas_call(
                stats_kernel,
                out_shape=jax.ShapeDtypeStruct((24, channels), f32),
                in_specs=[vmem] * (2 * n - LATE),
                out_specs=vmem,
                compiler_params=pltpu.CompilerParams(vmem_limit_bytes=2 * MEBI),
                cost_estimate=pl.CostEstimate(
                    flops=6 * positions * channels,
                    bytes_accessed=2 * positions * channels,
                    transcendentals=0,
                ),
                name="stats",
            )(*in_order(found, n)[: 2 * n - LATE])
        )
        return made_beside[-1:]

    pieces = gather(halves, n, beside_first)
    stats = made_beside[0]
    if inner == 2:
        chosen, out_own = after(chosen + [w_out], pieces[-6:-2])
        chosen = send(chosen, [(0, 1)])
        far = send(out_own, FAR)
    else:
        sets = [list(range(at, at + inner)) for at in range(0, n, inner)]
        weights = jnp.stack([w_query, w_key, w_value])
        weights = lax.all_gather(weights, "patch", axis=1, tiled=True, axis_index_groups=sets)
        weights = [weights.reshape(3 * SET_CHANNELS, channels)]
        out_weights = [lax.all_gather(w_out, "patch", axis=0, tiled=True)]

    kernel = conv_weight.reshape(3, 3 * own, channels)
    bias = channel_bias.reshape(1, own)
    half_hidden = jax.ShapeDtypeStruct((own, positions // 2), bf16)
    flops = 9 * positions * channels * own
    first_hidden, act, residual = pl.pallas_call(
        functools.partial(conv_kernel, columns),
        out_shape=[
            half_hidden,
            jax.ShapeDtypeStruct((positions + 2 * columns, channels), bf16),
            jax.ShapeDtypeStruct((own, positions), f32),
        ],
        in_specs=[smem] + [vmem] * (2 * n + 3),
        out_specs=[vmem] * 3,
        compiler_params=pltpu.CompilerParams(vmem_limit_bytes=20 * MEBI),
        cost_estimate=pl.CostEstimate(
            flops=flops,
            bytes_accessed=2 * (positions * channels + 9 * channels * own),
            transcendentals=positions * channels,
        ),
        name="norm_conv",
    )(sources, *pieces, stats, kernel, bias)
    second_hidden = pl.pallas_call(
        functools.partial(second_conv_kernel, columns),
        out_shape=half_hidden,
        in_specs=[vmem] * 4,
        out_specs=vmem,
        compiler_params=pltpu.CompilerParams(vmem_limit_bytes=16 * MEBI),
        cost_estimate=pl.CostEstimate(flops=flops, bytes_accessed=flops // 1000, transcendentals=0),
        name="second_conv",
    )(act, residual, kernel, bias)

    def beside_second(step, found):
        if step != far_step - 1:
            return []
        count = n - LATE // 2
        made_beside.append(
            pl.pallas_call(
                functools.partial(early_kernel, n),
                out_shape=[
                    jax.ShapeDtypeStruct((count * own, positions), bf16),
                    jax.ShapeDtypeStruct((count * own, block), bf16),
                ],
                in_specs=[vmem] * (2 * count),
                out_specs=[vmem] * 2,
                compiler_params=pltpu.CompilerParams(vmem_limit_bytes=8 * MEBI),
                cost_estimate=pl.CostEstimate(
                    flops=8 * positions * channels,
                    bytes_accessed=4 * positions * channels,
                    transcendentals=0,
                ),
                name="early_norm",
            )(*in_order(found, n)[: 2 * count])
        )
        return made_beside[-1][:1]

    hidden_pieces = gather((first_hidden, second_hidden), n, beside_second)
    if inner == 2:
        chosen, far = after([chosen, far], hidden_pieces[2:4])
        near = [chosen]
        near.append(swap(near[0], 1))
        weights = [w_query, w_key, w_value] + near
        far = [far, swap(far, 2)]

    made_rows = sum(weight.shape[0] for weight in weights)
    sums, some = pl.pallas_call(
        functools.partial(project_kernel, 2 * n),
        out_shape=[
            jax.ShapeDtypeStruct((made_rows, positions), f32),
            jax.ShapeDtypeStruct((channels, block), bf16),
        ],
        in_specs=[smem] + [vmem] * (LATE + len(weights)),
        out_specs=[vmem] * 2,
        scratch_shapes=[pltpu.VMEM((channels, positions), bf16)],
        compiler_params=pltpu.CompilerParams(vmem_limit_bytes=20 * MEBI),
        cost_estimate=pl.CostEstimate(
            flops=2 * positions * channels * made_rows,
            bytes_accessed=2 * (positions * channels + made_rows * channels),
            transcendentals=0,
        ),
        name="norm_project",
    )(sources, *made_beside[-1], *hidden_pieces[-LATE:-2], *weights)
    if inner == 2:
        far = after(far, hidden_pieces[-6:-2])
        place = lax.rem(lax.axis_index("batch"), QUAD)
        relayed = [send(jnp.where(place == QUAD - 1, far[1], far[0]), [(0, 1)])]
        relayed.append(send(far[1], [(0, 1), None]))
        far.append(swap(jnp.concatenate(far, axis=0), 1))
    one_block = jax.ShapeDtypeStruct((SET_CHANNELS, block), bf16)
    *sent, kept, made, key = pl.pallas_call(
        functools.partial(attention_kernel, 2 * n, inner),
        out_shape=[one_block] * len(SOONER)
        + [
            jax.ShapeDtypeStruct((channels, block), bf16),
            jax.ShapeDtypeStruct((made_rows, positions), bf16),
            jax.ShapeDtypeStruct((SET_HEADS, positions, HEAD_DIM), bf16),
        ],
        in_specs=[smem] + [vmem] * (4 + len(weights)),
        out_specs=[vmem] * (3 + len(SOONER)),
        scratch_shapes=[pltpu.VMEM((window_of(own), positions), bf16)],
        compiler_params=pltpu.CompilerParams(vmem_limit_bytes=28 * MEBI),
        cost_estimate=pl.CostEstimate(
            flops=2 * positions * window_of(own) * made_rows
            + 12 * positions * block * SET_CHANNELS,
            bytes_accessed=6 * made_rows * positions,
            transcendentals=positions * 3 * block * SET_HEADS,
        ),
        name="attention",
    )(sources, *hidden_pieces[-2:], *weights, sums, some)
    received = [None]
    for step, sent_block in zip(SOONER, sent):
        pairs = [(at, (at + step * inner) % n) for at in range(n)]
        received.append(lax.ppermute(sent_block, "patch", pairs))
    received[0] = pl.pallas_call(
        later_kernel,
        out_shape=one_block,
        in_specs=[vmem] * 2,
        out_specs=vmem,
        compiler_params=pltpu.CompilerParams(vmem_limit_bytes=16 * MEBI),
        cost_estimate=pl.CostEstimate(
            flops=4 * positions * block * SET_CHANNELS,
            bytes_accessed=8 * positions * SET_CHANNELS,
            transcendentals=positions * block * SET_HEADS,
        ),
        name="own_attention",
    )(made, key)
    if inner == 2:
        (relayed,) = after([jnp.concatenate(relayed, axis=0)], sent[:1])
        out_weights = [w_out] + far + [relayed, swap(relayed, 1)]

    output = pl.pallas_call(
        functools.partial(output_kernel, n),
        out_shape=jax.ShapeDtypeStruct((block, channels), bf16),
        in_specs=[vmem] * (OUTER + 1 + len(out_weights)),
        out_specs=vmem,
        scratch_shapes=[
            pltpu.VMEM((channels, block), bf16),
            pltpu.VMEM((channels, block), f32),
        ],
        compiler_params=pltpu.CompilerParams(vmem_limit_bytes=12 * MEBI),
        cost_estimate=pl.CostEstimate(
            flops=2 * block * channels * channels,
            bytes_accessed=2 * channels * (channels + 3 * block),
            transcendentals=0,
        ),
        name="project",
    )(*received, kept, *out_weights)
    return output.reshape(rows_local, columns, channels)


def solution(mesh):
    return jax.shard_map(
        on_device,
        mesh=mesh,
        in_specs=(
            P(("batch", "patch"), None, None),
            P(None, None, "patch", None),
            P("patch"),
            P("patch", None),
            P("patch", None),
            P("patch", None),
            P("patch", None),
        ),
        out_specs=P(("batch", "patch"), None, None),
        check_vma=False,
    )
```

```python
import functools

import jax
import jax.numpy as jnp
from jax import lax
from jax.experimental import pallas as pl
from jax.experimental.pallas import tpu as pltpu
from jax.sharding import PartitionSpec as P

C = 1280
HEADS = 20
HEAD_DIM = 64
GROUPS = 32
SPAN = C // GROUPS
OUTER = 4
SET_HEADS = HEADS // OUTER
SET_CHANNELS = SET_HEADS * HEAD_DIM
QUAD = 4
HANDED = (0, 2, 1, 3)
FAR = ((1, 0), (3, 0), (2, 0), (0, 1))
SOONER = tuple(range(1, OUTER))
WIDE = 256
EPSILON = 1e-05
LATE = 6
CHUNK = 16
MEBI = 1024 * 1024

f32 = jnp.float32
bf16 = jnp.bfloat16

NT = (((1,), (1,)), ((), ()))
NN = (((1,), (0,)), ((), ()))


def dot(left, right, dims=NN):
    return lax.dot_general(left, right, dims, preferred_element_type=f32)


def exact(row, member, dims=NN):
    high = row.astype(bf16).astype(f32)
    middle = (row - high).astype(bf16).astype(f32)
    parts = [high, middle, row - high - middle, jnp.zeros((13, row.shape[1]), f32)]
    return jnp.sum(dot(jnp.concatenate(parts, axis=0).astype(bf16), member, dims), axis=0, keepdims=True)


def stats_kernel(*refs):
    pieces, out_ref = refs[:-1], refs[-1]
    block = pieces[0].shape[0]
    steps = block // CHUNK

    def add(step, total):
        for piece in pieces[:2]:
            total = total + folded(piece[pl.ds(step * CHUNK, CHUNK), :].astype(f32))
        return total

    zero = jnp.zeros((8, C), f32)
    pivot = jnp.sum(lax.fori_loop(0, steps, add, zero), axis=0, keepdims=True) / (2 * block)
    first, second = add_moments(pieces, pivot, zero, zero)
    out_ref[0:8, :] = jnp.broadcast_to(pivot, (8, C))
    out_ref[8:16, :] = first
    out_ref[16:24, :] = second


def folded(rows):
    return rows[:8] + rows[8:]


def add_moments(pieces, pivot, first, second):
    def add(step, sums):
        first, second = sums
        for piece in pieces:
            away = piece[pl.ds(step * CHUNK, CHUNK), :].astype(f32) - pivot
            first = first + folded(away)
            second = second + folded(away * away)
        return first, second

    return lax.fori_loop(0, pieces[0].shape[0] // CHUNK, add, (first, second))


def conv_kernel(columns, sources_ref, *refs):
    count = len(refs) - 6
    pieces = refs[:count]
    stats_ref, kernel_ref, bias_ref = refs[count : count + 3]
    out_ref, act_ref, kept_ref = refs[count + 3 :]
    block = pieces[0].shape[0]
    positions = block * count
    own = out_ref.shape[0]
    me = lax.axis_index("patch")
    steps = block // CHUNK
    starts = [
        pl.multiple_of(sources_ref[me * count + index] * (2 * block) + (index % 2) * block, block)
        for index in range(count)
    ]

    member = (
        lax.broadcasted_iota(jnp.int32, (C, 128), 0) // SPAN
        == lax.broadcasted_iota(jnp.int32, (C, 128), 1)
    ).astype(bf16)

    def group_mean(per_channel):
        return exact(exact(per_channel, member) / SPAN, member, NT)

    pivot = stats_ref[0:1, :]
    first, second = add_moments(pieces[-LATE:], pivot, stats_ref[8:16, :], stats_ref[16:24, :])
    above = jnp.sum(first, axis=0, keepdims=True) / positions
    within = jnp.sum(second, axis=0, keepdims=True) / positions - above * above
    mean = pivot + above
    centre = group_mean(mean)
    spread = group_mean(within + (mean - centre) * (mean - centre))
    half_scale = 0.5 * lax.rsqrt(spread + EPSILON)

    act_ref[0:columns, :] = jnp.zeros((columns, C), bf16)
    act_ref[positions + columns :, :] = jnp.zeros((columns, C), bf16)

    def activate(step, carry):
        for start, piece in zip(starts, pieces):
            half = (piece[pl.ds(step * CHUNK, CHUNK), :].astype(f32) - centre) * half_scale
            value = half + half * jnp.tanh(half)
            row = pl.multiple_of(columns + start + step * CHUNK, CHUNK)
            act_ref[pl.ds(row, CHUNK), :] = value.astype(bf16)
        return carry

    lax.fori_loop(0, steps, activate, 0)

    window = window_of(own)
    base = jnp.minimum(lax.div(me * own, 128) * 128, C - window)
    lanes = pl.ds(pl.multiple_of(base, 128), window)
    choose = (
        lax.broadcasted_iota(jnp.int32, (own, window), 0) + (me * own - base)
        == lax.broadcasted_iota(jnp.int32, (own, window), 1)
    ).astype(bf16)
    for index in range(0, count, 2):
        pair = jnp.concatenate([pieces[index][:, lanes], pieces[index + 1][:, lanes]], axis=0)
        start = pl.multiple_of(starts[index], 2 * block)
        kept_ref[:, pl.ds(start, 2 * block)] = dot(choose, pair, NT)

    convolve(columns, 0, act_ref, kept_ref, kernel_ref, bias_ref, out_ref)


def second_conv_kernel(columns, act_ref, kept_ref, kernel_ref, bias_ref, out_ref):
    convolve(columns, out_ref.shape[1], act_ref, kept_ref, kernel_ref, bias_ref, out_ref)


def convolve(columns, start, act_ref, kept_ref, kernel_ref, bias_ref, out_ref):
    own = out_ref.shape[0]
    column = lax.broadcasted_iota(jnp.int32, (own, WIDE), 1) % columns
    square = (own, own)
    bias = jnp.where(
        lax.broadcasted_iota(jnp.int32, square, 0) == lax.broadcasted_iota(jnp.int32, square, 1),
        bias_ref[...],
        0.0,
    )
    bias = jnp.sum(bias, axis=1, keepdims=True)
    for low in range(0, out_ref.shape[1], WIDE):
        at = start + low
        taps = dot(kernel_ref[0], act_ref[at : at + WIDE, :], NT)
        for shift in (1, 2):
            first = at + shift * columns
            taps = taps + dot(kernel_ref[shift], act_ref[first : first + WIDE, :], NT)
        before = jnp.where(column > 0, pltpu.roll(taps[0:own], 1, 1), 0.0)
        after_ = jnp.where(column < columns - 1, pltpu.roll(taps[2 * own :], WIDE - 1, 1), 0.0)
        convolved = taps[own : 2 * own] + before + after_
        hidden = kept_ref[:, at : at + WIDE] + convolved + bias
        out_ref[:, low : low + WIDE] = hidden.astype(bf16)


def window_of(own):
    return min(C, (own + 127) // 128 * 128 + 128)


def norm_pair(pair):
    own = pair[0].shape[0]
    entries = float(2 * pair[0].shape[1] * SPAN)

    def whole(values):
        return jnp.sum(jnp.sum(values, axis=0, keepdims=True), axis=1, keepdims=True)

    def group_at(low):
        first, last = low // 16 * 16, -(-(low + SPAN) // 16) * 16
        return [ref[first:last, :].astype(f32)[low - first : low - first + SPAN] for ref in pair]

    lows = range(0, own, SPAN)
    means = [sum(whole(half) for half in group_at(low)) / entries for low in lows]
    squares = [
        sum(whole(jnp.square(half - mean)) for half in group_at(low))
        for low, mean in zip(lows, means)
    ]
    scales = [lax.rsqrt(square / entries + EPSILON) for square in squares]
    mean = jnp.concatenate([jnp.broadcast_to(one, (SPAN, 1)) for one in means], axis=0)
    scale = jnp.concatenate([jnp.broadcast_to(one, (SPAN, 1)) for one in scales], axis=0)
    return [((ref[...].astype(f32) - mean) * scale).astype(bf16) for ref in pair]


def own_lanes(pair, me, n):
    block = 2 * pair[0].shape[1] // n
    start = pl.multiple_of(lax.rem(me, n // 2) * block, block)
    low, high = (ref[:, pl.ds(start, block)] for ref in pair)
    return jnp.where(me < n // 2, low, high)


def early_kernel(n, *refs):
    pieces, outs = refs[:-2], refs[-2:]
    me = lax.axis_index("patch")
    own, part = pieces[0].shape
    for at in range(0, len(pieces), 2):
        pair = pieces[at : at + 2]
        rows = slice(at // 2 * own, (at // 2 + 1) * own)
        for half, normed in enumerate(norm_pair(pair)):
            outs[0][rows, half * part : (half + 1) * part] = normed
        outs[1][rows, :] = own_lanes(pair, me, n)


def project_kernel(count, sources_ref, *refs):
    early_ref, some_ref = refs[:2]
    pieces = refs[2:LATE]
    weight_refs = refs[LATE:-3]
    sums_ref, kept_ref, normed_ref = refs[-3:]
    own, part = pieces[0].shape
    me = lax.axis_index("patch")
    for at in range(0, count - 2, 2):
        rows = pl.ds(pl.multiple_of(sources_ref[me * count + at] * own, own), own)
        if at < count - LATE:
            there = slice(at // 2 * own, (at // 2 + 1) * own)
            normed_ref[rows, :] = early_ref[there, :]
            kept_ref[rows, :] = some_ref[there, :]
            continue
        pair = pieces[at - count + LATE :][:2]
        for half, normed in enumerate(norm_pair(pair)):
            normed_ref[rows, half * part : (half + 1) * part] = normed
        kept_ref[rows, :] = own_lanes(pair, me, count // 2)
    missing = pl.multiple_of(sources_ref[me * count + count - 2] * own, own)
    normed_ref[pl.ds(missing, own), :] = jnp.zeros((own, 2 * part), bf16)
    weights = jnp.concatenate([ref[...] for ref in weight_refs], axis=0)
    for at in range(0, 2 * part, WIDE):
        sums_ref[:, at : at + WIDE] = dot(weights, normed_ref[:, at : at + WIDE])


def attention_kernel(count, inner, sources_ref, *refs):
    pair = refs[:2]
    weight_refs = refs[2:-9]
    sums_ref, some_ref = refs[-9:-7]
    outs = refs[-7:-4]
    kept_ref, made_ref, key_ref, last_ref = refs[-4:]
    own, part = pair[0].shape
    n = count // 2
    me = lax.axis_index("patch")
    outer_at, inner_at = lax.div(me, inner), lax.rem(me, inner)
    source = sources_ref[me * count + count - 2]
    row = pl.multiple_of(source * own, own)
    kept_ref[...] = some_ref[...]
    kept_ref[pl.ds(row, own), :] = own_lanes(pair, me, n)

    window = last_ref.shape[0]
    base = jnp.minimum(lax.div(source * own, 128) * 128, C - window)
    lanes = pl.ds(pl.multiple_of(base, 128), window)
    last_ref[...] = jnp.zeros_like(last_ref)
    within = pl.ds(pl.multiple_of(source * own - base, 16), own)
    for half, normed in enumerate(norm_pair(pair)):
        last_ref[within, half * part : (half + 1) * part] = normed
    weights = jnp.concatenate([ref[:, lanes] for ref in weight_refs], axis=0)
    places = rows_of(weight_refs, own, inner, inner_at)
    for at in range(0, 2 * part, WIDE):
        made = dot(weights, last_ref[:, at : at + WIDE]) + sums_ref[:, at : at + WIDE]
        made = made.astype(bf16)
        for low, size, target in places:
            made_ref[pl.ds(target, size), at : at + WIDE] = made[low : low + size]

    for at in range(0, 2 * part, WIDE):
        for head in range(SET_HEADS):
            low = SET_CHANNELS + head * HEAD_DIM
            key = made_ref[low : low + HEAD_DIM, at : at + WIDE].astype(f32)
            key_ref[head, at : at + WIDE, :] = key.T.astype(bf16)

    targets = [lax.rem(outer_at + step, OUTER) * inner + inner_at for step in SOONER]
    attend(targets, made_ref, key_ref, outs)


def rows_of(weight_refs, own, inner, inner_at):
    if inner != 2:
        return [(0, weight_refs[0].shape[0], 0)]
    places = []
    for kind in range(3):
        place = kind * SET_CHANNELS + inner_at * own
        places.append((kind * own, own, pl.multiple_of(place, own)))
    core = lax.rem(lax.axis_index("batch"), 2)
    size = own // 2
    for order in range(2):
        half = core if order == 0 else 1 - core
        for at in range(3):
            part = 3 * half + at
            place = lax.div(part, 2) * SET_CHANNELS + (1 - inner_at) * own + lax.rem(part, 2) * size
            places.append((3 * own + (3 * order + at) * size, size, pl.multiple_of(place, 16)))
    return places


def later_kernel(made_ref, key_ref, out_ref):
    attend([lax.axis_index("patch")], made_ref, key_ref, [out_ref])


def attend(targets, made_ref, key_ref, outs):
    block = outs[0].shape[1]
    starts = [pl.multiple_of(target * block, block) for target in targets]
    for head in range(SET_HEADS):
        low = head * HEAD_DIM
        query = [made_ref[low : low + HEAD_DIM, pl.ds(start, block)] for start in starts]
        query = jnp.concatenate(query, axis=1).astype(f32) * HEAD_DIM ** (-0.5)
        scores = dot(key_ref[head], query.astype(bf16))
        peak = jnp.max(scores, axis=0, keepdims=True)
        unnormalized = jnp.exp(scores - peak)
        total = jnp.sum(unnormalized, axis=0, keepdims=True)
        value = made_ref[2 * SET_CHANNELS + low : 2 * SET_CHANNELS + low + HEAD_DIM, :]
        mixture = dot(value, unnormalized.astype(bf16))
        attended = (mixture / total).astype(bf16)
        for place, out in enumerate(outs):
            out[low : low + HEAD_DIM, :] = attended[:, place * block : (place + 1) * block]


def output_kernel(n, *refs):
    attended_refs = refs[:OUTER]
    hidden_ref = refs[OUTER]
    weight_refs = refs[OUTER + 1 : -3]
    out_ref, attended_ref, total_ref = refs[-3:]
    inner = n // OUTER
    own = C // n
    me = lax.axis_index("patch")
    outer_at, inner_at = lax.div(me, inner), lax.rem(me, inner)
    for step in range(OUTER):
        origin = lax.rem(outer_at + OUTER - step, OUTER)
        row = pl.multiple_of(origin * SET_CHANNELS, SET_CHANNELS)
        attended_ref[pl.ds(row, SET_CHANNELS), :] = attended_refs[step][...]
    attended = attended_ref[...]
    if inner != 2:
        total = dot(weight_refs[0][...], attended) + hidden_ref[...].astype(f32)
        out_ref[...] = total.T.astype(bf16)
        return

    total_ref[...] = hidden_ref[...].astype(f32)
    mine = lax.rem(lax.axis_index("batch"), QUAD)
    core = lax.rem(mine, 2)

    def add(weights, outer_step, inner_step, low=0):
        origin = lax.rem(outer_at + OUTER - outer_step, OUTER) * inner
        origin = origin + lax.rem(inner_at + inner_step, inner)
        rows = pl.ds(pl.multiple_of(origin * own + low, 16), weights.shape[0])
        total_ref[rows, :] += dot(weights, attended)

    own_ref, far_ref, across_ref, other_ref, mine_ref, others_ref = weight_refs
    side = lax.div(mine, 2)
    add(own_ref[...], 0, 0)
    far = [far_ref[...], across_ref[...], other_ref[:own, :], other_ref[own:, :]]
    for step, weights in zip(HANDED, far):
        which = jnp.bitwise_xor(mine, step)
        outer_step = jnp.where(which == 0, 1, jnp.where(which == 1, 3, jnp.where(which == 2, 2, 0)))
        add(weights, outer_step, lax.div(which, QUAD - 1))

    def add_relayed(two_ref, one_ref):
        add(two_ref[:own, :], 1 + side, 1)
        add(two_ref[own:, :], 2 - side, 1)
        add(one_ref[:own, :], 3, 1)

    @pl.when(core == 0)
    def _():
        add_relayed(mine_ref, others_ref)

    @pl.when(core == 1)
    def _():
        add_relayed(others_ref, mine_ref)

    out_ref[...] = total_ref[...].T.astype(bf16)


def ring_of(n):
    inner = n // OUTER
    path = [(0, 0)]
    for outer_at in range(OUTER):
        across = range(1, inner) if outer_at % 2 == 0 else range(inner - 1, 0, -1)
        path += [(outer_at, inner_at) for inner_at in across]
    path += [(outer_at, 0) for outer_at in range(OUTER - 1, 0, -1)]
    return [outer_at * inner + inner_at for outer_at, inner_at in path]


def pieces_of(n):
    far = n // 2
    return [0] + [away for step in range(1, far) for away in (-step, step)] + [far]


def sources_of(n):
    ring = ring_of(n)
    table = []
    for device in range(n):
        at = ring.index(device)
        table.append([ring[(at + away) % n] for away in pieces_of(n) for _ in (0, 1)])
    return table


def gather(halves, n, beside):
    ring = ring_of(n)
    forward = [(ring[at], ring[(at + 1) % n]) for at in range(n)]
    backward = [(target, start) for start, target in forward]
    far = n // 2
    found = {(0, 0): halves[0], (1, 0): halves[1]}
    for step in range(1, far + 1):
        for half in (0, 1):
            for sign, pairs in ((-1, forward), (1, backward)):
                if step == far and (half == 0) != (sign == -1):
                    continue
                found[half, sign * step] = lax.ppermute(
                    found[half, sign * (step - 1)], "patch", pairs
                )
        others = beside(step, found)
        if others:
            (found[0, -step],) = after([found[0, -step]], others)
    found[0, far] = found[0, -far]
    return in_order(found, n)


def in_order(found, n):
    places = [(half, away) for away in pieces_of(n) for half in (0, 1)]
    return [found[place] for place in places if place in found]


def send(block, shifts):
    batch, n = lax.axis_size("batch"), lax.axis_size("patch")
    pairs = []
    for at in range(batch):
        shift = shifts[at % len(shifts)]
        for start, target in moves(n, *shift) if shift else ():
            pairs.append((at * n + start, at * n + target))
    return lax.ppermute(block, ("batch", "patch"), pairs)


def swap(block, bit):
    pairs = [(at, at ^ bit) for at in range(lax.axis_size("batch"))]
    return lax.ppermute(block, "batch", pairs)


def moves(n, outer_step, inner_step):
    inner = n // OUTER
    pairs = []
    for start in range(n):
        outer_at = (start // inner + outer_step) % OUTER
        inner_at = (start % inner + inner_step) % inner
        pairs.append((start, outer_at * inner + inner_at))
    return pairs


def after(values, ready):
    anywhere = pl.BlockSpec(memory_space=pl.ANY)
    made = pl.pallas_call(
        lambda *refs: None,
        out_shape=[jax.ShapeDtypeStruct(value.shape, value.dtype) for value in values],
        in_specs=[anywhere] * (len(values) + len(ready)),
        out_specs=[anywhere] * len(values),
        input_output_aliases={at: at for at in range(len(values))},
        compiler_params=pltpu.CompilerParams(vmem_limit_bytes=MEBI),
        cost_estimate=pl.CostEstimate(flops=0, bytes_accessed=0, transcendentals=0),
        name="after",
    )(*values, *ready)
    return list(made)


def on_device(latent, conv_weight, channel_bias, w_query, w_key, w_value, w_out):
    rows_local, columns, channels = latent.shape
    n = lax.axis_size("patch")
    inner = n // OUTER
    own = channels // n
    block = rows_local * columns
    positions = block * n
    sources = jnp.asarray(sources_of(n), jnp.int32).reshape(-1)
    vmem = pl.BlockSpec(memory_space=pltpu.VMEM)
    smem = pl.BlockSpec(memory_space=pltpu.SMEM)
    anywhere = pl.BlockSpec(memory_space=pl.ANY)

    whole = latent.reshape(block, channels)
    halves = whole[: block // 2], whole[block // 2 :]
    chosen = []
    if inner == 2:
        core = lax.rem(lax.axis_index("batch"), 2)
        stacked = jnp.concatenate([w_query, w_key, w_value], axis=0)
        chosen = [lax.dynamic_slice_in_dim(stacked, core * (3 * own // 2), 3 * own // 2, 0)]
    far_step = n // 2
    made_beside = []

    def beside_first(step, found):
        if step == 1:
            return chosen
        if step != far_step - 1:
            return []
        made_beside.append(
            pl.pallas_call(
                stats_kernel,
                out_shape=jax.ShapeDtypeStruct((24, channels), f32),
                in_specs=[vmem] * (2 * n - LATE),
                out_specs=vmem,
                compiler_params=pltpu.CompilerParams(vmem_limit_bytes=2 * MEBI),
                cost_estimate=pl.CostEstimate(
                    flops=6 * positions * channels,
                    bytes_accessed=2 * positions * channels,
                    transcendentals=0,
                ),
                name="stats",
            )(*in_order(found, n)[: 2 * n - LATE])
        )
        return made_beside[-1:]

    pieces = gather(halves, n, beside_first)
    stats = made_beside[0]
    if inner == 2:
        chosen, out_own = after(chosen + [w_out], pieces[-6:-2])
        chosen = send(chosen, [(0, 1)])
        far = send(out_own, FAR)
    else:
        sets = [list(range(at, at + inner)) for at in range(0, n, inner)]
        weights = jnp.stack([w_query, w_key, w_value])
        weights = lax.all_gather(weights, "patch", axis=1, tiled=True, axis_index_groups=sets)
        weights = [weights.reshape(3 * SET_CHANNELS, channels)]
        out_weights = [lax.all_gather(w_out, "patch", axis=0, tiled=True)]

    kernel = conv_weight.reshape(3, 3 * own, channels)
    bias = channel_bias.reshape(1, own)
    half_hidden = jax.ShapeDtypeStruct((own, positions // 2), bf16)
    flops = 9 * positions * channels * own
    first_hidden, act, residual = pl.pallas_call(
        functools.partial(conv_kernel, columns),
        out_shape=[
            half_hidden,
            jax.ShapeDtypeStruct((positions + 2 * columns, channels), bf16),
            jax.ShapeDtypeStruct((own, positions), f32),
        ],
        in_specs=[smem] + [vmem] * (2 * n + 3),
        out_specs=[vmem] * 3,
        compiler_params=pltpu.CompilerParams(vmem_limit_bytes=20 * MEBI),
        cost_estimate=pl.CostEstimate(
            flops=flops,
            bytes_accessed=2 * (positions * channels + 9 * channels * own),
            transcendentals=positions * channels,
        ),
        name="norm_conv",
    )(sources, *pieces, stats, kernel, bias)
    second_hidden = pl.pallas_call(
        functools.partial(second_conv_kernel, columns),
        out_shape=half_hidden,
        in_specs=[vmem] * 4,
        out_specs=vmem,
        compiler_params=pltpu.CompilerParams(vmem_limit_bytes=16 * MEBI),
        cost_estimate=pl.CostEstimate(flops=flops, bytes_accessed=flops // 1000, transcendentals=0),
        name="second_conv",
    )(act, residual, kernel, bias)

    def beside_second(step, found):
        if step != far_step - 1:
            return []
        count = n - LATE // 2
        made_beside.append(
            pl.pallas_call(
                functools.partial(early_kernel, n),
                out_shape=[
                    jax.ShapeDtypeStruct((count * own, positions), bf16),
                    jax.ShapeDtypeStruct((count * own, block), bf16),
                ],
                in_specs=[vmem] * (2 * count),
                out_specs=[vmem] * 2,
                compiler_params=pltpu.CompilerParams(vmem_limit_bytes=8 * MEBI),
                cost_estimate=pl.CostEstimate(
                    flops=8 * positions * channels,
                    bytes_accessed=4 * positions * channels,
                    transcendentals=0,
                ),
                name="early_norm",
            )(*in_order(found, n)[: 2 * count])
        )
        return made_beside[-1][:1]

    hidden_pieces = gather((first_hidden, second_hidden), n, beside_second)
    if inner == 2:
        chosen, far = after([chosen, far], hidden_pieces[6:10])
        near = [chosen]
        near.append(swap(near[0], 1))
        weights = [w_query, w_key, w_value] + near
        far = [far, swap(far, 2)]

    made_rows = sum(weight.shape[0] for weight in weights)
    sums, some = pl.pallas_call(
        functools.partial(project_kernel, 2 * n),
        out_shape=[
            jax.ShapeDtypeStruct((made_rows, positions), f32),
            jax.ShapeDtypeStruct((channels, block), bf16),
        ],
        in_specs=[smem] + [vmem] * (LATE + len(weights)),
        out_specs=[vmem] * 2,
        scratch_shapes=[pltpu.VMEM((channels, positions), bf16)],
        compiler_params=pltpu.CompilerParams(vmem_limit_bytes=20 * MEBI),
        cost_estimate=pl.CostEstimate(
            flops=2 * positions * channels * made_rows,
            bytes_accessed=2 * (positions * channels + made_rows * channels),
            transcendentals=0,
        ),
        name="norm_project",
    )(sources, *made_beside[-1], *hidden_pieces[-LATE:-2], *weights)
    if inner == 2:
        far = after(far, hidden_pieces[-6:-2])
        place = lax.rem(lax.axis_index("batch"), QUAD)
        relayed = [send(jnp.where(place == QUAD - 1, far[1], far[0]), [(0, 1)])]
        relayed.append(send(far[1], [(0, 1), None]))
        far.append(swap(jnp.concatenate(far, axis=0), 1))
    one_block = jax.ShapeDtypeStruct((SET_CHANNELS, block), bf16)
    *sent, kept, made, key = pl.pallas_call(
        functools.partial(attention_kernel, 2 * n, inner),
        out_shape=[one_block] * len(SOONER)
        + [
            jax.ShapeDtypeStruct((channels, block), bf16),
            jax.ShapeDtypeStruct((made_rows, positions), bf16),
            jax.ShapeDtypeStruct((SET_HEADS, positions, HEAD_DIM), bf16),
        ],
        in_specs=[smem] + [vmem] * (4 + len(weights)),
        out_specs=[vmem] * (3 + len(SOONER)),
        scratch_shapes=[pltpu.VMEM((window_of(own), positions), bf16)],
        compiler_params=pltpu.CompilerParams(vmem_limit_bytes=28 * MEBI),
        cost_estimate=pl.CostEstimate(
            flops=2 * positions * window_of(own) * made_rows
            + 12 * positions * block * SET_CHANNELS,
            bytes_accessed=6 * made_rows * positions,
            transcendentals=positions * 3 * block * SET_HEADS,
        ),
        name="attention",
    )(sources, *hidden_pieces[-2:], *weights, sums, some)
    received = [None]
    for step, sent_block in zip(SOONER, sent):
        pairs = [(at, (at + step * inner) % n) for at in range(n)]
        received.append(lax.ppermute(sent_block, "patch", pairs))
    received[0] = pl.pallas_call(
        later_kernel,
        out_shape=one_block,
        in_specs=[vmem] * 2,
        out_specs=vmem,
        compiler_params=pltpu.CompilerParams(vmem_limit_bytes=16 * MEBI),
        cost_estimate=pl.CostEstimate(
            flops=4 * positions * block * SET_CHANNELS,
            bytes_accessed=8 * positions * SET_CHANNELS,
            transcendentals=positions * block * SET_HEADS,
        ),
        name="own_attention",
    )(made, key)
    if inner == 2:
        (relayed,) = after([jnp.concatenate(relayed, axis=0)], sent[:1])
        out_weights = [w_out] + far + [relayed, swap(relayed, 1)]

    output = pl.pallas_call(
        functools.partial(output_kernel, n),
        out_shape=jax.ShapeDtypeStruct((block, channels), bf16),
        in_specs=[vmem] * (OUTER + 1 + len(out_weights)),
        out_specs=vmem,
        scratch_shapes=[
            pltpu.VMEM((channels, block), bf16),
            pltpu.VMEM((channels, block), f32),
        ],
        compiler_params=pltpu.CompilerParams(vmem_limit_bytes=12 * MEBI),
        cost_estimate=pl.CostEstimate(
            flops=2 * block * channels * channels,
            bytes_accessed=2 * channels * (channels + 3 * block),
            transcendentals=0,
        ),
        name="project",
    )(*received, kept, *out_weights)
    return output.reshape(rows_local, columns, channels)


def solution(mesh):
    return jax.shard_map(
        on_device,
        mesh=mesh,
        in_specs=(
            P(("batch", "patch"), None, None),
            P(None, None, "patch", None),
            P("patch"),
            P("patch", None),
            P("patch", None),
            P("patch", None),
            P("patch", None),
        ),
        out_specs=P(("batch", "patch"), None, None),
        check_vma=False,
    )
```

```python
import functools

import jax
import jax.numpy as jnp
from jax import lax
from jax.experimental import pallas as pl
from jax.experimental.pallas import tpu as pltpu
from jax.sharding import PartitionSpec as P

C = 1280
HEADS = 20
HEAD_DIM = 64
GROUPS = 32
SPAN = C // GROUPS
OUTER = 4
SET_HEADS = HEADS // OUTER
SET_CHANNELS = SET_HEADS * HEAD_DIM
QUAD = 4
HANDED = (0, 2, 1, 3)
FAR = ((1, 0), (3, 0), (2, 0), (0, 1))
SOONER = tuple(range(1, OUTER))
WIDE = 256
EPSILON = 1e-05
LATE = 6
CHUNK = 16
MEBI = 1024 * 1024

f32 = jnp.float32
bf16 = jnp.bfloat16

NT = (((1,), (1,)), ((), ()))
NN = (((1,), (0,)), ((), ()))


def dot(left, right, dims=NN):
    return lax.dot_general(left, right, dims, preferred_element_type=f32)


def exact(row, member, dims=NN):
    high = row.astype(bf16).astype(f32)
    middle = (row - high).astype(bf16).astype(f32)
    parts = [high, middle, row - high - middle, jnp.zeros((13, row.shape[1]), f32)]
    return jnp.sum(dot(jnp.concatenate(parts, axis=0).astype(bf16), member, dims), axis=0, keepdims=True)


def stats_kernel(*refs):
    pieces, out_ref = refs[:-1], refs[-1]
    block = pieces[0].shape[0]
    steps = block // CHUNK

    def add(step, total):
        for piece in pieces[:2]:
            total = total + folded(piece[pl.ds(step * CHUNK, CHUNK), :].astype(f32))
        return total

    zero = jnp.zeros((8, C), f32)
    pivot = jnp.sum(lax.fori_loop(0, steps, add, zero), axis=0, keepdims=True) / (2 * block)
    first, second = add_moments(pieces, pivot, zero, zero)
    out_ref[0:8, :] = jnp.broadcast_to(pivot, (8, C))
    out_ref[8:16, :] = first
    out_ref[16:24, :] = second


def folded(rows):
    return rows[:8] + rows[8:]


def add_moments(pieces, pivot, first, second):
    def add(step, sums):
        first, second = sums
        for piece in pieces:
            away = piece[pl.ds(step * CHUNK, CHUNK), :].astype(f32) - pivot
            first = first + folded(away)
            second = second + folded(away * away)
        return first, second

    return lax.fori_loop(0, pieces[0].shape[0] // CHUNK, add, (first, second))


def conv_kernel(columns, sources_ref, *refs):
    count = len(refs) - 6
    pieces = refs[:count]
    stats_ref, kernel_ref, bias_ref = refs[count : count + 3]
    out_ref, act_ref, kept_ref = refs[count + 3 :]
    block = pieces[0].shape[0]
    positions = block * count
    own = out_ref.shape[0]
    me = lax.axis_index("patch")
    steps = block // CHUNK
    starts = [
        pl.multiple_of(sources_ref[me * count + index] * (2 * block) + (index % 2) * block, block)
        for index in range(count)
    ]

    member = (
        lax.broadcasted_iota(jnp.int32, (C, 128), 0) // SPAN
        == lax.broadcasted_iota(jnp.int32, (C, 128), 1)
    ).astype(bf16)

    def group_mean(per_channel):
        return exact(exact(per_channel, member) / SPAN, member, NT)

    pivot = stats_ref[0:1, :]
    first, second = add_moments(pieces[-LATE:], pivot, stats_ref[8:16, :], stats_ref[16:24, :])
    above = jnp.sum(first, axis=0, keepdims=True) / positions
    within = jnp.sum(second, axis=0, keepdims=True) / positions - above * above
    mean = pivot + above
    centre = group_mean(mean)
    spread = group_mean(within + (mean - centre) * (mean - centre))
    half_scale = 0.5 * lax.rsqrt(spread + EPSILON)

    act_ref[0:columns, :] = jnp.zeros((columns, C), bf16)
    act_ref[positions + columns :, :] = jnp.zeros((columns, C), bf16)

    def activate(step, carry):
        for start, piece in zip(starts, pieces):
            half = (piece[pl.ds(step * CHUNK, CHUNK), :].astype(f32) - centre) * half_scale
            value = half + half * jnp.tanh(half)
            row = pl.multiple_of(columns + start + step * CHUNK, CHUNK)
            act_ref[pl.ds(row, CHUNK), :] = value.astype(bf16)
        return carry

    lax.fori_loop(0, steps, activate, 0)

    window = window_of(own)
    base = jnp.minimum(lax.div(me * own, 128) * 128, C - window)
    lanes = pl.ds(pl.multiple_of(base, 128), window)
    choose = (
        lax.broadcasted_iota(jnp.int32, (own, window), 0) + (me * own - base)
        == lax.broadcasted_iota(jnp.int32, (own, window), 1)
    ).astype(bf16)
    for index in range(0, count, 2):
        pair = jnp.concatenate([pieces[index][:, lanes], pieces[index + 1][:, lanes]], axis=0)
        start = pl.multiple_of(starts[index], 2 * block)
        kept_ref[:, pl.ds(start, 2 * block)] = dot(choose, pair, NT)

    convolve(columns, 0, act_ref, kept_ref, kernel_ref, bias_ref, out_ref)


def second_conv_kernel(columns, act_ref, kept_ref, kernel_ref, bias_ref, out_ref):
    convolve(columns, out_ref.shape[1], act_ref, kept_ref, kernel_ref, bias_ref, out_ref)


def convolve(columns, start, act_ref, kept_ref, kernel_ref, bias_ref, out_ref):
    own = out_ref.shape[0]
    column = lax.broadcasted_iota(jnp.int32, (own, WIDE), 1) % columns
    square = (own, own)
    bias = jnp.where(
        lax.broadcasted_iota(jnp.int32, square, 0) == lax.broadcasted_iota(jnp.int32, square, 1),
        bias_ref[...],
        0.0,
    )
    bias = jnp.sum(bias, axis=1, keepdims=True)
    for low in range(0, out_ref.shape[1], WIDE):
        at = start + low
        taps = dot(kernel_ref[0], act_ref[at : at + WIDE, :], NT)
        for shift in (1, 2):
            first = at + shift * columns
            taps = taps + dot(kernel_ref[shift], act_ref[first : first + WIDE, :], NT)
        before = jnp.where(column > 0, pltpu.roll(taps[0:own], 1, 1), 0.0)
        after_ = jnp.where(column < columns - 1, pltpu.roll(taps[2 * own :], WIDE - 1, 1), 0.0)
        convolved = taps[own : 2 * own] + before + after_
        hidden = kept_ref[:, at : at + WIDE] + convolved + bias
        out_ref[:, low : low + WIDE] = hidden.astype(bf16)


def window_of(own):
    return min(C, (own + 127) // 128 * 128 + 128)


def norm_pair(pair):
    own = pair[0].shape[0]
    entries = float(2 * pair[0].shape[1] * SPAN)

    def whole(values):
        return jnp.sum(jnp.sum(values, axis=0, keepdims=True), axis=1, keepdims=True)

    def group_at(low):
        first, last = low // 16 * 16, -(-(low + SPAN) // 16) * 16
        return [ref[first:last, :].astype(f32)[low - first : low - first + SPAN] for ref in pair]

    lows = range(0, own, SPAN)
    means = [sum(whole(half) for half in group_at(low)) / entries for low in lows]
    squares = [
        sum(whole(jnp.square(half - mean)) for half in group_at(low))
        for low, mean in zip(lows, means)
    ]
    scales = [lax.rsqrt(square / entries + EPSILON) for square in squares]
    mean = jnp.concatenate([jnp.broadcast_to(one, (SPAN, 1)) for one in means], axis=0)
    scale = jnp.concatenate([jnp.broadcast_to(one, (SPAN, 1)) for one in scales], axis=0)
    return [((ref[...].astype(f32) - mean) * scale).astype(bf16) for ref in pair]


def own_lanes(pair, me, n):
    block = 2 * pair[0].shape[1] // n
    start = pl.multiple_of(lax.rem(me, n // 2) * block, block)
    low, high = (ref[:, pl.ds(start, block)] for ref in pair)
    return jnp.where(me < n // 2, low, high)


def early_kernel(n, *refs):
    pieces, outs = refs[:-2], refs[-2:]
    me = lax.axis_index("patch")
    own, part = pieces[0].shape
    for at in range(0, len(pieces), 2):
        pair = pieces[at : at + 2]
        rows = slice(at // 2 * own, (at // 2 + 1) * own)
        for half, normed in enumerate(norm_pair(pair)):
            outs[0][rows, half * part : (half + 1) * part] = normed
        outs[1][rows, :] = own_lanes(pair, me, n)


def project_kernel(count, sources_ref, *refs):
    early_ref, some_ref = refs[:2]
    pieces = refs[2:LATE]
    weight_refs = refs[LATE:-3]
    sums_ref, kept_ref, normed_ref = refs[-3:]
    own, part = pieces[0].shape
    me = lax.axis_index("patch")
    for at in range(0, count - 2, 2):
        rows = pl.ds(pl.multiple_of(sources_ref[me * count + at] * own, own), own)
        if at < count - LATE:
            there = slice(at // 2 * own, (at // 2 + 1) * own)
            normed_ref[rows, :] = early_ref[there, :]
            kept_ref[rows, :] = some_ref[there, :]
            continue
        pair = pieces[at - count + LATE :][:2]
        for half, normed in enumerate(norm_pair(pair)):
            normed_ref[rows, half * part : (half + 1) * part] = normed
        kept_ref[rows, :] = own_lanes(pair, me, count // 2)
    missing = pl.multiple_of(sources_ref[me * count + count - 2] * own, own)
    normed_ref[pl.ds(missing, own), :] = jnp.zeros((own, 2 * part), bf16)
    weights = jnp.concatenate([ref[...] for ref in weight_refs], axis=0)
    for at in range(0, 2 * part, WIDE):
        sums_ref[:, at : at + WIDE] = dot(weights, normed_ref[:, at : at + WIDE])


def attention_kernel(count, inner, sources_ref, *refs):
    pair = refs[:2]
    weight_refs = refs[2:-9]
    sums_ref, some_ref = refs[-9:-7]
    outs = refs[-7:-4]
    kept_ref, made_ref, key_ref, last_ref = refs[-4:]
    own, part = pair[0].shape
    n = count // 2
    me = lax.axis_index("patch")
    outer_at, inner_at = lax.div(me, inner), lax.rem(me, inner)
    source = sources_ref[me * count + count - 2]
    row = pl.multiple_of(source * own, own)
    kept_ref[...] = some_ref[...]
    kept_ref[pl.ds(row, own), :] = own_lanes(pair, me, n)

    window = last_ref.shape[0]
    base = jnp.minimum(lax.div(source * own, 128) * 128, C - window)
    lanes = pl.ds(pl.multiple_of(base, 128), window)
    last_ref[...] = jnp.zeros_like(last_ref)
    within = pl.ds(pl.multiple_of(source * own - base, 16), own)
    for half, normed in enumerate(norm_pair(pair)):
        last_ref[within, half * part : (half + 1) * part] = normed
    weights = jnp.concatenate([ref[:, lanes] for ref in weight_refs], axis=0)
    places = rows_of(weight_refs, own, inner, inner_at)
    for at in range(0, 2 * part, WIDE):
        made = dot(weights, last_ref[:, at : at + WIDE]) + sums_ref[:, at : at + WIDE]
        made = made.astype(bf16)
        for low, size, target in places:
            made_ref[pl.ds(target, size), at : at + WIDE] = made[low : low + size]

    for at in range(0, 2 * part, WIDE):
        for head in range(SET_HEADS):
            low = SET_CHANNELS + head * HEAD_DIM
            key = made_ref[low : low + HEAD_DIM, at : at + WIDE].astype(f32)
            key_ref[head, at : at + WIDE, :] = key.T.astype(bf16)

    targets = [lax.rem(outer_at + step, OUTER) * inner + inner_at for step in SOONER]
    attend(targets, made_ref, key_ref, outs)


def rows_of(weight_refs, own, inner, inner_at):
    if inner != 2:
        return [(0, weight_refs[0].shape[0], 0)]
    places = []
    for kind in range(3):
        place = kind * SET_CHANNELS + inner_at * own
        places.append((kind * own, own, pl.multiple_of(place, own)))
    core = lax.rem(lax.axis_index("batch"), 2)
    size = own // 2
    for order in range(2):
        half = core if order == 0 else 1 - core
        for at in range(3):
            part = 3 * half + at
            place = lax.div(part, 2) * SET_CHANNELS + (1 - inner_at) * own + lax.rem(part, 2) * size
            places.append((3 * own + (3 * order + at) * size, size, pl.multiple_of(place, 16)))
    return places


def later_kernel(made_ref, key_ref, out_ref):
    attend([lax.axis_index("patch")], made_ref, key_ref, [out_ref])


def attend(targets, made_ref, key_ref, outs):
    block = outs[0].shape[1]
    starts = [pl.multiple_of(target * block, block) for target in targets]
    for head in range(SET_HEADS):
        low = head * HEAD_DIM
        query = [made_ref[low : low + HEAD_DIM, pl.ds(start, block)] for start in starts]
        query = jnp.concatenate(query, axis=1).astype(f32) * HEAD_DIM ** (-0.5)
        scores = dot(key_ref[head], query.astype(bf16))
        peak = jnp.max(scores, axis=0, keepdims=True)
        unnormalized = jnp.exp(scores - peak)
        total = jnp.sum(unnormalized, axis=0, keepdims=True)
        value = made_ref[2 * SET_CHANNELS + low : 2 * SET_CHANNELS + low + HEAD_DIM, :]
        mixture = dot(value, unnormalized.astype(bf16))
        attended = (mixture / total).astype(bf16)
        for place, out in enumerate(outs):
            out[low : low + HEAD_DIM, :] = attended[:, place * block : (place + 1) * block]


def output_kernel(n, *refs):
    attended_refs = refs[:OUTER]
    hidden_ref = refs[OUTER]
    weight_refs = refs[OUTER + 1 : -3]
    out_ref, attended_ref, total_ref = refs[-3:]
    inner = n // OUTER
    own = C // n
    me = lax.axis_index("patch")
    outer_at, inner_at = lax.div(me, inner), lax.rem(me, inner)
    for step in range(OUTER):
        origin = lax.rem(outer_at + OUTER - step, OUTER)
        row = pl.multiple_of(origin * SET_CHANNELS, SET_CHANNELS)
        attended_ref[pl.ds(row, SET_CHANNELS), :] = attended_refs[step][...]
    attended = attended_ref[...]
    if inner != 2:
        total = dot(weight_refs[0][...], attended) + hidden_ref[...].astype(f32)
        out_ref[...] = total.T.astype(bf16)
        return

    total_ref[...] = hidden_ref[...].astype(f32)
    mine = lax.rem(lax.axis_index("batch"), QUAD)
    core = lax.rem(mine, 2)

    def add(weights, outer_step, inner_step, low=0):
        origin = lax.rem(outer_at + OUTER - outer_step, OUTER) * inner
        origin = origin + lax.rem(inner_at + inner_step, inner)
        rows = pl.ds(pl.multiple_of(origin * own + low, 16), weights.shape[0])
        total_ref[rows, :] += dot(weights, attended)

    own_ref, far_ref, across_ref, other_ref, mine_ref, others_ref = weight_refs
    side = lax.div(mine, 2)
    add(own_ref[...], 0, 0)
    far = [far_ref[...], across_ref[...], other_ref[:own, :], other_ref[own:, :]]
    for step, weights in zip(HANDED, far):
        which = jnp.bitwise_xor(mine, step)
        outer_step = jnp.where(which == 0, 1, jnp.where(which == 1, 3, jnp.where(which == 2, 2, 0)))
        add(weights, outer_step, lax.div(which, QUAD - 1))

    def add_relayed(two_ref, one_ref):
        add(two_ref[:own, :], 1 + side, 1)
        add(two_ref[own:, :], 2 - side, 1)
        add(one_ref[:own, :], 3, 1)

    @pl.when(core == 0)
    def _():
        add_relayed(mine_ref, others_ref)

    @pl.when(core == 1)
    def _():
        add_relayed(others_ref, mine_ref)

    out_ref[...] = total_ref[...].T.astype(bf16)


def ring_of(n):
    inner = n // OUTER
    path = [(0, 0)]
    for outer_at in range(OUTER):
        across = range(1, inner) if outer_at % 2 == 0 else range(inner - 1, 0, -1)
        path += [(outer_at, inner_at) for inner_at in across]
    path += [(outer_at, 0) for outer_at in range(OUTER - 1, 0, -1)]
    return [outer_at * inner + inner_at for outer_at, inner_at in path]


def pieces_of(n):
    far = n // 2
    return [0] + [away for step in range(1, far) for away in (-step, step)] + [far]


def sources_of(n):
    ring = ring_of(n)
    table = []
    for device in range(n):
        at = ring.index(device)
        table.append([ring[(at + away) % n] for away in pieces_of(n) for _ in (0, 1)])
    return table


def gather(halves, n, beside):
    ring = ring_of(n)
    forward = [(ring[at], ring[(at + 1) % n]) for at in range(n)]
    backward = [(target, start) for start, target in forward]
    far = n // 2
    found = {(0, 0): halves[0], (1, 0): halves[1]}
    for step in range(1, far + 1):
        for half in (0, 1):
            for sign, pairs in ((-1, forward), (1, backward)):
                if step == far and (half == 0) != (sign == -1):
                    continue
                found[half, sign * step] = lax.ppermute(
                    found[half, sign * (step - 1)], "patch", pairs
                )
        others = beside(step, found)
        if others:
            (found[0, -step],) = after([found[0, -step]], others)
    found[0, far] = found[0, -far]
    return in_order(found, n)


def in_order(found, n):
    places = [(half, away) for away in pieces_of(n) for half in (0, 1)]
    return [found[place] for place in places if place in found]


def send(block, shifts):
    batch, n = lax.axis_size("batch"), lax.axis_size("patch")
    pairs = []
    for at in range(batch):
        shift = shifts[at % len(shifts)]
        for start, target in moves(n, *shift) if shift else ():
            pairs.append((at * n + start, at * n + target))
    return lax.ppermute(block, ("batch", "patch"), pairs)


def swap(block, bit):
    pairs = [(at, at ^ bit) for at in range(lax.axis_size("batch"))]
    return lax.ppermute(block, "batch", pairs)


def moves(n, outer_step, inner_step):
    inner = n // OUTER
    pairs = []
    for start in range(n):
        outer_at = (start // inner + outer_step) % OUTER
        inner_at = (start % inner + inner_step) % inner
        pairs.append((start, outer_at * inner + inner_at))
    return pairs


def after(values, ready):
    anywhere = pl.BlockSpec(memory_space=pl.ANY)
    made = pl.pallas_call(
        lambda *refs: None,
        out_shape=[jax.ShapeDtypeStruct(value.shape, value.dtype) for value in values],
        in_specs=[anywhere] * (len(values) + len(ready)),
        out_specs=[anywhere] * len(values),
        input_output_aliases={at: at for at in range(len(values))},
        compiler_params=pltpu.CompilerParams(vmem_limit_bytes=MEBI),
        cost_estimate=pl.CostEstimate(flops=0, bytes_accessed=0, transcendentals=0),
        name="after",
    )(*values, *ready)
    return list(made)


def on_device(latent, conv_weight, channel_bias, w_query, w_key, w_value, w_out):
    rows_local, columns, channels = latent.shape
    n = lax.axis_size("patch")
    inner = n // OUTER
    own = channels // n
    block = rows_local * columns
    positions = block * n
    sources = jnp.asarray(sources_of(n), jnp.int32).reshape(-1)
    vmem = pl.BlockSpec(memory_space=pltpu.VMEM)
    smem = pl.BlockSpec(memory_space=pltpu.SMEM)
    anywhere = pl.BlockSpec(memory_space=pl.ANY)

    whole = latent.reshape(block, channels)
    halves = whole[: block // 2], whole[block // 2 :]
    chosen = []
    if inner == 2:
        core = lax.rem(lax.axis_index("batch"), 2)
        stacked = jnp.concatenate([w_query, w_key, w_value], axis=0)
        chosen = [lax.dynamic_slice_in_dim(stacked, core * (3 * own // 2), 3 * own // 2, 0)]
    far_step = n // 2
    made_beside = []

    def beside_first(step, found):
        if step == 1:
            return chosen
        if step != far_step - 1:
            return []
        made_beside.append(
            pl.pallas_call(
                stats_kernel,
                out_shape=jax.ShapeDtypeStruct((24, channels), f32),
                in_specs=[vmem] * (2 * n - LATE),
                out_specs=vmem,
                compiler_params=pltpu.CompilerParams(vmem_limit_bytes=2 * MEBI),
                cost_estimate=pl.CostEstimate(
                    flops=6 * positions * channels,
                    bytes_accessed=2 * positions * channels,
                    transcendentals=0,
                ),
                name="stats",
            )(*in_order(found, n)[: 2 * n - LATE])
        )
        return made_beside[-1:]

    pieces = gather(halves, n, beside_first)
    stats = made_beside[0]
    if inner == 2:
        (chosen,) = after(chosen, pieces[6:10])
        (out_own,) = after([w_out], pieces[-6:-2])
        chosen = send(chosen, [(0, 1)])
        far = send(out_own, FAR)
    else:
        sets = [list(range(at, at + inner)) for at in range(0, n, inner)]
        weights = jnp.stack([w_query, w_key, w_value])
        weights = lax.all_gather(weights, "patch", axis=1, tiled=True, axis_index_groups=sets)
        weights = [weights.reshape(3 * SET_CHANNELS, channels)]
        out_weights = [lax.all_gather(w_out, "patch", axis=0, tiled=True)]

    kernel = conv_weight.reshape(3, 3 * own, channels)
    bias = channel_bias.reshape(1, own)
    half_hidden = jax.ShapeDtypeStruct((own, positions // 2), bf16)
    flops = 9 * positions * channels * own
    first_hidden, act, residual = pl.pallas_call(
        functools.partial(conv_kernel, columns),
        out_shape=[
            half_hidden,
            jax.ShapeDtypeStruct((positions + 2 * columns, channels), bf16),
            jax.ShapeDtypeStruct((own, positions), f32),
        ],
        in_specs=[smem] + [vmem] * (2 * n + 3),
        out_specs=[vmem] * 3,
        compiler_params=pltpu.CompilerParams(vmem_limit_bytes=20 * MEBI),
        cost_estimate=pl.CostEstimate(
            flops=flops,
            bytes_accessed=2 * (positions * channels + 9 * channels * own),
            transcendentals=positions * channels,
        ),
        name="norm_conv",
    )(sources, *pieces, stats, kernel, bias)
    second_hidden = pl.pallas_call(
        functools.partial(second_conv_kernel, columns),
        out_shape=half_hidden,
        in_specs=[vmem] * 4,
        out_specs=vmem,
        compiler_params=pltpu.CompilerParams(vmem_limit_bytes=16 * MEBI),
        cost_estimate=pl.CostEstimate(flops=flops, bytes_accessed=flops // 1000, transcendentals=0),
        name="second_conv",
    )(act, residual, kernel, bias)

    def beside_second(step, found):
        if step != far_step - 1:
            return []
        count = n - LATE // 2
        made_beside.append(
            pl.pallas_call(
                functools.partial(early_kernel, n),
                out_shape=[
                    jax.ShapeDtypeStruct((count * own, positions), bf16),
                    jax.ShapeDtypeStruct((count * own, block), bf16),
                ],
                in_specs=[vmem] * (2 * count),
                out_specs=[vmem] * 2,
                compiler_params=pltpu.CompilerParams(vmem_limit_bytes=8 * MEBI),
                cost_estimate=pl.CostEstimate(
                    flops=8 * positions * channels,
                    bytes_accessed=4 * positions * channels,
                    transcendentals=0,
                ),
                name="early_norm",
            )(*in_order(found, n)[: 2 * count])
        )
        return made_beside[-1][:1]

    hidden_pieces = gather((first_hidden, second_hidden), n, beside_second)
    if inner == 2:
        chosen, far = after([chosen, far], hidden_pieces[2:4])
        near = [chosen]
        near.append(swap(near[0], 1))
        weights = [w_query, w_key, w_value] + near
        far = [far, swap(far, 2)]

    made_rows = sum(weight.shape[0] for weight in weights)
    sums, some = pl.pallas_call(
        functools.partial(project_kernel, 2 * n),
        out_shape=[
            jax.ShapeDtypeStruct((made_rows, positions), f32),
            jax.ShapeDtypeStruct((channels, block), bf16),
        ],
        in_specs=[smem] + [vmem] * (LATE + len(weights)),
        out_specs=[vmem] * 2,
        scratch_shapes=[pltpu.VMEM((channels, positions), bf16)],
        compiler_params=pltpu.CompilerParams(vmem_limit_bytes=20 * MEBI),
        cost_estimate=pl.CostEstimate(
            flops=2 * positions * channels * made_rows,
            bytes_accessed=2 * (positions * channels + made_rows * channels),
            transcendentals=0,
        ),
        name="norm_project",
    )(sources, *made_beside[-1], *hidden_pieces[-LATE:-2], *weights)
    if inner == 2:
        far = after(far, hidden_pieces[-6:-2])
        place = lax.rem(lax.axis_index("batch"), QUAD)
        relayed = [send(jnp.where(place == QUAD - 1, far[1], far[0]), [(0, 1)])]
        relayed.append(send(far[1], [(0, 1), None]))
        far.append(swap(jnp.concatenate(far, axis=0), 1))
    one_block = jax.ShapeDtypeStruct((SET_CHANNELS, block), bf16)
    *sent, kept, made, key = pl.pallas_call(
        functools.partial(attention_kernel, 2 * n, inner),
        out_shape=[one_block] * len(SOONER)
        + [
            jax.ShapeDtypeStruct((channels, block), bf16),
            jax.ShapeDtypeStruct((made_rows, positions), bf16),
            jax.ShapeDtypeStruct((SET_HEADS, positions, HEAD_DIM), bf16),
        ],
        in_specs=[smem] + [vmem] * (4 + len(weights)),
        out_specs=[vmem] * (3 + len(SOONER)),
        scratch_shapes=[pltpu.VMEM((window_of(own), positions), bf16)],
        compiler_params=pltpu.CompilerParams(vmem_limit_bytes=28 * MEBI),
        cost_estimate=pl.CostEstimate(
            flops=2 * positions * window_of(own) * made_rows
            + 12 * positions * block * SET_CHANNELS,
            bytes_accessed=6 * made_rows * positions,
            transcendentals=positions * 3 * block * SET_HEADS,
        ),
        name="attention",
    )(sources, *hidden_pieces[-2:], *weights, sums, some)
    received = [None]
    for step, sent_block in zip(SOONER, sent):
        pairs = [(at, (at + step * inner) % n) for at in range(n)]
        received.append(lax.ppermute(sent_block, "patch", pairs))
    received[0] = pl.pallas_call(
        later_kernel,
        out_shape=one_block,
        in_specs=[vmem] * 2,
        out_specs=vmem,
        compiler_params=pltpu.CompilerParams(vmem_limit_bytes=16 * MEBI),
        cost_estimate=pl.CostEstimate(
            flops=4 * positions * block * SET_CHANNELS,
            bytes_accessed=8 * positions * SET_CHANNELS,
            transcendentals=positions * block * SET_HEADS,
        ),
        name="own_attention",
    )(made, key)
    if inner == 2:
        (relayed,) = after([jnp.concatenate(relayed, axis=0)], sent[:1])
        out_weights = [w_out] + far + [relayed, swap(relayed, 1)]

    output = pl.pallas_call(
        functools.partial(output_kernel, n),
        out_shape=jax.ShapeDtypeStruct((block, channels), bf16),
        in_specs=[vmem] * (OUTER + 1 + len(out_weights)),
        out_specs=vmem,
        scratch_shapes=[
            pltpu.VMEM((channels, block), bf16),
            pltpu.VMEM((channels, block), f32),
        ],
        compiler_params=pltpu.CompilerParams(vmem_limit_bytes=12 * MEBI),
        cost_estimate=pl.CostEstimate(
            flops=2 * block * channels * channels,
            bytes_accessed=2 * channels * (channels + 3 * block),
            transcendentals=0,
        ),
        name="project",
    )(*received, kept, *out_weights)
    return output.reshape(rows_local, columns, channels)


def solution(mesh):
    return jax.shard_map(
        on_device,
        mesh=mesh,
        in_specs=(
            P(("batch", "patch"), None, None),
            P(None, None, "patch", None),
            P("patch"),
            P("patch", None),
            P("patch", None),
            P("patch", None),
            P("patch", None),
        ),
        out_specs=P(("batch", "patch"), None, None),
        check_vma=False,
    )
```

```python
import functools

import jax
import jax.numpy as jnp
from jax import lax
from jax.experimental import pallas as pl
from jax.experimental.pallas import tpu as pltpu
from jax.sharding import PartitionSpec as P

C = 1280
HEADS = 20
HEAD_DIM = 64
GROUPS = 32
SPAN = C // GROUPS
OUTER = 4
SET_HEADS = HEADS // OUTER
SET_CHANNELS = SET_HEADS * HEAD_DIM
QUAD = 4
HANDED = (0, 2, 1, 3)
FAR = ((1, 0), (3, 0), (2, 0), (0, 1))
SOONER = tuple(range(1, OUTER))
WIDE = 256
EPSILON = 1e-05
LATE = 6
CHUNK = 16
MEBI = 1024 * 1024

f32 = jnp.float32
bf16 = jnp.bfloat16

NT = (((1,), (1,)), ((), ()))
NN = (((1,), (0,)), ((), ()))


def dot(left, right, dims=NN):
    return lax.dot_general(left, right, dims, preferred_element_type=f32)


def exact(row, member, dims=NN):
    high = row.astype(bf16).astype(f32)
    middle = (row - high).astype(bf16).astype(f32)
    parts = [high, middle, row - high - middle, jnp.zeros((13, row.shape[1]), f32)]
    return jnp.sum(dot(jnp.concatenate(parts, axis=0).astype(bf16), member, dims), axis=0, keepdims=True)


def stats_kernel(*refs):
    pieces, out_ref = refs[:-1], refs[-1]
    block = pieces[0].shape[0]
    steps = block // CHUNK

    def add(step, total):
        for piece in pieces[:2]:
            total = total + folded(piece[pl.ds(step * CHUNK, CHUNK), :].astype(f32))
        return total

    zero = jnp.zeros((8, C), f32)
    pivot = jnp.sum(lax.fori_loop(0, steps, add, zero), axis=0, keepdims=True) / (2 * block)
    first, second = add_moments(pieces, pivot, zero, zero)
    out_ref[0:8, :] = jnp.broadcast_to(pivot, (8, C))
    out_ref[8:16, :] = first
    out_ref[16:24, :] = second


def folded(rows):
    return rows[:8] + rows[8:]


def add_moments(pieces, pivot, first, second):
    def add(step, sums):
        first, second = sums
        for piece in pieces:
            away = piece[pl.ds(step * CHUNK, CHUNK), :].astype(f32) - pivot
            first = first + folded(away)
            second = second + folded(away * away)
        return first, second

    return lax.fori_loop(0, pieces[0].shape[0] // CHUNK, add, (first, second))


def conv_kernel(columns, sources_ref, *refs):
    count = len(refs) - 6
    pieces = refs[:count]
    stats_ref, kernel_ref, bias_ref = refs[count : count + 3]
    out_ref, act_ref, kept_ref = refs[count + 3 :]
    block = pieces[0].shape[0]
    positions = block * count
    own = out_ref.shape[0]
    me = lax.axis_index("patch")
    steps = block // CHUNK
    starts = [
        pl.multiple_of(sources_ref[me * count + index] * (2 * block) + (index % 2) * block, block)
        for index in range(count)
    ]

    member = (
        lax.broadcasted_iota(jnp.int32, (C, 128), 0) // SPAN
        == lax.broadcasted_iota(jnp.int32, (C, 128), 1)
    ).astype(bf16)

    def group_mean(per_channel):
        return exact(exact(per_channel, member) / SPAN, member, NT)

    pivot = stats_ref[0:1, :]
    first, second = add_moments(pieces[-LATE:], pivot, stats_ref[8:16, :], stats_ref[16:24, :])
    above = jnp.sum(first, axis=0, keepdims=True) / positions
    within = jnp.sum(second, axis=0, keepdims=True) / positions - above * above
    mean = pivot + above
    centre = group_mean(mean)
    spread = group_mean(within + (mean - centre) * (mean - centre))
    half_scale = 0.5 * lax.rsqrt(spread + EPSILON)

    act_ref[0:columns, :] = jnp.zeros((columns, C), bf16)
    act_ref[positions + columns :, :] = jnp.zeros((columns, C), bf16)

    def activate(step, carry):
        for start, piece in zip(starts, pieces):
            half = (piece[pl.ds(step * CHUNK, CHUNK), :].astype(f32) - centre) * half_scale
            value = half + half * jnp.tanh(half)
            row = pl.multiple_of(columns + start + step * CHUNK, CHUNK)
            act_ref[pl.ds(row, CHUNK), :] = value.astype(bf16)
        return carry

    lax.fori_loop(0, steps, activate, 0)

    window = window_of(own)
    base = jnp.minimum(lax.div(me * own, 128) * 128, C - window)
    lanes = pl.ds(pl.multiple_of(base, 128), window)
    choose = (
        lax.broadcasted_iota(jnp.int32, (own, window), 0) + (me * own - base)
        == lax.broadcasted_iota(jnp.int32, (own, window), 1)
    ).astype(bf16)
    for index in range(0, count, 2):
        pair = jnp.concatenate([pieces[index][:, lanes], pieces[index + 1][:, lanes]], axis=0)
        start = pl.multiple_of(starts[index], 2 * block)
        kept_ref[:, pl.ds(start, 2 * block)] = dot(choose, pair, NT)

    convolve(columns, 0, act_ref, kept_ref, kernel_ref, bias_ref, out_ref)


def second_conv_kernel(columns, act_ref, kept_ref, kernel_ref, bias_ref, out_ref):
    convolve(columns, out_ref.shape[1], act_ref, kept_ref, kernel_ref, bias_ref, out_ref)


def convolve(columns, start, act_ref, kept_ref, kernel_ref, bias_ref, out_ref):
    own = out_ref.shape[0]
    column = lax.broadcasted_iota(jnp.int32, (own, WIDE), 1) % columns
    square = (own, own)
    bias = jnp.where(
        lax.broadcasted_iota(jnp.int32, square, 0) == lax.broadcasted_iota(jnp.int32, square, 1),
        bias_ref[...],
        0.0,
    )
    bias = jnp.sum(bias, axis=1, keepdims=True)
    for low in range(0, out_ref.shape[1], WIDE):
        at = start + low
        taps = dot(kernel_ref[0], act_ref[at : at + WIDE, :], NT)
        for shift in (1, 2):
            first = at + shift * columns
            taps = taps + dot(kernel_ref[shift], act_ref[first : first + WIDE, :], NT)
        before = jnp.where(column > 0, pltpu.roll(taps[0:own], 1, 1), 0.0)
        after_ = jnp.where(column < columns - 1, pltpu.roll(taps[2 * own :], WIDE - 1, 1), 0.0)
        convolved = taps[own : 2 * own] + before + after_
        hidden = kept_ref[:, at : at + WIDE] + convolved + bias
        out_ref[:, low : low + WIDE] = hidden.astype(bf16)


def window_of(own):
    return min(C, (own + 127) // 128 * 128 + 128)


def norm_pair(pair):
    own = pair[0].shape[0]
    entries = float(2 * pair[0].shape[1] * SPAN)

    def whole(values):
        return jnp.sum(jnp.sum(values, axis=0, keepdims=True), axis=1, keepdims=True)

    def group_at(low):
        first, last = low // 16 * 16, -(-(low + SPAN) // 16) * 16
        return [ref[first:last, :].astype(f32)[low - first : low - first + SPAN] for ref in pair]

    lows = range(0, own, SPAN)
    means = [sum(whole(half) for half in group_at(low)) / entries for low in lows]
    squares = [
        sum(whole(jnp.square(half - mean)) for half in group_at(low))
        for low, mean in zip(lows, means)
    ]
    scales = [lax.rsqrt(square / entries + EPSILON) for square in squares]
    mean = jnp.concatenate([jnp.broadcast_to(one, (SPAN, 1)) for one in means], axis=0)
    scale = jnp.concatenate([jnp.broadcast_to(one, (SPAN, 1)) for one in scales], axis=0)
    return [((ref[...].astype(f32) - mean) * scale).astype(bf16) for ref in pair]


def own_lanes(pair, me, n):
    block = 2 * pair[0].shape[1] // n
    start = pl.multiple_of(lax.rem(me, n // 2) * block, block)
    low, high = (ref[:, pl.ds(start, block)] for ref in pair)
    return jnp.where(me < n // 2, low, high)


def early_kernel(n, *refs):
    pieces, outs = refs[:-2], refs[-2:]
    me = lax.axis_index("patch")
    own, part = pieces[0].shape
    for at in range(0, len(pieces), 2):
        pair = pieces[at : at + 2]
        rows = slice(at // 2 * own, (at // 2 + 1) * own)
        for half, normed in enumerate(norm_pair(pair)):
            outs[0][rows, half * part : (half + 1) * part] = normed
        outs[1][rows, :] = own_lanes(pair, me, n)


def project_kernel(count, sources_ref, *refs):
    early_ref, some_ref = refs[:2]
    pieces = refs[2:LATE]
    weight_refs = refs[LATE:-3]
    sums_ref, kept_ref, normed_ref = refs[-3:]
    own, part = pieces[0].shape
    me = lax.axis_index("patch")
    for at in range(0, count - 2, 2):
        rows = pl.ds(pl.multiple_of(sources_ref[me * count + at] * own, own), own)
        if at < count - LATE:
            there = slice(at // 2 * own, (at // 2 + 1) * own)
            normed_ref[rows, :] = early_ref[there, :]
            kept_ref[rows, :] = some_ref[there, :]
            continue
        pair = pieces[at - count + LATE :][:2]
        for half, normed in enumerate(norm_pair(pair)):
            normed_ref[rows, half * part : (half + 1) * part] = normed
        kept_ref[rows, :] = own_lanes(pair, me, count // 2)
    missing = pl.multiple_of(sources_ref[me * count + count - 2] * own, own)
    normed_ref[pl.ds(missing, own), :] = jnp.zeros((own, 2 * part), bf16)
    weights = jnp.concatenate([ref[...] for ref in weight_refs], axis=0)
    for at in range(0, 2 * part, WIDE):
        sums_ref[:, at : at + WIDE] = dot(weights, normed_ref[:, at : at + WIDE])


def attention_kernel(count, inner, sources_ref, *refs):
    pair = refs[:2]
    weight_refs = refs[2:-9]
    sums_ref, some_ref = refs[-9:-7]
    outs = refs[-7:-4]
    kept_ref, made_ref, key_ref, last_ref = refs[-4:]
    own, part = pair[0].shape
    n = count // 2
    me = lax.axis_index("patch")
    outer_at, inner_at = lax.div(me, inner), lax.rem(me, inner)
    source = sources_ref[me * count + count - 2]
    row = pl.multiple_of(source * own, own)
    kept_ref[...] = some_ref[...]
    kept_ref[pl.ds(row, own), :] = own_lanes(pair, me, n)

    window = last_ref.shape[0]
    base = jnp.minimum(lax.div(source * own, 128) * 128, C - window)
    lanes = pl.ds(pl.multiple_of(base, 128), window)
    last_ref[...] = jnp.zeros_like(last_ref)
    within = pl.ds(pl.multiple_of(source * own - base, 16), own)
    for half, normed in enumerate(norm_pair(pair)):
        last_ref[within, half * part : (half + 1) * part] = normed
    weights = jnp.concatenate([ref[:, lanes] for ref in weight_refs], axis=0)
    places = rows_of(weight_refs, own, inner, inner_at)
    for at in range(0, 2 * part, WIDE):
        made = dot(weights, last_ref[:, at : at + WIDE]) + sums_ref[:, at : at + WIDE]
        made = made.astype(bf16)
        for low, size, target in places:
            made_ref[pl.ds(target, size), at : at + WIDE] = made[low : low + size]

    for at in range(0, 2 * part, WIDE):
        for head in range(SET_HEADS):
            low = SET_CHANNELS + head * HEAD_DIM
            key = made_ref[low : low + HEAD_DIM, at : at + WIDE].astype(f32)
            key_ref[head, at : at + WIDE, :] = key.T.astype(bf16)

    targets = [lax.rem(outer_at + step, OUTER) * inner + inner_at for step in SOONER]
    attend(targets, made_ref, key_ref, outs)


def rows_of(weight_refs, own, inner, inner_at):
    if inner != 2:
        return [(0, weight_refs[0].shape[0], 0)]
    places = []
    for kind in range(3):
        place = kind * SET_CHANNELS + inner_at * own
        places.append((kind * own, own, pl.multiple_of(place, own)))
    core = lax.rem(lax.axis_index("batch"), 2)
    size = own // 2
    for order in range(2):
        half = core if order == 0 else 1 - core
        for at in range(3):
            part = 3 * half + at
            place = lax.div(part, 2) * SET_CHANNELS + (1 - inner_at) * own + lax.rem(part, 2) * size
            places.append((3 * own + (3 * order + at) * size, size, pl.multiple_of(place, 16)))
    return places


def later_kernel(made_ref, key_ref, out_ref):
    attend([lax.axis_index("patch")], made_ref, key_ref, [out_ref])


def attend(targets, made_ref, key_ref, outs):
    block = outs[0].shape[1]
    starts = [pl.multiple_of(target * block, block) for target in targets]
    for head in range(SET_HEADS):
        low = head * HEAD_DIM
        query = [made_ref[low : low + HEAD_DIM, pl.ds(start, block)] for start in starts]
        query = jnp.concatenate(query, axis=1).astype(f32) * HEAD_DIM ** (-0.5)
        scores = dot(key_ref[head], query.astype(bf16))
        peak = jnp.max(scores, axis=0, keepdims=True)
        unnormalized = jnp.exp(scores - peak)
        total = jnp.sum(unnormalized, axis=0, keepdims=True)
        value = made_ref[2 * SET_CHANNELS + low : 2 * SET_CHANNELS + low + HEAD_DIM, :]
        mixture = dot(value, unnormalized.astype(bf16))
        attended = (mixture / total).astype(bf16)
        for place, out in enumerate(outs):
            out[low : low + HEAD_DIM, :] = attended[:, place * block : (place + 1) * block]


def output_kernel(n, *refs):
    attended_refs = refs[:OUTER]
    hidden_ref = refs[OUTER]
    weight_refs = refs[OUTER + 1 : -3]
    out_ref, attended_ref, total_ref = refs[-3:]
    inner = n // OUTER
    own = C // n
    me = lax.axis_index("patch")
    outer_at, inner_at = lax.div(me, inner), lax.rem(me, inner)
    for step in range(OUTER):
        origin = lax.rem(outer_at + OUTER - step, OUTER)
        row = pl.multiple_of(origin * SET_CHANNELS, SET_CHANNELS)
        attended_ref[pl.ds(row, SET_CHANNELS), :] = attended_refs[step][...]
    attended = attended_ref[...]
    if inner != 2:
        total = dot(weight_refs[0][...], attended) + hidden_ref[...].astype(f32)
        out_ref[...] = total.T.astype(bf16)
        return

    total_ref[...] = hidden_ref[...].astype(f32)
    mine = lax.rem(lax.axis_index("batch"), QUAD)
    core = lax.rem(mine, 2)

    def add(weights, outer_step, inner_step, low=0):
        origin = lax.rem(outer_at + OUTER - outer_step, OUTER) * inner
        origin = origin + lax.rem(inner_at + inner_step, inner)
        rows = pl.ds(pl.multiple_of(origin * own + low, 16), weights.shape[0])
        total_ref[rows, :] += dot(weights, attended)

    own_ref, far_ref, across_ref, other_ref, mine_ref, others_ref = weight_refs
    side = lax.div(mine, 2)
    add(own_ref[...], 0, 0)
    far = [far_ref[...], across_ref[...], other_ref[:own, :], other_ref[own:, :]]
    for step, weights in zip(HANDED, far):
        which = jnp.bitwise_xor(mine, step)
        outer_step = jnp.where(which == 0, 1, jnp.where(which == 1, 3, jnp.where(which == 2, 2, 0)))
        add(weights, outer_step, lax.div(which, QUAD - 1))

    def add_relayed(two_ref, one_ref):
        add(two_ref[:own, :], 1 + side, 1)
        add(two_ref[own:, :], 2 - side, 1)
        add(one_ref[:own, :], 3, 1)

    @pl.when(core == 0)
    def _():
        add_relayed(mine_ref, others_ref)

    @pl.when(core == 1)
    def _():
        add_relayed(others_ref, mine_ref)

    out_ref[...] = total_ref[...].T.astype(bf16)


def ring_of(n):
    inner = n // OUTER
    path = [(0, 0)]
    for outer_at in range(OUTER):
        across = range(1, inner) if outer_at % 2 == 0 else range(inner - 1, 0, -1)
        path += [(outer_at, inner_at) for inner_at in across]
    path += [(outer_at, 0) for outer_at in range(OUTER - 1, 0, -1)]
    return [outer_at * inner + inner_at for outer_at, inner_at in path]


def pieces_of(n):
    far = n // 2
    return [0] + [away for step in range(1, far) for away in (-step, step)] + [far]


def sources_of(n):
    ring = ring_of(n)
    table = []
    for device in range(n):
        at = ring.index(device)
        table.append([ring[(at + away) % n] for away in pieces_of(n) for _ in (0, 1)])
    return table


def gather(halves, n, beside):
    ring = ring_of(n)
    forward = [(ring[at], ring[(at + 1) % n]) for at in range(n)]
    backward = [(target, start) for start, target in forward]
    far = n // 2
    found = {(0, 0): halves[0], (1, 0): halves[1]}
    for step in range(1, far + 1):
        for half in (0, 1):
            for sign, pairs in ((-1, forward), (1, backward)):
                if step == far and (half == 0) != (sign == -1):
                    continue
                found[half, sign * step] = lax.ppermute(
                    found[half, sign * (step - 1)], "patch", pairs
                )
        others = beside(step, found)
        if others:
            (found[0, -step],) = after([found[0, -step]], others)
    found[0, far] = found[0, -far]
    return in_order(found, n)


def in_order(found, n):
    places = [(half, away) for away in pieces_of(n) for half in (0, 1)]
    return [found[place] for place in places if place in found]


def send(block, shifts):
    batch, n = lax.axis_size("batch"), lax.axis_size("patch")
    pairs = []
    for at in range(batch):
        shift = shifts[at % len(shifts)]
        for start, target in moves(n, *shift) if shift else ():
            pairs.append((at * n + start, at * n + target))
    return lax.ppermute(block, ("batch", "patch"), pairs)


def swap(block, bit):
    pairs = [(at, at ^ bit) for at in range(lax.axis_size("batch"))]
    return lax.ppermute(block, "batch", pairs)


def moves(n, outer_step, inner_step):
    inner = n // OUTER
    pairs = []
    for start in range(n):
        outer_at = (start // inner + outer_step) % OUTER
        inner_at = (start % inner + inner_step) % inner
        pairs.append((start, outer_at * inner + inner_at))
    return pairs


def after(values, ready):
    anywhere = pl.BlockSpec(memory_space=pl.ANY)
    made = pl.pallas_call(
        lambda *refs: None,
        out_shape=[jax.ShapeDtypeStruct(value.shape, value.dtype) for value in values],
        in_specs=[anywhere] * (len(values) + len(ready)),
        out_specs=[anywhere] * len(values),
        input_output_aliases={at: at for at in range(len(values))},
        compiler_params=pltpu.CompilerParams(vmem_limit_bytes=MEBI),
        cost_estimate=pl.CostEstimate(flops=0, bytes_accessed=0, transcendentals=0),
        name="after",
    )(*values, *ready)
    return list(made)


def on_device(latent, conv_weight, channel_bias, w_query, w_key, w_value, w_out):
    rows_local, columns, channels = latent.shape
    n = lax.axis_size("patch")
    inner = n // OUTER
    own = channels // n
    block = rows_local * columns
    positions = block * n
    sources = jnp.asarray(sources_of(n), jnp.int32).reshape(-1)
    vmem = pl.BlockSpec(memory_space=pltpu.VMEM)
    smem = pl.BlockSpec(memory_space=pltpu.SMEM)
    anywhere = pl.BlockSpec(memory_space=pl.ANY)

    whole = latent.reshape(block, channels)
    halves = whole[: block // 2], whole[block // 2 :]
    chosen = []
    if inner == 2:
        core = lax.rem(lax.axis_index("batch"), 2)
        stacked = jnp.concatenate([w_query, w_key, w_value], axis=0)
        chosen = [lax.dynamic_slice_in_dim(stacked, core * (3 * own // 2), 3 * own // 2, 0)]
    far_step = n // 2
    made_beside = []

    def beside_first(step, found):
        if step == 1:
            return chosen
        if step != far_step - 1:
            return []
        made_beside.append(
            pl.pallas_call(
                stats_kernel,
                out_shape=jax.ShapeDtypeStruct((24, channels), f32),
                in_specs=[vmem] * (2 * n - LATE),
                out_specs=vmem,
                compiler_params=pltpu.CompilerParams(vmem_limit_bytes=2 * MEBI),
                cost_estimate=pl.CostEstimate(
                    flops=6 * positions * channels,
                    bytes_accessed=2 * positions * channels,
                    transcendentals=0,
                ),
                name="stats",
            )(*in_order(found, n)[: 2 * n - LATE])
        )
        return made_beside[-1:]

    pieces = gather(halves, n, beside_first)
    stats = made_beside[0]
    if inner == 2:
        (chosen,) = after(chosen, pieces[6:10])
        (out_own,) = after([w_out], pieces[-6:-2])
        chosen = send(chosen, [(0, 1)])
        far = send(out_own, FAR)
    else:
        sets = [list(range(at, at + inner)) for at in range(0, n, inner)]
        weights = jnp.stack([w_query, w_key, w_value])
        weights = lax.all_gather(weights, "patch", axis=1, tiled=True, axis_index_groups=sets)
        weights = [weights.reshape(3 * SET_CHANNELS, channels)]
        out_weights = [lax.all_gather(w_out, "patch", axis=0, tiled=True)]

    kernel = conv_weight.reshape(3, 3 * own, channels)
    bias = channel_bias.reshape(1, own)
    half_hidden = jax.ShapeDtypeStruct((own, positions // 2), bf16)
    flops = 9 * positions * channels * own
    first_hidden, act, residual = pl.pallas_call(
        functools.partial(conv_kernel, columns),
        out_shape=[
            half_hidden,
            jax.ShapeDtypeStruct((positions + 2 * columns, channels), bf16),
            jax.ShapeDtypeStruct((own, positions), f32),
        ],
        in_specs=[smem] + [vmem] * (2 * n + 3),
        out_specs=[vmem] * 3,
        compiler_params=pltpu.CompilerParams(vmem_limit_bytes=20 * MEBI),
        cost_estimate=pl.CostEstimate(
            flops=flops,
            bytes_accessed=2 * (positions * channels + 9 * channels * own),
            transcendentals=positions * channels,
        ),
        name="norm_conv",
    )(sources, *pieces, stats, kernel, bias)
    second_hidden = pl.pallas_call(
        functools.partial(second_conv_kernel, columns),
        out_shape=half_hidden,
        in_specs=[vmem] * 4,
        out_specs=vmem,
        compiler_params=pltpu.CompilerParams(vmem_limit_bytes=16 * MEBI),
        cost_estimate=pl.CostEstimate(flops=flops, bytes_accessed=flops // 1000, transcendentals=0),
        name="second_conv",
    )(act, residual, kernel, bias)

    def beside_second(step, found):
        if step != far_step - 1:
            return []
        count = n - LATE // 2
        made_beside.append(
            pl.pallas_call(
                functools.partial(early_kernel, n),
                out_shape=[
                    jax.ShapeDtypeStruct((count * own, positions), bf16),
                    jax.ShapeDtypeStruct((count * own, block), bf16),
                ],
                in_specs=[vmem] * (2 * count),
                out_specs=[vmem] * 2,
                compiler_params=pltpu.CompilerParams(vmem_limit_bytes=8 * MEBI),
                cost_estimate=pl.CostEstimate(
                    flops=8 * positions * channels,
                    bytes_accessed=4 * positions * channels,
                    transcendentals=0,
                ),
                name="early_norm",
            )(*in_order(found, n)[: 2 * count])
        )
        return made_beside[-1][:1]

    hidden_pieces = gather((first_hidden, second_hidden), n, beside_second)
    if inner == 2:
        chosen, far = after([chosen, far], [second_hidden])
        near = [chosen]
        near.append(swap(near[0], 1))
        weights = [w_query, w_key, w_value] + near
        far = [far, swap(far, 2)]

    made_rows = sum(weight.shape[0] for weight in weights)
    sums, some = pl.pallas_call(
        functools.partial(project_kernel, 2 * n),
        out_shape=[
            jax.ShapeDtypeStruct((made_rows, positions), f32),
            jax.ShapeDtypeStruct((channels, block), bf16),
        ],
        in_specs=[smem] + [vmem] * (LATE + len(weights)),
        out_specs=[vmem] * 2,
        scratch_shapes=[pltpu.VMEM((channels, positions), bf16)],
        compiler_params=pltpu.CompilerParams(vmem_limit_bytes=20 * MEBI),
        cost_estimate=pl.CostEstimate(
            flops=2 * positions * channels * made_rows,
            bytes_accessed=2 * (positions * channels + made_rows * channels),
            transcendentals=0,
        ),
        name="norm_project",
    )(sources, *made_beside[-1], *hidden_pieces[-LATE:-2], *weights)
    if inner == 2:
        far = after(far, hidden_pieces[-6:-2])
        place = lax.rem(lax.axis_index("batch"), QUAD)
        relayed = [send(jnp.where(place == QUAD - 1, far[1], far[0]), [(0, 1)])]
        relayed.append(send(far[1], [(0, 1), None]))
        far.append(swap(jnp.concatenate(far, axis=0), 1))
    one_block = jax.ShapeDtypeStruct((SET_CHANNELS, block), bf16)
    *sent, kept, made, key = pl.pallas_call(
        functools.partial(attention_kernel, 2 * n, inner),
        out_shape=[one_block] * len(SOONER)
        + [
            jax.ShapeDtypeStruct((channels, block), bf16),
            jax.ShapeDtypeStruct((made_rows, positions), bf16),
            jax.ShapeDtypeStruct((SET_HEADS, positions, HEAD_DIM), bf16),
        ],
        in_specs=[smem] + [vmem] * (4 + len(weights)),
        out_specs=[vmem] * (3 + len(SOONER)),
        scratch_shapes=[pltpu.VMEM((window_of(own), positions), bf16)],
        compiler_params=pltpu.CompilerParams(vmem_limit_bytes=28 * MEBI),
        cost_estimate=pl.CostEstimate(
            flops=2 * positions * window_of(own) * made_rows
            + 12 * positions * block * SET_CHANNELS,
            bytes_accessed=6 * made_rows * positions,
            transcendentals=positions * 3 * block * SET_HEADS,
        ),
        name="attention",
    )(sources, *hidden_pieces[-2:], *weights, sums, some)
    received = [None]
    for step, sent_block in zip(SOONER, sent):
        pairs = [(at, (at + step * inner) % n) for at in range(n)]
        received.append(lax.ppermute(sent_block, "patch", pairs))
    received[0] = pl.pallas_call(
        later_kernel,
        out_shape=one_block,
        in_specs=[vmem] * 2,
        out_specs=vmem,
        compiler_params=pltpu.CompilerParams(vmem_limit_bytes=16 * MEBI),
        cost_estimate=pl.CostEstimate(
            flops=4 * positions * block * SET_CHANNELS,
            bytes_accessed=8 * positions * SET_CHANNELS,
            transcendentals=positions * block * SET_HEADS,
        ),
        name="own_attention",
    )(made, key)
    if inner == 2:
        (relayed,) = after([jnp.concatenate(relayed, axis=0)], sent[:1])
        out_weights = [w_out] + far + [relayed, swap(relayed, 1)]

    output = pl.pallas_call(
        functools.partial(output_kernel, n),
        out_shape=jax.ShapeDtypeStruct((block, channels), bf16),
        in_specs=[vmem] * (OUTER + 1 + len(out_weights)),
        out_specs=vmem,
        scratch_shapes=[
            pltpu.VMEM((channels, block), bf16),
            pltpu.VMEM((channels, block), f32),
        ],
        compiler_params=pltpu.CompilerParams(vmem_limit_bytes=12 * MEBI),
        cost_estimate=pl.CostEstimate(
            flops=2 * block * channels * channels,
            bytes_accessed=2 * channels * (channels + 3 * block),
            transcendentals=0,
        ),
        name="project",
    )(*received, kept, *out_weights)
    return output.reshape(rows_local, columns, channels)


def solution(mesh):
    return jax.shard_map(
        on_device,
        mesh=mesh,
        in_specs=(
            P(("batch", "patch"), None, None),
            P(None, None, "patch", None),
            P("patch"),
            P("patch", None),
            P("patch", None),
            P("patch", None),
            P("patch", None),
        ),
        out_specs=P(("batch", "patch"), None, None),
        check_vma=False,
    )
```

```python
import functools

import jax
import jax.numpy as jnp
from jax import lax
from jax.experimental import pallas as pl
from jax.experimental.pallas import tpu as pltpu
from jax.sharding import PartitionSpec as P

C = 1280
HEADS = 20
HEAD_DIM = 64
GROUPS = 32
SPAN = C // GROUPS
OUTER = 4
SET_HEADS = HEADS // OUTER
SET_CHANNELS = SET_HEADS * HEAD_DIM
QUAD = 4
HANDED = (0, 2, 1, 3)
FAR = ((1, 0), (3, 0), (2, 0), (0, 1))
SOONER = tuple(range(1, OUTER))
WIDE = 256
EPSILON = 1e-05
LATE = 6
CHUNK = 16
MEBI = 1024 * 1024

f32 = jnp.float32
bf16 = jnp.bfloat16

NT = (((1,), (1,)), ((), ()))
NN = (((1,), (0,)), ((), ()))


def dot(left, right, dims=NN):
    return lax.dot_general(left, right, dims, preferred_element_type=f32)


def exact(row, member, dims=NN):
    high = row.astype(bf16).astype(f32)
    middle = (row - high).astype(bf16).astype(f32)
    parts = [high, middle, row - high - middle, jnp.zeros((13, row.shape[1]), f32)]
    return jnp.sum(dot(jnp.concatenate(parts, axis=0).astype(bf16), member, dims), axis=0, keepdims=True)


def stats_kernel(*refs):
    pieces, out_ref = refs[:-1], refs[-1]
    block = pieces[0].shape[0]
    steps = block // CHUNK

    def add(step, total):
        for piece in pieces[:2]:
            total = total + folded(piece[pl.ds(step * CHUNK, CHUNK), :].astype(f32))
        return total

    zero = jnp.zeros((8, C), f32)
    pivot = jnp.sum(lax.fori_loop(0, steps, add, zero), axis=0, keepdims=True) / (2 * block)
    first, second = add_moments(pieces, pivot, zero, zero)
    out_ref[0:8, :] = jnp.broadcast_to(pivot, (8, C))
    out_ref[8:16, :] = first
    out_ref[16:24, :] = second


def folded(rows):
    return rows[:8] + rows[8:]


def add_moments(pieces, pivot, first, second):
    def add(step, sums):
        first, second = sums
        for piece in pieces:
            away = piece[pl.ds(step * CHUNK, CHUNK), :].astype(f32) - pivot
            first = first + folded(away)
            second = second + folded(away * away)
        return first, second

    return lax.fori_loop(0, pieces[0].shape[0] // CHUNK, add, (first, second))


def conv_kernel(columns, sources_ref, *refs):
    count = len(refs) - 6
    pieces = refs[:count]
    stats_ref, kernel_ref, bias_ref = refs[count : count + 3]
    out_ref, act_ref, kept_ref = refs[count + 3 :]
    block = pieces[0].shape[0]
    positions = block * count
    own = out_ref.shape[0]
    me = lax.axis_index("patch")
    steps = block // CHUNK
    starts = [
        pl.multiple_of(sources_ref[me * count + index] * (2 * block) + (index % 2) * block, block)
        for index in range(count)
    ]

    member = (
        lax.broadcasted_iota(jnp.int32, (C, 128), 0) // SPAN
        == lax.broadcasted_iota(jnp.int32, (C, 128), 1)
    ).astype(bf16)

    def group_mean(per_channel):
        return exact(exact(per_channel, member) / SPAN, member, NT)

    pivot = stats_ref[0:1, :]
    first, second = add_moments(pieces[-LATE:], pivot, stats_ref[8:16, :], stats_ref[16:24, :])
    above = jnp.sum(first, axis=0, keepdims=True) / positions
    within = jnp.sum(second, axis=0, keepdims=True) / positions - above * above
    mean = pivot + above
    centre = group_mean(mean)
    spread = group_mean(within + (mean - centre) * (mean - centre))
    half_scale = 0.5 * lax.rsqrt(spread + EPSILON)

    act_ref[0:columns, :] = jnp.zeros((columns, C), bf16)
    act_ref[positions + columns :, :] = jnp.zeros((columns, C), bf16)

    def activate(step, carry):
        for start, piece in zip(starts, pieces):
            half = (piece[pl.ds(step * CHUNK, CHUNK), :].astype(f32) - centre) * half_scale
            value = half + half * jnp.tanh(half)
            row = pl.multiple_of(columns + start + step * CHUNK, CHUNK)
            act_ref[pl.ds(row, CHUNK), :] = value.astype(bf16)
        return carry

    lax.fori_loop(0, steps, activate, 0)

    window = window_of(own)
    base = jnp.minimum(lax.div(me * own, 128) * 128, C - window)
    lanes = pl.ds(pl.multiple_of(base, 128), window)
    choose = (
        lax.broadcasted_iota(jnp.int32, (own, window), 0) + (me * own - base)
        == lax.broadcasted_iota(jnp.int32, (own, window), 1)
    ).astype(bf16)
    for index in range(0, count, 2):
        pair = jnp.concatenate([pieces[index][:, lanes], pieces[index + 1][:, lanes]], axis=0)
        start = pl.multiple_of(starts[index], 2 * block)
        kept_ref[:, pl.ds(start, 2 * block)] = dot(choose, pair, NT)

    convolve(columns, 0, act_ref, kept_ref, kernel_ref, bias_ref, out_ref)


def second_conv_kernel(columns, act_ref, kept_ref, kernel_ref, bias_ref, out_ref):
    convolve(columns, out_ref.shape[1], act_ref, kept_ref, kernel_ref, bias_ref, out_ref)


def convolve(columns, start, act_ref, kept_ref, kernel_ref, bias_ref, out_ref):
    own = out_ref.shape[0]
    column = lax.broadcasted_iota(jnp.int32, (own, WIDE), 1) % columns
    square = (own, own)
    bias = jnp.where(
        lax.broadcasted_iota(jnp.int32, square, 0) == lax.broadcasted_iota(jnp.int32, square, 1),
        bias_ref[...],
        0.0,
    )
    bias = jnp.sum(bias, axis=1, keepdims=True)
    for low in range(0, out_ref.shape[1], WIDE):
        at = start + low
        taps = dot(kernel_ref[0], act_ref[at : at + WIDE, :], NT)
        for shift in (1, 2):
            first = at + shift * columns
            taps = taps + dot(kernel_ref[shift], act_ref[first : first + WIDE, :], NT)
        before = jnp.where(column > 0, pltpu.roll(taps[0:own], 1, 1), 0.0)
        after_ = jnp.where(column < columns - 1, pltpu.roll(taps[2 * own :], WIDE - 1, 1), 0.0)
        convolved = taps[own : 2 * own] + before + after_
        hidden = kept_ref[:, at : at + WIDE] + convolved + bias
        out_ref[:, low : low + WIDE] = hidden.astype(bf16)


def window_of(own):
    return min(C, (own + 127) // 128 * 128 + 128)


def norm_pair(pair):
    own = pair[0].shape[0]
    entries = float(2 * pair[0].shape[1] * SPAN)

    def whole(values):
        return jnp.sum(jnp.sum(values, axis=0, keepdims=True), axis=1, keepdims=True)

    def group_at(low):
        first, last = low // 16 * 16, -(-(low + SPAN) // 16) * 16
        return [ref[first:last, :].astype(f32)[low - first : low - first + SPAN] for ref in pair]

    lows = range(0, own, SPAN)
    means = [sum(whole(half) for half in group_at(low)) / entries for low in lows]
    squares = [
        sum(whole(jnp.square(half - mean)) for half in group_at(low))
        for low, mean in zip(lows, means)
    ]
    scales = [lax.rsqrt(square / entries + EPSILON) for square in squares]
    mean = jnp.concatenate([jnp.broadcast_to(one, (SPAN, 1)) for one in means], axis=0)
    scale = jnp.concatenate([jnp.broadcast_to(one, (SPAN, 1)) for one in scales], axis=0)
    return [((ref[...].astype(f32) - mean) * scale).astype(bf16) for ref in pair]


def own_lanes(pair, me, n):
    block = 2 * pair[0].shape[1] // n
    start = pl.multiple_of(lax.rem(me, n // 2) * block, block)
    low, high = (ref[:, pl.ds(start, block)] for ref in pair)
    return jnp.where(me < n // 2, low, high)


def early_kernel(n, *refs):
    pieces, outs = refs[:-2], refs[-2:]
    me = lax.axis_index("patch")
    own, part = pieces[0].shape
    for at in range(0, len(pieces), 2):
        pair = pieces[at : at + 2]
        rows = slice(at // 2 * own, (at // 2 + 1) * own)
        for half, normed in enumerate(norm_pair(pair)):
            outs[0][rows, half * part : (half + 1) * part] = normed
        outs[1][rows, :] = own_lanes(pair, me, n)


def project_kernel(count, sources_ref, *refs):
    early_ref, some_ref = refs[:2]
    pieces = refs[2:LATE]
    weight_refs = refs[LATE:-3]
    sums_ref, kept_ref, normed_ref = refs[-3:]
    own, part = pieces[0].shape
    me = lax.axis_index("patch")
    for at in range(0, count - 2, 2):
        rows = pl.ds(pl.multiple_of(sources_ref[me * count + at] * own, own), own)
        if at < count - LATE:
            there = slice(at // 2 * own, (at // 2 + 1) * own)
            normed_ref[rows, :] = early_ref[there, :]
            kept_ref[rows, :] = some_ref[there, :]
            continue
        pair = pieces[at - count + LATE :][:2]
        for half, normed in enumerate(norm_pair(pair)):
            normed_ref[rows, half * part : (half + 1) * part] = normed
        kept_ref[rows, :] = own_lanes(pair, me, count // 2)
    missing = pl.multiple_of(sources_ref[me * count + count - 2] * own, own)
    normed_ref[pl.ds(missing, own), :] = jnp.zeros((own, 2 * part), bf16)
    weights = jnp.concatenate([ref[...] for ref in weight_refs], axis=0)
    for at in range(0, 2 * part, WIDE):
        sums_ref[:, at : at + WIDE] = dot(weights, normed_ref[:, at : at + WIDE])


def attention_kernel(count, inner, sources_ref, *refs):
    pair = refs[:2]
    weight_refs = refs[2:-9]
    sums_ref, some_ref = refs[-9:-7]
    outs = refs[-7:-4]
    kept_ref, made_ref, key_ref, last_ref = refs[-4:]
    own, part = pair[0].shape
    n = count // 2
    me = lax.axis_index("patch")
    outer_at, inner_at = lax.div(me, inner), lax.rem(me, inner)
    source = sources_ref[me * count + count - 2]
    row = pl.multiple_of(source * own, own)
    kept_ref[...] = some_ref[...]
    kept_ref[pl.ds(row, own), :] = own_lanes(pair, me, n)

    window = last_ref.shape[0]
    base = jnp.minimum(lax.div(source * own, 128) * 128, C - window)
    lanes = pl.ds(pl.multiple_of(base, 128), window)
    last_ref[...] = jnp.zeros_like(last_ref)
    within = pl.ds(pl.multiple_of(source * own - base, 16), own)
    for half, normed in enumerate(norm_pair(pair)):
        last_ref[within, half * part : (half + 1) * part] = normed
    weights = jnp.concatenate([ref[:, lanes] for ref in weight_refs], axis=0)
    places = rows_of(weight_refs, own, inner, inner_at)
    for at in range(0, 2 * part, WIDE):
        made = dot(weights, last_ref[:, at : at + WIDE]) + sums_ref[:, at : at + WIDE]
        made = made.astype(bf16)
        for low, size, target in places:
            made_ref[pl.ds(target, size), at : at + WIDE] = made[low : low + size]

    for at in range(0, 2 * part, WIDE):
        for head in range(SET_HEADS):
            low = SET_CHANNELS + head * HEAD_DIM
            key = made_ref[low : low + HEAD_DIM, at : at + WIDE].astype(f32)
            key_ref[head, at : at + WIDE, :] = key.T.astype(bf16)

    targets = [lax.rem(outer_at + step, OUTER) * inner + inner_at for step in SOONER]
    attend(targets, made_ref, key_ref, outs)


def rows_of(weight_refs, own, inner, inner_at):
    if inner != 2:
        return [(0, weight_refs[0].shape[0], 0)]
    places = []
    for kind in range(3):
        place = kind * SET_CHANNELS + inner_at * own
        places.append((kind * own, own, pl.multiple_of(place, own)))
    core = lax.rem(lax.axis_index("batch"), 2)
    size = own // 2
    for order in range(2):
        half = core if order == 0 else 1 - core
        for at in range(3):
            part = 3 * half + at
            place = lax.div(part, 2) * SET_CHANNELS + (1 - inner_at) * own + lax.rem(part, 2) * size
            places.append((3 * own + (3 * order + at) * size, size, pl.multiple_of(place, 16)))
    return places


def later_kernel(made_ref, key_ref, out_ref):
    attend([lax.axis_index("patch")], made_ref, key_ref, [out_ref])


def attend(targets, made_ref, key_ref, outs):
    block = outs[0].shape[1]
    starts = [pl.multiple_of(target * block, block) for target in targets]
    for head in range(SET_HEADS):
        low = head * HEAD_DIM
        query = [made_ref[low : low + HEAD_DIM, pl.ds(start, block)] for start in starts]
        query = jnp.concatenate(query, axis=1).astype(f32) * HEAD_DIM ** (-0.5)
        scores = dot(key_ref[head], query.astype(bf16))
        peak = jnp.max(scores, axis=0, keepdims=True)
        unnormalized = jnp.exp(scores - peak)
        total = jnp.sum(unnormalized, axis=0, keepdims=True)
        value = made_ref[2 * SET_CHANNELS + low : 2 * SET_CHANNELS + low + HEAD_DIM, :]
        mixture = dot(value, unnormalized.astype(bf16))
        attended = (mixture / total).astype(bf16)
        for place, out in enumerate(outs):
            out[low : low + HEAD_DIM, :] = attended[:, place * block : (place + 1) * block]


def output_kernel(n, *refs):
    attended_refs = refs[:OUTER]
    hidden_ref = refs[OUTER]
    weight_refs = refs[OUTER + 1 : -3]
    out_ref, attended_ref, total_ref = refs[-3:]
    inner = n // OUTER
    own = C // n
    me = lax.axis_index("patch")
    outer_at, inner_at = lax.div(me, inner), lax.rem(me, inner)
    for step in range(OUTER):
        origin = lax.rem(outer_at + OUTER - step, OUTER)
        row = pl.multiple_of(origin * SET_CHANNELS, SET_CHANNELS)
        attended_ref[pl.ds(row, SET_CHANNELS), :] = attended_refs[step][...]
    attended = attended_ref[...]
    if inner != 2:
        total = dot(weight_refs[0][...], attended) + hidden_ref[...].astype(f32)
        out_ref[...] = total.T.astype(bf16)
        return

    total_ref[...] = hidden_ref[...].astype(f32)
    mine = lax.rem(lax.axis_index("batch"), QUAD)
    core = lax.rem(mine, 2)

    def add(weights, outer_step, inner_step, low=0):
        origin = lax.rem(outer_at + OUTER - outer_step, OUTER) * inner
        origin = origin + lax.rem(inner_at + inner_step, inner)
        rows = pl.ds(pl.multiple_of(origin * own + low, 16), weights.shape[0])
        total_ref[rows, :] += dot(weights, attended)

    own_ref, far_ref, across_ref, other_ref, mine_ref, others_ref = weight_refs
    side = lax.div(mine, 2)
    add(own_ref[...], 0, 0)
    far = [far_ref[...], across_ref[...], other_ref[:own, :], other_ref[own:, :]]
    for step, weights in zip(HANDED, far):
        which = jnp.bitwise_xor(mine, step)
        outer_step = jnp.where(which == 0, 1, jnp.where(which == 1, 3, jnp.where(which == 2, 2, 0)))
        add(weights, outer_step, lax.div(which, QUAD - 1))

    def add_relayed(two_ref, one_ref):
        add(two_ref[:own, :], 1 + side, 1)
        add(two_ref[own:, :], 2 - side, 1)
        add(one_ref[:own, :], 3, 1)

    @pl.when(core == 0)
    def _():
        add_relayed(mine_ref, others_ref)

    @pl.when(core == 1)
    def _():
        add_relayed(others_ref, mine_ref)

    out_ref[...] = total_ref[...].T.astype(bf16)


def ring_of(n):
    inner = n // OUTER
    path = [(0, 0)]
    for outer_at in range(OUTER):
        across = range(1, inner) if outer_at % 2 == 0 else range(inner - 1, 0, -1)
        path += [(outer_at, inner_at) for inner_at in across]
    path += [(outer_at, 0) for outer_at in range(OUTER - 1, 0, -1)]
    return [outer_at * inner + inner_at for outer_at, inner_at in path]


def pieces_of(n):
    far = n // 2
    return [0] + [away for step in range(1, far) for away in (-step, step)] + [far]


def sources_of(n):
    ring = ring_of(n)
    table = []
    for device in range(n):
        at = ring.index(device)
        table.append([ring[(at + away) % n] for away in pieces_of(n) for _ in (0, 1)])
    return table


def gather(halves, n, beside):
    ring = ring_of(n)
    forward = [(ring[at], ring[(at + 1) % n]) for at in range(n)]
    backward = [(target, start) for start, target in forward]
    far = n // 2
    found = {(0, 0): halves[0], (1, 0): halves[1]}
    for step in range(1, far + 1):
        for half in (0, 1):
            for sign, pairs in ((-1, forward), (1, backward)):
                if step == far and (half == 0) != (sign == -1):
                    continue
                found[half, sign * step] = lax.ppermute(
                    found[half, sign * (step - 1)], "patch", pairs
                )
        others = beside(step, found)
        if others:
            (found[0, -step],) = after([found[0, -step]], others)
    found[0, far] = found[0, -far]
    return in_order(found, n)


def in_order(found, n):
    places = [(half, away) for away in pieces_of(n) for half in (0, 1)]
    return [found[place] for place in places if place in found]


def send(block, shifts):
    batch, n = lax.axis_size("batch"), lax.axis_size("patch")
    pairs = []
    for at in range(batch):
        shift = shifts[at % len(shifts)]
        for start, target in moves(n, *shift) if shift else ():
            pairs.append((at * n + start, at * n + target))
    return lax.ppermute(block, ("batch", "patch"), pairs)


def swap(block, bit):
    pairs = [(at, at ^ bit) for at in range(lax.axis_size("batch"))]
    return lax.ppermute(block, "batch", pairs)


def moves(n, outer_step, inner_step):
    inner = n // OUTER
    pairs = []
    for start in range(n):
        outer_at = (start // inner + outer_step) % OUTER
        inner_at = (start % inner + inner_step) % inner
        pairs.append((start, outer_at * inner + inner_at))
    return pairs


def after(values, ready):
    anywhere = pl.BlockSpec(memory_space=pl.ANY)
    made = pl.pallas_call(
        lambda *refs: None,
        out_shape=[jax.ShapeDtypeStruct(value.shape, value.dtype) for value in values],
        in_specs=[anywhere] * (len(values) + len(ready)),
        out_specs=[anywhere] * len(values),
        input_output_aliases={at: at for at in range(len(values))},
        compiler_params=pltpu.CompilerParams(vmem_limit_bytes=MEBI),
        cost_estimate=pl.CostEstimate(flops=0, bytes_accessed=0, transcendentals=0),
        name="after",
    )(*values, *ready)
    return list(made)


def on_device(latent, conv_weight, channel_bias, w_query, w_key, w_value, w_out):
    rows_local, columns, channels = latent.shape
    n = lax.axis_size("patch")
    inner = n // OUTER
    own = channels // n
    block = rows_local * columns
    positions = block * n
    sources = jnp.asarray(sources_of(n), jnp.int32).reshape(-1)
    vmem = pl.BlockSpec(memory_space=pltpu.VMEM)
    smem = pl.BlockSpec(memory_space=pltpu.SMEM)
    anywhere = pl.BlockSpec(memory_space=pl.ANY)

    whole = latent.reshape(block, channels)
    halves = whole[: block // 2], whole[block // 2 :]
    chosen = []
    if inner == 2:
        core = lax.rem(lax.axis_index("batch"), 2)
        stacked = jnp.concatenate([w_query, w_key, w_value], axis=0)
        chosen = [lax.dynamic_slice_in_dim(stacked, core * (3 * own // 2), 3 * own // 2, 0)]
    far_step = n // 2
    made_beside = []

    def beside_first(step, found):
        if step == 1:
            return chosen
        if step != far_step - 1:
            return []
        made_beside.append(
            pl.pallas_call(
                stats_kernel,
                out_shape=jax.ShapeDtypeStruct((24, channels), f32),
                in_specs=[vmem] * (2 * n - LATE),
                out_specs=vmem,
                compiler_params=pltpu.CompilerParams(vmem_limit_bytes=2 * MEBI),
                cost_estimate=pl.CostEstimate(
                    flops=6 * positions * channels,
                    bytes_accessed=2 * positions * channels,
                    transcendentals=0,
                ),
                name="stats",
            )(*in_order(found, n)[: 2 * n - LATE])
        )
        return made_beside[-1:]

    pieces = gather(halves, n, beside_first)
    stats = made_beside[0]
    if inner == 2:
        chosen, out_own = after(chosen + [w_out], pieces[-5:])
        chosen = send(chosen, [(0, 1)])
        far = send(out_own, FAR)
    else:
        sets = [list(range(at, at + inner)) for at in range(0, n, inner)]
        weights = jnp.stack([w_query, w_key, w_value])
        weights = lax.all_gather(weights, "patch", axis=1, tiled=True, axis_index_groups=sets)
        weights = [weights.reshape(3 * SET_CHANNELS, channels)]
        out_weights = [lax.all_gather(w_out, "patch", axis=0, tiled=True)]

    kernel = conv_weight.reshape(3, 3 * own, channels)
    bias = channel_bias.reshape(1, own)
    half_hidden = jax.ShapeDtypeStruct((own, positions // 2), bf16)
    flops = 9 * positions * channels * own
    first_hidden, act, residual = pl.pallas_call(
        functools.partial(conv_kernel, columns),
        out_shape=[
            half_hidden,
            jax.ShapeDtypeStruct((positions + 2 * columns, channels), bf16),
            jax.ShapeDtypeStruct((own, positions), f32),
        ],
        in_specs=[smem] + [vmem] * (2 * n + 3),
        out_specs=[vmem] * 3,
        compiler_params=pltpu.CompilerParams(vmem_limit_bytes=20 * MEBI),
        cost_estimate=pl.CostEstimate(
            flops=flops,
            bytes_accessed=2 * (positions * channels + 9 * channels * own),
            transcendentals=positions * channels,
        ),
        name="norm_conv",
    )(sources, *pieces, stats, kernel, bias)
    second_hidden = pl.pallas_call(
        functools.partial(second_conv_kernel, columns),
        out_shape=half_hidden,
        in_specs=[vmem] * 4,
        out_specs=vmem,
        compiler_params=pltpu.CompilerParams(vmem_limit_bytes=16 * MEBI),
        cost_estimate=pl.CostEstimate(flops=flops, bytes_accessed=flops // 1000, transcendentals=0),
        name="second_conv",
    )(act, residual, kernel, bias)

    def beside_second(step, found):
        if step != far_step - 1:
            return []
        count = n - LATE // 2
        made_beside.append(
            pl.pallas_call(
                functools.partial(early_kernel, n),
                out_shape=[
                    jax.ShapeDtypeStruct((count * own, positions), bf16),
                    jax.ShapeDtypeStruct((count * own, block), bf16),
                ],
                in_specs=[vmem] * (2 * count),
                out_specs=[vmem] * 2,
                compiler_params=pltpu.CompilerParams(vmem_limit_bytes=8 * MEBI),
                cost_estimate=pl.CostEstimate(
                    flops=8 * positions * channels,
                    bytes_accessed=4 * positions * channels,
                    transcendentals=0,
                ),
                name="early_norm",
            )(*in_order(found, n)[: 2 * count])
        )
        return made_beside[-1][:1]

    hidden_pieces = gather((first_hidden, second_hidden), n, beside_second)
    if inner == 2:
        chosen, far = after([chosen, far], [second_hidden])
        near = [chosen]
        near.append(swap(near[0], 1))
        weights = [w_query, w_key, w_value] + near
        far = [far, swap(far, 2)]

    made_rows = sum(weight.shape[0] for weight in weights)
    sums, some = pl.pallas_call(
        functools.partial(project_kernel, 2 * n),
        out_shape=[
            jax.ShapeDtypeStruct((made_rows, positions), f32),
            jax.ShapeDtypeStruct((channels, block), bf16),
        ],
        in_specs=[smem] + [vmem] * (LATE + len(weights)),
        out_specs=[vmem] * 2,
        scratch_shapes=[pltpu.VMEM((channels, positions), bf16)],
        compiler_params=pltpu.CompilerParams(vmem_limit_bytes=20 * MEBI),
        cost_estimate=pl.CostEstimate(
            flops=2 * positions * channels * made_rows,
            bytes_accessed=2 * (positions * channels + made_rows * channels),
            transcendentals=0,
        ),
        name="norm_project",
    )(sources, *made_beside[-1], *hidden_pieces[-LATE:-2], *weights)
    if inner == 2:
        far = after(far, hidden_pieces[-6:-2])
        place = lax.rem(lax.axis_index("batch"), QUAD)
        relayed = [send(jnp.where(place == QUAD - 1, far[1], far[0]), [(0, 1)])]
        relayed.append(send(far[1], [(0, 1), None]))
        far.append(swap(jnp.concatenate(far, axis=0), 1))
    one_block = jax.ShapeDtypeStruct((SET_CHANNELS, block), bf16)
    *sent, kept, made, key = pl.pallas_call(
        functools.partial(attention_kernel, 2 * n, inner),
        out_shape=[one_block] * len(SOONER)
        + [
            jax.ShapeDtypeStruct((channels, block), bf16),
            jax.ShapeDtypeStruct((made_rows, positions), bf16),
            jax.ShapeDtypeStruct((SET_HEADS, positions, HEAD_DIM), bf16),
        ],
        in_specs=[smem] + [vmem] * (4 + len(weights)),
        out_specs=[vmem] * (3 + len(SOONER)),
        scratch_shapes=[pltpu.VMEM((window_of(own), positions), bf16)],
        compiler_params=pltpu.CompilerParams(vmem_limit_bytes=28 * MEBI),
        cost_estimate=pl.CostEstimate(
            flops=2 * positions * window_of(own) * made_rows
            + 12 * positions * block * SET_CHANNELS,
            bytes_accessed=6 * made_rows * positions,
            transcendentals=positions * 3 * block * SET_HEADS,
        ),
        name="attention",
    )(sources, *hidden_pieces[-2:], *weights, sums, some)
    received = [None]
    for step, sent_block in zip(SOONER, sent):
        pairs = [(at, (at + step * inner) % n) for at in range(n)]
        received.append(lax.ppermute(sent_block, "patch", pairs))
    received[0] = pl.pallas_call(
        later_kernel,
        out_shape=one_block,
        in_specs=[vmem] * 2,
        out_specs=vmem,
        compiler_params=pltpu.CompilerParams(vmem_limit_bytes=16 * MEBI),
        cost_estimate=pl.CostEstimate(
            flops=4 * positions * block * SET_CHANNELS,
            bytes_accessed=8 * positions * SET_CHANNELS,
            transcendentals=positions * block * SET_HEADS,
        ),
        name="own_attention",
    )(made, key)
    if inner == 2:
        (relayed,) = after([jnp.concatenate(relayed, axis=0)], sent[:1])
        out_weights = [w_out] + far + [relayed, swap(relayed, 1)]

    output = pl.pallas_call(
        functools.partial(output_kernel, n),
        out_shape=jax.ShapeDtypeStruct((block, channels), bf16),
        in_specs=[vmem] * (OUTER + 1 + len(out_weights)),
        out_specs=vmem,
        scratch_shapes=[
            pltpu.VMEM((channels, block), bf16),
            pltpu.VMEM((channels, block), f32),
        ],
        compiler_params=pltpu.CompilerParams(vmem_limit_bytes=12 * MEBI),
        cost_estimate=pl.CostEstimate(
            flops=2 * block * channels * channels,
            bytes_accessed=2 * channels * (channels + 3 * block),
            transcendentals=0,
        ),
        name="project",
    )(*received, kept, *out_weights)
    return output.reshape(rows_local, columns, channels)


def solution(mesh):
    return jax.shard_map(
        on_device,
        mesh=mesh,
        in_specs=(
            P(("batch", "patch"), None, None),
            P(None, None, "patch", None),
            P("patch"),
            P("patch", None),
            P("patch", None),
            P("patch", None),
            P("patch", None),
        ),
        out_specs=P(("batch", "patch"), None, None),
        check_vma=False,
    )
```

```python
import functools

import jax
import jax.numpy as jnp
from jax import lax
from jax.experimental import pallas as pl
from jax.experimental.pallas import tpu as pltpu
from jax.sharding import PartitionSpec as P

C = 1280
HEADS = 20
HEAD_DIM = 64
GROUPS = 32
SPAN = C // GROUPS
OUTER = 4
SET_HEADS = HEADS // OUTER
SET_CHANNELS = SET_HEADS * HEAD_DIM
QUAD = 4
HANDED = (0, 2, 1, 3)
FAR = ((1, 0), (3, 0), (2, 0), (0, 1))
SOONER = tuple(range(1, OUTER))
WIDE = 256
EPSILON = 1e-05
LATE = 6
CHUNK = 16
MEBI = 1024 * 1024

f32 = jnp.float32
bf16 = jnp.bfloat16

NT = (((1,), (1,)), ((), ()))
NN = (((1,), (0,)), ((), ()))


def dot(left, right, dims=NN):
    return lax.dot_general(left, right, dims, preferred_element_type=f32)


def exact(row, member, dims=NN):
    high = row.astype(bf16).astype(f32)
    middle = (row - high).astype(bf16).astype(f32)
    parts = [high, middle, row - high - middle, jnp.zeros((13, row.shape[1]), f32)]
    return jnp.sum(dot(jnp.concatenate(parts, axis=0).astype(bf16), member, dims), axis=0, keepdims=True)


def stats_kernel(*refs):
    pieces, out_ref = refs[:-1], refs[-1]
    block = pieces[0].shape[0]
    steps = block // CHUNK

    def add(step, total):
        for piece in pieces[:2]:
            total = total + folded(piece[pl.ds(step * CHUNK, CHUNK), :].astype(f32))
        return total

    zero = jnp.zeros((8, C), f32)
    pivot = jnp.sum(lax.fori_loop(0, steps, add, zero), axis=0, keepdims=True) / (2 * block)
    first, second = add_moments(pieces, pivot, zero, zero)
    out_ref[0:8, :] = jnp.broadcast_to(pivot, (8, C))
    out_ref[8:16, :] = first
    out_ref[16:24, :] = second


def folded(rows):
    return rows[:8] + rows[8:]


def add_moments(pieces, pivot, first, second):
    def add(step, sums):
        first, second = sums
        for piece in pieces:
            away = piece[pl.ds(step * CHUNK, CHUNK), :].astype(f32) - pivot
            first = first + folded(away)
            second = second + folded(away * away)
        return first, second

    return lax.fori_loop(0, pieces[0].shape[0] // CHUNK, add, (first, second))


def conv_kernel(columns, sources_ref, *refs):
    count = len(refs) - 6
    pieces = refs[:count]
    stats_ref, kernel_ref, bias_ref = refs[count : count + 3]
    out_ref, act_ref, kept_ref = refs[count + 3 :]
    block = pieces[0].shape[0]
    positions = block * count
    own = out_ref.shape[0]
    me = lax.axis_index("patch")
    steps = block // CHUNK
    starts = [
        pl.multiple_of(sources_ref[me * count + index] * (2 * block) + (index % 2) * block, block)
        for index in range(count)
    ]

    member = (
        lax.broadcasted_iota(jnp.int32, (C, 128), 0) // SPAN
        == lax.broadcasted_iota(jnp.int32, (C, 128), 1)
    ).astype(bf16)

    def group_mean(per_channel):
        return exact(exact(per_channel, member) / SPAN, member, NT)

    pivot = stats_ref[0:1, :]
    first, second = add_moments(pieces[-LATE:], pivot, stats_ref[8:16, :], stats_ref[16:24, :])
    above = jnp.sum(first, axis=0, keepdims=True) / positions
    within = jnp.sum(second, axis=0, keepdims=True) / positions - above * above
    mean = pivot + above
    centre = group_mean(mean)
    spread = group_mean(within + (mean - centre) * (mean - centre))
    half_scale = 0.5 * lax.rsqrt(spread + EPSILON)

    act_ref[0:columns, :] = jnp.zeros((columns, C), bf16)
    act_ref[positions + columns :, :] = jnp.zeros((columns, C), bf16)

    def activate(step, carry):
        for start, piece in zip(starts, pieces):
            half = (piece[pl.ds(step * CHUNK, CHUNK), :].astype(f32) - centre) * half_scale
            value = half + half * jnp.tanh(half)
            row = pl.multiple_of(columns + start + step * CHUNK, CHUNK)
            act_ref[pl.ds(row, CHUNK), :] = value.astype(bf16)
        return carry

    lax.fori_loop(0, steps, activate, 0)

    window = window_of(own)
    base = jnp.minimum(lax.div(me * own, 128) * 128, C - window)
    lanes = pl.ds(pl.multiple_of(base, 128), window)
    choose = (
        lax.broadcasted_iota(jnp.int32, (own, window), 0) + (me * own - base)
        == lax.broadcasted_iota(jnp.int32, (own, window), 1)
    ).astype(bf16)
    for index in range(0, count, 2):
        pair = jnp.concatenate([pieces[index][:, lanes], pieces[index + 1][:, lanes]], axis=0)
        start = pl.multiple_of(starts[index], 2 * block)
        kept_ref[:, pl.ds(start, 2 * block)] = dot(choose, pair, NT)

    convolve(columns, 0, act_ref, kept_ref, kernel_ref, bias_ref, out_ref)


def second_conv_kernel(columns, act_ref, kept_ref, kernel_ref, bias_ref, out_ref):
    convolve(columns, out_ref.shape[1], act_ref, kept_ref, kernel_ref, bias_ref, out_ref)


def convolve(columns, start, act_ref, kept_ref, kernel_ref, bias_ref, out_ref):
    own = out_ref.shape[0]
    column = lax.broadcasted_iota(jnp.int32, (own, WIDE), 1) % columns
    square = (own, own)
    bias = jnp.where(
        lax.broadcasted_iota(jnp.int32, square, 0) == lax.broadcasted_iota(jnp.int32, square, 1),
        bias_ref[...],
        0.0,
    )
    bias = jnp.sum(bias, axis=1, keepdims=True)
    for low in range(0, out_ref.shape[1], WIDE):
        at = start + low
        taps = dot(kernel_ref[0], act_ref[at : at + WIDE, :], NT)
        for shift in (1, 2):
            first = at + shift * columns
            taps = taps + dot(kernel_ref[shift], act_ref[first : first + WIDE, :], NT)
        before = jnp.where(column > 0, pltpu.roll(taps[0:own], 1, 1), 0.0)
        after_ = jnp.where(column < columns - 1, pltpu.roll(taps[2 * own :], WIDE - 1, 1), 0.0)
        convolved = taps[own : 2 * own] + before + after_
        hidden = kept_ref[:, at : at + WIDE] + convolved + bias
        out_ref[:, low : low + WIDE] = hidden.astype(bf16)


def window_of(own):
    return min(C, (own + 127) // 128 * 128 + 128)


def norm_pair(pair):
    own = pair[0].shape[0]
    entries = float(2 * pair[0].shape[1] * SPAN)

    def whole(values):
        return jnp.sum(jnp.sum(values, axis=0, keepdims=True), axis=1, keepdims=True)

    def group_at(low):
        first, last = low // 16 * 16, -(-(low + SPAN) // 16) * 16
        return [ref[first:last, :].astype(f32)[low - first : low - first + SPAN] for ref in pair]

    lows = range(0, own, SPAN)
    means = [sum(whole(half) for half in group_at(low)) / entries for low in lows]
    squares = [
        sum(whole(jnp.square(half - mean)) for half in group_at(low))
        for low, mean in zip(lows, means)
    ]
    scales = [lax.rsqrt(square / entries + EPSILON) for square in squares]
    mean = jnp.concatenate([jnp.broadcast_to(one, (SPAN, 1)) for one in means], axis=0)
    scale = jnp.concatenate([jnp.broadcast_to(one, (SPAN, 1)) for one in scales], axis=0)
    return [((ref[...].astype(f32) - mean) * scale).astype(bf16) for ref in pair]


def own_lanes(pair, me, n):
    block = 2 * pair[0].shape[1] // n
    start = pl.multiple_of(lax.rem(me, n // 2) * block, block)
    low, high = (ref[:, pl.ds(start, block)] for ref in pair)
    return jnp.where(me < n // 2, low, high)


def early_kernel(n, *refs):
    pieces, outs = refs[:-2], refs[-2:]
    me = lax.axis_index("patch")
    own, part = pieces[0].shape
    for at in range(0, len(pieces), 2):
        pair = pieces[at : at + 2]
        rows = slice(at // 2 * own, (at // 2 + 1) * own)
        for half, normed in enumerate(norm_pair(pair)):
            outs[0][rows, half * part : (half + 1) * part] = normed
        outs[1][rows, :] = own_lanes(pair, me, n)


def project_kernel(count, sources_ref, *refs):
    early_ref, some_ref = refs[:2]
    pieces = refs[2:LATE]
    weight_refs = refs[LATE:-3]
    sums_ref, kept_ref, normed_ref = refs[-3:]
    own, part = pieces[0].shape
    me = lax.axis_index("patch")
    for at in range(0, count - 2, 2):
        rows = pl.ds(pl.multiple_of(sources_ref[me * count + at] * own, own), own)
        if at < count - LATE:
            there = slice(at // 2 * own, (at // 2 + 1) * own)
            normed_ref[rows, :] = early_ref[there, :]
            kept_ref[rows, :] = some_ref[there, :]
            continue
        pair = pieces[at - count + LATE :][:2]
        for half, normed in enumerate(norm_pair(pair)):
            normed_ref[rows, half * part : (half + 1) * part] = normed
        kept_ref[rows, :] = own_lanes(pair, me, count // 2)
    missing = pl.multiple_of(sources_ref[me * count + count - 2] * own, own)
    normed_ref[pl.ds(missing, own), :] = jnp.zeros((own, 2 * part), bf16)
    weights = jnp.concatenate([ref[...] for ref in weight_refs], axis=0)
    for at in range(0, 2 * part, WIDE):
        sums_ref[:, at : at + WIDE] = dot(weights, normed_ref[:, at : at + WIDE])


def attention_kernel(count, inner, sources_ref, *refs):
    pair = refs[:2]
    weight_refs = refs[2:-9]
    sums_ref, some_ref = refs[-9:-7]
    outs = refs[-7:-4]
    kept_ref, made_ref, key_ref, last_ref = refs[-4:]
    own, part = pair[0].shape
    n = count // 2
    me = lax.axis_index("patch")
    outer_at, inner_at = lax.div(me, inner), lax.rem(me, inner)
    source = sources_ref[me * count + count - 2]
    row = pl.multiple_of(source * own, own)
    kept_ref[...] = some_ref[...]
    kept_ref[pl.ds(row, own), :] = own_lanes(pair, me, n)

    window = last_ref.shape[0]
    base = jnp.minimum(lax.div(source * own, 128) * 128, C - window)
    lanes = pl.ds(pl.multiple_of(base, 128), window)
    last_ref[...] = jnp.zeros_like(last_ref)
    within = pl.ds(pl.multiple_of(source * own - base, 16), own)
    for half, normed in enumerate(norm_pair(pair)):
        last_ref[within, half * part : (half + 1) * part] = normed
    weights = jnp.concatenate([ref[:, lanes] for ref in weight_refs], axis=0)
    places = rows_of(weight_refs, own, inner, inner_at)
    for at in range(0, 2 * part, WIDE):
        made = dot(weights, last_ref[:, at : at + WIDE]) + sums_ref[:, at : at + WIDE]
        made = made.astype(bf16)
        for low, size, target in places:
            made_ref[pl.ds(target, size), at : at + WIDE] = made[low : low + size]

    for at in range(0, 2 * part, WIDE):
        for head in range(SET_HEADS):
            low = SET_CHANNELS + head * HEAD_DIM
            key = made_ref[low : low + HEAD_DIM, at : at + WIDE].astype(f32)
            key_ref[head, at : at + WIDE, :] = key.T.astype(bf16)

    targets = [lax.rem(outer_at + step, OUTER) * inner + inner_at for step in SOONER]
    attend(targets, made_ref, key_ref, outs)


def rows_of(weight_refs, own, inner, inner_at):
    if inner != 2:
        return [(0, weight_refs[0].shape[0], 0)]
    places = []
    for kind in range(3):
        place = kind * SET_CHANNELS + inner_at * own
        places.append((kind * own, own, pl.multiple_of(place, own)))
    core = lax.rem(lax.axis_index("batch"), 2)
    size = own // 2
    for order in range(2):
        half = core if order == 0 else 1 - core
        for at in range(3):
            part = 3 * half + at
            place = lax.div(part, 2) * SET_CHANNELS + (1 - inner_at) * own + lax.rem(part, 2) * size
            places.append((3 * own + (3 * order + at) * size, size, pl.multiple_of(place, 16)))
    return places


def later_kernel(made_ref, key_ref, out_ref):
    attend([lax.axis_index("patch")], made_ref, key_ref, [out_ref])


def attend(targets, made_ref, key_ref, outs):
    block = outs[0].shape[1]
    starts = [pl.multiple_of(target * block, block) for target in targets]
    for head in range(SET_HEADS):
        low = head * HEAD_DIM
        query = [made_ref[low : low + HEAD_DIM, pl.ds(start, block)] for start in starts]
        query = jnp.concatenate(query, axis=1).astype(f32) * HEAD_DIM ** (-0.5)
        scores = dot(key_ref[head], query.astype(bf16))
        peak = jnp.max(scores, axis=0, keepdims=True)
        unnormalized = jnp.exp(scores - peak)
        total = jnp.sum(unnormalized, axis=0, keepdims=True)
        value = made_ref[2 * SET_CHANNELS + low : 2 * SET_CHANNELS + low + HEAD_DIM, :]
        mixture = dot(value, unnormalized.astype(bf16))
        attended = (mixture / total).astype(bf16)
        for place, out in enumerate(outs):
            out[low : low + HEAD_DIM, :] = attended[:, place * block : (place + 1) * block]


def output_kernel(n, *refs):
    attended_refs = refs[:OUTER]
    hidden_ref = refs[OUTER]
    weight_refs = refs[OUTER + 1 : -3]
    out_ref, attended_ref, total_ref = refs[-3:]
    inner = n // OUTER
    own = C // n
    me = lax.axis_index("patch")
    outer_at, inner_at = lax.div(me, inner), lax.rem(me, inner)
    for step in range(OUTER):
        origin = lax.rem(outer_at + OUTER - step, OUTER)
        row = pl.multiple_of(origin * SET_CHANNELS, SET_CHANNELS)
        attended_ref[pl.ds(row, SET_CHANNELS), :] = attended_refs[step][...]
    attended = attended_ref[...]
    if inner != 2:
        total = dot(weight_refs[0][...], attended) + hidden_ref[...].astype(f32)
        out_ref[...] = total.T.astype(bf16)
        return

    total_ref[...] = hidden_ref[...].astype(f32)
    mine = lax.rem(lax.axis_index("batch"), QUAD)
    core = lax.rem(mine, 2)

    def add(weights, outer_step, inner_step, low=0):
        origin = lax.rem(outer_at + OUTER - outer_step, OUTER) * inner
        origin = origin + lax.rem(inner_at + inner_step, inner)
        rows = pl.ds(pl.multiple_of(origin * own + low, 16), weights.shape[0])
        total_ref[rows, :] += dot(weights, attended)

    own_ref, far_ref, across_ref, other_ref, mine_ref, others_ref = weight_refs
    side = lax.div(mine, 2)
    add(own_ref[...], 0, 0)
    far = [far_ref[...], across_ref[...], other_ref[:own, :], other_ref[own:, :]]
    for step, weights in zip(HANDED, far):
        which = jnp.bitwise_xor(mine, step)
        outer_step = jnp.where(which == 0, 1, jnp.where(which == 1, 3, jnp.where(which == 2, 2, 0)))
        add(weights, outer_step, lax.div(which, QUAD - 1))

    def add_relayed(two_ref, one_ref):
        add(two_ref[:own, :], 1 + side, 1)
        add(two_ref[own:, :], 2 - side, 1)
        add(one_ref[:own, :], 3, 1)

    @pl.when(core == 0)
    def _():
        add_relayed(mine_ref, others_ref)

    @pl.when(core == 1)
    def _():
        add_relayed(others_ref, mine_ref)

    out_ref[...] = total_ref[...].T.astype(bf16)


def ring_of(n):
    inner = n // OUTER
    path = [(0, 0)]
    for outer_at in range(OUTER):
        across = range(1, inner) if outer_at % 2 == 0 else range(inner - 1, 0, -1)
        path += [(outer_at, inner_at) for inner_at in across]
    path += [(outer_at, 0) for outer_at in range(OUTER - 1, 0, -1)]
    return [outer_at * inner + inner_at for outer_at, inner_at in path]


def pieces_of(n):
    far = n // 2
    return [0] + [away for step in range(1, far) for away in (-step, step)] + [far]


def sources_of(n):
    ring = ring_of(n)
    table = []
    for device in range(n):
        at = ring.index(device)
        table.append([ring[(at + away) % n] for away in pieces_of(n) for _ in (0, 1)])
    return table


def gather(halves, n, beside):
    ring = ring_of(n)
    forward = [(ring[at], ring[(at + 1) % n]) for at in range(n)]
    backward = [(target, start) for start, target in forward]
    far = n // 2
    found = {(0, 0): halves[0], (1, 0): halves[1]}
    for step in range(1, far + 1):
        for half in (0, 1):
            for sign, pairs in ((-1, forward), (1, backward)):
                if step == far and (half == 0) != (sign == -1):
                    continue
                found[half, sign * step] = lax.ppermute(
                    found[half, sign * (step - 1)], "patch", pairs
                )
        others = beside(step, found)
        if others:
            (found[0, -step],) = after([found[0, -step]], others)
    found[0, far] = found[0, -far]
    return in_order(found, n)


def in_order(found, n):
    places = [(half, away) for away in pieces_of(n) for half in (0, 1)]
    return [found[place] for place in places if place in found]


def send(block, shifts):
    batch, n = lax.axis_size("batch"), lax.axis_size("patch")
    pairs = []
    for at in range(batch):
        shift = shifts[at % len(shifts)]
        for start, target in moves(n, *shift) if shift else ():
            pairs.append((at * n + start, at * n + target))
    return lax.ppermute(block, ("batch", "patch"), pairs)


def swap(block, bit):
    pairs = [(at, at ^ bit) for at in range(lax.axis_size("batch"))]
    return lax.ppermute(block, "batch", pairs)


def moves(n, outer_step, inner_step):
    inner = n // OUTER
    pairs = []
    for start in range(n):
        outer_at = (start // inner + outer_step) % OUTER
        inner_at = (start % inner + inner_step) % inner
        pairs.append((start, outer_at * inner + inner_at))
    return pairs


def after(values, ready):
    anywhere = pl.BlockSpec(memory_space=pl.ANY)
    made = pl.pallas_call(
        lambda *refs: None,
        out_shape=[jax.ShapeDtypeStruct(value.shape, value.dtype) for value in values],
        in_specs=[anywhere] * (len(values) + len(ready)),
        out_specs=[anywhere] * len(values),
        input_output_aliases={at: at for at in range(len(values))},
        compiler_params=pltpu.CompilerParams(vmem_limit_bytes=MEBI),
        cost_estimate=pl.CostEstimate(flops=0, bytes_accessed=0, transcendentals=0),
        name="after",
    )(*values, *ready)
    return list(made)


def on_device(latent, conv_weight, channel_bias, w_query, w_key, w_value, w_out):
    rows_local, columns, channels = latent.shape
    n = lax.axis_size("patch")
    inner = n // OUTER
    own = channels // n
    block = rows_local * columns
    positions = block * n
    sources = jnp.asarray(sources_of(n), jnp.int32).reshape(-1)
    vmem = pl.BlockSpec(memory_space=pltpu.VMEM)
    smem = pl.BlockSpec(memory_space=pltpu.SMEM)
    anywhere = pl.BlockSpec(memory_space=pl.ANY)

    whole = latent.reshape(block, channels)
    halves = whole[: block // 2], whole[block // 2 :]
    chosen = []
    if inner == 2:
        core = lax.rem(lax.axis_index("batch"), 2)
        stacked = jnp.concatenate([w_query, w_key, w_value], axis=0)
        chosen = [lax.dynamic_slice_in_dim(stacked, core * (3 * own // 2), 3 * own // 2, 0)]
    far_step = n // 2
    made_beside = []

    def beside_first(step, found):
        if step == 1:
            return chosen
        if step != far_step - 1:
            return []
        made_beside.append(
            pl.pallas_call(
                stats_kernel,
                out_shape=jax.ShapeDtypeStruct((24, channels), f32),
                in_specs=[vmem] * (2 * n - LATE),
                out_specs=vmem,
                compiler_params=pltpu.CompilerParams(vmem_limit_bytes=2 * MEBI),
                cost_estimate=pl.CostEstimate(
                    flops=6 * positions * channels,
                    bytes_accessed=2 * positions * channels,
                    transcendentals=0,
                ),
                name="stats",
            )(*in_order(found, n)[: 2 * n - LATE])
        )
        return made_beside[-1:]

    pieces = gather(halves, n, beside_first)
    stats = made_beside[0]
    if inner == 2:
        chosen, out_own = after(chosen + [w_out], pieces[-5:])
        chosen = send(chosen, [(0, 1)])
        far = send(out_own, FAR)
    else:
        sets = [list(range(at, at + inner)) for at in range(0, n, inner)]
        weights = jnp.stack([w_query, w_key, w_value])
        weights = lax.all_gather(weights, "patch", axis=1, tiled=True, axis_index_groups=sets)
        weights = [weights.reshape(3 * SET_CHANNELS, channels)]
        out_weights = [lax.all_gather(w_out, "patch", axis=0, tiled=True)]

    kernel = conv_weight.reshape(3, 3 * own, channels)
    bias = channel_bias.reshape(1, own)
    half_hidden = jax.ShapeDtypeStruct((own, positions // 2), bf16)
    flops = 9 * positions * channels * own
    first_hidden, act, residual = pl.pallas_call(
        functools.partial(conv_kernel, columns),
        out_shape=[
            half_hidden,
            jax.ShapeDtypeStruct((positions + 2 * columns, channels), bf16),
            jax.ShapeDtypeStruct((own, positions), f32),
        ],
        in_specs=[smem] + [vmem] * (2 * n + 3),
        out_specs=[vmem] * 3,
        compiler_params=pltpu.CompilerParams(vmem_limit_bytes=20 * MEBI),
        cost_estimate=pl.CostEstimate(
            flops=flops,
            bytes_accessed=2 * (positions * channels + 9 * channels * own),
            transcendentals=positions * channels,
        ),
        name="norm_conv",
    )(sources, *pieces, stats, kernel, bias)
    second_hidden = pl.pallas_call(
        functools.partial(second_conv_kernel, columns),
        out_shape=half_hidden,
        in_specs=[vmem] * 4,
        out_specs=vmem,
        compiler_params=pltpu.CompilerParams(vmem_limit_bytes=16 * MEBI),
        cost_estimate=pl.CostEstimate(flops=flops, bytes_accessed=flops // 1000, transcendentals=0),
        name="second_conv",
    )(act, residual, kernel, bias)

    def beside_second(step, found):
        if step != far_step - 1:
            return []
        count = n - LATE // 2
        made_beside.append(
            pl.pallas_call(
                functools.partial(early_kernel, n),
                out_shape=[
                    jax.ShapeDtypeStruct((count * own, positions), bf16),
                    jax.ShapeDtypeStruct((count * own, block), bf16),
                ],
                in_specs=[vmem] * (2 * count),
                out_specs=[vmem] * 2,
                compiler_params=pltpu.CompilerParams(vmem_limit_bytes=8 * MEBI),
                cost_estimate=pl.CostEstimate(
                    flops=8 * positions * channels,
                    bytes_accessed=4 * positions * channels,
                    transcendentals=0,
                ),
                name="early_norm",
            )(*in_order(found, n)[: 2 * count])
        )
        return made_beside[-1][:1]

    hidden_pieces = gather((first_hidden, second_hidden), n, beside_second)
    if inner == 2:
        chosen, far = after([chosen, far], [second_hidden])
        near = [chosen]
        near.append(swap(near[0], 1))
        weights = [w_query, w_key, w_value] + near
        far = [far, swap(far, 2)]

    made_rows = sum(weight.shape[0] for weight in weights)
    sums, some = pl.pallas_call(
        functools.partial(project_kernel, 2 * n),
        out_shape=[
            jax.ShapeDtypeStruct((made_rows, positions), f32),
            jax.ShapeDtypeStruct((channels, block), bf16),
        ],
        in_specs=[smem] + [vmem] * (LATE + len(weights)),
        out_specs=[vmem] * 2,
        scratch_shapes=[pltpu.VMEM((channels, positions), bf16)],
        compiler_params=pltpu.CompilerParams(vmem_limit_bytes=20 * MEBI),
        cost_estimate=pl.CostEstimate(
            flops=2 * positions * channels * made_rows,
            bytes_accessed=2 * (positions * channels + made_rows * channels),
            transcendentals=0,
        ),
        name="norm_project",
    )(sources, *made_beside[-1], *hidden_pieces[-LATE:-2], *weights)
    if inner == 2:
        far = after(far, hidden_pieces[-6:-2])
        place = lax.rem(lax.axis_index("batch"), QUAD)
        relayed = [send(jnp.where(place == QUAD - 1, far[1], far[0]), [(0, 1)])]
        relayed.append(send(far[1], [(0, 1), None]))
        far.append(swap(jnp.concatenate(far, axis=0), 1))
    one_block = jax.ShapeDtypeStruct((SET_CHANNELS, block), bf16)
    *sent, kept, made, key = pl.pallas_call(
        functools.partial(attention_kernel, 2 * n, inner),
        out_shape=[one_block] * len(SOONER)
        + [
            jax.ShapeDtypeStruct((channels, block), bf16),
            jax.ShapeDtypeStruct((made_rows, positions), bf16),
            jax.ShapeDtypeStruct((SET_HEADS, positions, HEAD_DIM), bf16),
        ],
        in_specs=[smem] + [vmem] * (4 + len(weights)),
        out_specs=[vmem] * (3 + len(SOONER)),
        scratch_shapes=[pltpu.VMEM((window_of(own), positions), bf16)],
        compiler_params=pltpu.CompilerParams(vmem_limit_bytes=28 * MEBI),
        cost_estimate=pl.CostEstimate(
            flops=2 * positions * window_of(own) * made_rows
            + 12 * positions * block * SET_CHANNELS,
            bytes_accessed=6 * made_rows * positions,
            transcendentals=positions * 3 * block * SET_HEADS,
        ),
        name="attention",
    )(sources, *hidden_pieces[-2:], *weights, sums, some)
    received = [None]
    for step, sent_block in zip(SOONER, sent):
        pairs = [(at, (at + step * inner) % n) for at in range(n)]
        received.append(lax.ppermute(sent_block, "patch", pairs))
    received[0] = pl.pallas_call(
        later_kernel,
        out_shape=one_block,
        in_specs=[vmem] * 2,
        out_specs=vmem,
        compiler_params=pltpu.CompilerParams(vmem_limit_bytes=16 * MEBI),
        cost_estimate=pl.CostEstimate(
            flops=4 * positions * block * SET_CHANNELS,
            bytes_accessed=8 * positions * SET_CHANNELS,
            transcendentals=positions * block * SET_HEADS,
        ),
        name="own_attention",
    )(made, key)
    if inner == 2:
        (relayed,) = after([jnp.concatenate(relayed, axis=0)], received[1:2])
        out_weights = [w_out] + far + [relayed, swap(relayed, 1)]

    output = pl.pallas_call(
        functools.partial(output_kernel, n),
        out_shape=jax.ShapeDtypeStruct((block, channels), bf16),
        in_specs=[vmem] * (OUTER + 1 + len(out_weights)),
        out_specs=vmem,
        scratch_shapes=[
            pltpu.VMEM((channels, block), bf16),
            pltpu.VMEM((channels, block), f32),
        ],
        compiler_params=pltpu.CompilerParams(vmem_limit_bytes=12 * MEBI),
        cost_estimate=pl.CostEstimate(
            flops=2 * block * channels * channels,
            bytes_accessed=2 * channels * (channels + 3 * block),
            transcendentals=0,
        ),
        name="project",
    )(*received, kept, *out_weights)
    return output.reshape(rows_local, columns, channels)


def solution(mesh):
    return jax.shard_map(
        on_device,
        mesh=mesh,
        in_specs=(
            P(("batch", "patch"), None, None),
            P(None, None, "patch", None),
            P("patch"),
            P("patch", None),
            P("patch", None),
            P("patch", None),
            P("patch", None),
        ),
        out_specs=P(("batch", "patch"), None, None),
        check_vma=False,
    )
```

```python
import functools

import jax
import jax.numpy as jnp
from jax import lax
from jax.experimental import pallas as pl
from jax.experimental.pallas import tpu as pltpu
from jax.sharding import PartitionSpec as P

C = 1280
HEADS = 20
HEAD_DIM = 64
GROUPS = 32
SPAN = C // GROUPS
OUTER = 4
SET_HEADS = HEADS // OUTER
SET_CHANNELS = SET_HEADS * HEAD_DIM
QUAD = 4
HANDED = (0, 2, 1, 3)
FAR = ((1, 0), (3, 0), (2, 0), (0, 1))
SOONER = tuple(range(1, OUTER))
WIDE = 512
EPSILON = 1e-05
LATE = 6
CHUNK = 16
MEBI = 1024 * 1024

f32 = jnp.float32
bf16 = jnp.bfloat16

NT = (((1,), (1,)), ((), ()))
NN = (((1,), (0,)), ((), ()))


def dot(left, right, dims=NN):
    return lax.dot_general(left, right, dims, preferred_element_type=f32)


def exact(row, member, dims=NN):
    high = row.astype(bf16).astype(f32)
    middle = (row - high).astype(bf16).astype(f32)
    parts = [high, middle, row - high - middle, jnp.zeros((13, row.shape[1]), f32)]
    return jnp.sum(dot(jnp.concatenate(parts, axis=0).astype(bf16), member, dims), axis=0, keepdims=True)


def stats_kernel(*refs):
    pieces, out_ref = refs[:-1], refs[-1]
    block = pieces[0].shape[0]
    steps = block // CHUNK

    def add(step, total):
        for piece in pieces[:2]:
            total = total + folded(piece[pl.ds(step * CHUNK, CHUNK), :].astype(f32))
        return total

    zero = jnp.zeros((8, C), f32)
    pivot = jnp.sum(lax.fori_loop(0, steps, add, zero), axis=0, keepdims=True) / (2 * block)
    first, second = add_moments(pieces, pivot, zero, zero)
    out_ref[0:8, :] = jnp.broadcast_to(pivot, (8, C))
    out_ref[8:16, :] = first
    out_ref[16:24, :] = second


def folded(rows):
    return rows[:8] + rows[8:]


def add_moments(pieces, pivot, first, second):
    def add(step, sums):
        first, second = sums
        for piece in pieces:
            away = piece[pl.ds(step * CHUNK, CHUNK), :].astype(f32) - pivot
            first = first + folded(away)
            second = second + folded(away * away)
        return first, second

    return lax.fori_loop(0, pieces[0].shape[0] // CHUNK, add, (first, second))


def conv_kernel(columns, sources_ref, *refs):
    count = len(refs) - 6
    pieces = refs[:count]
    stats_ref, kernel_ref, bias_ref = refs[count : count + 3]
    out_ref, act_ref, kept_ref = refs[count + 3 :]
    block = pieces[0].shape[0]
    positions = block * count
    own = out_ref.shape[0]
    me = lax.axis_index("patch")
    steps = block // CHUNK
    starts = [
        pl.multiple_of(sources_ref[me * count + index] * (2 * block) + (index % 2) * block, block)
        for index in range(count)
    ]

    member = (
        lax.broadcasted_iota(jnp.int32, (C, 128), 0) // SPAN
        == lax.broadcasted_iota(jnp.int32, (C, 128), 1)
    ).astype(bf16)

    def group_mean(per_channel):
        return exact(exact(per_channel, member) / SPAN, member, NT)

    pivot = stats_ref[0:1, :]
    first, second = add_moments(pieces[-LATE:], pivot, stats_ref[8:16, :], stats_ref[16:24, :])
    above = jnp.sum(first, axis=0, keepdims=True) / positions
    within = jnp.sum(second, axis=0, keepdims=True) / positions - above * above
    mean = pivot + above
    centre = group_mean(mean)
    spread = group_mean(within + (mean - centre) * (mean - centre))
    half_scale = 0.5 * lax.rsqrt(spread + EPSILON)

    act_ref[0:columns, :] = jnp.zeros((columns, C), bf16)
    act_ref[positions + columns :, :] = jnp.zeros((columns, C), bf16)

    def activate(step, carry):
        for start, piece in zip(starts, pieces):
            half = (piece[pl.ds(step * CHUNK, CHUNK), :].astype(f32) - centre) * half_scale
            value = half + half * jnp.tanh(half)
            row = pl.multiple_of(columns + start + step * CHUNK, CHUNK)
            act_ref[pl.ds(row, CHUNK), :] = value.astype(bf16)
        return carry

    lax.fori_loop(0, steps, activate, 0)

    window = window_of(own)
    base = jnp.minimum(lax.div(me * own, 128) * 128, C - window)
    lanes = pl.ds(pl.multiple_of(base, 128), window)
    choose = (
        lax.broadcasted_iota(jnp.int32, (own, window), 0) + (me * own - base)
        == lax.broadcasted_iota(jnp.int32, (own, window), 1)
    ).astype(bf16)
    for index in range(0, count, 2):
        pair = jnp.concatenate([pieces[index][:, lanes], pieces[index + 1][:, lanes]], axis=0)
        start = pl.multiple_of(starts[index], 2 * block)
        kept_ref[:, pl.ds(start, 2 * block)] = dot(choose, pair, NT)

    convolve(columns, 0, act_ref, kept_ref, kernel_ref, bias_ref, out_ref)


def second_conv_kernel(columns, act_ref, kept_ref, kernel_ref, bias_ref, out_ref):
    convolve(columns, out_ref.shape[1], act_ref, kept_ref, kernel_ref, bias_ref, out_ref)


def convolve(columns, start, act_ref, kept_ref, kernel_ref, bias_ref, out_ref):
    own = out_ref.shape[0]
    column = lax.broadcasted_iota(jnp.int32, (own, WIDE), 1) % columns
    square = (own, own)
    bias = jnp.where(
        lax.broadcasted_iota(jnp.int32, square, 0) == lax.broadcasted_iota(jnp.int32, square, 1),
        bias_ref[...],
        0.0,
    )
    bias = jnp.sum(bias, axis=1, keepdims=True)
    for low in range(0, out_ref.shape[1], WIDE):
        at = start + low
        taps = dot(kernel_ref[0], act_ref[at : at + WIDE, :], NT)
        for shift in (1, 2):
            first = at + shift * columns
            taps = taps + dot(kernel_ref[shift], act_ref[first : first + WIDE, :], NT)
        before = jnp.where(column > 0, pltpu.roll(taps[0:own], 1, 1), 0.0)
        after_ = jnp.where(column < columns - 1, pltpu.roll(taps[2 * own :], WIDE - 1, 1), 0.0)
        convolved = taps[own : 2 * own] + before + after_
        hidden = kept_ref[:, at : at + WIDE] + convolved + bias
        out_ref[:, low : low + WIDE] = hidden.astype(bf16)


def window_of(own):
    return min(C, (own + 127) // 128 * 128 + 128)


def norm_pair(pair):
    own = pair[0].shape[0]
    entries = float(2 * pair[0].shape[1] * SPAN)

    def whole(values):
        return jnp.sum(jnp.sum(values, axis=0, keepdims=True), axis=1, keepdims=True)

    def group_at(low):
        first, last = low // 16 * 16, -(-(low + SPAN) // 16) * 16
        return [ref[first:last, :].astype(f32)[low - first : low - first + SPAN] for ref in pair]

    lows = range(0, own, SPAN)
    means = [sum(whole(half) for half in group_at(low)) / entries for low in lows]
    squares = [
        sum(whole(jnp.square(half - mean)) for half in group_at(low))
        for low, mean in zip(lows, means)
    ]
    scales = [lax.rsqrt(square / entries + EPSILON) for square in squares]
    mean = jnp.concatenate([jnp.broadcast_to(one, (SPAN, 1)) for one in means], axis=0)
    scale = jnp.concatenate([jnp.broadcast_to(one, (SPAN, 1)) for one in scales], axis=0)
    return [((ref[...].astype(f32) - mean) * scale).astype(bf16) for ref in pair]


def own_lanes(pair, me, n):
    block = 2 * pair[0].shape[1] // n
    start = pl.multiple_of(lax.rem(me, n // 2) * block, block)
    low, high = (ref[:, pl.ds(start, block)] for ref in pair)
    return jnp.where(me < n // 2, low, high)


def early_kernel(n, *refs):
    pieces, outs = refs[:-2], refs[-2:]
    me = lax.axis_index("patch")
    own, part = pieces[0].shape
    for at in range(0, len(pieces), 2):
        pair = pieces[at : at + 2]
        rows = slice(at // 2 * own, (at // 2 + 1) * own)
        for half, normed in enumerate(norm_pair(pair)):
            outs[0][rows, half * part : (half + 1) * part] = normed
        outs[1][rows, :] = own_lanes(pair, me, n)


def project_kernel(count, sources_ref, *refs):
    early_ref, some_ref = refs[:2]
    pieces = refs[2:LATE]
    weight_refs = refs[LATE:-3]
    sums_ref, kept_ref, normed_ref = refs[-3:]
    own, part = pieces[0].shape
    me = lax.axis_index("patch")
    for at in range(0, count - 2, 2):
        rows = pl.ds(pl.multiple_of(sources_ref[me * count + at] * own, own), own)
        if at < count - LATE:
            there = slice(at // 2 * own, (at // 2 + 1) * own)
            normed_ref[rows, :] = early_ref[there, :]
            kept_ref[rows, :] = some_ref[there, :]
            continue
        pair = pieces[at - count + LATE :][:2]
        for half, normed in enumerate(norm_pair(pair)):
            normed_ref[rows, half * part : (half + 1) * part] = normed
        kept_ref[rows, :] = own_lanes(pair, me, count // 2)
    missing = pl.multiple_of(sources_ref[me * count + count - 2] * own, own)
    normed_ref[pl.ds(missing, own), :] = jnp.zeros((own, 2 * part), bf16)
    weights = jnp.concatenate([ref[...] for ref in weight_refs], axis=0)
    for at in range(0, 2 * part, WIDE):
        sums_ref[:, at : at + WIDE] = dot(weights, normed_ref[:, at : at + WIDE])


def attention_kernel(count, inner, sources_ref, *refs):
    pair = refs[:2]
    weight_refs = refs[2:-9]
    sums_ref, some_ref = refs[-9:-7]
    outs = refs[-7:-4]
    kept_ref, made_ref, key_ref, last_ref = refs[-4:]
    own, part = pair[0].shape
    n = count // 2
    me = lax.axis_index("patch")
    outer_at, inner_at = lax.div(me, inner), lax.rem(me, inner)
    source = sources_ref[me * count + count - 2]
    row = pl.multiple_of(source * own, own)
    kept_ref[...] = some_ref[...]
    kept_ref[pl.ds(row, own), :] = own_lanes(pair, me, n)

    window = last_ref.shape[0]
    base = jnp.minimum(lax.div(source * own, 128) * 128, C - window)
    lanes = pl.ds(pl.multiple_of(base, 128), window)
    last_ref[...] = jnp.zeros_like(last_ref)
    within = pl.ds(pl.multiple_of(source * own - base, 16), own)
    for half, normed in enumerate(norm_pair(pair)):
        last_ref[within, half * part : (half + 1) * part] = normed
    weights = jnp.concatenate([ref[:, lanes] for ref in weight_refs], axis=0)
    places = rows_of(weight_refs, own, inner, inner_at)
    for at in range(0, 2 * part, WIDE):
        made = dot(weights, last_ref[:, at : at + WIDE]) + sums_ref[:, at : at + WIDE]
        made = made.astype(bf16)
        for low, size, target in places:
            made_ref[pl.ds(target, size), at : at + WIDE] = made[low : low + size]

    for at in range(0, 2 * part, WIDE):
        for head in range(SET_HEADS):
            low = SET_CHANNELS + head * HEAD_DIM
            key = made_ref[low : low + HEAD_DIM, at : at + WIDE].astype(f32)
            key_ref[head, at : at + WIDE, :] = key.T.astype(bf16)

    targets = [lax.rem(outer_at + step, OUTER) * inner + inner_at for step in SOONER]
    attend(targets, made_ref, key_ref, outs)


def rows_of(weight_refs, own, inner, inner_at):
    if inner != 2:
        return [(0, weight_refs[0].shape[0], 0)]
    places = []
    for kind in range(3):
        place = kind * SET_CHANNELS + inner_at * own
        places.append((kind * own, own, pl.multiple_of(place, own)))
    core = lax.rem(lax.axis_index("batch"), 2)
    size = own // 2
    for order in range(2):
        half = core if order == 0 else 1 - core
        for at in range(3):
            part = 3 * half + at
            place = lax.div(part, 2) * SET_CHANNELS + (1 - inner_at) * own + lax.rem(part, 2) * size
            places.append((3 * own + (3 * order + at) * size, size, pl.multiple_of(place, 16)))
    return places


def later_kernel(made_ref, key_ref, out_ref):
    attend([lax.axis_index("patch")], made_ref, key_ref, [out_ref])


def attend(targets, made_ref, key_ref, outs):
    block = outs[0].shape[1]
    starts = [pl.multiple_of(target * block, block) for target in targets]
    for head in range(SET_HEADS):
        low = head * HEAD_DIM
        query = [made_ref[low : low + HEAD_DIM, pl.ds(start, block)] for start in starts]
        query = jnp.concatenate(query, axis=1).astype(f32) * HEAD_DIM ** (-0.5)
        scores = dot(key_ref[head], query.astype(bf16))
        peak = jnp.max(scores, axis=0, keepdims=True)
        unnormalized = jnp.exp(scores - peak)
        total = jnp.sum(unnormalized, axis=0, keepdims=True)
        value = made_ref[2 * SET_CHANNELS + low : 2 * SET_CHANNELS + low + HEAD_DIM, :]
        mixture = dot(value, unnormalized.astype(bf16))
        attended = (mixture / total).astype(bf16)
        for place, out in enumerate(outs):
            out[low : low + HEAD_DIM, :] = attended[:, place * block : (place + 1) * block]


def output_kernel(n, *refs):
    attended_refs = refs[:OUTER]
    hidden_ref = refs[OUTER]
    weight_refs = refs[OUTER + 1 : -3]
    out_ref, attended_ref, total_ref = refs[-3:]
    inner = n // OUTER
    own = C // n
    me = lax.axis_index("patch")
    outer_at, inner_at = lax.div(me, inner), lax.rem(me, inner)
    for step in range(OUTER):
        origin = lax.rem(outer_at + OUTER - step, OUTER)
        row = pl.multiple_of(origin * SET_CHANNELS, SET_CHANNELS)
        attended_ref[pl.ds(row, SET_CHANNELS), :] = attended_refs[step][...]
    attended = attended_ref[...]
    if inner != 2:
        total = dot(weight_refs[0][...], attended) + hidden_ref[...].astype(f32)
        out_ref[...] = total.T.astype(bf16)
        return

    total_ref[...] = hidden_ref[...].astype(f32)
    mine = lax.rem(lax.axis_index("batch"), QUAD)
    core = lax.rem(mine, 2)

    def add(weights, outer_step, inner_step, low=0):
        origin = lax.rem(outer_at + OUTER - outer_step, OUTER) * inner
        origin = origin + lax.rem(inner_at + inner_step, inner)
        rows = pl.ds(pl.multiple_of(origin * own + low, 16), weights.shape[0])
        total_ref[rows, :] += dot(weights, attended)

    own_ref, far_ref, across_ref, other_ref, mine_ref, others_ref = weight_refs
    side = lax.div(mine, 2)
    add(own_ref[...], 0, 0)
    far = [far_ref[...], across_ref[...], other_ref[:own, :], other_ref[own:, :]]
    for step, weights in zip(HANDED, far):
        which = jnp.bitwise_xor(mine, step)
        outer_step = jnp.where(which == 0, 1, jnp.where(which == 1, 3, jnp.where(which == 2, 2, 0)))
        add(weights, outer_step, lax.div(which, QUAD - 1))

    def add_relayed(two_ref, one_ref):
        add(two_ref[:own, :], 1 + side, 1)
        add(two_ref[own:, :], 2 - side, 1)
        add(one_ref[:own, :], 3, 1)

    @pl.when(core == 0)
    def _():
        add_relayed(mine_ref, others_ref)

    @pl.when(core == 1)
    def _():
        add_relayed(others_ref, mine_ref)

    out_ref[...] = total_ref[...].T.astype(bf16)


def ring_of(n):
    inner = n // OUTER
    path = [(0, 0)]
    for outer_at in range(OUTER):
        across = range(1, inner) if outer_at % 2 == 0 else range(inner - 1, 0, -1)
        path += [(outer_at, inner_at) for inner_at in across]
    path += [(outer_at, 0) for outer_at in range(OUTER - 1, 0, -1)]
    return [outer_at * inner + inner_at for outer_at, inner_at in path]


def pieces_of(n):
    far = n // 2
    return [0] + [away for step in range(1, far) for away in (-step, step)] + [far]


def sources_of(n):
    ring = ring_of(n)
    table = []
    for device in range(n):
        at = ring.index(device)
        table.append([ring[(at + away) % n] for away in pieces_of(n) for _ in (0, 1)])
    return table


def gather(halves, n, beside):
    ring = ring_of(n)
    forward = [(ring[at], ring[(at + 1) % n]) for at in range(n)]
    backward = [(target, start) for start, target in forward]
    far = n // 2
    found = {(0, 0): halves[0], (1, 0): halves[1]}
    for step in range(1, far + 1):
        for half in (0, 1):
            for sign, pairs in ((-1, forward), (1, backward)):
                if step == far and (half == 0) != (sign == -1):
                    continue
                found[half, sign * step] = lax.ppermute(
                    found[half, sign * (step - 1)], "patch", pairs
                )
        others = beside(step, found)
        if others:
            (found[0, -step],) = after([found[0, -step]], others)
    found[0, far] = found[0, -far]
    return in_order(found, n)


def in_order(found, n):
    places = [(half, away) for away in pieces_of(n) for half in (0, 1)]
    return [found[place] for place in places if place in found]


def send(block, shifts):
    batch, n = lax.axis_size("batch"), lax.axis_size("patch")
    pairs = []
    for at in range(batch):
        shift = shifts[at % len(shifts)]
        for start, target in moves(n, *shift) if shift else ():
            pairs.append((at * n + start, at * n + target))
    return lax.ppermute(block, ("batch", "patch"), pairs)


def swap(block, bit):
    pairs = [(at, at ^ bit) for at in range(lax.axis_size("batch"))]
    return lax.ppermute(block, "batch", pairs)


def moves(n, outer_step, inner_step):
    inner = n // OUTER
    pairs = []
    for start in range(n):
        outer_at = (start // inner + outer_step) % OUTER
        inner_at = (start % inner + inner_step) % inner
        pairs.append((start, outer_at * inner + inner_at))
    return pairs


def after(values, ready):
    anywhere = pl.BlockSpec(memory_space=pl.ANY)
    made = pl.pallas_call(
        lambda *refs: None,
        out_shape=[jax.ShapeDtypeStruct(value.shape, value.dtype) for value in values],
        in_specs=[anywhere] * (len(values) + len(ready)),
        out_specs=[anywhere] * len(values),
        input_output_aliases={at: at for at in range(len(values))},
        compiler_params=pltpu.CompilerParams(vmem_limit_bytes=MEBI),
        cost_estimate=pl.CostEstimate(flops=0, bytes_accessed=0, transcendentals=0),
        name="after",
    )(*values, *ready)
    return list(made)


def on_device(latent, conv_weight, channel_bias, w_query, w_key, w_value, w_out):
    rows_local, columns, channels = latent.shape
    n = lax.axis_size("patch")
    inner = n // OUTER
    own = channels // n
    block = rows_local * columns
    positions = block * n
    sources = jnp.asarray(sources_of(n), jnp.int32).reshape(-1)
    vmem = pl.BlockSpec(memory_space=pltpu.VMEM)
    smem = pl.BlockSpec(memory_space=pltpu.SMEM)
    anywhere = pl.BlockSpec(memory_space=pl.ANY)

    whole = latent.reshape(block, channels)
    halves = whole[: block // 2], whole[block // 2 :]
    chosen = []
    if inner == 2:
        core = lax.rem(lax.axis_index("batch"), 2)
        stacked = jnp.concatenate([w_query, w_key, w_value], axis=0)
        chosen = [lax.dynamic_slice_in_dim(stacked, core * (3 * own // 2), 3 * own // 2, 0)]
    far_step = n // 2
    made_beside = []

    def beside_first(step, found):
        if step == 1:
            return chosen
        if step != far_step - 1:
            return []
        made_beside.append(
            pl.pallas_call(
                stats_kernel,
                out_shape=jax.ShapeDtypeStruct((24, channels), f32),
                in_specs=[vmem] * (2 * n - LATE),
                out_specs=vmem,
                compiler_params=pltpu.CompilerParams(vmem_limit_bytes=2 * MEBI),
                cost_estimate=pl.CostEstimate(
                    flops=6 * positions * channels,
                    bytes_accessed=2 * positions * channels,
                    transcendentals=0,
                ),
                name="stats",
            )(*in_order(found, n)[: 2 * n - LATE])
        )
        return made_beside[-1:]

    pieces = gather(halves, n, beside_first)
    stats = made_beside[0]
    if inner == 2:
        chosen, out_own = after(chosen + [w_out], pieces[-5:])
        chosen = send(chosen, [(0, 1)])
        far = send(out_own, FAR)
    else:
        sets = [list(range(at, at + inner)) for at in range(0, n, inner)]
        weights = jnp.stack([w_query, w_key, w_value])
        weights = lax.all_gather(weights, "patch", axis=1, tiled=True, axis_index_groups=sets)
        weights = [weights.reshape(3 * SET_CHANNELS, channels)]
        out_weights = [lax.all_gather(w_out, "patch", axis=0, tiled=True)]

    kernel = conv_weight.reshape(3, 3 * own, channels)
    bias = channel_bias.reshape(1, own)
    half_hidden = jax.ShapeDtypeStruct((own, positions // 2), bf16)
    flops = 9 * positions * channels * own
    first_hidden, act, residual = pl.pallas_call(
        functools.partial(conv_kernel, columns),
        out_shape=[
            half_hidden,
            jax.ShapeDtypeStruct((positions + 2 * columns, channels), bf16),
            jax.ShapeDtypeStruct((own, positions), f32),
        ],
        in_specs=[smem] + [vmem] * (2 * n + 3),
        out_specs=[vmem] * 3,
        compiler_params=pltpu.CompilerParams(vmem_limit_bytes=20 * MEBI),
        cost_estimate=pl.CostEstimate(
            flops=flops,
            bytes_accessed=2 * (positions * channels + 9 * channels * own),
            transcendentals=positions * channels,
        ),
        name="norm_conv",
    )(sources, *pieces, stats, kernel, bias)
    second_hidden = pl.pallas_call(
        functools.partial(second_conv_kernel, columns),
        out_shape=half_hidden,
        in_specs=[vmem] * 4,
        out_specs=vmem,
        compiler_params=pltpu.CompilerParams(vmem_limit_bytes=16 * MEBI),
        cost_estimate=pl.CostEstimate(flops=flops, bytes_accessed=flops // 1000, transcendentals=0),
        name="second_conv",
    )(act, residual, kernel, bias)

    def beside_second(step, found):
        if step != far_step - 1:
            return []
        count = n - LATE // 2
        made_beside.append(
            pl.pallas_call(
                functools.partial(early_kernel, n),
                out_shape=[
                    jax.ShapeDtypeStruct((count * own, positions), bf16),
                    jax.ShapeDtypeStruct((count * own, block), bf16),
                ],
                in_specs=[vmem] * (2 * count),
                out_specs=[vmem] * 2,
                compiler_params=pltpu.CompilerParams(vmem_limit_bytes=8 * MEBI),
                cost_estimate=pl.CostEstimate(
                    flops=8 * positions * channels,
                    bytes_accessed=4 * positions * channels,
                    transcendentals=0,
                ),
                name="early_norm",
            )(*in_order(found, n)[: 2 * count])
        )
        return made_beside[-1][:1]

    hidden_pieces = gather((first_hidden, second_hidden), n, beside_second)
    if inner == 2:
        chosen, far = after([chosen, far], [second_hidden])
        near = [chosen]
        near.append(swap(near[0], 1))
        weights = [w_query, w_key, w_value] + near
        far = [far, swap(far, 2)]

    made_rows = sum(weight.shape[0] for weight in weights)
    sums, some = pl.pallas_call(
        functools.partial(project_kernel, 2 * n),
        out_shape=[
            jax.ShapeDtypeStruct((made_rows, positions), f32),
            jax.ShapeDtypeStruct((channels, block), bf16),
        ],
        in_specs=[smem] + [vmem] * (LATE + len(weights)),
        out_specs=[vmem] * 2,
        scratch_shapes=[pltpu.VMEM((channels, positions), bf16)],
        compiler_params=pltpu.CompilerParams(vmem_limit_bytes=20 * MEBI),
        cost_estimate=pl.CostEstimate(
            flops=2 * positions * channels * made_rows,
            bytes_accessed=2 * (positions * channels + made_rows * channels),
            transcendentals=0,
        ),
        name="norm_project",
    )(sources, *made_beside[-1], *hidden_pieces[-LATE:-2], *weights)
    if inner == 2:
        far = after(far, hidden_pieces[-6:-2])
        place = lax.rem(lax.axis_index("batch"), QUAD)
        relayed = [send(jnp.where(place == QUAD - 1, far[1], far[0]), [(0, 1)])]
        relayed.append(send(far[1], [(0, 1), None]))
        far.append(swap(jnp.concatenate(far, axis=0), 1))
    one_block = jax.ShapeDtypeStruct((SET_CHANNELS, block), bf16)
    *sent, kept, made, key = pl.pallas_call(
        functools.partial(attention_kernel, 2 * n, inner),
        out_shape=[one_block] * len(SOONER)
        + [
            jax.ShapeDtypeStruct((channels, block), bf16),
            jax.ShapeDtypeStruct((made_rows, positions), bf16),
            jax.ShapeDtypeStruct((SET_HEADS, positions, HEAD_DIM), bf16),
        ],
        in_specs=[smem] + [vmem] * (4 + len(weights)),
        out_specs=[vmem] * (3 + len(SOONER)),
        scratch_shapes=[pltpu.VMEM((window_of(own), positions), bf16)],
        compiler_params=pltpu.CompilerParams(vmem_limit_bytes=28 * MEBI),
        cost_estimate=pl.CostEstimate(
            flops=2 * positions * window_of(own) * made_rows
            + 12 * positions * block * SET_CHANNELS,
            bytes_accessed=6 * made_rows * positions,
            transcendentals=positions * 3 * block * SET_HEADS,
        ),
        name="attention",
    )(sources, *hidden_pieces[-2:], *weights, sums, some)
    received = [None]
    for step, sent_block in zip(SOONER, sent):
        pairs = [(at, (at + step * inner) % n) for at in range(n)]
        received.append(lax.ppermute(sent_block, "patch", pairs))
    received[0] = pl.pallas_call(
        later_kernel,
        out_shape=one_block,
        in_specs=[vmem] * 2,
        out_specs=vmem,
        compiler_params=pltpu.CompilerParams(vmem_limit_bytes=16 * MEBI),
        cost_estimate=pl.CostEstimate(
            flops=4 * positions * block * SET_CHANNELS,
            bytes_accessed=8 * positions * SET_CHANNELS,
            transcendentals=positions * block * SET_HEADS,
        ),
        name="own_attention",
    )(made, key)
    if inner == 2:
        (relayed,) = after([jnp.concatenate(relayed, axis=0)], sent[:1])
        out_weights = [w_out] + far + [relayed, swap(relayed, 1)]

    output = pl.pallas_call(
        functools.partial(output_kernel, n),
        out_shape=jax.ShapeDtypeStruct((block, channels), bf16),
        in_specs=[vmem] * (OUTER + 1 + len(out_weights)),
        out_specs=vmem,
        scratch_shapes=[
            pltpu.VMEM((channels, block), bf16),
            pltpu.VMEM((channels, block), f32),
        ],
        compiler_params=pltpu.CompilerParams(vmem_limit_bytes=12 * MEBI),
        cost_estimate=pl.CostEstimate(
            flops=2 * block * channels * channels,
            bytes_accessed=2 * channels * (channels + 3 * block),
            transcendentals=0,
        ),
        name="project",
    )(*received, kept, *out_weights)
    return output.reshape(rows_local, columns, channels)


def solution(mesh):
    return jax.shard_map(
        on_device,
        mesh=mesh,
        in_specs=(
            P(("batch", "patch"), None, None),
            P(None, None, "patch", None),
            P("patch"),
            P("patch", None),
            P("patch", None),
            P("patch", None),
            P("patch", None),
        ),
        out_specs=P(("batch", "patch"), None, None),
        check_vma=False,
    )
```
